32 devices in a mesh: leaf: 4 (over z), front: 8 (over y, x, core).
Axes of the slice: x: 2, y: 2, z: 4, core: 2. Of those that a mesh axis runs over, the one named last changes fastest.
Arguments:
- leaf_lower_inv: float32 [2, 4, 512, 512], P(None, 'leaf', 'front'), may hold values from -0.1875 to 0.1875
- leaf_upper_inv: float32 [2, 4, 512, 512], P(None, 'leaf', 'front'), may hold values from -0.1875 to 0.1875
- leaf_to_mid_lower: float32 [2, 4, 1024, 512], P(None, 'leaf', 'front'), may hold values from -0.125 to 0.125
- leaf_to_root_lower: float32 [2, 4, 2048, 512], P(None, 'leaf', 'front'), may hold values from -0.125 to 0.125
- leaf_to_mid_upper: float32 [2, 4, 512, 1024], P(None, 'leaf', None, 'front'), may hold values from -0.125 to 0.125
- leaf_to_root_upper: float32 [2, 4, 512, 2048], P(None, 'leaf', None, 'front'), may hold values from -0.09375 to 0.09375
- mid_lower_inv: float32 [2, 2, 1024, 1024], P(None, None, 'front'), may hold values from -0.125 to 0.125
- mid_upper_inv: float32 [2, 2, 1024, 1024], P(None, None, 'front'), may hold values from -0.125 to 0.125
- mid_to_root_lower: float32 [2, 2, 2048, 1024], P(None, None, 'front'), may hold values from -0.09375 to 0.09375
- mid_to_root_upper: float32 [2, 2, 1024, 2048], P(None, None, None, 'front'), may hold values from -0.09375 to 0.09375
- root_lower_inv: float32 [2, 2048, 2048], P(None, 'front'), may hold values from -0.09375 to 0.09375
- root_upper_inv: float32 [2, 2048, 2048], P(None, 'front'), may hold values from -0.09375 to 0.09375
- leaf_sources: float32 [2, 2048, 32], P(None, ('leaf', 'front')), may hold values from -6 to 6
- mid_sources: float32 [2, 2, 1024, 32], P(None, None, 'front'), may hold values from -6 to 6
- root_sources: float32 [2, 2048, 32], P(None, 'front'), may hold values from -6 to 6
- receiver_data: float32 [2, 1024, 32], P(None, ('leaf', 'front')), may hold values from -6 to 6
- receiver_block: int32 [1024, 1], P(('leaf', 'front')), may hold values from 0 to 31; in each aligned block of 32 rows (0 to 31, 32 to 63, ...) at most 2 rows name the same one
- receiver_offset: int32 [1024], P(('leaf', 'front')), may hold values from 0 to 63
Outputs:
- leaf_field: float32 [2, 2048, 32], P(None, ('leaf', 'front'))
- mid_field: float32 [2, 2, 1024, 32], P(None, None, 'front')
- root_field: float32 [2, 2048, 32], P(None, 'front')
- leaf_adjoint: float32 [2, 2048, 32], P(None, ('leaf', 'front'))
- mid_adjoint: float32 [2, 2, 1024, 32], P(None, None, 'front')
- root_adjoint: float32 [2, 2048, 32], P(None, 'front')
The draws below stay inside these ranges and needn't reach their ends.
Inputs may be any that keep to these rules, and one draw needn't show every extreme that they name: `receiver_block`: among the 32 receivers of one device, at most 2 name the same block.
All inputs are finite; a program needn't handle non-finite values.
Results may differ from the reference program's by a relative error of at most 0.00018.
Values sent between devices are 32-bit elements; how exact they have to be, the bound alone decides.
No kernel may reach another device: no remote copies, remote signals or barrier semaphores. Data moves between devices by JAX's collectives and lax.ppermute only.
A program may use at most 64 MiB of HBM per device.

```python
import math
import jax
import jax.numpy as jnp
import numpy as np
from jax import lax

S0 = 512
S1 = 1024
S2 = 2048
NRHS = 32
CAP = 2
NREC_DEV = 32
RECEIVERS = 1024
LEAF_ROWS = 64
N_LEAF = 4
DEVICES = 32


def set_ends(drawn, rng, smallest, top_value):
    place = [jax.random.randint(jax.random.fold_in(rng, axis), (), 0, length) for axis, length in enumerate(drawn.shape)]
    main_axis = drawn.shape.index(max(drawn.shape))
    neighbour = place[:main_axis] + [(place[main_axis] + 1) % drawn.shape[main_axis]] + place[main_axis + 1:]
    return drawn.at[tuple(place)].set(smallest).at[tuple(neighbour)].set(top_value)


def with_spikes(values, own_key, source, target, shards_of, factor):
    def block_of(position):
        return (jnp.arange(values.shape[position]) // (values.shape[position] // shards_of)).reshape((-1,) + (1,) * (values.ndim - 1 - position))

    one_side = jax.random.permutation(own_key, shards_of)[block_of(target)]
    far = (block_of(target) + shards_of // 2) % shards_of
    return jnp.where((block_of(source) == one_side) | (block_of(source) == far), factor * values, values)


def shard_levels(stream_key, extent, shards, smallest, top_value):
    def one(dim, parts):
        heights = jax.random.uniform(jax.random.fold_in(jax.random.fold_in(stream_key, 6), dim), (parts,), jnp.float32, smallest / len(shards), top_value / len(shards))
        return jnp.repeat(jnp.exp(heights), extent[dim] // parts).reshape((-1,) + (1,) * (len(extent) - dim - 1))

    gain = one(*shards[0])
    for cut in shards[1:]:
        gain = gain * one(*cut)
    return gain


def routed_block(rng, own, number, rows, amount, top, bound, lean):
    order = jax.random.permutation(rng, amount)
    heavy_load, ordinary = load_shares(amount, rows * top, bound, lean, True), load_shares(amount, rows * top, bound, lean, False)
    places = jnp.arange(amount)

    def named(lengths, turn):
        used = int((lengths > 0).sum())
        fixed = max(1, used // 4)
        passed = fixed + (places - fixed + turn * (used - fixed)) % max(1, amount - fixed)
        return jnp.zeros((amount,), jnp.int32).at[order[jnp.where(places < fixed, places, passed)]].set(jnp.asarray(lengths, jnp.int32))

    lengths = jnp.where(number % 4 == 0, named(heavy_load, number // 4), named(ordinary, number - number // 4 - 1))
    mixed = jax.random.permutation(jax.random.fold_in(own, 3), amount)
    donor, sink = mixed[0:amount // 2 * 2:2], mixed[1:amount // 2 * 2:2]
    room = jnp.minimum(lengths[donor] - 1, bound - lengths[sink]) // 2
    room = jnp.where((donor == order[0]) | (sink == order[0]) | (lengths[sink] == 0), 0, jnp.maximum(room, 0))
    passed = jax.random.randint(jax.random.fold_in(own, 4), (amount // 2,), 0, 1 << 20) % (room + 1)
    lengths = lengths.at[donor].add(-passed).at[sink].add(passed)
    items = jnp.searchsorted(jnp.cumsum(lengths), jnp.arange(rows * top), side="right").astype(jnp.int32)
    table = items.reshape(top, rows).T
    table = table[jax.random.permutation(jax.random.fold_in(own, 1), rows)]
    turn = jax.random.randint(jax.random.fold_in(own, 2), (rows, 1), 0, top)
    return jnp.take_along_axis(table, (jnp.arange(top)[None, :] + turn) % top, axis=1)


def load_shares(number_of, total, reach, lean, full):
    portions = [(1 << 20) // math.isqrt(rank ** lean) + 1 for rank in range(1, number_of + 1)]
    largest = reach if full else min(reach, max(-(-total // number_of), total * portions[0] // sum(portions)))
    least = 1 if total - largest >= number_of - 1 else 0
    given, surplus = [largest] + [least] * (number_of - 1), total - largest - least * (number_of - 1)
    while surplus > 0:
        free = [i for i in range(1, number_of) if given[i] < largest] or [i for i in range(1, number_of) if given[i] < reach]
        mass, budget = sum([portions[i] for i in free]), surplus
        for i in free:
            extra = min(reach - given[i], max(1, budget * portions[i] // mass), surplus)
            given[i] = given[i] + extra
            surplus = surplus - extra
    return np.array(given)


def noise(own_key, extent, spread, limit, split=(), kind=jnp.bfloat16):
    values = jax.random.normal(own_key, extent, jnp.float32) * spread
    if len(split) > 0:
        values = shard_levels(own_key, extent, split, -0.22, 0.18) * values
    return jnp.clip(values, min=-limit, max=limit).astype(kind)


def bell_draw_with(stream_key, dims, deviation, most, shards, heavy, held_as=jnp.bfloat16):
    drawn = deviation * jax.random.normal(stream_key, dims, jnp.float32)
    if shards:
        drawn = drawn * shard_levels(stream_key, dims, shards, -0.22, 0.18)
    return jnp.clip(with_spikes(drawn, jax.random.fold_in(stream_key, 3), *heavy), -most, most).astype(held_as)


def setup_inputs(seed: int = 0) -> dict:
    key_of = jax.random.split(jax.random.key(seed), 19)
    leaf_lower_inv = noise(key_of[0], (2, N_LEAF, S0, S0), (2 * S0) ** -0.5, 0.1875, ((1, 4), (2, 8)), jnp.float32)
    leaf_upper_inv = noise(key_of[1], (2, N_LEAF, S0, S0), (2 * S0) ** -0.5, 0.1875, ((1, 4), (2, 8)), jnp.float32)
    leaf_to_mid_lower = noise(key_of[2], (2, N_LEAF, S1, S0), (4 * S0) ** -0.5, 0.125, ((1, 4), (2, 8)), jnp.float32)
    leaf_to_root_lower = noise(key_of[3], (2, N_LEAF, S2, S0), (4 * S0) ** -0.5, 0.125, ((1, 4), (2, 8)), jnp.float32)
    leaf_to_mid_upper = bell_draw_with(key_of[4], (2, N_LEAF, S0, S1), (4 * S1) ** -0.5, 0.125, ((1, 4), (3, 8)), (3, 2, 8, 2.0), jnp.float32)
    leaf_to_root_upper = bell_draw_with(key_of[5], (2, N_LEAF, S0, S2), (4 * S2) ** -0.5, 0.09375, ((1, 4), (3, 8)), (3, 2, 8, 2.0), jnp.float32)
    mid_lower_inv = noise(key_of[6], (2, 2, S1, S1), (2 * S1) ** -0.5, 0.125, ((2, 8),), jnp.float32)
    mid_upper_inv = noise(key_of[7], (2, 2, S1, S1), (2 * S1) ** -0.5, 0.125, ((2, 8),), jnp.float32)
    mid_to_root_lower = noise(key_of[8], (2, 2, S2, S1), (4 * S1) ** -0.5, 0.09375, ((2, 8),), jnp.float32)
    mid_to_root_upper = bell_draw_with(key_of[9], (2, 2, S1, S2), (4 * S2) ** -0.5, 0.09375, ((3, 8),), (3, 2, 8, 2.0), jnp.float32)
    root_lower_inv = noise(key_of[10], (2, S2, S2), (2 * S2) ** -0.5, 0.09375, ((1, 8),), jnp.float32)
    root_upper_inv = noise(key_of[11], (2, S2, S2), (2 * S2) ** -0.5, 0.09375, ((1, 8),), jnp.float32)
    leaf_sources = noise(key_of[12], (2, N_LEAF * S0, NRHS), 1.0, 6.0, ((1, 32),), jnp.float32)
    mid_sources = noise(key_of[13], (2, 2, S1, NRHS), 1.0, 6.0, ((2, 8),), jnp.float32)
    root_sources = noise(key_of[14], (2, S2, NRHS), 1.0, 6.0, ((1, 8),), jnp.float32)
    receiver_data = noise(key_of[15], (2, RECEIVERS, NRHS), 1.0, 6.0, ((1, 32),), jnp.float32)
    receiver_block_keys = jax.random.split(jax.random.fold_in(key_of[16], 1), RECEIVERS // NREC_DEV)
    receiver_block_turns = jax.random.permutation(jax.random.fold_in(key_of[16], 3), RECEIVERS // NREC_DEV)
    receiver_block = jax.vmap(lambda own, number: routed_block(jax.random.fold_in(key_of[16], 2), own, number, NREC_DEV, DEVICES, 1, CAP, 2))(receiver_block_keys, receiver_block_turns).reshape((RECEIVERS, 1))
    receiver_offset = set_ends(jax.random.randint(key_of[17], (RECEIVERS,), 0, LEAF_ROWS), jax.random.fold_in(key_of[17], 1), 0, LEAF_ROWS - 1).astype(jnp.int32)
    return dict(leaf_lower_inv=leaf_lower_inv, leaf_upper_inv=leaf_upper_inv, leaf_to_mid_lower=leaf_to_mid_lower, leaf_to_root_lower=leaf_to_root_lower, leaf_to_mid_upper=leaf_to_mid_upper, leaf_to_root_upper=leaf_to_root_upper, mid_lower_inv=mid_lower_inv, mid_upper_inv=mid_upper_inv, mid_to_root_lower=mid_to_root_lower, mid_to_root_upper=mid_to_root_upper, root_lower_inv=root_lower_inv, root_upper_inv=root_upper_inv, leaf_sources=leaf_sources, mid_sources=mid_sources, root_sources=root_sources, receiver_data=receiver_data, receiver_block=receiver_block, receiver_offset=receiver_offset)


def product(a, b):
    real_part = jnp.matmul(a[0], b[0], precision=lax.Precision.HIGHEST) - jnp.matmul(a[1], b[1], precision=lax.Precision.HIGHEST)
    imag_part = jnp.matmul(a[0], b[1], precision=lax.Precision.HIGHEST) + jnp.matmul(a[1], b[0], precision=lax.Precision.HIGHEST)
    return jnp.stack([real_part, imag_part])


def solve_tree(leaf_rhs, mid_rhs, root_rhs, leaf_lower_inv, leaf_upper_inv, leaf_to_mid_lower, leaf_to_root_lower, leaf_to_mid_upper, leaf_to_root_upper, mid_lower_inv, mid_upper_inv, mid_to_root_lower, mid_to_root_upper, root_lower_inv, root_upper_inv):
    columns = leaf_rhs.shape[2]
    leaf_blocks = leaf_rhs.reshape(2, N_LEAF, S0, columns)
    leaf_pass = product(leaf_lower_inv, leaf_blocks)
    to_mid = product(leaf_to_mid_lower, leaf_pass)
    mid_cut = mid_rhs - to_mid.reshape(2, 2, 2, S1, columns).sum(axis=2)
    mid_pass = product(mid_lower_inv, mid_cut)
    root_cut = root_rhs - product(leaf_to_root_lower, leaf_pass).sum(axis=1) - product(mid_to_root_lower, mid_pass).sum(axis=1)
    root_pass = product(root_lower_inv, root_cut)
    root_solution = product(root_upper_inv, root_pass)
    mid_solution = product(mid_upper_inv, mid_pass - product(mid_to_root_upper, root_solution[:, None]))
    parent_solution = jnp.repeat(mid_solution, 2, axis=1)
    leaf_tail = product(leaf_to_mid_upper, parent_solution) + product(leaf_to_root_upper, root_solution[:, None])
    leaf_solution = product(leaf_upper_inv, leaf_pass - leaf_tail)
    return leaf_solution.reshape(2, N_LEAF * S0, columns), mid_solution, root_solution


def reference(leaf_lower_inv, leaf_upper_inv, leaf_to_mid_lower, leaf_to_root_lower, leaf_to_mid_upper, leaf_to_root_upper, mid_lower_inv, mid_upper_inv, mid_to_root_lower, mid_to_root_upper, root_lower_inv, root_upper_inv, leaf_sources, mid_sources, root_sources, receiver_data, receiver_block, receiver_offset):
    factors = (leaf_lower_inv, leaf_upper_inv, leaf_to_mid_lower, leaf_to_root_lower, leaf_to_mid_upper, leaf_to_root_upper, mid_lower_inv, mid_upper_inv, mid_to_root_lower, mid_to_root_upper, root_lower_inv, root_upper_inv)
    leaf_field, mid_field, root_field = solve_tree(leaf_sources, mid_sources, root_sources, *factors)
    rows = (receiver_block[:, 0] * LEAF_ROWS + receiver_offset).astype(jnp.int32)
    adjoint_rhs = jnp.zeros((2, N_LEAF * S0, NRHS), jnp.float32).at[:, rows, :].add(receiver_data)
    conjugate_sign = jnp.array([1.0, -1.0], jnp.float32).reshape(2, 1, 1)
    mid_zero = jnp.zeros((2, 2, S1, NRHS), jnp.float32)
    root_zero = jnp.zeros((2, S2, NRHS), jnp.float32)
    leaf_back, mid_back, root_back = solve_tree(adjoint_rhs * conjugate_sign, mid_zero, root_zero, *factors)
    return (leaf_field, mid_field, root_field, leaf_back * conjugate_sign, mid_back * conjugate_sign[:, None], root_back * conjugate_sign)
```

```python
import functools

import jax
import jax.numpy as jnp
from jax import lax
from jax.experimental import pallas as pl
from jax.experimental.pallas import tpu as pltpu
from jax.sharding import PartitionSpec as P

CAP = 2
LANES = 128
F32 = jnp.float32
BF16 = jnp.bfloat16
VM = pl.BlockSpec(memory_space=pltpu.VMEM)
SM = pl.BlockSpec(memory_space=pltpu.SMEM)


def call(kernel, outs, *args, scalars=1, flops=0, nbytes=0, vmem=24):
    return pl.pallas_call(
        kernel,
        out_shape=[jax.ShapeDtypeStruct(shape, F32) for shape in outs],
        in_specs=[SM] * scalars + [VM] * (len(args) - scalars),
        out_specs=[VM] * len(outs),
        compiler_params=pltpu.CompilerParams(vmem_limit_bytes=vmem * 2**20),
        cost_estimate=pl.CostEstimate(flops=flops, bytes_accessed=nbytes, transcendentals=0),
    )(*args)


def split(x):
    high = x.astype(BF16)
    return high, (x - high.astype(F32)).astype(BF16)


def dot(a, b):
    return jnp.dot(a, b, preferred_element_type=F32)


def turned(x):
    half = x.shape[1] // 2
    return jnp.concatenate([-x[:, half:], x[:, :half]], axis=1)


def columns_of(x):
    return jnp.concatenate(split(x), axis=1), jnp.concatenate(split(turned(x)), axis=1)


def complex_dot(real, imag, w, wt):
    n = w.shape[1] // 2
    real_high, real_low = split(real)
    imag_high, imag_low = split(imag)
    wide = dot(real_high, w) + dot(imag_high, wt)
    rest = dot(real_low, w[:, :n]) + dot(imag_low, wt[:, :n])
    return (wide[:, :n] + wide[:, n:]) + rest


def apply_rows(matrix, x, step=512):
    depth = x.shape[0]
    step = min(step, depth)
    total = None
    for at in range(0, depth, step):
        w, wt = columns_of(x[at : at + step])
        part = complex_dot(matrix[0, :, at : at + step], matrix[1, :, at : at + step], w, wt)
        total = part if total is None else total + part
    return total


def assemble(where, parts, here):
    rows = parts[0].shape[0]
    for k, part in enumerate(parts):
        start = pl.multiple_of((here ^ k) * rows, 8)
        where[pl.ds(start, rows), :] = part[...]


def unpacked(x):
    return jnp.concatenate([x[:, 32 * j : 32 * j + 32] for j in range(4)], axis=0)


def packed(x):
    rows = x.shape[0] // 4
    return jnp.concatenate([x[rows * j : rows * j + rows] for j in range(4)], axis=1)


def exchange(axis, blocks):
    size = lax.axis_size(axis)
    return [blocks[0]] + [
        lax.ppermute(blocks[k], axis, [(i, i ^ k) for i in range(size)]) for k in range(1, size)
    ]


def gather(axis, block):
    return exchange(axis, [block] * lax.axis_size(axis))


def pack_receivers(groups, fronts, rows, ids, data, block, offset, *out):
    count = data.shape[1]
    slots = fronts * CAP
    down = lax.broadcasted_iota(jnp.int32, (count, count), 0)
    across = lax.broadcasted_iota(jnp.int32, (count, count), 1)
    eye = down == across
    block_col = block[...]
    block_row = jnp.sum(jnp.where(eye, block_col, 0), axis=0, keepdims=True)
    offset_col = jnp.sum(jnp.where(eye, offset[...], 0), axis=1, keepdims=True)
    same = (block_col == block_row) & (down < across)
    slot_row = block_row * CAP + jnp.sum(same.astype(jnp.int32), axis=0, keepdims=True)
    row_col = (block_col & (fronts - 1)) * rows + offset_col + 1
    width = data.shape[2]
    lane = lax.broadcasted_iota(jnp.int32, (count, width), 1)
    index = jnp.where(lane == 0, row_col, 0).astype(F32)
    lines = jnp.concatenate([index, data[0], jnp.zeros((count, width), F32), -data[1]], axis=1)
    for k in range(groups):
        first = (ids[0] ^ k) * slots
        pick = lax.broadcasted_iota(jnp.int32, (slots, count), 0) + first == slot_row
        out[k][...] = jnp.dot(
            pick.astype(F32), lines, precision=lax.Precision.HIGHEST, preferred_element_type=F32
        )


def message_rows(rows, slots):
    return max(rows, slots), 8 * -(-slots // (8 * LANES))


def pack_leaf(groups, sources, *refs):
    arrived, out = refs[:groups], refs[groups]
    rows, width = sources.shape[1], sources.shape[2]
    lines = jnp.concatenate([ref[...] for ref in arrived], axis=0)
    slots = lines.shape[0]
    body, tail = message_rows(rows, slots)
    zero = jnp.zeros((rows, width), F32)
    own = jnp.concatenate([sources[0], zero, sources[1], zero], axis=1)
    lane = lax.broadcasted_iota(jnp.int32, (slots, LANES), 1)
    data = jnp.where((lane // width) % 2 == 1, lines, 0.0)
    index = lines[:, 0:1]

    def padded(x):
        if x.shape[0] == body:
            return x
        return jnp.concatenate([x, jnp.zeros((body - x.shape[0], LANES), F32)], axis=0)

    out[0:body, :] = padded(own) + padded(data)
    out[body:, :] = jnp.zeros((tail, LANES), F32)
    for at in range(0, slots, LANES):
        size = min(LANES, slots - at)
        eye = lax.broadcasted_iota(jnp.int32, (size, size), 0) == lax.broadcasted_iota(
            jnp.int32, (size, size), 1
        )
        line = jnp.sum(jnp.where(eye, index[at : at + size], 0.0), axis=0, keepdims=True)
        out[body + at // LANES : body + at // LANES + 1, 0:size] = line


def leaf_lower(fronts, slots, ids, matrix, *refs):
    messages, out, rhs = refs[:fronts], refs[fronts], refs[fronts + 1]
    rows = matrix.shape[1]
    total = rows * fronts
    body, _ = message_rows(rows, slots)
    lane = lax.broadcasted_iota(jnp.int32, (slots, LANES), 1)
    taken = (lane // 32) % 2 == 1
    own = lax.broadcasted_iota(jnp.int32, (rows, LANES), 1)
    own = (own // 32) % 2 == 0
    for k in range(fronts):
        start = pl.multiple_of((ids[1] ^ k) * rows, 8)
        rhs[pl.ds(start, rows), :] = jnp.where(own, messages[k][0:rows, :], 0.0)
    group = max(1, 512 // slots)
    for k in range(0, fronts, group):
        chosen = messages[k : k + group]
        lines = jnp.concatenate([jnp.where(taken, ref[0:slots, :], 0.0) for ref in chosen], axis=0)
        index = jnp.concatenate(
            [
                ref[body + at // LANES : body + at // LANES + 1, 0 : min(LANES, slots - at)]
                for ref in chosen
                for at in range(0, slots, LANES)
            ],
            axis=1,
        )
        row = lax.broadcasted_iota(jnp.int32, (total, index.shape[1]), 0)
        pick = (row + 1 == index.astype(jnp.int32)).astype(BF16)
        both = dot(pick, jnp.concatenate(split(lines), axis=1))
        rhs[...] += both[:, :LANES] + both[:, LANES:]
    out[...] = apply_rows(matrix, rhs[...])


def leaf_to_mid(fronts, ids, matrix, sources, *refs):
    parts, out, full, whole = refs[:fronts], refs[fronts], refs[fronts + 1], refs[fronts + 2]
    assemble(whole, parts, ids[1])
    y = whole[...]
    full[...] = y
    zero = jnp.zeros_like(sources[0])
    own = jnp.concatenate([sources[0], zero, sources[1], zero], axis=1)
    first = ((ids[0] & 1) == 0).astype(F32)
    out[...] = own * first - apply_rows(matrix, y)


def leaf_to_root(matrix, full, out):
    out[...] = apply_rows(matrix, full[...])


def mid_lower(fronts, ids, matrix, *refs):
    parts, out, whole = refs[:fronts], refs[fronts], refs[fronts + 1]
    assemble(whole, parts, ids[1])
    out[...] = apply_rows(matrix, whole[...])


def mid_to_root(fronts, groups, ids, matrix, from_leaf, *refs):
    parts, outs = refs[:fronts], refs[fronts : fronts + groups]
    whole, quarters = refs[fronts + groups :]
    assemble(whole, parts, ids[1])
    cut = -(from_leaf[...] + apply_rows(matrix, whole[...]))
    for q in range(groups):
        piece = jnp.concatenate([cut[:, 16 * q : 16 * q + 16], cut[:, 64 + 16 * q : 80 + 16 * q]], axis=1)
        quarters[q] = packed(piece)
    for k in range(groups):
        outs[k][...] = quarters[ids[0] ^ k]


def root_sum(groups, own, *refs):
    total = own[...]
    for ref in refs[:groups]:
        total = total + ref[...]
    refs[groups][...] = total


def root_rows(fronts, ids, matrix, *refs):
    parts, out, whole = refs[:fronts], refs[fronts], refs[fronts + 1]
    rows = matrix.shape[1]
    for k, part in enumerate(parts):
        start = pl.multiple_of((ids[1] ^ k) * rows, 8)
        whole[pl.ds(start, rows), :] = unpacked(part[...])
    out[...] = packed(apply_rows(matrix, whole[...]))


def root_spread(groups, ids, *refs):
    parts, out, forward, adjoint, whole = refs[:groups], *refs[groups:]
    for k, part in enumerate(parts):
        whole[ids[0] ^ k] = unpacked(part[...])
    pieces = [whole[q] for q in range(groups)]
    x = jnp.concatenate([p[:, :16] for p in pieces] + [p[:, 16:] for p in pieces], axis=1)
    out[...] = x
    forward[0] = x[:, 0:32]
    forward[1] = x[:, 64:96]
    adjoint[0] = x[:, 32:64]
    adjoint[1] = -x[:, 96:128]


def send_rows(product, blocks, here, outs):
    rows = outs[0].shape[0]
    blocks[...] = product
    for k, out in enumerate(outs):
        out[...] = blocks[pl.ds(pl.multiple_of((here ^ k) * rows, 8), rows), :]


def apply_columns(matrix, x, out, step=256):
    w, wt = columns_of(x)
    for at in range(0, matrix.shape[1], step):
        out[at : at + step, :] = complex_dot(matrix[0, at : at + step, :], matrix[1, at : at + step, :], w, wt)


def root_to_mid(fronts, ids, matrix, x, *refs):
    outs, blocks = refs[:fronts], refs[fronts]
    apply_columns(matrix, x[...], blocks)
    rows = outs[0].shape[0]
    for k, out in enumerate(outs):
        out[...] = blocks[pl.ds(pl.multiple_of((ids[1] ^ k) * rows, 8), rows), :]


def root_to_leaf(matrix, x, out):
    apply_columns(matrix, x[...], out)


def subtract_sum(fronts, *refs):
    rest, out = refs[fronts:-1], refs[-1]
    tail = refs[0][...]
    for ref in refs[1:fronts]:
        tail = tail + ref[...]
    value = rest[0][...]
    for ref in rest[1:]:
        value = value + ref[...]
    out[...] = value - tail


def mid_upper(fronts, ids, matrix, coupling, from_root, *refs):
    parts, out, outs = refs[:fronts], refs[fronts], refs[fronts + 1 : 2 * fronts + 1]
    whole, blocks = refs[2 * fronts + 1 :]
    assemble(whole, parts, ids[1])
    x = apply_rows(matrix, whole[...])
    out[...] = x
    apply_columns(coupling, x, blocks)
    blocks[...] += from_root[...]
    rows = outs[0].shape[0]
    for k, ref in enumerate(outs):
        ref[...] = blocks[pl.ds(pl.multiple_of((ids[1] ^ k) * rows, 8), rows), :]


def leaf_upper(fronts, ids, matrix, *refs):
    parts, forward, adjoint, whole = refs[:fronts], *refs[fronts:]
    assemble(whole, parts, ids[1])
    x = apply_rows(matrix, whole[...])
    forward[0] = x[:, 0:32]
    forward[1] = x[:, 64:96]
    adjoint[0] = x[:, 32:64]
    adjoint[1] = -x[:, 96:128]


def mid_outputs(ids, mine, other, forward, adjoint):
    parent = ids[0] // 2
    for at, ref in ((parent, mine), (1 - parent, other)):
        x = ref[...]
        forward[0, at] = x[:, 0:32]
        forward[1, at] = x[:, 64:96]
        adjoint[0, at] = x[:, 32:64]
        adjoint[1, at] = -x[:, 96:128]


def body(
    leaf_lower_inv,
    leaf_upper_inv,
    leaf_to_mid_lower,
    leaf_to_root_lower,
    leaf_to_mid_upper,
    leaf_to_root_upper,
    mid_lower_inv,
    mid_upper_inv,
    mid_to_root_lower,
    mid_to_root_upper,
    root_lower_inv,
    root_upper_inv,
    leaf_sources,
    mid_sources,
    root_sources,
    receiver_data,
    receiver_block,
    receiver_offset,
):
    groups, fronts = lax.axis_size("leaf"), lax.axis_size("front")
    group, front = lax.axis_index("leaf"), lax.axis_index("front")
    ids = jnp.stack([group, front]).astype(jnp.int32)
    parent = group // 2
    n0, n1, n2 = leaf_sources.shape[1], mid_sources.shape[2], root_sources.shape[1]
    slots = fronts * CAP

    def own(array):
        return lax.dynamic_index_in_dim(array, parent, 1, keepdims=False)

    def kernel(fn, outs, *args, scratch=(), vmem=24, scalars=1):
        weights = sum(a.size for a in args[scalars : scalars + 1])
        return pl.pallas_call(
            fn,
            out_shape=[jax.ShapeDtypeStruct(shape, F32) for shape in outs],
            in_specs=[SM] * scalars + [VM] * (len(args) - scalars),
            out_specs=[VM] * len(outs),
            scratch_shapes=[pltpu.VMEM(shape, F32) for shape in scratch],
            compiler_params=pltpu.CompilerParams(vmem_limit_bytes=vmem * 2**20),
            cost_estimate=pl.CostEstimate(
                flops=weights * 6 * 128, bytes_accessed=weights * 4, transcendentals=0
            ),
        )(*args)

    with jax.named_scope("right_hand_sides"):
        payload = kernel(
            functools.partial(pack_receivers, groups, fronts, n0),
            [(slots, LANES)] * groups,
            ids,
            receiver_data,
            receiver_block,
            receiver_offset.reshape(1, -1),
        )
        arrived = exchange("leaf", payload)
        (message,) = kernel(
            functools.partial(pack_leaf, groups),
            [(sum(message_rows(n0, groups * slots)), LANES)],
            leaf_sources,
            *arrived,
            scalars=0,
        )
    with jax.named_scope("leaf_lower"):
        messages = gather("front", message)
        (y_leaf,) = kernel(
            functools.partial(leaf_lower, fronts, groups * slots),
            [(n0, LANES)],
            ids,
            leaf_lower_inv[:, 0],
            *messages,
            scratch=[(n0 * fronts, LANES)],
        )
    with jax.named_scope("mid_lower"):
        parts = gather("front", y_leaf)
        cut_mid, y_full = kernel(
            functools.partial(leaf_to_mid, fronts),
            [(n1, LANES), (n0 * fronts, LANES)],
            ids,
            leaf_to_mid_lower[:, 0],
            own(mid_sources),
            *parts,
            scratch=[(n0 * fronts, LANES)],
        )
        parts = gather("front", cut_mid)
        (from_leaf,) = kernel(leaf_to_root, [(n2, LANES)], leaf_to_root_lower[:, 0], y_full, scalars=0)
        (y_mid,) = kernel(
            functools.partial(mid_lower, fronts),
            [(n1, LANES)],
            ids,
            own(mid_lower_inv),
            *parts,
            scratch=[(n1 * fronts, LANES)],
        )
    with jax.named_scope("root_cut"):
        parts = gather("front", y_mid)
        y_sibling = lax.ppermute(y_mid, "leaf", [(i, i ^ 1) for i in range(groups)])
        quarters = kernel(
            functools.partial(mid_to_root, fronts, groups),
            [(n2 // 4, LANES)] * groups,
            ids,
            own(mid_to_root_lower),
            from_leaf,
            *parts,
            scratch=[(n1 * fronts, LANES), (groups, n2 // 4, LANES)],
        )
        both = jnp.concatenate([root_sources, jnp.zeros_like(root_sources)], axis=2)
        quarter = lax.dynamic_slice_in_dim(both, group * 16, 16, 2)
        quarter = jnp.concatenate([quarter[0], quarter[1]], axis=1)
        quarter = quarter.reshape(4, n2 // 4, 32).transpose(1, 0, 2).reshape(n2 // 4, LANES)
        arrived = exchange("leaf", quarters)
        (cut_root,) = kernel(
            functools.partial(root_sum, groups), [(n2 // 4, LANES)], quarter, *arrived, scalars=0
        )
    with jax.named_scope("root_solve"):
        parts = gather("front", cut_root)
        (y_root,) = kernel(
            functools.partial(root_rows, fronts),
            [(n2 // 4, LANES)],
            ids,
            root_lower_inv,
            *parts,
            scratch=[(n2 * fronts, 32)],
        )
        parts = gather("front", y_root)
        (x_quarter,) = kernel(
            functools.partial(root_rows, fronts),
            [(n2 // 4, LANES)],
            ids,
            root_upper_inv,
            *parts,
            scratch=[(n2 * fronts, 32)],
        )
        arrived = gather("leaf", x_quarter)
        x_root, root_field, root_adjoint = kernel(
            functools.partial(root_spread, groups),
            [(n2, LANES), (2, n2, 32), (2, n2, 32)],
            ids,
            *arrived,
            scratch=[(groups, n2, 32)],
        )
    with jax.named_scope("mid_upper"):
        blocks = kernel(
            functools.partial(root_to_mid, fronts),
            [(n1, LANES)] * fronts,
            ids,
            own(mid_to_root_upper),
            x_root,
            scratch=[(n1 * fronts, LANES)],
        )
        parts = exchange("front", blocks)
        (from_root,) = kernel(
            root_to_leaf, [(n0 * fronts, LANES)], leaf_to_root_upper[:, 0], x_root, scalars=0
        )
        (rest,) = kernel(
            functools.partial(subtract_sum, fronts), [(n1, LANES)], *parts, y_mid, y_sibling, scalars=0
        )
        parts = gather("front", rest)
        x_mid, *blocks = kernel(
            functools.partial(mid_upper, fronts),
            [(n1, LANES)] + [(n0, LANES)] * fronts,
            ids,
            own(mid_upper_inv),
            leaf_to_mid_upper[:, 0],
            from_root,
            *parts,
            scratch=[(n1 * fronts, LANES), (n0 * fronts, LANES)],
        )
    with jax.named_scope("leaf_upper"):
        parts = exchange("front", blocks)
        x_other = lax.ppermute(x_mid, "leaf", [(i, i ^ 2) for i in range(groups)])
        (rest,) = kernel(
            functools.partial(subtract_sum, fronts), [(n0, LANES)], *parts, y_leaf, scalars=0
        )
        parts = gather("front", rest)
        mid_field, mid_adjoint = kernel(
            mid_outputs, [(2, 2, n1, 32)] * 2, ids, x_mid, x_other
        )
        leaf_field, leaf_adjoint = kernel(
            functools.partial(leaf_upper, fronts),
            [(2, n0, 32)] * 2,
            ids,
            leaf_upper_inv[:, 0],
            *parts,
            scratch=[(n0 * fronts, LANES)],
        )
    return leaf_field, mid_field, root_field, leaf_adjoint, mid_adjoint, root_adjoint


def solution(mesh):
    in_specs = (
        P(None, "leaf", "front", None),
        P(None, "leaf", "front", None),
        P(None, "leaf", "front", None),
        P(None, "leaf", "front", None),
        P(None, "leaf", None, "front"),
        P(None, "leaf", None, "front"),
        P(None, None, "front", None),
        P(None, None, "front", None),
        P(None, None, "front", None),
        P(None, None, None, "front"),
        P(None, "front", None),
        P(None, "front", None),
        P(None, ("leaf", "front"), None),
        P(None, None, "front", None),
        P(None, "front", None),
        P(None, ("leaf", "front"), None),
        P(("leaf", "front"), None),
        P(("leaf", "front")),
    )
    out_specs = (
        P(None, ("leaf", "front"), None),
        P(None, None, "front", None),
        P(None, "front", None),
        P(None, ("leaf", "front"), None),
        P(None, None, "front", None),
        P(None, "front", None),
    )
    return jax.shard_map(body, mesh=mesh, in_specs=in_specs, out_specs=out_specs, check_vma=False)
```

```python
import functools

import jax
import jax.numpy as jnp
from jax import lax
from jax.experimental import pallas as pl
from jax.experimental.pallas import tpu as pltpu
from jax.sharding import PartitionSpec as P

CAP = 2
LANES = 128
F32 = jnp.float32
BF16 = jnp.bfloat16
VM = pl.BlockSpec(memory_space=pltpu.VMEM)
SM = pl.BlockSpec(memory_space=pltpu.SMEM)


def split(x):
    high = x.astype(BF16)
    return high, (x - high.astype(F32)).astype(BF16)


def dot(a, b):
    return jnp.dot(a, b, preferred_element_type=F32)


def turned(x):
    half = x.shape[1] // 2
    return jnp.concatenate([-x[:, half:], x[:, :half]], axis=1)


def columns_of(x):
    return jnp.concatenate(split(x), axis=1), jnp.concatenate(split(turned(x)), axis=1)


def complex_dot(real, imag, w, wt):
    n = w.shape[1] // 2
    real_high, real_low = split(real)
    imag_high, imag_low = split(imag)
    wide = dot(real_high, w) + dot(imag_high, wt)
    rest = dot(real_low, w[:, :n]) + dot(imag_low, wt[:, :n])
    return (wide[:, :n] + wide[:, n:]) + rest


def apply_rows(matrix, x, step=512):
    depth = x.shape[0]
    step = min(step, depth)
    total = None
    for at in range(0, depth, step):
        w, wt = columns_of(x[at : at + step])
        part = complex_dot(matrix[0, :, at : at + step], matrix[1, :, at : at + step], w, wt)
        total = part if total is None else total + part
    return total


def unpacked(x):
    return jnp.concatenate([x[:, 32 * j : 32 * j + 32] for j in range(4)], axis=0)


def packed(x):
    rows = x.shape[0] // 4
    return jnp.concatenate([x[rows * j : rows * j + rows] for j in range(4)], axis=1)


def exchange(axis, blocks):
    return lax.all_to_all(blocks, axis, split_axis=0, concat_axis=0, tiled=True)


def to_all(out, value):
    for k in range(out.shape[0]):
        out[k] = value


def flat(ref):
    return ref[...].reshape(-1, ref.shape[2])


def row_blocks(out, value):
    rows = out.shape[1]
    for k in range(out.shape[0]):
        out[k] = value[rows * k : rows * k + rows]


def lanes_of(sources):
    real, imag = sources[0].T, sources[1].T
    zero = jnp.zeros_like(real)
    return jnp.concatenate([real, zero, imag, zero], axis=1)


def fields_of(x, forward, adjoint, where):
    y = x.T
    forward[(0, *where)] = y[0:32]
    forward[(1, *where)] = y[64:96]
    adjoint[(0, *where)] = y[32:64]
    adjoint[(1, *where)] = -y[96:128]


def pack_receivers(fronts, rows, data, block, offset, out):
    count = data.shape[1]
    groups, slots = out.shape[0], out.shape[1]
    down = lax.broadcasted_iota(jnp.int32, (count, count), 0)
    across = lax.broadcasted_iota(jnp.int32, (count, count), 1)
    eye = down == across
    block_row = block[...]
    block_col = jnp.sum(jnp.where(eye, block_row, 0), axis=1, keepdims=True)
    offset_col = jnp.sum(jnp.where(eye, offset[...], 0), axis=1, keepdims=True)
    same = (block_col == block_row) & (down < across)
    slot_row = block_row * CAP + jnp.sum(same.astype(jnp.int32), axis=0, keepdims=True)
    row_col = (block_col & (fronts - 1)) * rows + offset_col + 1
    width = data.shape[2]
    lane = lax.broadcasted_iota(jnp.int32, (count, width), 1)
    index = jnp.where(lane == 0, row_col, 0).astype(F32)
    lines = jnp.concatenate([index, data[0], jnp.zeros((count, width), F32), -data[1]], axis=1)
    pick = lax.broadcasted_iota(jnp.int32, (groups * slots, count), 0) == slot_row
    out[...] = jnp.dot(
        pick.astype(F32), lines, precision=lax.Precision.HIGHEST, preferred_element_type=F32
    ).reshape(groups, slots, LANES)


def message_rows(rows, slots):
    return max(rows, slots), 8 * -(-slots // (8 * LANES))


def pack_leaf(sources, arrived, out):
    lines = flat(arrived)
    slots = lines.shape[0]
    own = lanes_of(sources)
    body, tail = message_rows(own.shape[0], slots)
    lane = lax.broadcasted_iota(jnp.int32, (slots, LANES), 1)
    data = jnp.where((lane // 32) % 2 == 1, lines, 0.0)
    index = lines[:, 0:1]

    def padded(x):
        if x.shape[0] == body:
            return x
        return jnp.concatenate([x, jnp.zeros((body - x.shape[0], LANES), F32)], axis=0)

    value = padded(own) + padded(data)
    places = []
    for at in range(0, slots, LANES):
        size = min(LANES, slots - at)
        eye = lax.broadcasted_iota(jnp.int32, (size, size), 0) == lax.broadcasted_iota(
            jnp.int32, (size, size), 1
        )
        line = jnp.sum(jnp.where(eye, index[at : at + size], 0.0), axis=0, keepdims=True)
        places.append(jnp.concatenate([line, jnp.zeros((1, LANES - size), F32)], axis=1) if size < LANES else line)
    for k in range(out.shape[0]):
        out[k, 0:body, :] = value
        out[k, body:, :] = jnp.zeros((tail, LANES), F32)
        for r, line in enumerate(places):
            out[k, body + r : body + r + 1, :] = line


def leaf_lower(slots, matrix, messages, out, y_own, rhs):
    fronts, rows = messages.shape[0], matrix.shape[1]
    total = rows * fronts
    body, _ = message_rows(rows, slots)
    lane = lax.broadcasted_iota(jnp.int32, (slots, LANES), 1)
    taken = (lane // 32) % 2 == 1
    own = lax.broadcasted_iota(jnp.int32, (rows, LANES), 1)
    own = (own // 32) % 2 == 0
    for k in range(fronts):
        rhs[rows * k : rows * k + rows, :] = jnp.where(own, messages[k, 0:rows, :], 0.0)
    group = max(1, 512 // slots)
    for k in range(0, fronts, group):
        chosen = range(k, min(k + group, fronts))
        lines = jnp.concatenate([jnp.where(taken, messages[i, 0:slots, :], 0.0) for i in chosen], axis=0)
        index = jnp.concatenate(
            [
                messages[i, body + at // LANES : body + at // LANES + 1, 0 : min(LANES, slots - at)]
                for i in chosen
                for at in range(0, slots, LANES)
            ],
            axis=1,
        )
        row = lax.broadcasted_iota(jnp.int32, (total, index.shape[1]), 0)
        pick = (row + 1 == index.astype(jnp.int32)).astype(BF16)
        both = dot(pick, jnp.concatenate(split(lines), axis=1))
        rhs[...] += both[:, :LANES] + both[:, LANES:]
    y = apply_rows(matrix, rhs[...])
    to_all(out, y)
    y_own[...] = y


def leaf_to_mid(ids, matrix, sources, y, out):
    own = lanes_of(sources)
    first = ((ids[0] & 1) == 0).astype(F32)
    to_all(out, own * first - apply_rows(matrix, flat(y)))


def leaf_to_root(matrix, y, out):
    out[...] = apply_rows(matrix, flat(y))


def mid_lower(matrix, parts, out, y_own):
    y = apply_rows(matrix, flat(parts))
    to_all(out, y)
    y_own[...] = y


def mid_to_root(matrix, from_leaf, parts, out):
    cut = -(from_leaf[...] + apply_rows(matrix, flat(parts)))
    for q in range(out.shape[0]):
        piece = jnp.concatenate([cut[:, 16 * q : 16 * q + 16], cut[:, 64 + 16 * q : 80 + 16 * q]], axis=1)
        out[q] = packed(piece)


def root_quarter(ids, sources, out):
    rows = sources.shape[2]
    q = ids[0]
    start = pl.multiple_of((q & 1) * 16, 16)
    piece = jnp.concatenate([sources[0, pl.ds(start, 16), :], sources[1, pl.ds(start, 16), :]], axis=0)
    piece = piece * (q < 2).astype(F32)
    out[...] = packed(piece.T)


def root_sum(own, parts, out):
    total = own[...]
    for k in range(parts.shape[0]):
        total = total + parts[k]
    to_all(out, total)


def root_rows(matrix, parts, out):
    x = jnp.concatenate([unpacked(parts[k]) for k in range(parts.shape[0])], axis=0)
    to_all(out, packed(apply_rows(matrix, x)))


def apply_columns(matrix, x, out, step=256):
    w, wt = columns_of(x)
    for at in range(0, matrix.shape[1], step):
        out[at : at + step, :] = complex_dot(matrix[0, at : at + step, :], matrix[1, at : at + step, :], w, wt)


def root_to_mid(matrix, quarters, out, x_root, blocks):
    pieces = [unpacked(quarters[q]) for q in range(quarters.shape[0])]
    x = jnp.concatenate([p[:, :16] for p in pieces] + [p[:, 16:] for p in pieces], axis=1)
    x_root[...] = x
    apply_columns(matrix, x, blocks)
    row_blocks(out, blocks[...])


def root_to_leaf(matrix, x, out, forward, adjoint):
    apply_columns(matrix, x[...], out)
    fields_of(x[...], forward, adjoint, ())


def rest_of(parts, *refs):
    value = refs[0][...]
    for ref in refs[1:-1]:
        value = value + ref[...]
    tail = parts[0]
    for k in range(1, parts.shape[0]):
        tail = tail + parts[k]
    to_all(refs[-1], value - tail)


def mid_upper(matrix, coupling, from_root, parts, out, x_own, blocks):
    x = apply_rows(matrix, flat(parts))
    x_own[...] = x
    apply_columns(coupling, x, blocks)
    row_blocks(out, blocks[...] + from_root[...])


def leaf_upper(matrix, parts, forward, adjoint):
    fields_of(apply_rows(matrix, flat(parts)), forward, adjoint, ())


def mid_outputs(ids, mine, other, forward, adjoint):
    parent = ids[0] // 2
    fields_of(mine[...], forward, adjoint, (parent,))
    fields_of(other[...], forward, adjoint, (1 - parent,))


def body(
    leaf_lower_inv,
    leaf_upper_inv,
    leaf_to_mid_lower,
    leaf_to_root_lower,
    leaf_to_mid_upper,
    leaf_to_root_upper,
    mid_lower_inv,
    mid_upper_inv,
    mid_to_root_lower,
    mid_to_root_upper,
    root_lower_inv,
    root_upper_inv,
    leaf_sources,
    mid_sources,
    root_sources,
    receiver_data,
    receiver_block,
    receiver_offset,
):
    groups, fronts = lax.axis_size("leaf"), lax.axis_size("front")
    group, front = lax.axis_index("leaf"), lax.axis_index("front")
    ids = jnp.stack([group, front]).astype(jnp.int32)
    parent = group // 2
    n0, n1, n2 = leaf_sources.shape[1], mid_sources.shape[2], root_sources.shape[1]
    slots = fronts * CAP

    def own(array):
        return lax.dynamic_index_in_dim(array, parent, 1, keepdims=False)

    def kernel(fn, outs, *args, scratch=(), vmem=6, scalars=0):
        weights = max(a.size for a in args)
        return pl.pallas_call(
            fn,
            out_shape=[jax.ShapeDtypeStruct(shape, F32) for shape in outs],
            in_specs=[SM] * scalars + [VM] * (len(args) - scalars),
            out_specs=[VM] * len(outs),
            scratch_shapes=[pltpu.VMEM(shape, F32) for shape in scratch],
            compiler_params=pltpu.CompilerParams(vmem_limit_bytes=vmem * 2**20),
            cost_estimate=pl.CostEstimate(
                flops=weights * 6 * 128, bytes_accessed=weights * 4, transcendentals=0
            ),
        )(*args)

    leaf_sources = leaf_sources.transpose(0, 2, 1)
    mid_sources = mid_sources.transpose(0, 1, 3, 2)
    root_sources = root_sources.transpose(0, 2, 1)
    with jax.named_scope("right_hand_sides"):
        (payload,) = kernel(
            functools.partial(pack_receivers, fronts, n0),
            [(groups, slots, LANES)],
            receiver_data,
            receiver_block.reshape(1, -1),
            receiver_offset.reshape(1, -1),
        )
        arrived = exchange("leaf", payload)
        (message,) = kernel(
            pack_leaf, [(fronts, sum(message_rows(n0, groups * slots)), LANES)], leaf_sources, arrived
        )
    with jax.named_scope("leaf_lower"):
        y, y_leaf = kernel(
            functools.partial(leaf_lower, groups * slots),
            [(fronts, n0, LANES), (n0, LANES)],
            leaf_lower_inv[:, 0],
            exchange("front", message),
            scratch=[(n0 * fronts, LANES)],
        )
    with jax.named_scope("mid_lower"):
        y = exchange("front", y)
        (cut_mid,) = kernel(
            leaf_to_mid,
            [(fronts, n1, LANES)],
            ids,
            leaf_to_mid_lower[:, 0],
            own(mid_sources),
            y,
            scalars=1,
        )
        (from_leaf,) = kernel(leaf_to_root, [(n2, LANES)], leaf_to_root_lower[:, 0], y)
        parts, y_mid = kernel(
            mid_lower,
            [(fronts, n1, LANES), (n1, LANES)],
            own(mid_lower_inv),
            exchange("front", cut_mid),
        )
    with jax.named_scope("root_cut"):
        (quarters,) = kernel(
            mid_to_root,
            [(groups, n2 // 4, LANES)],
            own(mid_to_root_lower),
            from_leaf,
            exchange("front", parts),
        )
        y_sibling = lax.ppermute(y_mid, "leaf", [(i, i ^ 1) for i in range(groups)])
        (quarter,) = kernel(root_quarter, [(n2 // 4, LANES)], ids, root_sources, scalars=1)
        (cut_root,) = kernel(
            root_sum, [(fronts, n2 // 4, LANES)], quarter, exchange("leaf", quarters)
        )
    with jax.named_scope("root_solve"):
        (y_root,) = kernel(
            root_rows, [(fronts, n2 // 4, LANES)], root_lower_inv, exchange("front", cut_root)
        )
        (x_quarter,) = kernel(
            root_rows, [(groups, n2 // 4, LANES)], root_upper_inv, exchange("front", y_root)
        )
    with jax.named_scope("mid_upper"):
        blocks, x_root = kernel(
            root_to_mid,
            [(fronts, n1, LANES), (n2, LANES)],
            own(mid_to_root_upper),
            exchange("leaf", x_quarter),
            scratch=[(n1 * fronts, LANES)],
        )
        from_root, root_field, root_adjoint = kernel(
            root_to_leaf,
            [(n0 * fronts, LANES), (2, 32, n2), (2, 32, n2)],
            leaf_to_root_upper[:, 0],
            x_root,
        )
        (rest,) = kernel(
            rest_of, [(fronts, n1, LANES)], exchange("front", blocks), y_mid, y_sibling
        )
        blocks, x_mid = kernel(
            mid_upper,
            [(fronts, n0, LANES), (n1, LANES)],
            own(mid_upper_inv),
            leaf_to_mid_upper[:, 0],
            from_root,
            exchange("front", rest),
            scratch=[(n0 * fronts, LANES)],
        )
    with jax.named_scope("leaf_upper"):
        x_other = lax.ppermute(x_mid, "leaf", [(i, i ^ 2) for i in range(groups)])
        (rest,) = kernel(rest_of, [(fronts, n0, LANES)], exchange("front", blocks), y_leaf)
        mid_field, mid_adjoint = kernel(
            mid_outputs, [(2, 2, 32, n1)] * 2, ids, x_mid, x_other, scalars=1
        )
        leaf_field, leaf_adjoint = kernel(
            leaf_upper, [(2, 32, n0)] * 2, leaf_upper_inv[:, 0], exchange("front", rest)
        )
    return tuple(
        jnp.swapaxes(x, -1, -2)
        for x in (leaf_field, mid_field, root_field, leaf_adjoint, mid_adjoint, root_adjoint)
    )


def solution(mesh):
    in_specs = (
        P(None, "leaf", "front", None),
        P(None, "leaf", "front", None),
        P(None, "leaf", "front", None),
        P(None, "leaf", "front", None),
        P(None, "leaf", None, "front"),
        P(None, "leaf", None, "front"),
        P(None, None, "front", None),
        P(None, None, "front", None),
        P(None, None, "front", None),
        P(None, None, None, "front"),
        P(None, "front", None),
        P(None, "front", None),
        P(None, ("leaf", "front"), None),
        P(None, None, "front", None),
        P(None, "front", None),
        P(None, ("leaf", "front"), None),
        P(("leaf", "front"), None),
        P(("leaf", "front")),
    )
    out_specs = (
        P(None, ("leaf", "front"), None),
        P(None, None, "front", None),
        P(None, "front", None),
        P(None, ("leaf", "front"), None),
        P(None, None, "front", None),
        P(None, "front", None),
    )
    return jax.shard_map(body, mesh=mesh, in_specs=in_specs, out_specs=out_specs, check_vma=False)
```

```python
import functools

import jax
import jax.numpy as jnp
from jax import lax
from jax.experimental import pallas as pl
from jax.experimental.pallas import tpu as pltpu
from jax.sharding import PartitionSpec as P

CAP = 2
LANES = 128
COLS = 32
F32 = jnp.float32
BF16 = jnp.bfloat16
VM = pl.BlockSpec(memory_space=pltpu.VMEM)
HB = pl.BlockSpec(memory_space=pltpu.HBM)


def split(x):
    high = x.astype(BF16)
    return high, (x - high.astype(F32)).astype(BF16)


def dot(a, b):
    return jnp.dot(a, b, preferred_element_type=F32)


def complex_dot(matrix, x):
    half = x.shape[1] // 2
    turned = jnp.concatenate([-x[:, half:], x[:, :half]], axis=1)
    both = jnp.concatenate([x, turned], axis=0)
    columns = jnp.concatenate(split(both), axis=1)
    product = dot(matrix, columns)
    rows, n = product.shape[0] // 2, x.shape[1]
    return (product[:rows, n:] + product[rows:, :n]) + product[:rows, :n]


def pack(x):
    chunks = LANES // x.shape[1]
    rows = x.shape[0] // chunks
    return jnp.concatenate([x[rows * j : rows * j + rows] for j in range(chunks)], axis=1)


def unpack(x, width):
    return jnp.concatenate([x[:, at : at + width] for at in range(0, LANES, width)], axis=0)


def halves(x):
    c = COLS
    return (
        jnp.concatenate([x[:, :c], x[:, 2 * c : 3 * c]], axis=1),
        jnp.concatenate([x[:, c : 2 * c], x[:, 3 * c :]], axis=1),
    )


def joined(forward, adjoint):
    c = COLS
    return jnp.concatenate([forward[:, :c], adjoint[:, :c], forward[:, c:], adjoint[:, c:]], axis=1)


def own_first(group, forward, adjoint):
    even = (group & 1) == 0
    return jnp.where(even, forward, adjoint), jnp.where(even, adjoint, forward)


def by_solve(group, own, other):
    even = (group & 1) == 0
    return joined(jnp.where(even, own, other), jnp.where(even, other, own))


def assemble(where, parts, here, width=LANES):
    rows = parts[0].shape[0] * (LANES // width)
    for k, part in enumerate(parts):
        start = pl.multiple_of((here ^ k) * rows, 8)
        where[pl.ds(start, rows), :] = part[...] if width == LANES else unpack(part[...], width)


def fields_of(x, forward, adjoint, where):
    y = x.T
    c = COLS
    forward[(0, *where)] = y[0:c]
    forward[(1, *where)] = y[2 * c : 3 * c]
    adjoint[(0, *where)] = y[c : 2 * c]
    adjoint[(1, *where)] = -y[3 * c :]


def swap(axis, x, k):
    size = lax.axis_size(axis)
    return lax.ppermute(x, axis, [(i, i ^ k) for i in range(size)])


def gather_front(x):
    fronts = lax.axis_size("front")
    mine = [x] + [swap("front", x, k) for k in range(2, fronts, 2)]
    other = [swap("front", y, 1) for y in mine]
    return [block for pair in zip(mine, other) for block in pair]


def kernel(fn, outs, *args, scratch=(), vmem=8, work=0, hbm=()):
    outs = [o if isinstance(o[0], tuple) else (o, F32) for o in outs]
    return pl.pallas_call(
        fn,
        out_shape=[jax.ShapeDtypeStruct(*o) for o in outs],
        in_specs=[HB if i in hbm else VM for i in range(len(args))],
        out_specs=[VM] * len(outs),
        scratch_shapes=list(scratch),
        compiler_params=pltpu.CompilerParams(vmem_limit_bytes=vmem * 2**20),
        cost_estimate=pl.CostEstimate(flops=work, bytes_accessed=work // 700, transcendentals=0),
    )(*args)


def load_matrices(picks, *refs):
    count = len(picks)
    sources, outs, buffers, sems = (
        refs[:count],
        refs[count : 2 * count],
        refs[2 * count : 3 * count],
        refs[3 * count],
    )
    parent = lax.axis_index("leaf") // 2
    copies = []
    for i, (src, pick) in enumerate(zip(sources, picks)):
        rows = buffers[i].shape[1]
        step = rows // 2 if rows >= 128 else rows
        for n, at in enumerate(range(0, rows, step)):
            span = pl.ds(at, step)
            view = src.at[:, span, :] if pick is None else src.at[:, parent if pick == "own" else 0, span, :]
            copy = pltpu.make_async_copy(view, buffers[i].at[:, span, :], sems.at[2 * i + n])
            copy.start()
            copies.append((i, at, step, copy))
    for i, at, step, copy in copies:
        copy.wait()
        rows, depth = buffers[i].shape[1:]
        for part in range(2):
            high, low = split(buffers[i][part, at : at + step, :])
            outs[i][at : at + step, part * depth : part * depth + depth] = high
            outs[i][rows + at : rows + at + step, part * depth : part * depth + depth] = low


def load(*matrices):
    shapes = [m.shape[-2:] for m, _ in matrices]
    size = sum(r * d for r, d in shapes)
    return kernel(
        functools.partial(load_matrices, tuple(pick for _, pick in matrices)),
        [((2 * r, 2 * d), BF16) for r, d in shapes],
        *[m for m, _ in matrices],
        scratch=[pltpu.VMEM((2, r, d), F32) for r, d in shapes]
        + [pltpu.SemaphoreType.DMA((2 * len(shapes),))],
        hbm=range(len(shapes)),
        vmem=4 + -(-size * 8 // 2**20),
        work=size * 1000,
    )


def pack_receivers(fronts, rows, data_hbm, block_hbm, offset_hbm, *refs):
    groups = lax.axis_size("leaf")
    outs = refs[:groups]
    data, block, offset, sems = refs[groups:]
    copies = [
        pltpu.make_async_copy(src, dst, sems.at[i])
        for i, (src, dst) in enumerate(((data_hbm, data), (block_hbm, block), (offset_hbm, offset)))
    ]
    for copy in copies:
        copy.start()
    for copy in copies:
        copy.wait()
    group = lax.axis_index("leaf")
    count = data.shape[1]
    slots = fronts * CAP
    down = lax.broadcasted_iota(jnp.int32, (count, count), 0)
    across = lax.broadcasted_iota(jnp.int32, (count, count), 1)
    eye = down == across
    block_row = block[...]
    block_col = jnp.sum(jnp.where(eye, block_row, 0), axis=1, keepdims=True)
    offset_col = jnp.sum(jnp.where(eye, offset[...], 0), axis=1, keepdims=True)
    same = (block_col == block_row) & (down < across)
    slot_row = block_row * CAP + jnp.sum(same.astype(jnp.int32), axis=0, keepdims=True)
    row_col = (block_col & (fronts - 1)) * rows + offset_col + 1
    lane = lax.broadcasted_iota(jnp.int32, (count, COLS), 1)
    index = jnp.where(lane == 0, row_col, 0).astype(F32)
    lines = jnp.concatenate([index, data[0], jnp.zeros((count, COLS), F32), -data[1]], axis=1)
    for k, out in enumerate(outs):
        first = (group ^ k) * slots
        pick = lax.broadcasted_iota(jnp.int32, (slots, count), 0) + first == slot_row
        out[...] = jnp.dot(
            pick.astype(F32), lines, precision=lax.Precision.HIGHEST, preferred_element_type=F32
        )


def load_sources(leaf_hbm, mid_hbm, root_hbm, leaf_out, mid_out, root_out, leaf, mid, root, sems):
    group = lax.axis_index("leaf")
    copies = [
        pltpu.make_async_copy(src, dst, sems.at[i])
        for i, (src, dst) in enumerate(
            ((leaf_hbm, leaf), (mid_hbm.at[:, group // 2], mid), (root_hbm, root))
        )
    ]
    for copy in copies:
        copy.start()
    for copy in copies:
        copy.wait()
    forward = ((group & 1) == 0).astype(F32)
    real, imag = leaf[0].T, leaf[1].T
    zero = jnp.zeros_like(real)
    leaf_out[...] = jnp.concatenate([real, zero, imag, zero], axis=1)
    mid_out[...] = pack(jnp.concatenate([mid[0], mid[1]], axis=0).T) * forward
    width = COLS // 2
    low = jnp.concatenate([root[0, :width], root[1, :width]], axis=0)
    high = jnp.concatenate([root[0, width:], root[1, width:]], axis=0)
    root_out[...] = pack(jnp.where(group < 2, low, high).T) * forward


def message_rows(rows, slots):
    return max(rows, slots), 8 * -(-slots // (8 * LANES))


def pack_leaf(own, *refs):
    arrived, out = refs[:-1], refs[-1]
    lines = jnp.concatenate([ref[...] for ref in arrived], axis=0)
    slots = lines.shape[0]
    body, tail = message_rows(own.shape[0], slots)
    lane = lax.broadcasted_iota(jnp.int32, (slots, LANES), 1)
    data = jnp.where((lane // COLS) % 2 == 1, lines, 0.0)
    index = lines[:, 0:1]

    def padded(x):
        if x.shape[0] == body:
            return x
        return jnp.concatenate([x, jnp.zeros((body - x.shape[0], LANES), F32)], axis=0)

    out[0:body, :] = padded(own[...]) + padded(data)
    out[body:, :] = jnp.zeros((tail, LANES), F32)
    for at in range(0, slots, LANES):
        size = min(LANES, slots - at)
        eye = lax.broadcasted_iota(jnp.int32, (size, size), 0) == lax.broadcasted_iota(
            jnp.int32, (size, size), 1
        )
        line = jnp.sum(jnp.where(eye, index[at : at + size], 0.0), axis=0, keepdims=True)
        out[body + at // LANES : body + at // LANES + 1, 0:size] = line


def leaf_lower(slots, matrix, *refs):
    messages, (out, rhs) = refs[:-2], refs[-2:]
    fronts, rows = len(messages), out.shape[0]
    here = lax.axis_index("front")
    total = rows * fronts
    body, _ = message_rows(rows, slots)
    lane = lax.broadcasted_iota(jnp.int32, (slots, LANES), 1)
    taken = (lane // COLS) % 2 == 1
    own = lax.broadcasted_iota(jnp.int32, (rows, LANES), 1)
    own = (own // COLS) % 2 == 0
    for k in range(fronts):
        start = pl.multiple_of((here ^ k) * rows, 8)
        rhs[pl.ds(start, rows), :] = jnp.where(own, messages[k][0:rows, :], 0.0)
    group = max(1, 512 // slots)
    for k in range(0, fronts, group):
        chosen = messages[k : k + group]
        lines = jnp.concatenate([jnp.where(taken, ref[0:slots, :], 0.0) for ref in chosen], axis=0)
        index = jnp.concatenate(
            [
                ref[body + at // LANES : body + at // LANES + 1, 0 : min(LANES, slots - at)]
                for ref in chosen
                for at in range(0, slots, LANES)
            ],
            axis=1,
        )
        row = lax.broadcasted_iota(jnp.int32, (total, index.shape[1]), 0)
        pick = (row + 1 == index.astype(jnp.int32)).astype(BF16)
        both = dot(pick, jnp.concatenate(split(lines), axis=1))
        rhs[...] += both[:, :LANES] + both[:, LANES:]
    out[...] = complex_dot(matrix[...], rhs[...])


def leaf_to_mid(matrix, sources, *refs):
    parts, (keep, send, full) = refs[:-3], refs[-3:]
    assemble(full, parts, lax.axis_index("front"))
    mine, theirs = own_first(lax.axis_index("leaf"), *halves(complex_dot(matrix[...], full[...])))
    keep[...] = sources[...] - pack(mine)
    send[...] = -pack(theirs)


def leaf_to_root(matrix, full, keep, send):
    keep[...], send[...] = own_first(lax.axis_index("leaf"), *halves(complex_dot(matrix[...], full[...])))


def add(*refs):
    total = refs[0][...]
    for ref in refs[1:-1]:
        total = total + ref[...]
    refs[-1][...] = total


def mid_lower(matrix, *refs):
    parts, (out, whole) = refs[:-2], refs[-2:]
    assemble(whole, parts, lax.axis_index("front"), 2 * COLS)
    out[...] = pack(complex_dot(matrix[...], whole[...]))


def mid_to_root(matrix, kept, came, sources, *refs):
    parts, (keep, send, full) = refs[:-3], refs[-3:]
    assemble(full, parts, lax.axis_index("front"), 2 * COLS)
    cut = -(kept[...] + came[...] + complex_dot(matrix[...], full[...]))
    width = COLS // 2
    low = pack(jnp.concatenate([cut[:, :width], cut[:, COLS : COLS + width]], axis=1))
    high = pack(jnp.concatenate([cut[:, width:COLS], cut[:, COLS + width :]], axis=1))
    first = lax.axis_index("leaf") < 2
    keep[...] = jnp.where(first, low, high) + sources[...]
    send[...] = jnp.where(first, high, low)


def root_rows(matrix, *refs):
    parts, (out, whole) = refs[:-2], refs[-2:]
    assemble(whole, parts, lax.axis_index("front"), COLS)
    out[...] = pack(complex_dot(matrix[...], whole[...]))


def halved(value, keep, send):
    rows = keep.shape[0]
    odd = (lax.axis_index("front") & 1) == 1
    low, high = value[:rows], value[rows:]
    keep[...] = jnp.where(odd, high, low)
    send[...] = jnp.where(odd, low, high)


def root_to_mid(matrix, mine, other, keep, send, x_root):
    first = lax.axis_index("leaf") < 2
    mine, other = unpack(mine[...], COLS), unpack(other[...], COLS)
    low, high = jnp.where(first, mine, other), jnp.where(first, other, mine)
    width = COLS // 2
    x = jnp.concatenate([low[:, :width], high[:, :width], low[:, width:], high[:, width:]], axis=1)
    x_root[...] = pack(x)
    halved(pack(complex_dot(matrix[...], x)), keep, send)


def root_to_leaf(matrix, mine, other, out, forward, adjoint):
    x = by_solve(lax.axis_index("leaf"), unpack(mine[...], 2 * COLS), unpack(other[...], 2 * COLS))
    out[...] = complex_dot(matrix[...], x)
    fields_of(x, forward, adjoint, ())


def add_halves(kept, came, first, second):
    rows = first.shape[0]
    first[...] = kept[0:rows, :] + came[0:rows, :]
    second[...] = kept[rows:, :] + came[rows:, :]


def add_pair(a, b, c, d, first, second):
    first[...] = a[...] + b[...]
    second[...] = c[...] + d[...]


def sum_front(kept, sent):
    fronts = lax.axis_size("front")
    rows = kept.shape[0] // 2
    shapes = [(rows, LANES)] * 2
    a, b = kernel(add_halves, shapes, kept, swap("front", sent, 1))
    hops = [1 << i for i in range(1, fronts.bit_length() - 1)]
    for i, hop in enumerate(hops):
        back = hops[-1 - i]
        a, b = kernel(add_pair, shapes, a, swap("front", a, hop), b, swap("front", b, back))
    return [a, b, swap("front", a, 1), swap("front", b, 1)]


def summed(pieces):
    a, b, c, d = (ref[...] for ref in pieces)
    odd = (lax.axis_index("front") & 1) == 1
    mine, theirs = jnp.concatenate([a, b], axis=0), jnp.concatenate([c, d], axis=0)
    return jnp.concatenate([jnp.where(odd, theirs, mine), jnp.where(odd, mine, theirs)], axis=0)


def mid_upper(matrix, y, *refs):
    tail, out = unpack(summed(refs[:4]), 2 * COLS), refs[4]
    out[...] = pack(complex_dot(matrix[...], y[...] - tail))


def mid_to_leaf(matrix, from_root, mine, other, keep, send, x_mid):
    x = by_solve(lax.axis_index("leaf"), unpack(mine[...], 2 * COLS), unpack(other[...], 2 * COLS))
    x_mid[...] = x
    halved(complex_dot(matrix[...], x) + from_root[...], keep, send)


def leaf_upper(matrix, y, *refs):
    forward, adjoint = refs[4:]
    fields_of(complex_dot(matrix[...], y[...] - summed(refs[:4])), forward, adjoint, ())


def mid_outputs(mine, other, forward, adjoint):
    parent = lax.axis_index("leaf") // 2
    fields_of(mine[...], forward, adjoint, (parent,))
    fields_of(other[...], forward, adjoint, (1 - parent,))


def after(x, *others):
    return lax.optimization_barrier((x, *others))[0]


def body(
    leaf_lower_inv,
    leaf_upper_inv,
    leaf_to_mid_lower,
    leaf_to_root_lower,
    leaf_to_mid_upper,
    leaf_to_root_upper,
    mid_lower_inv,
    mid_upper_inv,
    mid_to_root_lower,
    mid_to_root_upper,
    root_lower_inv,
    root_upper_inv,
    leaf_sources,
    mid_sources,
    root_sources,
    receiver_data,
    receiver_block,
    receiver_offset,
):
    groups, fronts = lax.axis_size("leaf"), lax.axis_size("front")
    n0, n1, n2 = leaf_sources.shape[1], mid_sources.shape[2], root_sources.shape[1]
    s0, s1, s2 = n0 * fronts, n1 * fronts, n2 * fronts
    slots, count = fronts * CAP, receiver_data.shape[1]
    dma = pltpu.SemaphoreType.DMA

    with jax.named_scope("right_hand_sides"):
        payload = kernel(
            functools.partial(pack_receivers, fronts, n0),
            [(slots, LANES)] * groups,
            receiver_data,
            receiver_block.reshape(1, -1),
            receiver_offset.reshape(1, -1),
            scratch=[
                pltpu.VMEM((2, count, COLS), F32),
                pltpu.VMEM((1, count), jnp.int32),
                pltpu.VMEM((1, count), jnp.int32),
                dma((3,)),
            ],
            hbm=range(3),
        )
        arrived = [payload[0]] + [swap("leaf", payload[k], k) for k in range(1, groups)]
        leaf_own, mid_own, root_own = kernel(
            load_sources,
            [(n0, LANES), (n1 // 2, LANES), (n2 // 4, LANES)],
            after(leaf_sources.transpose(0, 2, 1), *payload),
            mid_sources.transpose(0, 1, 3, 2),
            root_sources.transpose(0, 2, 1),
            scratch=[
                pltpu.VMEM((2, COLS, n0), F32),
                pltpu.VMEM((2, COLS, n1), F32),
                pltpu.VMEM((2, COLS, n2), F32),
                dma((3,)),
            ],
            hbm=range(3),
        )
        ll, l2m = load((after(leaf_lower_inv, leaf_own), "leaf"), (leaf_to_mid_lower, "leaf"))
        (message,) = kernel(
            pack_leaf, [(sum(message_rows(n0, groups * slots)), LANES)], after(leaf_own, ll), *arrived
        )
    with jax.named_scope("leaf_lower"):
        messages = gather_front(message)
        ml, m2r = load((after(mid_lower_inv, message), "own"), (mid_to_root_lower, "own"))
        (y_leaf,) = kernel(
            functools.partial(leaf_lower, groups * slots),
            [(n0, LANES)],
            after(ll, ml),
            *messages,
            scratch=[pltpu.VMEM((s0, LANES), F32)],
        )
    with jax.named_scope("mid_lower"):
        parts = gather_front(y_leaf)
        (l2r,) = load((after(leaf_to_root_lower, y_leaf), "leaf"))
        keep, send, y_full = kernel(
            leaf_to_mid,
            [(n1 // 2, LANES), (n1 // 2, LANES), (s0, LANES)],
            after(l2m, l2r),
            mid_own,
            *parts,
        )
        came = swap("leaf", send, 1)
        root_kept, root_sent = kernel(leaf_to_root, [(n2, 2 * COLS)] * 2, l2r, after(y_full, send))
        (cut_mid,) = kernel(add, [(n1 // 2, LANES)], after(keep, root_kept), came)
        parts = gather_front(cut_mid)
        root_came = swap("leaf", root_sent, 1)
        (rl,) = load((after(root_lower_inv, cut_mid), None))
        (y_mid,) = kernel(
            mid_lower,
            [(n1 // 2, LANES)],
            after(ml, rl),
            *parts,
            scratch=[pltpu.VMEM((s1, 2 * COLS), F32)],
        )
    with jax.named_scope("root_cut"):
        parts = gather_front(y_mid)
        (ru,) = load((after(root_upper_inv, y_mid), None))
        keep, send, y_mid_full = kernel(
            mid_to_root,
            [(n2 // 4, LANES), (n2 // 4, LANES), (s1, 2 * COLS)],
            after(m2r, ru),
            root_kept,
            root_came,
            root_own,
            *parts,
        )
        came = swap("leaf", send, 2)
        mu, l2r_up = load((after(mid_upper_inv, send), "own"), (leaf_to_root_upper, "leaf"))
        (cut_root,) = kernel(add, [(n2 // 4, LANES)], after(keep, mu), came)
    with jax.named_scope("root_solve"):
        parts = gather_front(cut_root)
        (m2r_up,) = load((after(mid_to_root_upper, cut_root), "own"))
        (y_root,) = kernel(
            root_rows,
            [(n2 // 4, LANES)],
            after(rl, m2r_up),
            *parts,
            scratch=[pltpu.VMEM((s2, COLS), F32)],
        )
        parts = gather_front(y_root)
        l2m_up, lu = load((after(leaf_to_mid_upper, y_root), "leaf"), (leaf_upper_inv, "leaf"))
        (x_root,) = kernel(
            root_rows,
            [(n2 // 4, LANES)],
            after(ru, lu),
            *parts,
            scratch=[pltpu.VMEM((s2, COLS), F32)],
        )
    with jax.named_scope("mid_upper"):
        keep, send, x_root = kernel(
            root_to_mid,
            [(s1 // 4, LANES)] * 2 + [(n2 // 2, LANES)],
            m2r_up,
            x_root,
            swap("leaf", x_root, 2),
        )
        pieces = sum_front(keep, send)
        (x_mid,) = kernel(mid_upper, [(n1 // 2, LANES)], mu, y_mid_full, *pieces)
        from_root, root_field, root_adjoint = kernel(
            root_to_leaf,
            [(s0, LANES), (2, COLS, n2), (2, COLS, n2)],
            l2r_up,
            x_root,
            swap("leaf", after(x_root, send), 1),
        )
    with jax.named_scope("leaf_upper"):
        keep, send, x_mid = kernel(
            mid_to_leaf,
            [(s0 // 2, LANES)] * 2 + [(n1, LANES)],
            l2m_up,
            from_root,
            x_mid,
            swap("leaf", x_mid, 1),
        )
        pieces = sum_front(keep, send)
        x_other = swap("leaf", after(x_mid, send), 2)
        mid_field, mid_adjoint = kernel(mid_outputs, [(2, 2, COLS, n1)] * 2, x_mid, x_other)
        leaf_field, leaf_adjoint = kernel(leaf_upper, [(2, COLS, n0)] * 2, lu, y_full, *pieces)
    return tuple(
        jnp.swapaxes(x, -1, -2)
        for x in (leaf_field, mid_field, root_field, leaf_adjoint, mid_adjoint, root_adjoint)
    )


def solution(mesh):
    in_specs = (
        P(None, "leaf", "front", None),
        P(None, "leaf", "front", None),
        P(None, "leaf", "front", None),
        P(None, "leaf", "front", None),
        P(None, "leaf", None, "front"),
        P(None, "leaf", None, "front"),
        P(None, None, "front", None),
        P(None, None, "front", None),
        P(None, None, "front", None),
        P(None, None, None, "front"),
        P(None, "front", None),
        P(None, "front", None),
        P(None, ("leaf", "front"), None),
        P(None, None, "front", None),
        P(None, "front", None),
        P(None, ("leaf", "front"), None),
        P(("leaf", "front"), None),
        P(("leaf", "front")),
    )
    out_specs = (
        P(None, ("leaf", "front"), None),
        P(None, None, "front", None),
        P(None, "front", None),
        P(None, ("leaf", "front"), None),
        P(None, None, "front", None),
        P(None, "front", None),
    )
    return jax.shard_map(body, mesh=mesh, in_specs=in_specs, out_specs=out_specs, check_vma=False)
```

```python
import functools

import jax
import jax.numpy as jnp
from jax import lax
from jax.experimental import pallas as pl
from jax.experimental.pallas import tpu as pltpu
from jax.sharding import PartitionSpec as P

CAP = 2
LANES = 128
COLS = 32
F32 = jnp.float32
BF16 = jnp.bfloat16
VM = pl.BlockSpec(memory_space=pltpu.VMEM)
HB = pl.BlockSpec(memory_space=pltpu.HBM)


def split(x):
    high = x.astype(BF16)
    return high, (x - high.astype(F32)).astype(BF16)


def dot(a, b):
    return jnp.dot(a, b, preferred_element_type=F32)


def complex_dot(matrix, x):
    half = x.shape[1] // 2
    turned = jnp.concatenate([-x[:, half:], x[:, :half]], axis=1)
    both = jnp.concatenate([x, turned], axis=0)
    columns = jnp.concatenate(split(both), axis=1)
    product = dot(matrix, columns)
    rows, n = product.shape[0] // 2, x.shape[1]
    return (product[:rows, n:] + product[rows:, :n]) + product[:rows, :n]


def pack(x):
    chunks = LANES // x.shape[1]
    rows = x.shape[0] // chunks
    return jnp.concatenate([x[rows * j : rows * j + rows] for j in range(chunks)], axis=1)


def unpack(x, width):
    return jnp.concatenate([x[:, at : at + width] for at in range(0, LANES, width)], axis=0)


def quarter_of(x, q):
    w = COLS // 2
    return pack(jnp.concatenate([x[:, w * q : w * q + w], x[:, 64 + w * q : 64 + w * q + w]], axis=1))


def all_quarters(quarters):
    w = COLS // 2
    return jnp.concatenate([x[:, :w] for x in quarters] + [x[:, w:] for x in quarters], axis=1)


def send_quarters(x, held, outs):
    here = lax.axis_index("leaf")
    for q in range(len(outs)):
        held[q] = quarter_of(x, q)
    for k, out in enumerate(outs):
        out[...] = held[here ^ k]


def take_quarters(parts, held):
    here = lax.axis_index("leaf")
    for k, part in enumerate(parts):
        held[here ^ k] = part[...]
    return all_quarters([unpack(held[q], COLS) for q in range(len(parts))])


def assemble(where, parts, here, width=LANES):
    rows = parts[0].shape[0] * (LANES // width)
    for k, part in enumerate(parts):
        start = pl.multiple_of((here ^ k) * rows, 8)
        where[pl.ds(start, rows), :] = part[...] if width == LANES else unpack(part[...], width)


def fields_of(x, forward, adjoint, where):
    y = x.T
    c = COLS
    forward[(0, *where)] = y[0:c]
    forward[(1, *where)] = y[2 * c : 3 * c]
    adjoint[(0, *where)] = y[c : 2 * c]
    adjoint[(1, *where)] = -y[3 * c :]


def swap(axis, x, k):
    size = lax.axis_size(axis)
    return lax.ppermute(x, axis, [(i, i ^ k) for i in range(size)])


def gather_front(x, meanwhile=None):
    fronts = lax.axis_size("front")
    mine = {0: x}
    for k in range(fronts - 2, 0, -2):
        mine[k] = swap("front", x, k)
    extra = tuple(meanwhile(x)) if meanwhile else ()
    other = {}
    for k in range(fronts - 2, -1, -2):
        other[k] = swap("front", after(mine[k], *extra) if k and extra else mine[k], 1)
    return [held[k] for k in range(0, fronts, 2) for held in (mine, other)], extra


def planes(x):
    groups = lax.axis_size("leaf")
    blocks = x if isinstance(x, (list, tuple)) else [x] * groups
    came = {k: swap("leaf", blocks[k], k) for k in range(groups - 1, 0, -1)}
    return [blocks[0]] + [came[k] for k in range(1, groups)]


def kernel(fn, outs, *args, scratch=(), vmem=8, work=0, hbm=()):
    outs = [o if isinstance(o[0], tuple) else (o, F32) for o in outs]
    return pl.pallas_call(
        fn,
        out_shape=[jax.ShapeDtypeStruct(*o) for o in outs],
        in_specs=[HB if i in hbm else VM for i in range(len(args))],
        out_specs=[VM] * len(outs),
        scratch_shapes=list(scratch),
        compiler_params=pltpu.CompilerParams(vmem_limit_bytes=vmem * 2**20),
        cost_estimate=pl.CostEstimate(flops=work, bytes_accessed=work // 700, transcendentals=0),
    )(*(pltpu.with_memory_space_constraint(a, pltpu.HBM) if i in hbm else a for i, a in enumerate(args)))


def load_matrices(picks, *refs):
    count = len(picks)
    sources, outs, buffers, sems = (
        refs[:count],
        refs[count : 2 * count],
        refs[2 * count : 3 * count],
        refs[3 * count],
    )
    copies = []
    for i, (src, pick) in enumerate(zip(sources, picks)):
        rows = buffers[i].shape[1]
        step = rows // 2 if rows >= 128 else rows
        for n, at in enumerate(range(0, rows, step)):
            span = pl.ds(at, step)
            view = src.at[:, span, :] if pick is None else src.at[:, pick, span, :]
            copy = pltpu.make_async_copy(view, buffers[i].at[:, span, :], sems.at[2 * i + n])
            copy.start()
            copies.append((i, at, step, copy))
    for i, at, step, copy in copies:
        copy.wait()
        rows, depth = buffers[i].shape[1:]
        for part in range(2):
            high, low = split(buffers[i][part, at : at + step, :])
            outs[i][at : at + step, part * depth : part * depth + depth] = high
            outs[i][rows + at : rows + at + step, part * depth : part * depth + depth] = low


def load(*matrices):
    shapes = [m.shape[-2:] for m, _ in matrices]
    size = sum(r * d for r, d in shapes)
    return kernel(
        functools.partial(load_matrices, tuple(pick for _, pick in matrices)),
        [((2 * r, 2 * d), BF16) for r, d in shapes],
        *[m for m, _ in matrices],
        scratch=[pltpu.VMEM((2, r, d), F32) for r, d in shapes]
        + [pltpu.SemaphoreType.DMA((2 * len(shapes),))],
        hbm=range(len(shapes)),
        vmem=4 + -(-size * 8 // 2**20),
        work=size * 1000,
    )


def pack_receivers(fronts, rows, data_hbm, block_hbm, offset_hbm, *refs):
    groups = lax.axis_size("leaf")
    outs = refs[:groups]
    data, block, offset, sems = refs[groups:]
    copies = [
        pltpu.make_async_copy(src, dst, sems.at[i])
        for i, (src, dst) in enumerate(((data_hbm, data), (block_hbm, block), (offset_hbm, offset)))
    ]
    for copy in copies:
        copy.start()
    for copy in copies:
        copy.wait()
    group = lax.axis_index("leaf")
    count = data.shape[1]
    slots = fronts * CAP
    down = lax.broadcasted_iota(jnp.int32, (count, count), 0)
    across = lax.broadcasted_iota(jnp.int32, (count, count), 1)
    eye = down == across
    block_row = block[...]
    block_col = jnp.sum(jnp.where(eye, block_row, 0), axis=1, keepdims=True)
    offset_col = jnp.sum(jnp.where(eye, offset[...], 0), axis=1, keepdims=True)
    same = (block_col == block_row) & (down < across)
    slot_row = block_row * CAP + jnp.sum(same.astype(jnp.int32), axis=0, keepdims=True)
    row_col = (block_col & (fronts - 1)) * rows + offset_col + 1
    lane = lax.broadcasted_iota(jnp.int32, (count, COLS), 1)
    index = jnp.where(lane == 0, row_col, 0).astype(F32)
    lines = jnp.concatenate([index, data[0], jnp.zeros((count, COLS), F32), -data[1]], axis=1)
    for k, out in enumerate(outs):
        first = (group ^ k) * slots
        pick = lax.broadcasted_iota(jnp.int32, (slots, count), 0) + first == slot_row
        out[...] = jnp.dot(
            pick.astype(F32), lines, precision=lax.Precision.HIGHEST, preferred_element_type=F32
        )


def load_sources(leaf_hbm, mid_hbm, root_hbm, leaf_out, mid_out, root_out, leaf, mid, root, sems):
    group = lax.axis_index("leaf")
    copies = [
        pltpu.make_async_copy(src, dst, sems.at[i])
        for i, (src, dst) in enumerate(((leaf_hbm, leaf), (mid_hbm, mid), (root_hbm, root)))
    ]
    for copy in copies:
        copy.start()
    for copy in copies:
        copy.wait()
    forward = (group < 2).astype(F32)
    real, imag = leaf[0].T, leaf[1].T
    zero = jnp.zeros_like(real)
    leaf_out[...] = jnp.concatenate([real, zero, imag, zero], axis=1)
    width = COLS // 2

    def quarter(real, imag):
        low = jnp.concatenate([real[:width], imag[:width]], axis=0)
        high = jnp.concatenate([real[width:], imag[width:]], axis=0)
        return pack(jnp.where(group == 0, low, high).T) * forward

    mid_out[...] = jnp.concatenate([quarter(mid[0, p], mid[1, p]) for p in range(2)], axis=0)
    root_out[...] = quarter(root[0], root[1])


def message_rows(rows, slots):
    return max(rows, slots), 8 * -(-slots // (8 * LANES))


def pack_leaf(own, *refs):
    arrived, out = refs[:-1], refs[-1]
    lines = jnp.concatenate([ref[...] for ref in arrived], axis=0)
    slots = lines.shape[0]
    body, tail = message_rows(own.shape[0], slots)
    lane = lax.broadcasted_iota(jnp.int32, (slots, LANES), 1)
    data = jnp.where((lane // COLS) % 2 == 1, lines, 0.0)
    index = lines[:, 0:1]

    def padded(x):
        if x.shape[0] == body:
            return x
        return jnp.concatenate([x, jnp.zeros((body - x.shape[0], LANES), F32)], axis=0)

    out[0:body, :] = padded(own[...]) + padded(data)
    out[body:, :] = jnp.zeros((tail, LANES), F32)
    for at in range(0, slots, LANES):
        size = min(LANES, slots - at)
        eye = lax.broadcasted_iota(jnp.int32, (size, size), 0) == lax.broadcasted_iota(
            jnp.int32, (size, size), 1
        )
        line = jnp.sum(jnp.where(eye, index[at : at + size], 0.0), axis=0, keepdims=True)
        out[body + at // LANES : body + at // LANES + 1, 0:size] = line


def leaf_lower(slots, matrix, *refs):
    messages, (out, rhs) = refs[:-2], refs[-2:]
    fronts, rows = len(messages), out.shape[0]
    here = lax.axis_index("front")
    total = rows * fronts
    body, _ = message_rows(rows, slots)
    lane = lax.broadcasted_iota(jnp.int32, (slots, LANES), 1)
    taken = (lane // COLS) % 2 == 1
    own = lax.broadcasted_iota(jnp.int32, (rows, LANES), 1)
    own = (own // COLS) % 2 == 0
    for k in range(fronts):
        start = pl.multiple_of((here ^ k) * rows, 8)
        rhs[pl.ds(start, rows), :] = jnp.where(own, messages[k][0:rows, :], 0.0)
    group = max(1, 512 // slots)
    for k in range(0, fronts, group):
        chosen = messages[k : k + group]
        lines = jnp.concatenate([jnp.where(taken, ref[0:slots, :], 0.0) for ref in chosen], axis=0)
        index = jnp.concatenate(
            [
                ref[body + at // LANES : body + at // LANES + 1, 0 : min(LANES, slots - at)]
                for ref in chosen
                for at in range(0, slots, LANES)
            ],
            axis=1,
        )
        row = lax.broadcasted_iota(jnp.int32, (total, index.shape[1]), 0)
        pick = (row + 1 == index.astype(jnp.int32)).astype(BF16)
        both = dot(pick, jnp.concatenate(split(lines), axis=1))
        rhs[...] += both[:, :LANES] + both[:, LANES:]
    out[...] = complex_dot(matrix[...], rhs[...])


def leaf_to_mid(matrix, *refs):
    parts, outs, (full, held) = refs[:-6], refs[-6:-2], refs[-2:]
    assemble(full, parts, lax.axis_index("front"))
    send_quarters(complex_dot(matrix[...], full[...]), held, outs)


def leaf_to_root(matrix, full, *refs):
    send_quarters(complex_dot(matrix[...], full[...]), refs[-1], refs[:-1])


def cut_mids(sources, own, sibling, far, other, out):
    parent = lax.axis_index("leaf") // 2
    rows = own.shape[0]
    for at, value in ((parent, own[...] + sibling[...]), (1 - parent, far[...] + other[...])):
        span = pl.ds(pl.multiple_of(at * rows, 8), rows)
        out[span, :] = sources[span, :] - value


def assemble_mids(where, parts):
    here = lax.axis_index("front")
    for k, part in enumerate(parts):
        half = part.shape[0] // 2
        rows = half * (LANES // COLS)
        start = pl.multiple_of((here ^ k) * rows, 8)
        for p in range(2):
            where[p, pl.ds(start, rows), :] = unpack(part[half * p : half * p + half, :], COLS)


def mid_lower(first, second, *refs):
    parts, (out, whole) = refs[:-2], refs[-2:]
    assemble_mids(whole, parts)
    out[...] = jnp.concatenate(
        [pack(complex_dot(matrix[...], whole[p])) for p, matrix in enumerate((first, second))], axis=0
    )


def mid_to_root(first, second, sources, a, b, c, d, *refs):
    parts, (out, whole) = refs[:-2], refs[-2:]
    assemble_mids(whole, parts)
    known = sources[...] - ((a[...] + b[...]) + (c[...] + d[...]))
    out[...] = known - pack(complex_dot(first[...], whole[0]) + complex_dot(second[...], whole[1]))


def root_rows(matrix, *refs):
    parts, (out, whole) = refs[:-2], refs[-2:]
    assemble(whole, parts, lax.axis_index("front"), COLS)
    out[...] = pack(complex_dot(matrix[...], whole[...]))


def halved(value, keep, send):
    rows = keep.shape[0]
    odd = (lax.axis_index("front") & 1) == 1
    low, high = value[:rows], value[rows:]
    keep[...] = jnp.where(odd, high, low)
    send[...] = jnp.where(odd, low, high)


def root_to_mid(first, second, quarter, y, keep, send, terms):
    x = unpack(quarter[...], COLS)
    rows = keep.shape[0]
    half = y.shape[0] // 2
    height = half * (LANES // COLS)
    start = pl.multiple_of(lax.axis_index("front") * height, 8)
    for p, matrix in enumerate((first, second)):
        terms[...] = complex_dot(matrix[...], x)
        terms[pl.ds(start, height), :] -= unpack(y[half * p : half * p + half, :], COLS)
        value = pack(terms[...])
        kept = (lax.axis_index("front") & 1) == p

        @pl.when(kept)
        def _():
            keep[...] = value

        @pl.when(jnp.logical_not(kept))
        def _():
            send[...] = value


def root_to_leaf(matrix, *refs):
    parts, (out, forward, adjoint, held) = refs[:-4], refs[-4:]
    x = take_quarters(parts, held)
    out[...] = complex_dot(matrix[...], x)
    fields_of(x, forward, adjoint, ())


def halved(value, keep, send):
    rows = keep.shape[0]
    odd = (lax.axis_index("front") & 1) == 1
    low, high = value[:rows], value[rows:]
    keep[...] = jnp.where(odd, high, low)
    send[...] = jnp.where(odd, low, high)


def add_halves(kept, came, first, second):
    rows = first.shape[0]
    first[...] = kept[0:rows, :] + came[0:rows, :]
    second[...] = kept[rows:, :] + came[rows:, :]


def add_pair(a, b, c, d, first, second):
    first[...] = a[...] + b[...]
    second[...] = c[...] + d[...]


def sum_front(kept, sent):
    fronts = lax.axis_size("front")
    rows = kept.shape[0] // 2
    shapes = [(rows, LANES)] * 2
    a, b = kernel(add_halves, shapes, kept, swap("front", sent, 1))
    hops = [1 << i for i in range(1, fronts.bit_length() - 1)]
    for i, hop in enumerate(hops):
        back = hops[-1 - i]
        a, b = kernel(add_pair, shapes, a, swap("front", a, hop), b, swap("front", b, back))
    return [a, b, swap("front", a, 1), swap("front", b, 1)]


def summed(pieces):
    a, b, c, d = (ref[...] for ref in pieces)
    odd = (lax.axis_index("front") & 1) == 1
    mine, theirs = jnp.concatenate([a, b], axis=0), jnp.concatenate([c, d], axis=0)
    return jnp.concatenate([jnp.where(odd, theirs, mine), jnp.where(odd, mine, theirs)], axis=0)


def mid_upper(first, second, *refs):
    value, out = summed(refs[:4]), refs[4]
    rows = value.shape[0] // 2
    out[...] = -jnp.concatenate(
        [
            pack(complex_dot(matrix[...], unpack(value[rows * p : rows * p + rows], COLS)))
            for p, matrix in enumerate((first, second))
        ],
        axis=0,
    )


def mid_to_leaf(matrix, from_root, *refs):
    parts, (keep, send, held) = refs[:-3], refs[-3:]
    half = parts[0].shape[0] // 2
    start = pl.multiple_of(lax.axis_index("leaf") // 2 * half, 8)
    x = take_quarters([part[pl.ds(start, half), :] for part in parts], held)
    halved(complex_dot(matrix[...], x) + from_root[...], keep, send)


def leaf_upper(matrix, y, *refs):
    forward, adjoint = refs[4:]
    fields_of(complex_dot(matrix[...], y[...] - summed(refs[:4])), forward, adjoint, ())


def mid_outputs(*refs):
    parts, (forward, adjoint, held) = refs[:-3], refs[-3:]
    half = parts[0].shape[0] // 2
    for p in range(2):
        x = take_quarters([part[half * p : half * p + half, :] for part in parts], held)
        fields_of(x, forward, adjoint, (p,))


def after(x, *others):
    return lax.optimization_barrier((x, *others))[0]


def body(
    leaf_lower_inv,
    leaf_upper_inv,
    leaf_to_mid_lower,
    leaf_to_root_lower,
    leaf_to_mid_upper,
    leaf_to_root_upper,
    mid_lower_inv,
    mid_upper_inv,
    mid_to_root_lower,
    mid_to_root_upper,
    root_lower_inv,
    root_upper_inv,
    leaf_sources,
    mid_sources,
    root_sources,
    receiver_data,
    receiver_block,
    receiver_offset,
):
    groups, fronts = lax.axis_size("leaf"), lax.axis_size("front")
    n0, n1, n2 = leaf_sources.shape[1], mid_sources.shape[2], root_sources.shape[1]
    s0, s1, s2 = n0 * fronts, n1 * fronts, n2 * fronts
    slots, count = fronts * CAP, receiver_data.shape[1]
    dma = pltpu.SemaphoreType.DMA

    vmem = pltpu.VMEM

    with jax.named_scope("right_hand_sides"):
        payload = kernel(
            functools.partial(pack_receivers, fronts, n0),
            [(slots, LANES)] * groups,
            receiver_data,
            receiver_block.reshape(1, -1),
            receiver_offset.reshape(1, -1),
            scratch=[
                vmem((2, count, COLS), F32),
                vmem((1, count), jnp.int32),
                vmem((1, count), jnp.int32),
                dma((3,)),
            ],
            hbm=range(3),
        )
        arrived = planes(payload)
        leaf_own, mid_own, root_own = kernel(
            load_sources,
            [(n0, LANES), (n1 // 2, LANES), (n2 // 4, LANES)],
            after(leaf_sources.transpose(0, 2, 1), *payload),
            mid_sources.transpose(0, 1, 3, 2),
            root_sources.transpose(0, 2, 1),
            scratch=[
                vmem((2, COLS, n0), F32),
                vmem((2, 2, COLS, n1), F32),
                vmem((2, COLS, n2), F32),
                dma((3,)),
            ],
            hbm=range(3),
        )
        ll, l2m, l2r = load(
            (after(leaf_lower_inv, leaf_own), 0), (leaf_to_mid_lower, 0), (leaf_to_root_lower, 0)
        )
        (message,) = kernel(
            pack_leaf, [(sum(message_rows(n0, groups * slots)), LANES)], after(leaf_own, ll), *arrived
        )
    with jax.named_scope("leaf_lower"):
        messages, ml = gather_front(
            message, lambda x: load((after(mid_lower_inv, x), 0), (mid_lower_inv, 1))
        )
        (y_leaf,) = kernel(
            functools.partial(leaf_lower, groups * slots),
            [(n0, LANES)],
            ll,
            *messages,
            scratch=[vmem((s0, LANES), F32)],
        )
    with jax.named_scope("mid_lower"):
        parts, m2r = gather_front(
            y_leaf, lambda x: load((after(mid_to_root_lower, x), 0), (mid_to_root_lower, 1))
        )
        *blocks, y_full = kernel(
            leaf_to_mid,
            [(n1 // 4, LANES)] * groups + [(s0, LANES)],
            l2m,
            *parts,
            scratch=[vmem((groups, n1 // 4, LANES), F32)],
        )
        came = planes(blocks)
        to_root = kernel(
            leaf_to_root,
            [(n2 // 4, LANES)] * groups,
            l2r,
            after(y_full, *blocks),
            scratch=[vmem((groups, n2 // 4, LANES), F32)],
        )
        (cut_mid,) = kernel(cut_mids, [(n1 // 2, LANES)], after(mid_own, *to_root), *came)
        parts, (rl,) = gather_front(cut_mid, lambda x: load((after(root_lower_inv, x), None)))
        (y_mid,) = kernel(
            mid_lower, [(n1 // 2, LANES)], *ml, *parts, scratch=[vmem((2, s1, COLS), F32)]
        )
    with jax.named_scope("root_cut"):
        parts, (ru,) = gather_front(y_mid, lambda x: load((after(root_upper_inv, x), None)))
        from_leaves = planes([after(block, cut_mid) for block in to_root])
        (cut_root,) = kernel(
            mid_to_root,
            [(n2 // 4, LANES)],
            *m2r,
            root_own,
            *from_leaves,
            *parts,
            scratch=[vmem((2, s1, COLS), F32)],
        )
    with jax.named_scope("root_solve"):
        parts, m2r_up = gather_front(
            cut_root, lambda x: load((after(mid_to_root_upper, x), 0), (mid_to_root_upper, 1))
        )
        (y_root,) = kernel(
            root_rows, [(n2 // 4, LANES)], rl, *parts, scratch=[vmem((s2, COLS), F32)]
        )
        parts, (*mu, l2r_up, l2m_up, lu) = gather_front(
            y_root,
            lambda x: load(
                (after(mid_upper_inv, x), 0),
                (mid_upper_inv, 1),
                (leaf_to_root_upper, 0),
                (leaf_to_mid_upper, 0),
                (leaf_upper_inv, 0),
            ),
        )
        (x_root,) = kernel(
            root_rows, [(n2 // 4, LANES)], ru, *parts, scratch=[vmem((s2, COLS), F32)]
        )
    with jax.named_scope("mid_upper"):
        keep, send = kernel(
            root_to_mid,
            [(s1 // 4, LANES)] * 2,
            *m2r_up,
            x_root,
            y_mid,
            scratch=[vmem((s1, COLS), F32)],
        )
        pieces = sum_front(keep, send)
        (x_mid,) = kernel(mid_upper, [(n1 // 2, LANES)], *mu, *pieces)
        from_root, root_field, root_adjoint = kernel(
            root_to_leaf,
            [(s0, LANES), (2, COLS, n2), (2, COLS, n2)],
            l2r_up,
            *planes(after(x_root, send)),
            scratch=[vmem((groups, n2 // 4, LANES), F32)],
        )
    with jax.named_scope("leaf_upper"):
        x_mids = planes(x_mid)
        keep, send = kernel(
            mid_to_leaf,
            [(s0 // 2, LANES)] * 2,
            l2m_up,
            from_root,
            *x_mids,
            scratch=[vmem((groups, n1 // 4, LANES), F32)],
        )
        pieces = sum_front(keep, send)
        mid_field, mid_adjoint = kernel(
            mid_outputs,
            [(2, 2, COLS, n1)] * 2,
            after(x_mids[0], send),
            *x_mids[1:],
            scratch=[vmem((groups, n1 // 4, LANES), F32)],
        )
        leaf_field, leaf_adjoint = kernel(leaf_upper, [(2, COLS, n0)] * 2, lu, y_full, *pieces)
    return tuple(
        jnp.swapaxes(x, -1, -2)
        for x in (leaf_field, mid_field, root_field, leaf_adjoint, mid_adjoint, root_adjoint)
    )


def solution(mesh):
    in_specs = (
        P(None, "leaf", "front", None),
        P(None, "leaf", "front", None),
        P(None, "leaf", "front", None),
        P(None, "leaf", "front", None),
        P(None, "leaf", None, "front"),
        P(None, "leaf", None, "front"),
        P(None, None, "front", None),
        P(None, None, "front", None),
        P(None, None, "front", None),
        P(None, None, None, "front"),
        P(None, "front", None),
        P(None, "front", None),
        P(None, ("leaf", "front"), None),
        P(None, None, "front", None),
        P(None, "front", None),
        P(None, ("leaf", "front"), None),
        P(("leaf", "front"), None),
        P(("leaf", "front")),
    )
    out_specs = (
        P(None, ("leaf", "front"), None),
        P(None, None, "front", None),
        P(None, "front", None),
        P(None, ("leaf", "front"), None),
        P(None, None, "front", None),
        P(None, "front", None),
    )
    return jax.shard_map(body, mesh=mesh, in_specs=in_specs, out_specs=out_specs, check_vma=False)
```

```python
import functools

import jax
import jax.numpy as jnp
from jax import lax
from jax.experimental import pallas as pl
from jax.experimental.pallas import tpu as pltpu
from jax.sharding import PartitionSpec as P

CAP = 2
CHUNKS = 4
LANES = 128
COLS = 32
F32 = jnp.float32
BF16 = jnp.bfloat16
VM = pl.BlockSpec(memory_space=pltpu.VMEM)
HB = pl.BlockSpec(memory_space=pltpu.HBM)


def split(x):
    high = x.astype(BF16)
    return high, (x - high.astype(F32)).astype(BF16)


def dot(a, b):
    return jnp.dot(a, b, preferred_element_type=F32)


def complex_dot(matrix, x):
    half = x.shape[1] // 2
    turned = jnp.concatenate([-x[:, half:], x[:, :half]], axis=1)
    both = jnp.concatenate([x, turned], axis=0)
    columns = jnp.concatenate(split(both), axis=1)
    product = dot(matrix, columns)
    rows, n = product.shape[0] // 2, x.shape[1]
    return (product[:rows, n:] + product[rows:, :n]) + product[:rows, :n]


def pack(x):
    chunks = LANES // x.shape[1]
    rows = x.shape[0] // chunks
    return jnp.concatenate([x[rows * j : rows * j + rows] for j in range(chunks)], axis=1)


def unpack(x, width):
    return jnp.concatenate([x[:, at : at + width] for at in range(0, LANES, width)], axis=0)


def halves(x):
    c = COLS
    return (
        jnp.concatenate([x[:, :c], x[:, 2 * c : 3 * c]], axis=1),
        jnp.concatenate([x[:, c : 2 * c], x[:, 3 * c :]], axis=1),
    )


def joined(forward, adjoint):
    c = COLS
    return jnp.concatenate([forward[:, :c], adjoint[:, :c], forward[:, c:], adjoint[:, c:]], axis=1)


def own_first(group, forward, adjoint):
    even = (group & 1) == 0
    return jnp.where(even, forward, adjoint), jnp.where(even, adjoint, forward)


def by_solve(group, own, other):
    even = (group & 1) == 0
    return joined(jnp.where(even, own, other), jnp.where(even, other, own))


def assemble(where, parts, here, width=LANES):
    rows = parts[0].shape[0] * (LANES // width)
    for k, part in zip(origins(len(parts)), parts):
        start = pl.multiple_of((here ^ k) * rows, 8)
        where[pl.ds(start, rows), :] = part[...] if width == LANES else unpack(part[...], width)


def fields_of(x, forward, adjoint, where):
    y = x.T
    c = COLS
    forward[(0, *where)] = y[0:c]
    forward[(1, *where)] = y[2 * c : 3 * c]
    adjoint[(0, *where)] = y[c : 2 * c]
    adjoint[(1, *where)] = -y[3 * c :]


def swap(axis, x, k):
    size = lax.axis_size(axis)
    return lax.ppermute(x, axis, [(i, i ^ k) for i in range(size)])


def gather_front(x, meanwhile=None):
    fronts = lax.axis_size("front")
    mine = [x] + [swap("front", x, k) for k in range(2, fronts, 2)]
    extra = tuple(meanwhile(x)) if meanwhile else ()
    other = [swap("front", after(y, *extra) if i == 1 and extra else y, 1) for i, y in enumerate(mine)]
    pairs = list(zip(mine, other))
    return [block for pair in pairs[:1] + pairs[:0:-1] for block in pair], extra


def origins(count):
    evens = [0, *range(count - 2, 0, -2)]
    return [e + core for e in evens for core in range(2)]


def kernel(fn, outs, *args, scratch=(), vmem=8, work=0, hbm=(), pinned=()):
    outs = [o if isinstance(o[0], tuple) else (o, F32) for o in outs]
    return pl.pallas_call(
        fn,
        out_shape=[jax.ShapeDtypeStruct(*o) for o in outs],
        in_specs=[HB if i in hbm else VM for i in range(len(args))],
        out_specs=[VM] * len(outs),
        scratch_shapes=list(scratch),
        compiler_params=pltpu.CompilerParams(vmem_limit_bytes=vmem * 2**20),
        cost_estimate=pl.CostEstimate(flops=work, bytes_accessed=work // 700, transcendentals=0),
    )(*(pltpu.with_memory_space_constraint(a, pltpu.HBM) if i in pinned else a for i, a in enumerate(args)))


def load_matrices(picks, *refs):
    count = len(picks)
    sources, outs, buffers, sems = (
        refs[:count],
        refs[count : 2 * count],
        refs[2 * count : 3 * count],
        refs[3 * count],
    )
    parent = lax.axis_index("leaf") // 2
    copies = []
    for i, (src, pick) in enumerate(zip(sources, picks)):
        rows = buffers[i].shape[1]
        step = max(rows // CHUNKS, 16)
        for n, at in enumerate(range(0, rows, step)):
            span = pl.ds(at, step)
            view = src.at[:, span, :] if pick is None else src.at[:, parent if pick == "own" else 0, span, :]
            copy = pltpu.make_async_copy(view, buffers[i].at[:, span, :], sems.at[CHUNKS * i + n])
            copy.start()
            copies.append((i, at, step, copy))
    for i, at, step, copy in copies:
        copy.wait()
        rows, depth = buffers[i].shape[1:]
        for part in range(2):
            high, low = split(buffers[i][part, at : at + step, :])
            outs[i][at : at + step, part * depth : part * depth + depth] = high
            outs[i][rows + at : rows + at + step, part * depth : part * depth + depth] = low


def load(*matrices, pinned=False):
    shapes = [m.shape[-2:] for m, _ in matrices]
    size = sum(r * d for r, d in shapes)
    return kernel(
        functools.partial(load_matrices, tuple(pick for _, pick in matrices)),
        [((2 * r, 2 * d), BF16) for r, d in shapes],
        *[m for m, _ in matrices],
        scratch=[pltpu.VMEM((2, r, d), F32) for r, d in shapes]
        + [pltpu.SemaphoreType.DMA((CHUNKS * len(shapes),))],
        hbm=range(len(shapes)),
        pinned=range(len(shapes)) if pinned else (),
        vmem=4 + -(-size * 8 // 2**20),
        work=size * 1000,
    )


def pack_receivers(fronts, rows, data_hbm, block_hbm, offset_hbm, *refs):
    groups = lax.axis_size("leaf")
    outs = refs[:groups]
    data, block, offset, sems = refs[groups:]
    copies = [
        pltpu.make_async_copy(src, dst, sems.at[i])
        for i, (src, dst) in enumerate(((data_hbm, data), (block_hbm, block), (offset_hbm, offset)))
    ]
    for copy in copies:
        copy.start()
    for copy in copies:
        copy.wait()
    group = lax.axis_index("leaf")
    count = data.shape[1]
    slots = fronts * CAP
    down = lax.broadcasted_iota(jnp.int32, (count, count), 0)
    across = lax.broadcasted_iota(jnp.int32, (count, count), 1)
    eye = down == across
    block_row = block[...]
    block_col = jnp.sum(jnp.where(eye, block_row, 0), axis=1, keepdims=True)
    offset_col = jnp.sum(jnp.where(eye, offset[...], 0), axis=1, keepdims=True)
    same = (block_col == block_row) & (down < across)
    slot_row = block_row * CAP + jnp.sum(same.astype(jnp.int32), axis=0, keepdims=True)
    row_col = (block_col & (fronts - 1)) * rows + offset_col + 1
    lane = lax.broadcasted_iota(jnp.int32, (count, COLS), 1)
    index = jnp.where(lane == 0, row_col, 0).astype(F32)
    lines = jnp.concatenate([index, data[0], jnp.zeros((count, COLS), F32), -data[1]], axis=1)
    for k, out in enumerate(outs):
        first = (group ^ k) * slots
        pick = lax.broadcasted_iota(jnp.int32, (slots, count), 0) + first == slot_row
        out[...] = jnp.dot(
            pick.astype(F32), lines, precision=lax.Precision.HIGHEST, preferred_element_type=F32
        )


def load_sources(leaf_hbm, mid_hbm, root_hbm, leaf_out, mid_out, root_out, leaf, mid, root, sems):
    group = lax.axis_index("leaf")
    copies = [
        pltpu.make_async_copy(src, dst, sems.at[i])
        for i, (src, dst) in enumerate(
            ((leaf_hbm, leaf), (mid_hbm.at[:, group // 2], mid), (root_hbm, root))
        )
    ]
    for copy in copies:
        copy.start()
    for copy in copies:
        copy.wait()
    forward = ((group & 1) == 0).astype(F32)
    real, imag = leaf[0].T, leaf[1].T
    zero = jnp.zeros_like(real)
    leaf_out[...] = jnp.concatenate([real, zero, imag, zero], axis=1)
    mid_out[...] = pack(jnp.concatenate([mid[0], mid[1]], axis=0).T) * forward
    width = COLS // 2
    low = jnp.concatenate([root[0, :width], root[1, :width]], axis=0)
    high = jnp.concatenate([root[0, width:], root[1, width:]], axis=0)
    root_out[...] = pack(jnp.where(group < 2, low, high).T) * forward


def message_rows(rows, slots):
    return max(rows, slots), 8 * -(-slots // (8 * LANES))


def pack_leaf(own, *refs):
    arrived, out = refs[:-1], refs[-1]
    lines = jnp.concatenate([ref[...] for ref in arrived], axis=0)
    slots = lines.shape[0]
    body, tail = message_rows(own.shape[0], slots)
    lane = lax.broadcasted_iota(jnp.int32, (slots, LANES), 1)
    data = jnp.where((lane // COLS) % 2 == 1, lines, 0.0)
    index = lines[:, 0:1]

    def padded(x):
        if x.shape[0] == body:
            return x
        return jnp.concatenate([x, jnp.zeros((body - x.shape[0], LANES), F32)], axis=0)

    out[0:body, :] = padded(own[...]) + padded(data)
    out[body:, :] = jnp.zeros((tail, LANES), F32)
    for at in range(0, slots, LANES):
        size = min(LANES, slots - at)
        eye = lax.broadcasted_iota(jnp.int32, (size, size), 0) == lax.broadcasted_iota(
            jnp.int32, (size, size), 1
        )
        line = jnp.sum(jnp.where(eye, index[at : at + size], 0.0), axis=0, keepdims=True)
        out[body + at // LANES : body + at // LANES + 1, 0:size] = line


def leaf_lower(slots, matrix, *refs):
    messages, (out, rhs) = refs[:-2], refs[-2:]
    fronts, rows = len(messages), out.shape[0]
    here = lax.axis_index("front")
    total = rows * fronts
    body, _ = message_rows(rows, slots)
    lane = lax.broadcasted_iota(jnp.int32, (slots, LANES), 1)
    taken = (lane // COLS) % 2 == 1
    own = lax.broadcasted_iota(jnp.int32, (rows, LANES), 1)
    own = (own // COLS) % 2 == 0
    for k, message in zip(origins(fronts), messages):
        start = pl.multiple_of((here ^ k) * rows, 8)
        rhs[pl.ds(start, rows), :] = jnp.where(own, message[0:rows, :], 0.0)
    group = max(1, 512 // slots)
    for k in range(0, fronts, group):
        chosen = messages[k : k + group]
        lines = jnp.concatenate([jnp.where(taken, ref[0:slots, :], 0.0) for ref in chosen], axis=0)
        index = jnp.concatenate(
            [
                ref[body + at // LANES : body + at // LANES + 1, 0 : min(LANES, slots - at)]
                for ref in chosen
                for at in range(0, slots, LANES)
            ],
            axis=1,
        )
        row = lax.broadcasted_iota(jnp.int32, (total, index.shape[1]), 0)
        pick = (row + 1 == index.astype(jnp.int32)).astype(BF16)
        both = dot(pick, jnp.concatenate(split(lines), axis=1))
        rhs[...] += both[:, :LANES] + both[:, LANES:]
    out[...] = complex_dot(matrix[...], rhs[...])


def leaf_to_mid(matrix, sources, *refs):
    parts, (keep, send, full) = refs[:-3], refs[-3:]
    assemble(full, parts, lax.axis_index("front"))
    mine, theirs = own_first(lax.axis_index("leaf"), *halves(complex_dot(matrix[...], full[...])))
    keep[...] = sources[...] - pack(mine)
    send[...] = -pack(theirs)


def leaf_to_root(matrix, full, keep, send):
    keep[...], send[...] = own_first(lax.axis_index("leaf"), *halves(complex_dot(matrix[...], full[...])))


def add(*refs):
    total = refs[0][...]
    for ref in refs[1:-1]:
        total = total + ref[...]
    refs[-1][...] = total


def mid_lower(matrix, *refs):
    parts, (out, whole) = refs[:-2], refs[-2:]
    assemble(whole, parts, lax.axis_index("front"), 2 * COLS)
    out[...] = pack(complex_dot(matrix[...], whole[...]))


def mid_to_root(matrix, kept, came, sources, *refs):
    parts, (keep, send, full) = refs[:-3], refs[-3:]
    assemble(full, parts, lax.axis_index("front"), 2 * COLS)
    cut = -(kept[...] + came[...] + complex_dot(matrix[...], full[...]))
    width = COLS // 2
    low = pack(jnp.concatenate([cut[:, :width], cut[:, COLS : COLS + width]], axis=1))
    high = pack(jnp.concatenate([cut[:, width:COLS], cut[:, COLS + width :]], axis=1))
    first = lax.axis_index("leaf") < 2
    keep[...] = jnp.where(first, low, high) + sources[...]
    send[...] = jnp.where(first, high, low)


def root_rows(matrix, *refs):
    parts, (out, whole) = refs[:-2], refs[-2:]
    assemble(whole, parts, lax.axis_index("front"), COLS)
    out[...] = pack(complex_dot(matrix[...], whole[...]))


def halved(value, keep, send):
    rows = keep.shape[0]
    odd = (lax.axis_index("front") & 1) == 1
    low, high = value[:rows], value[rows:]
    keep[...] = jnp.where(odd, high, low)
    send[...] = jnp.where(odd, low, high)


def root_to_mid(matrix, mine, other, keep, send, x_root):
    first = lax.axis_index("leaf") < 2
    mine, other = unpack(mine[...], COLS), unpack(other[...], COLS)
    low, high = jnp.where(first, mine, other), jnp.where(first, other, mine)
    width = COLS // 2
    x = jnp.concatenate([low[:, :width], high[:, :width], low[:, width:], high[:, width:]], axis=1)
    x_root[...] = pack(x)
    halved(pack(complex_dot(matrix[...], x)), keep, send)


def root_to_leaf(matrix, mine, other, out, forward, adjoint):
    x = by_solve(lax.axis_index("leaf"), unpack(mine[...], 2 * COLS), unpack(other[...], 2 * COLS))
    out[...] = complex_dot(matrix[...], x)
    fields_of(x, forward, adjoint, ())


def add_halves(kept, came, first, second):
    rows = first.shape[0]
    first[...] = kept[0:rows, :] + came[0:rows, :]
    second[...] = kept[rows:, :] + came[rows:, :]


def add_pair(a, b, c, d, first, second):
    first[...] = a[...] + b[...]
    second[...] = c[...] + d[...]


def sum_front(kept, sent):
    fronts = lax.axis_size("front")
    rows = kept.shape[0] // 2
    shapes = [(rows, LANES)] * 2
    a, b = kernel(add_halves, shapes, kept, swap("front", sent, 1))
    hops = [1 << i for i in range(1, fronts.bit_length() - 1)]
    for i, hop in enumerate(hops):
        back = hops[-1 - i]
        a, b = kernel(add_pair, shapes, a, swap("front", a, hop), b, swap("front", b, back))
    return [a, b, swap("front", a, 1), swap("front", b, 1)]


def summed(pieces):
    a, b, c, d = (ref[...] for ref in pieces)
    odd = (lax.axis_index("front") & 1) == 1
    mine, theirs = jnp.concatenate([a, b], axis=0), jnp.concatenate([c, d], axis=0)
    return jnp.concatenate([jnp.where(odd, theirs, mine), jnp.where(odd, mine, theirs)], axis=0)


def mid_upper(matrix, y, *refs):
    tail, out = unpack(summed(refs[:4]), 2 * COLS), refs[4]
    out[...] = pack(complex_dot(matrix[...], y[...] - tail))


def mid_to_leaf(matrix, from_root, mine, other, keep, send, x_mid):
    x = by_solve(lax.axis_index("leaf"), unpack(mine[...], 2 * COLS), unpack(other[...], 2 * COLS))
    x_mid[...] = x
    halved(complex_dot(matrix[...], x) + from_root[...], keep, send)


def leaf_upper(matrix, y, *refs):
    forward, adjoint = refs[4:]
    fields_of(complex_dot(matrix[...], y[...] - summed(refs[:4])), forward, adjoint, ())


def mid_outputs(mine, other, forward, adjoint):
    parent = lax.axis_index("leaf") // 2
    fields_of(mine[...], forward, adjoint, (parent,))
    fields_of(other[...], forward, adjoint, (1 - parent,))


def after(x, *others):
    return lax.optimization_barrier((x, *others))[0]


def body(
    leaf_lower_inv,
    leaf_upper_inv,
    leaf_to_mid_lower,
    leaf_to_root_lower,
    leaf_to_mid_upper,
    leaf_to_root_upper,
    mid_lower_inv,
    mid_upper_inv,
    mid_to_root_lower,
    mid_to_root_upper,
    root_lower_inv,
    root_upper_inv,
    leaf_sources,
    mid_sources,
    root_sources,
    receiver_data,
    receiver_block,
    receiver_offset,
):
    groups, fronts = lax.axis_size("leaf"), lax.axis_size("front")
    n0, n1, n2 = leaf_sources.shape[1], mid_sources.shape[2], root_sources.shape[1]
    s0, s1, s2 = n0 * fronts, n1 * fronts, n2 * fronts
    slots, count = fronts * CAP, receiver_data.shape[1]
    dma = pltpu.SemaphoreType.DMA

    with jax.named_scope("right_hand_sides"):
        payload = kernel(
            functools.partial(pack_receivers, fronts, n0),
            [(slots, LANES)] * groups,
            receiver_data,
            receiver_block.reshape(1, -1),
            receiver_offset.reshape(1, -1),
            scratch=[
                pltpu.VMEM((2, count, COLS), F32),
                pltpu.VMEM((1, count), jnp.int32),
                pltpu.VMEM((1, count), jnp.int32),
                dma((3,)),
            ],
            hbm=range(3),
            pinned=range(3),
        )
        arrived = [payload[0]] + [swap("leaf", payload[k], k) for k in range(1, groups)]
        leaf_own, mid_own, root_own = kernel(
            load_sources,
            [(n0, LANES), (n1 // 2, LANES), (n2 // 4, LANES)],
            after(leaf_sources.transpose(0, 2, 1), *payload),
            mid_sources.transpose(0, 1, 3, 2),
            root_sources.transpose(0, 2, 1),
            scratch=[
                pltpu.VMEM((2, COLS, n0), F32),
                pltpu.VMEM((2, COLS, n1), F32),
                pltpu.VMEM((2, COLS, n2), F32),
                dma((3,)),
            ],
            hbm=range(3),
            pinned=range(3),
        )
        (message,) = kernel(
            pack_leaf, [(sum(message_rows(n0, groups * slots)), LANES)], leaf_own, *arrived
        )
    with jax.named_scope("leaf_lower"):
        messages, (ll, l2m) = gather_front(
            message,
            lambda x: load((after(leaf_lower_inv, x), "leaf"), (leaf_to_mid_lower, "leaf"), pinned=True),
        )
        (y_leaf,) = kernel(
            functools.partial(leaf_lower, groups * slots),
            [(n0, LANES)],
            ll,
            *messages,
            scratch=[pltpu.VMEM((s0, LANES), F32)],
        )
    with jax.named_scope("mid_lower"):
        parts, (l2r, ml) = gather_front(
            y_leaf,
            lambda x: load((after(leaf_to_root_lower, x), "leaf"), (mid_lower_inv, "own"), pinned=True),
        )
        keep, send, y_full = kernel(
            leaf_to_mid,
            [(n1 // 2, LANES), (n1 // 2, LANES), (s0, LANES)],
            l2m,
            mid_own,
            *parts,
        )
        came = swap("leaf", send, 1)
        root_kept, root_sent = kernel(leaf_to_root, [(n2, 2 * COLS)] * 2, l2r, after(y_full, send))
        (cut_mid,) = kernel(add, [(n1 // 2, LANES)], after(keep, root_kept), came)
        parts, (m2r,) = gather_front(
            cut_mid, lambda x: load((after(mid_to_root_lower, x), "own"), pinned=True)
        )
        root_came = swap("leaf", root_sent, 1)
        (y_mid,) = kernel(
            mid_lower,
            [(n1 // 2, LANES)],
            ml,
            *parts,
            scratch=[pltpu.VMEM((s1, 2 * COLS), F32)],
        )
    with jax.named_scope("root_cut"):
        parts, (rl,) = gather_front(y_mid, lambda x: load((after(root_lower_inv, x), None)))
        keep, send, y_mid_full = kernel(
            mid_to_root,
            [(n2 // 4, LANES), (n2 // 4, LANES), (s1, 2 * COLS)],
            m2r,
            root_kept,
            root_came,
            root_own,
            *parts,
        )
        came = swap("leaf", send, 2)
        mu, l2r_up = load((after(mid_upper_inv, send), "own"), (leaf_to_root_upper, "leaf"))
        (cut_root,) = kernel(add, [(n2 // 4, LANES)], after(keep, mu), came)
    with jax.named_scope("root_solve"):
        parts, (ru,) = gather_front(cut_root, lambda x: load((after(root_upper_inv, x), None)))
        (y_root,) = kernel(
            root_rows,
            [(n2 // 4, LANES)],
            rl,
            *parts,
            scratch=[pltpu.VMEM((s2, COLS), F32)],
        )
        parts, (m2r_up, l2m_up, lu) = gather_front(
            y_root,
            lambda x: load(
                (after(mid_to_root_upper, x), "own"), (leaf_to_mid_upper, "leaf"), (leaf_upper_inv, "leaf")
            ),
        )
        (x_root,) = kernel(
            root_rows,
            [(n2 // 4, LANES)],
            ru,
            *parts,
            scratch=[pltpu.VMEM((s2, COLS), F32)],
        )
    with jax.named_scope("mid_upper"):
        keep, send, x_root = kernel(
            root_to_mid,
            [(s1 // 4, LANES)] * 2 + [(n2 // 2, LANES)],
            m2r_up,
            x_root,
            swap("leaf", x_root, 2),
        )
        pieces = sum_front(keep, send)
        (x_mid,) = kernel(mid_upper, [(n1 // 2, LANES)], mu, y_mid_full, *pieces)
        from_root, root_field, root_adjoint = kernel(
            root_to_leaf,
            [(s0, LANES), (2, COLS, n2), (2, COLS, n2)],
            l2r_up,
            x_root,
            swap("leaf", after(x_root, send), 1),
        )
    with jax.named_scope("leaf_upper"):
        keep, send, x_mid = kernel(
            mid_to_leaf,
            [(s0 // 2, LANES)] * 2 + [(n1, LANES)],
            l2m_up,
            from_root,
            x_mid,
            swap("leaf", x_mid, 1),
        )
        pieces = sum_front(keep, send)
        x_other = swap("leaf", after(x_mid, send), 2)
        mid_field, mid_adjoint = kernel(mid_outputs, [(2, 2, COLS, n1)] * 2, x_mid, x_other)
        leaf_field, leaf_adjoint = kernel(leaf_upper, [(2, COLS, n0)] * 2, lu, y_full, *pieces)
    return tuple(
        jnp.swapaxes(x, -1, -2)
        for x in (leaf_field, mid_field, root_field, leaf_adjoint, mid_adjoint, root_adjoint)
    )


def solution(mesh):
    in_specs = (
        P(None, "leaf", "front", None),
        P(None, "leaf", "front", None),
        P(None, "leaf", "front", None),
        P(None, "leaf", "front", None),
        P(None, "leaf", None, "front"),
        P(None, "leaf", None, "front"),
        P(None, None, "front", None),
        P(None, None, "front", None),
        P(None, None, "front", None),
        P(None, None, None, "front"),
        P(None, "front", None),
        P(None, "front", None),
        P(None, ("leaf", "front"), None),
        P(None, None, "front", None),
        P(None, "front", None),
        P(None, ("leaf", "front"), None),
        P(("leaf", "front"), None),
        P(("leaf", "front")),
    )
    out_specs = (
        P(None, ("leaf", "front"), None),
        P(None, None, "front", None),
        P(None, "front", None),
        P(None, ("leaf", "front"), None),
        P(None, None, "front", None),
        P(None, "front", None),
    )
    return jax.shard_map(body, mesh=mesh, in_specs=in_specs, out_specs=out_specs, check_vma=False)
```

```python
import functools

import jax
import jax.numpy as jnp
from jax import lax
from jax.experimental import pallas as pl
from jax.experimental.pallas import tpu as pltpu
from jax.sharding import PartitionSpec as P

CAP = 2
CHUNKS = 4
LANES = 128
COLS = 32
F32 = jnp.float32
BF16 = jnp.bfloat16
VM = pl.BlockSpec(memory_space=pltpu.VMEM)
HB = pl.BlockSpec(memory_space=pltpu.HBM)


def split(x):
    high = x.astype(BF16)
    return high, (x - high.astype(F32)).astype(BF16)


def dot(a, b):
    return jnp.dot(a, b, preferred_element_type=F32)


def complex_dot(matrix, x):
    half = x.shape[1] // 2
    turned = jnp.concatenate([-x[:, half:], x[:, :half]], axis=1)
    both = jnp.concatenate([x, turned], axis=0)
    columns = jnp.concatenate(split(both), axis=1)
    product = dot(matrix, columns)
    rows, n = product.shape[0] // 2, x.shape[1]
    return (product[:rows, n:] + product[rows:, :n]) + product[:rows, :n]


def pack(x):
    chunks = LANES // x.shape[1]
    rows = x.shape[0] // chunks
    return jnp.concatenate([x[rows * j : rows * j + rows] for j in range(chunks)], axis=1)


def unpack(x, width):
    return jnp.concatenate([x[:, at : at + width] for at in range(0, LANES, width)], axis=0)


def halves(x):
    c = COLS
    return (
        jnp.concatenate([x[:, :c], x[:, 2 * c : 3 * c]], axis=1),
        jnp.concatenate([x[:, c : 2 * c], x[:, 3 * c :]], axis=1),
    )


def joined(forward, adjoint):
    c = COLS
    return jnp.concatenate([forward[:, :c], adjoint[:, :c], forward[:, c:], adjoint[:, c:]], axis=1)


def own_first(group, forward, adjoint):
    even = (group & 1) == 0
    return jnp.where(even, forward, adjoint), jnp.where(even, adjoint, forward)


def by_solve(group, own, other):
    even = (group & 1) == 0
    return joined(jnp.where(even, own, other), jnp.where(even, other, own))


def assemble(where, parts, here, width=LANES):
    rows = parts[0].shape[0]
    for (k, at), part in zip(origins(parts), parts):
        for chunk in range(LANES // width):
            start = pl.multiple_of((here ^ k) * rows * (LANES // width) + chunk * rows + at, 8)
            where[pl.ds(start, part.shape[0]), :] = part[:, chunk * width : chunk * width + width]


def fields_of(x, forward, adjoint, where):
    y = x.T
    c = COLS
    forward[(0, *where)] = y[0:c]
    forward[(1, *where)] = y[2 * c : 3 * c]
    adjoint[(0, *where)] = y[c : 2 * c]
    adjoint[(1, *where)] = -y[3 * c :]


def swap(axis, x, k):
    size = lax.axis_size(axis)
    return lax.ppermute(x, axis, [(i, i ^ k) for i in range(size)])


def rows_of(at, count, src, out):
    out[...] = src[at : at + count, :]


def gather_front(x, meanwhile=None):
    fronts = lax.axis_size("front")
    if fronts != 8:
        mine = [x] + [swap("front", x, k) for k in range(2, fronts, 2)]
        return [b for y in mine for b in (y, swap("front", y, 1))], tuple(meanwhile(x)) if meanwhile else ()
    one, two = 2, 4
    near, far = swap("front", x, one), swap("front", x, two)
    extra = tuple(meanwhile(x)) if meanwhile else ()
    if extra:
        near = after(near, *extra)
    rows = x.shape[0]
    cut = -(-rows // 16) * 8
    (top,) = kernel(functools.partial(rows_of, 0, cut), [(cut, LANES)], near)
    (low,) = kernel(functools.partial(rows_of, cut, rows - cut), [(rows - cut, LANES)], far)
    top, low = swap("front", top, two), swap("front", low, one)
    return [b for y in (x, near, far, top, low) for b in (y, swap("front", y, 1))], extra


def origins(blocks):
    if len(blocks) == 10:
        cut = blocks[6].shape[0]
        places = [(0, 0), (2, 0), (4, 0), (6, 0), (6, cut)]
    else:
        places = [(k, 0) for k in range(0, len(blocks), 2)]
    return [(k + core, at) for k, at in places for core in range(2)]


def kernel(fn, outs, *args, scratch=(), vmem=8, work=0, hbm=(), pinned=()):
    outs = [o if isinstance(o[0], tuple) else (o, F32) for o in outs]
    return pl.pallas_call(
        fn,
        out_shape=[jax.ShapeDtypeStruct(*o) for o in outs],
        in_specs=[HB if i in hbm else VM for i in range(len(args))],
        out_specs=[VM] * len(outs),
        scratch_shapes=list(scratch),
        compiler_params=pltpu.CompilerParams(vmem_limit_bytes=vmem * 2**20),
        cost_estimate=pl.CostEstimate(flops=work, bytes_accessed=work // 700, transcendentals=0),
    )(*(pltpu.with_memory_space_constraint(a, pltpu.HBM) if i in pinned else a for i, a in enumerate(args)))


def load_matrices(picks, *refs):
    count = len(picks)
    sources, outs, buffers, sems = (
        refs[:count],
        refs[count : 2 * count],
        refs[2 * count : 3 * count],
        refs[3 * count],
    )
    parent = lax.axis_index("leaf") // 2
    copies = []
    for i, (src, pick) in enumerate(zip(sources, picks)):
        rows = buffers[i].shape[1]
        step = max(rows // CHUNKS, 16)
        for n, at in enumerate(range(0, rows, step)):
            span = pl.ds(at, step)
            view = src.at[:, span, :] if pick is None else src.at[:, parent if pick == "own" else 0, span, :]
            copy = pltpu.make_async_copy(view, buffers[i].at[:, span, :], sems.at[CHUNKS * i + n])
            copy.start()
            copies.append((i, at, step, copy))
    for i, at, step, copy in copies:
        copy.wait()
        rows, depth = buffers[i].shape[1:]
        for part in range(2):
            high, low = split(buffers[i][part, at : at + step, :])
            outs[i][at : at + step, part * depth : part * depth + depth] = high
            outs[i][rows + at : rows + at + step, part * depth : part * depth + depth] = low


def load(*matrices, pinned=False):
    shapes = [m.shape[-2:] for m, _ in matrices]
    size = sum(r * d for r, d in shapes)
    return kernel(
        functools.partial(load_matrices, tuple(pick for _, pick in matrices)),
        [((2 * r, 2 * d), BF16) for r, d in shapes],
        *[m for m, _ in matrices],
        scratch=[pltpu.VMEM((2, r, d), F32) for r, d in shapes]
        + [pltpu.SemaphoreType.DMA((CHUNKS * len(shapes),))],
        hbm=range(len(shapes)),
        pinned=range(len(shapes)) if pinned else (),
        vmem=4 + -(-size * 8 // 2**20),
        work=size * 1000,
    )


def pack_receivers(fronts, rows, data_hbm, block_hbm, offset_hbm, *refs):
    own, far, near = refs[:3]
    data, block, offset, sems = refs[3:]
    copies = [
        pltpu.make_async_copy(src, dst, sems.at[i])
        for i, (src, dst) in enumerate(((data_hbm, data), (block_hbm, block), (offset_hbm, offset)))
    ]
    for copy in copies:
        copy.start()
    for copy in copies:
        copy.wait()
    group = lax.axis_index("leaf")
    count = data.shape[1]
    slots = fronts * CAP
    down = lax.broadcasted_iota(jnp.int32, (count, count), 0)
    across = lax.broadcasted_iota(jnp.int32, (count, count), 1)
    eye = down == across
    block_row = block[...]
    block_col = jnp.sum(jnp.where(eye, block_row, 0), axis=1, keepdims=True)
    offset_col = jnp.sum(jnp.where(eye, offset[...], 0), axis=1, keepdims=True)
    same = (block_col == block_row) & (down < across)
    slot_row = block_row * CAP + jnp.sum(same.astype(jnp.int32), axis=0, keepdims=True)
    row_col = (block_col & (fronts - 1)) * rows + offset_col + 1
    lane = lax.broadcasted_iota(jnp.int32, (count, COLS), 1)
    index = jnp.where(lane == 0, row_col, 0).astype(F32)
    lines = jnp.concatenate([index, data[0], jnp.zeros((count, COLS), F32), -data[1]], axis=1)
    targets = [group, group ^ 2, group ^ 1, group ^ 3]
    place = lax.broadcasted_iota(jnp.int32, (slots, count), 0)
    pick = jnp.concatenate([place + target * slots == slot_row for target in targets], axis=0)
    picked = jnp.dot(
        pick.astype(F32), lines, precision=lax.Precision.HIGHEST, preferred_element_type=F32
    )
    own[...] = picked[:slots]
    far[...] = picked[slots : 2 * slots]
    near[...] = picked[2 * slots :]


def pass_on(far, came, out):
    rows = far.shape[0]
    out[0:rows, :] = far[...]
    out[rows:, :] = came[rows:, :]


def load_sources(leaf_hbm, mid_hbm, root_hbm, leaf_out, mid_out, root_out, leaf, mid, root, sems):
    group = lax.axis_index("leaf")
    copies = [
        pltpu.make_async_copy(src, dst, sems.at[i])
        for i, (src, dst) in enumerate(
            ((leaf_hbm, leaf), (mid_hbm.at[:, group // 2], mid), (root_hbm, root))
        )
    ]
    for copy in copies:
        copy.start()
    for copy in copies:
        copy.wait()
    forward = ((group & 1) == 0).astype(F32)
    real, imag = leaf[0].T, leaf[1].T
    zero = jnp.zeros_like(real)
    leaf_out[...] = jnp.concatenate([real, zero, imag, zero], axis=1)
    mid_out[...] = pack(jnp.concatenate([mid[0], mid[1]], axis=0).T) * forward
    width = COLS // 2
    low = jnp.concatenate([root[0, :width], root[1, :width]], axis=0)
    high = jnp.concatenate([root[0, width:], root[1, width:]], axis=0)
    root_out[...] = pack(jnp.where(group < 2, low, high).T) * forward


def message_rows(rows, slots):
    return max(rows, slots), 8 * -(-slots // (8 * LANES))


def pack_leaf(own, mine, near, far, out):
    lines = jnp.concatenate([mine[...], near[0 : mine.shape[0], :], far[...]], axis=0)
    slots = lines.shape[0]
    body, tail = message_rows(own.shape[0], slots)
    lane = lax.broadcasted_iota(jnp.int32, (slots, LANES), 1)
    data = jnp.where((lane // COLS) % 2 == 1, lines, 0.0)
    index = lines[:, 0:1]

    def padded(x):
        if x.shape[0] == body:
            return x
        return jnp.concatenate([x, jnp.zeros((body - x.shape[0], LANES), F32)], axis=0)

    out[0:body, :] = padded(own[...]) + padded(data)
    out[body:, :] = jnp.zeros((tail, LANES), F32)
    for at in range(0, slots, LANES):
        size = min(LANES, slots - at)
        eye = lax.broadcasted_iota(jnp.int32, (size, size), 0) == lax.broadcasted_iota(
            jnp.int32, (size, size), 1
        )
        line = jnp.sum(jnp.where(eye, index[at : at + size], 0.0), axis=0, keepdims=True)
        out[body + at // LANES : body + at // LANES + 1, 0:size] = line


def leaf_lower(slots, matrix, *refs):
    parts, (out, rhs, messages) = refs[:-3], refs[-3:]
    rows = out.shape[0]
    here = lax.axis_index("front")
    for (k, at), part in zip(origins(parts), parts):
        messages[here ^ k, at : at + part.shape[0], :] = part[...]
    fronts = messages.shape[0]
    total = rows * fronts
    body, _ = message_rows(rows, slots)
    lane = lax.broadcasted_iota(jnp.int32, (slots, LANES), 1)
    taken = (lane // COLS) % 2 == 1
    own = lax.broadcasted_iota(jnp.int32, (rows, LANES), 1)
    own = (own // COLS) % 2 == 0
    for k in range(fronts):
        rhs[rows * k : rows * k + rows, :] = jnp.where(own, messages[k, 0:rows, :], 0.0)
    group = max(1, 512 // slots)
    for k in range(0, fronts, group):
        chosen = range(k, min(k + group, fronts))
        lines = jnp.concatenate([jnp.where(taken, messages[i, 0:slots, :], 0.0) for i in chosen], axis=0)
        index = jnp.concatenate(
            [
                messages[i, body + at // LANES : body + at // LANES + 1, 0 : min(LANES, slots - at)]
                for i in chosen
                for at in range(0, slots, LANES)
            ],
            axis=1,
        )
        row = lax.broadcasted_iota(jnp.int32, (total, index.shape[1]), 0)
        pick = (row + 1 == index.astype(jnp.int32)).astype(BF16)
        both = dot(pick, jnp.concatenate(split(lines), axis=1))
        rhs[...] += both[:, :LANES] + both[:, LANES:]
    out[...] = complex_dot(matrix[...], rhs[...])


def leaf_to_mid(matrix, sources, *refs):
    parts, (keep, send, full) = refs[:-3], refs[-3:]
    assemble(full, parts, lax.axis_index("front"))
    mine, theirs = own_first(lax.axis_index("leaf"), *halves(complex_dot(matrix[...], full[...])))
    keep[...] = sources[...] - pack(mine)
    send[...] = -pack(theirs)


def leaf_to_root(matrix, full, keep, send):
    keep[...], send[...] = own_first(lax.axis_index("leaf"), *halves(complex_dot(matrix[...], full[...])))


def add(*refs):
    total = refs[0][...]
    for ref in refs[1:-1]:
        total = total + ref[...]
    refs[-1][...] = total


def mid_lower(matrix, *refs):
    parts, (out, whole) = refs[:-2], refs[-2:]
    assemble(whole, parts, lax.axis_index("front"), 2 * COLS)
    out[...] = pack(complex_dot(matrix[...], whole[...]))


def mid_to_root(matrix, kept, came, sources, *refs):
    parts, (keep, send, full) = refs[:-3], refs[-3:]
    assemble(full, parts, lax.axis_index("front"), 2 * COLS)
    cut = -(kept[...] + came[...] + complex_dot(matrix[...], full[...]))
    width = COLS // 2
    low = pack(jnp.concatenate([cut[:, :width], cut[:, COLS : COLS + width]], axis=1))
    high = pack(jnp.concatenate([cut[:, width:COLS], cut[:, COLS + width :]], axis=1))
    first = lax.axis_index("leaf") < 2
    keep[...] = jnp.where(first, low, high) + sources[...]
    send[...] = jnp.where(first, high, low)


def root_rows(matrix, *refs):
    parts, (out, whole) = refs[:-2], refs[-2:]
    assemble(whole, parts, lax.axis_index("front"), COLS)
    out[...] = pack(complex_dot(matrix[...], whole[...]))


def halved(value, keep, send):
    rows = keep.shape[0]
    odd = (lax.axis_index("front") & 1) == 1
    low, high = value[:rows], value[rows:]
    keep[...] = jnp.where(odd, high, low)
    send[...] = jnp.where(odd, low, high)


def root_to_mid(matrix, mine, other, keep, send, x_root):
    first = lax.axis_index("leaf") < 2
    mine, other = unpack(mine[...], COLS), unpack(other[...], COLS)
    low, high = jnp.where(first, mine, other), jnp.where(first, other, mine)
    width = COLS // 2
    x = jnp.concatenate([low[:, :width], high[:, :width], low[:, width:], high[:, width:]], axis=1)
    x_root[...] = pack(x)
    halved(pack(complex_dot(matrix[...], x)), keep, send)


def root_to_leaf(matrix, mine, other, out, forward, adjoint):
    x = by_solve(lax.axis_index("leaf"), unpack(mine[...], 2 * COLS), unpack(other[...], 2 * COLS))
    out[...] = complex_dot(matrix[...], x)
    fields_of(x, forward, adjoint, ())


def add_halves(kept, came, first, second):
    rows = first.shape[0]
    first[...] = kept[0:rows, :] + came[0:rows, :]
    second[...] = kept[rows:, :] + came[rows:, :]


def add_pair(a, b, c, d, first, second):
    first[...] = a[...] + b[...]
    second[...] = c[...] + d[...]


def sum_front(kept, sent):
    fronts = lax.axis_size("front")
    rows = kept.shape[0] // 2
    shapes = [(rows, LANES)] * 2
    a, b = kernel(add_halves, shapes, kept, swap("front", sent, 1))
    hops = [1 << i for i in range(1, fronts.bit_length() - 1)]
    for i, hop in enumerate(hops):
        back = hops[-1 - i]
        a, b = kernel(add_pair, shapes, a, swap("front", a, hop), b, swap("front", b, back))
    return [a, b, swap("front", a, 1), swap("front", b, 1)]


def summed(pieces):
    a, b, c, d = (ref[...] for ref in pieces)
    odd = (lax.axis_index("front") & 1) == 1
    mine, theirs = jnp.concatenate([a, b], axis=0), jnp.concatenate([c, d], axis=0)
    return jnp.concatenate([jnp.where(odd, theirs, mine), jnp.where(odd, mine, theirs)], axis=0)


def mid_upper(matrix, y, *refs):
    tail, out = unpack(summed(refs[:4]), 2 * COLS), refs[4]
    out[...] = pack(complex_dot(matrix[...], y[...] - tail))


def mid_to_leaf(matrix, from_root, mine, other, keep, send, x_mid):
    x = by_solve(lax.axis_index("leaf"), unpack(mine[...], 2 * COLS), unpack(other[...], 2 * COLS))
    x_mid[...] = x
    halved(complex_dot(matrix[...], x) + from_root[...], keep, send)


def leaf_upper(matrix, y, *refs):
    forward, adjoint = refs[4:]
    fields_of(complex_dot(matrix[...], y[...] - summed(refs[:4])), forward, adjoint, ())


def mid_outputs(mine, other, forward, adjoint):
    parent = lax.axis_index("leaf") // 2
    fields_of(mine[...], forward, adjoint, (parent,))
    fields_of(other[...], forward, adjoint, (1 - parent,))


def after(x, *others):
    return lax.optimization_barrier((x, *others))[0]


def body(
    leaf_lower_inv,
    leaf_upper_inv,
    leaf_to_mid_lower,
    leaf_to_root_lower,
    leaf_to_mid_upper,
    leaf_to_root_upper,
    mid_lower_inv,
    mid_upper_inv,
    mid_to_root_lower,
    mid_to_root_upper,
    root_lower_inv,
    root_upper_inv,
    leaf_sources,
    mid_sources,
    root_sources,
    receiver_data,
    receiver_block,
    receiver_offset,
):
    groups, fronts = lax.axis_size("leaf"), lax.axis_size("front")
    n0, n1, n2 = leaf_sources.shape[1], mid_sources.shape[2], root_sources.shape[1]
    s0, s1, s2 = n0 * fronts, n1 * fronts, n2 * fronts
    slots, count = fronts * CAP, receiver_data.shape[1]
    dma = pltpu.SemaphoreType.DMA

    with jax.named_scope("right_hand_sides"):
        payload = kernel(
            functools.partial(pack_receivers, fronts, n0),
            [(slots, LANES), (slots, LANES), (2 * slots, LANES)],
            receiver_data,
            receiver_block.reshape(1, -1),
            receiver_offset.reshape(1, -1),
            scratch=[
                pltpu.VMEM((2, count, COLS), F32),
                pltpu.VMEM((1, count), jnp.int32),
                pltpu.VMEM((1, count), jnp.int32),
                dma((3,)),
            ],
            hbm=range(3),
            pinned=range(3),
        )
        own, far, near = payload
        came = swap("leaf", near, 1)
        (both,) = kernel(pass_on, [(2 * slots, LANES)], far, came)
        arrived = [own, came, swap("leaf", both, 2)]
        leaf_own, mid_own, root_own = kernel(
            load_sources,
            [(n0, LANES), (n1 // 2, LANES), (n2 // 4, LANES)],
            after(leaf_sources.transpose(0, 2, 1), *payload),
            mid_sources.transpose(0, 1, 3, 2),
            root_sources.transpose(0, 2, 1),
            scratch=[
                pltpu.VMEM((2, COLS, n0), F32),
                pltpu.VMEM((2, COLS, n1), F32),
                pltpu.VMEM((2, COLS, n2), F32),
                dma((3,)),
            ],
            hbm=range(3),
            pinned=range(3),
        )
        (message,) = kernel(
            pack_leaf, [(sum(message_rows(n0, groups * slots)), LANES)], leaf_own, *arrived
        )
    with jax.named_scope("leaf_lower"):
        messages, (ll, l2m) = gather_front(
            message,
            lambda x: load((after(leaf_lower_inv, x), "leaf"), (leaf_to_mid_lower, "leaf"), pinned=True),
        )
        (y_leaf,) = kernel(
            functools.partial(leaf_lower, groups * slots),
            [(n0, LANES)],
            ll,
            *messages,
            scratch=[pltpu.VMEM((s0, LANES), F32), pltpu.VMEM((fronts, *message.shape), F32)],
        )
    with jax.named_scope("mid_lower"):
        parts, (l2r, ml) = gather_front(
            y_leaf,
            lambda x: load((after(leaf_to_root_lower, x), "leaf"), (mid_lower_inv, "own"), pinned=True),
        )
        keep, send, y_full = kernel(
            leaf_to_mid,
            [(n1 // 2, LANES), (n1 // 2, LANES), (s0, LANES)],
            l2m,
            mid_own,
            *parts,
        )
        came = swap("leaf", send, 1)
        root_kept, root_sent = kernel(leaf_to_root, [(n2, 2 * COLS)] * 2, l2r, after(y_full, send))
        (cut_mid,) = kernel(add, [(n1 // 2, LANES)], after(keep, root_kept), came)
        parts, (m2r,) = gather_front(
            cut_mid, lambda x: load((after(mid_to_root_lower, x), "own"), pinned=True)
        )
        root_came = swap("leaf", root_sent, 1)
        (y_mid,) = kernel(
            mid_lower,
            [(n1 // 2, LANES)],
            ml,
            *parts,
            scratch=[pltpu.VMEM((s1, 2 * COLS), F32)],
        )
    with jax.named_scope("root_cut"):
        parts, (rl,) = gather_front(y_mid, lambda x: load((after(root_lower_inv, x), None)))
        keep, send, y_mid_full = kernel(
            mid_to_root,
            [(n2 // 4, LANES), (n2 // 4, LANES), (s1, 2 * COLS)],
            m2r,
            root_kept,
            root_came,
            root_own,
            *parts,
        )
        came = swap("leaf", send, 2)
        mu, l2r_up = load((after(mid_upper_inv, send), "own"), (leaf_to_root_upper, "leaf"))
        (cut_root,) = kernel(add, [(n2 // 4, LANES)], after(keep, mu), came)
    with jax.named_scope("root_solve"):
        parts, (ru,) = gather_front(cut_root, lambda x: load((after(root_upper_inv, x), None)))
        (y_root,) = kernel(
            root_rows,
            [(n2 // 4, LANES)],
            rl,
            *parts,
            scratch=[pltpu.VMEM((s2, COLS), F32)],
        )
        parts, (m2r_up, l2m_up, lu) = gather_front(
            y_root,
            lambda x: load(
                (after(mid_to_root_upper, x), "own"), (leaf_to_mid_upper, "leaf"), (leaf_upper_inv, "leaf")
            ),
        )
        (x_root,) = kernel(
            root_rows,
            [(n2 // 4, LANES)],
            ru,
            *parts,
            scratch=[pltpu.VMEM((s2, COLS), F32)],
        )
    with jax.named_scope("mid_upper"):
        keep, send, x_root = kernel(
            root_to_mid,
            [(s1 // 4, LANES)] * 2 + [(n2 // 2, LANES)],
            m2r_up,
            x_root,
            swap("leaf", x_root, 2),
        )
        pieces = sum_front(keep, send)
        (x_mid,) = kernel(mid_upper, [(n1 // 2, LANES)], mu, y_mid_full, *pieces)
        from_root, root_field, root_adjoint = kernel(
            root_to_leaf,
            [(s0, LANES), (2, COLS, n2), (2, COLS, n2)],
            l2r_up,
            x_root,
            swap("leaf", after(x_root, send), 1),
        )
    with jax.named_scope("leaf_upper"):
        keep, send, x_mid = kernel(
            mid_to_leaf,
            [(s0 // 2, LANES)] * 2 + [(n1, LANES)],
            l2m_up,
            from_root,
            x_mid,
            swap("leaf", x_mid, 1),
        )
        pieces = sum_front(keep, send)
        x_other = swap("leaf", after(x_mid, send), 2)
        mid_field, mid_adjoint = kernel(mid_outputs, [(2, 2, COLS, n1)] * 2, x_mid, x_other)
        leaf_field, leaf_adjoint = kernel(leaf_upper, [(2, COLS, n0)] * 2, lu, y_full, *pieces)
    return tuple(
        jnp.swapaxes(x, -1, -2)
        for x in (leaf_field, mid_field, root_field, leaf_adjoint, mid_adjoint, root_adjoint)
    )


def solution(mesh):
    in_specs = (
        P(None, "leaf", "front", None),
        P(None, "leaf", "front", None),
        P(None, "leaf", "front", None),
        P(None, "leaf", "front", None),
        P(None, "leaf", None, "front"),
        P(None, "leaf", None, "front"),
        P(None, None, "front", None),
        P(None, None, "front", None),
        P(None, None, "front", None),
        P(None, None, None, "front"),
        P(None, "front", None),
        P(None, "front", None),
        P(None, ("leaf", "front"), None),
        P(None, None, "front", None),
        P(None, "front", None),
        P(None, ("leaf", "front"), None),
        P(("leaf", "front"), None),
        P(("leaf", "front")),
    )
    out_specs = (
        P(None, ("leaf", "front"), None),
        P(None, None, "front", None),
        P(None, "front", None),
        P(None, ("leaf", "front"), None),
        P(None, None, "front", None),
        P(None, "front", None),
    )
    return jax.shard_map(body, mesh=mesh, in_specs=in_specs, out_specs=out_specs, check_vma=False)
```

```python
import functools

import jax
import jax.numpy as jnp
from jax import lax
from jax.experimental import pallas as pl
from jax.experimental.pallas import tpu as pltpu
from jax.sharding import PartitionSpec as P

CAP = 2
CHUNKS = 4
LANES = 128
COLS = 32
F32 = jnp.float32
BF16 = jnp.bfloat16
VM = pl.BlockSpec(memory_space=pltpu.VMEM)
HB = pl.BlockSpec(memory_space=pltpu.HBM)


def split(x):
    high = x.astype(BF16)
    return high, (x - high.astype(F32)).astype(BF16)


def dot(a, b):
    return jnp.dot(a, b, preferred_element_type=F32)


def complex_dot(matrix, x):
    half = x.shape[1] // 2
    turned = jnp.concatenate([-x[:, half:], x[:, :half]], axis=1)
    both = jnp.concatenate([x, turned], axis=0)
    columns = jnp.concatenate(split(both), axis=1)
    product = dot(matrix, columns)
    rows, n = product.shape[0] // 2, x.shape[1]
    return (product[:rows, n:] + product[rows:, :n]) + product[:rows, :n]


def pack(x):
    chunks = LANES // x.shape[1]
    rows = x.shape[0] // chunks
    return jnp.concatenate([x[rows * j : rows * j + rows] for j in range(chunks)], axis=1)


def unpack(x, width):
    return jnp.concatenate([x[:, at : at + width] for at in range(0, LANES, width)], axis=0)


def halves(x):
    c = COLS
    return (
        jnp.concatenate([x[:, :c], x[:, 2 * c : 3 * c]], axis=1),
        jnp.concatenate([x[:, c : 2 * c], x[:, 3 * c :]], axis=1),
    )


def joined(forward, adjoint):
    c = COLS
    return jnp.concatenate([forward[:, :c], adjoint[:, :c], forward[:, c:], adjoint[:, c:]], axis=1)


def own_first(group, forward, adjoint):
    even = (group & 1) == 0
    return jnp.where(even, forward, adjoint), jnp.where(even, adjoint, forward)


def by_solve(group, own, other):
    even = (group & 1) == 0
    return joined(jnp.where(even, own, other), jnp.where(even, other, own))


def assemble(where, parts, here, width=LANES):
    rows = parts[0].shape[0] * (LANES // width)
    for k, part in blocks_of(parts):
        start = pl.multiple_of((here ^ k) * rows, 8)
        where[pl.ds(start, rows), :] = part[...] if width == LANES else unpack(part[...], width)


def fields_of(x, forward, adjoint, where):
    y = x.T
    c = COLS
    forward[(0, *where)] = y[0:c]
    forward[(1, *where)] = y[2 * c : 3 * c]
    adjoint[(0, *where)] = y[c : 2 * c]
    adjoint[(1, *where)] = -y[3 * c :]


def swap(axis, x, k):
    size = lax.axis_size(axis)
    return lax.ppermute(x, axis, [(i, i ^ k) for i in range(size)])


def stack(*refs):
    at = 0
    for ref in refs[:-1]:
        refs[-1][at : at + ref.shape[0], :] = ref[...]
        at += ref.shape[0]


def gather_front(x, meanwhile=None):
    fronts = lax.axis_size("front")
    mine = [swap("front", x, k) for k in range(2, fronts, 2)]
    extra = tuple(meanwhile(x)) if meanwhile else ()
    near, last = mine[:-1], mine[-1]
    if extra:
        near = [after(near[0], *extra), *near[1:]]
    (both,) = kernel(stack, [(len(near) * x.shape[0], LANES)], *near)
    return [x, swap("front", x, 1), last, *near[::-1], swap("front", last, 1), swap("front", both, 1)], extra


def blocks_of(parts):
    rows, fronts = parts[0].shape[0], 2 * len(parts) - 6
    evens = list(range(2, fronts, 2))
    yield 0, parts[0]
    yield 1, parts[1]
    for k, part in zip(evens[::-1], parts[2:-2]):
        yield k, part
    yield evens[-1] + 1, parts[-2]
    for i, k in enumerate(evens[:-1]):
        yield k + 1, parts[-1].at[rows * i : rows * i + rows, :]


def kernel(fn, outs, *args, scratch=(), vmem=8, work=0, hbm=(), pinned=()):
    outs = [o if isinstance(o[0], tuple) else (o, F32) for o in outs]
    return pl.pallas_call(
        fn,
        out_shape=[jax.ShapeDtypeStruct(*o) for o in outs],
        in_specs=[HB if i in hbm else VM for i in range(len(args))],
        out_specs=[VM] * len(outs),
        scratch_shapes=list(scratch),
        compiler_params=pltpu.CompilerParams(vmem_limit_bytes=vmem * 2**20),
        cost_estimate=pl.CostEstimate(flops=work, bytes_accessed=work // 700, transcendentals=0),
    )(*(pltpu.with_memory_space_constraint(a, pltpu.HBM) if i in pinned else a for i, a in enumerate(args)))


def load_matrices(picks, *refs):
    count = len(picks)
    sources, outs, buffers, sems = (
        refs[:count],
        refs[count : 2 * count],
        refs[2 * count : 3 * count],
        refs[3 * count],
    )
    parent = lax.axis_index("leaf") // 2
    copies = []
    for i, (src, pick) in enumerate(zip(sources, picks)):
        rows = buffers[i].shape[1]
        step = max(rows // CHUNKS, 16)
        for n, at in enumerate(range(0, rows, step)):
            span = pl.ds(at, step)
            view = src.at[:, span, :] if pick is None else src.at[:, parent if pick == "own" else 0, span, :]
            copy = pltpu.make_async_copy(view, buffers[i].at[:, span, :], sems.at[CHUNKS * i + n])
            copy.start()
            copies.append((i, at, step, copy))
    for i, at, step, copy in copies:
        copy.wait()
        rows, depth = buffers[i].shape[1:]
        for part in range(2):
            high, low = split(buffers[i][part, at : at + step, :])
            outs[i][at : at + step, part * depth : part * depth + depth] = high
            outs[i][rows + at : rows + at + step, part * depth : part * depth + depth] = low


def load(*matrices, pinned=False):
    shapes = [m.shape[-2:] for m, _ in matrices]
    size = sum(r * d for r, d in shapes)
    return kernel(
        functools.partial(load_matrices, tuple(pick for _, pick in matrices)),
        [((2 * r, 2 * d), BF16) for r, d in shapes],
        *[m for m, _ in matrices],
        scratch=[pltpu.VMEM((2, r, d), F32) for r, d in shapes]
        + [pltpu.SemaphoreType.DMA((CHUNKS * len(shapes),))],
        hbm=range(len(shapes)),
        pinned=range(len(shapes)) if pinned else (),
        vmem=4 + -(-size * 8 // 2**20),
        work=size * 1000,
    )


def pack_receivers(fronts, rows, data_hbm, block_hbm, offset_hbm, *refs):
    own, far, near = refs[:3]
    data, block, offset, sems = refs[3:]
    copies = [
        pltpu.make_async_copy(src, dst, sems.at[i])
        for i, (src, dst) in enumerate(((data_hbm, data), (block_hbm, block), (offset_hbm, offset)))
    ]
    for copy in copies:
        copy.start()
    for copy in copies:
        copy.wait()
    group = lax.axis_index("leaf")
    count = data.shape[1]
    slots = fronts * CAP
    down = lax.broadcasted_iota(jnp.int32, (count, count), 0)
    across = lax.broadcasted_iota(jnp.int32, (count, count), 1)
    eye = down == across
    block_row = block[...]
    block_col = jnp.sum(jnp.where(eye, block_row, 0), axis=1, keepdims=True)
    offset_col = jnp.sum(jnp.where(eye, offset[...], 0), axis=1, keepdims=True)
    same = (block_col == block_row) & (down < across)
    slot_row = block_row * CAP + jnp.sum(same.astype(jnp.int32), axis=0, keepdims=True)
    row_col = (block_col & (fronts - 1)) * rows + offset_col + 1
    lane = lax.broadcasted_iota(jnp.int32, (count, COLS), 1)
    index = jnp.where(lane == 0, row_col, 0).astype(F32)
    lines = jnp.concatenate([index, data[0], jnp.zeros((count, COLS), F32), -data[1]], axis=1)
    targets = [group, group ^ 2, group ^ 1, group ^ 3]
    place = lax.broadcasted_iota(jnp.int32, (slots, count), 0)
    pick = jnp.concatenate([place + target * slots == slot_row for target in targets], axis=0)
    picked = jnp.dot(
        pick.astype(F32), lines, precision=lax.Precision.HIGHEST, preferred_element_type=F32
    )
    own[...] = picked[:slots]
    far[...] = picked[slots : 2 * slots]
    near[...] = picked[2 * slots :]


def pass_on(far, came, out):
    rows = far.shape[0]
    out[0:rows, :] = far[...]
    out[rows:, :] = came[rows:, :]


def load_sources(leaf_hbm, mid_hbm, root_hbm, leaf_out, mid_out, root_out, leaf, mid, root, sems):
    group = lax.axis_index("leaf")
    copies = [
        pltpu.make_async_copy(src, dst, sems.at[i])
        for i, (src, dst) in enumerate(
            ((leaf_hbm, leaf), (mid_hbm.at[:, group // 2], mid), (root_hbm, root))
        )
    ]
    for copy in copies:
        copy.start()
    for copy in copies:
        copy.wait()
    forward = ((group & 1) == 0).astype(F32)
    real, imag = leaf[0].T, leaf[1].T
    zero = jnp.zeros_like(real)
    leaf_out[...] = jnp.concatenate([real, zero, imag, zero], axis=1)
    mid_out[...] = pack(jnp.concatenate([mid[0], mid[1]], axis=0).T) * forward
    width = COLS // 2
    low = jnp.concatenate([root[0, :width], root[1, :width]], axis=0)
    high = jnp.concatenate([root[0, width:], root[1, width:]], axis=0)
    root_out[...] = pack(jnp.where(group < 2, low, high).T) * forward


def message_rows(rows, slots):
    return max(rows, slots), 8 * -(-slots // (8 * LANES))


def pack_leaf(own, mine, near, far, out):
    lines = jnp.concatenate([mine[...], near[0 : mine.shape[0], :], far[...]], axis=0)
    slots = lines.shape[0]
    body, tail = message_rows(own.shape[0], slots)
    lane = lax.broadcasted_iota(jnp.int32, (slots, LANES), 1)
    data = jnp.where((lane // COLS) % 2 == 1, lines, 0.0)
    index = lines[:, 0:1]

    def padded(x):
        if x.shape[0] == body:
            return x
        return jnp.concatenate([x, jnp.zeros((body - x.shape[0], LANES), F32)], axis=0)

    out[0:body, :] = padded(own[...]) + padded(data)
    out[body:, :] = jnp.zeros((tail, LANES), F32)
    for at in range(0, slots, LANES):
        size = min(LANES, slots - at)
        eye = lax.broadcasted_iota(jnp.int32, (size, size), 0) == lax.broadcasted_iota(
            jnp.int32, (size, size), 1
        )
        line = jnp.sum(jnp.where(eye, index[at : at + size], 0.0), axis=0, keepdims=True)
        out[body + at // LANES : body + at // LANES + 1, 0:size] = line


def leaf_lower(slots, matrix, *refs):
    parts, (out, rhs, messages) = refs[:-3], refs[-3:]
    rows = out.shape[0]
    here = lax.axis_index("front")
    for k, part in blocks_of(parts):
        messages[here ^ k] = part[...]
    fronts = messages.shape[0]
    total = rows * fronts
    body, _ = message_rows(rows, slots)
    lane = lax.broadcasted_iota(jnp.int32, (slots, LANES), 1)
    taken = (lane // COLS) % 2 == 1
    own = lax.broadcasted_iota(jnp.int32, (rows, LANES), 1)
    own = (own // COLS) % 2 == 0
    for k in range(fronts):
        rhs[rows * k : rows * k + rows, :] = jnp.where(own, messages[k, 0:rows, :], 0.0)
    group = max(1, 512 // slots)
    for k in range(0, fronts, group):
        chosen = range(k, min(k + group, fronts))
        lines = jnp.concatenate([jnp.where(taken, messages[i, 0:slots, :], 0.0) for i in chosen], axis=0)
        index = jnp.concatenate(
            [
                messages[i, body + at // LANES : body + at // LANES + 1, 0 : min(LANES, slots - at)]
                for i in chosen
                for at in range(0, slots, LANES)
            ],
            axis=1,
        )
        row = lax.broadcasted_iota(jnp.int32, (total, index.shape[1]), 0)
        pick = (row + 1 == index.astype(jnp.int32)).astype(BF16)
        both = dot(pick, jnp.concatenate(split(lines), axis=1))
        rhs[...] += both[:, :LANES] + both[:, LANES:]
    out[...] = complex_dot(matrix[...], rhs[...])


def leaf_to_mid(matrix, sources, *refs):
    parts, (keep, send, full) = refs[:-3], refs[-3:]
    assemble(full, parts, lax.axis_index("front"))
    mine, theirs = own_first(lax.axis_index("leaf"), *halves(complex_dot(matrix[...], full[...])))
    keep[...] = sources[...] - pack(mine)
    send[...] = -pack(theirs)


def leaf_to_root(matrix, full, keep, send):
    keep[...], send[...] = own_first(lax.axis_index("leaf"), *halves(complex_dot(matrix[...], full[...])))


def add(*refs):
    total = refs[0][...]
    for ref in refs[1:-1]:
        total = total + ref[...]
    refs[-1][...] = total


def mid_lower(matrix, *refs):
    parts, (out, whole) = refs[:-2], refs[-2:]
    assemble(whole, parts, lax.axis_index("front"), 2 * COLS)
    out[...] = pack(complex_dot(matrix[...], whole[...]))


def mid_to_root(matrix, kept, came, sources, *refs):
    parts, (keep, send, full) = refs[:-3], refs[-3:]
    assemble(full, parts, lax.axis_index("front"), 2 * COLS)
    cut = -(kept[...] + came[...] + complex_dot(matrix[...], full[...]))
    width = COLS // 2
    low = pack(jnp.concatenate([cut[:, :width], cut[:, COLS : COLS + width]], axis=1))
    high = pack(jnp.concatenate([cut[:, width:COLS], cut[:, COLS + width :]], axis=1))
    first = lax.axis_index("leaf") < 2
    keep[...] = jnp.where(first, low, high) + sources[...]
    send[...] = jnp.where(first, high, low)


def root_rows(matrix, *refs):
    parts, (out, whole) = refs[:-2], refs[-2:]
    assemble(whole, parts, lax.axis_index("front"), COLS)
    out[...] = pack(complex_dot(matrix[...], whole[...]))


def halved(value, keep, send):
    rows = keep.shape[0]
    odd = (lax.axis_index("front") & 1) == 1
    low, high = value[:rows], value[rows:]
    keep[...] = jnp.where(odd, high, low)
    send[...] = jnp.where(odd, low, high)


def root_to_mid(matrix, mine, other, keep, send, x_root):
    first = lax.axis_index("leaf") < 2
    mine, other = unpack(mine[...], COLS), unpack(other[...], COLS)
    low, high = jnp.where(first, mine, other), jnp.where(first, other, mine)
    width = COLS // 2
    x = jnp.concatenate([low[:, :width], high[:, :width], low[:, width:], high[:, width:]], axis=1)
    x_root[...] = pack(x)
    halved(pack(complex_dot(matrix[...], x)), keep, send)


def root_to_leaf(matrix, mine, other, out, forward, adjoint):
    x = by_solve(lax.axis_index("leaf"), unpack(mine[...], 2 * COLS), unpack(other[...], 2 * COLS))
    out[...] = complex_dot(matrix[...], x)
    fields_of(x, forward, adjoint, ())


def sum_front(kept, sent):
    fronts = lax.axis_size("front")
    (total,) = kernel(add, [kept.shape], kept, swap("front", sent, 1))
    hops = [1 << i for i in range(1, fronts.bit_length() - 1)]
    for hop, back in zip(hops, hops[::-1]):
        pairs = [(i, i ^ (back if i & 1 else hop)) for i in range(fronts)]
        (total,) = kernel(add, [kept.shape], total, lax.ppermute(total, "front", pairs))
    return [total, swap("front", total, 1)]


def summed(pieces):
    mine, theirs = (ref[...] for ref in pieces)
    odd = (lax.axis_index("front") & 1) == 1
    return jnp.concatenate([jnp.where(odd, theirs, mine), jnp.where(odd, mine, theirs)], axis=0)


def mid_upper(matrix, y, *refs):
    tail, out = unpack(summed(refs[:2]), 2 * COLS), refs[2]
    out[...] = pack(complex_dot(matrix[...], y[...] - tail))


def mid_to_leaf(matrix, from_root, mine, other, keep, send, x_mid):
    x = by_solve(lax.axis_index("leaf"), unpack(mine[...], 2 * COLS), unpack(other[...], 2 * COLS))
    x_mid[...] = x
    halved(complex_dot(matrix[...], x) + from_root[...], keep, send)


def leaf_upper(matrix, y, *refs):
    forward, adjoint = refs[2:]
    fields_of(complex_dot(matrix[...], y[...] - summed(refs[:2])), forward, adjoint, ())


def mid_outputs(mine, other, forward, adjoint):
    parent = lax.axis_index("leaf") // 2
    fields_of(mine[...], forward, adjoint, (parent,))
    fields_of(other[...], forward, adjoint, (1 - parent,))


def after(x, *others):
    return lax.optimization_barrier((x, *others))[0]


def body(
    leaf_lower_inv,
    leaf_upper_inv,
    leaf_to_mid_lower,
    leaf_to_root_lower,
    leaf_to_mid_upper,
    leaf_to_root_upper,
    mid_lower_inv,
    mid_upper_inv,
    mid_to_root_lower,
    mid_to_root_upper,
    root_lower_inv,
    root_upper_inv,
    leaf_sources,
    mid_sources,
    root_sources,
    receiver_data,
    receiver_block,
    receiver_offset,
):
    groups, fronts = lax.axis_size("leaf"), lax.axis_size("front")
    n0, n1, n2 = leaf_sources.shape[1], mid_sources.shape[2], root_sources.shape[1]
    s0, s1, s2 = n0 * fronts, n1 * fronts, n2 * fronts
    slots, count = fronts * CAP, receiver_data.shape[1]
    dma = pltpu.SemaphoreType.DMA

    with jax.named_scope("right_hand_sides"):
        payload = kernel(
            functools.partial(pack_receivers, fronts, n0),
            [(slots, LANES), (slots, LANES), (2 * slots, LANES)],
            receiver_data,
            receiver_block.reshape(1, -1),
            receiver_offset.reshape(1, -1),
            scratch=[
                pltpu.VMEM((2, count, COLS), F32),
                pltpu.VMEM((1, count), jnp.int32),
                pltpu.VMEM((1, count), jnp.int32),
                dma((3,)),
            ],
            hbm=range(3),
            pinned=range(3),
        )
        own, far, near = payload
        came = swap("leaf", near, 1)
        (both,) = kernel(pass_on, [(2 * slots, LANES)], far, came)
        arrived = [own, came, swap("leaf", both, 2)]
        leaf_own, mid_own, root_own = kernel(
            load_sources,
            [(n0, LANES), (n1 // 2, LANES), (n2 // 4, LANES)],
            after(leaf_sources.transpose(0, 2, 1), *payload),
            mid_sources.transpose(0, 1, 3, 2),
            root_sources.transpose(0, 2, 1),
            scratch=[
                pltpu.VMEM((2, COLS, n0), F32),
                pltpu.VMEM((2, COLS, n1), F32),
                pltpu.VMEM((2, COLS, n2), F32),
                dma((3,)),
            ],
            hbm=range(3),
            pinned=range(3),
        )
        (message,) = kernel(
            pack_leaf, [(sum(message_rows(n0, groups * slots)), LANES)], leaf_own, *arrived
        )
    with jax.named_scope("leaf_lower"):
        messages, (ll, l2m) = gather_front(
            message,
            lambda x: load((after(leaf_lower_inv, x), "leaf"), (leaf_to_mid_lower, "leaf"), pinned=True),
        )
        (y_leaf,) = kernel(
            functools.partial(leaf_lower, groups * slots),
            [(n0, LANES)],
            ll,
            *messages,
            scratch=[pltpu.VMEM((s0, LANES), F32), pltpu.VMEM((fronts, *message.shape), F32)],
        )
    with jax.named_scope("mid_lower"):
        parts, (l2r, ml) = gather_front(
            y_leaf,
            lambda x: load((after(leaf_to_root_lower, x), "leaf"), (mid_lower_inv, "own"), pinned=True),
        )
        keep, send, y_full = kernel(
            leaf_to_mid,
            [(n1 // 2, LANES), (n1 // 2, LANES), (s0, LANES)],
            l2m,
            mid_own,
            *parts,
        )
        came = swap("leaf", send, 1)
        root_kept, root_sent = kernel(leaf_to_root, [(n2, 2 * COLS)] * 2, l2r, after(y_full, send))
        (cut_mid,) = kernel(add, [(n1 // 2, LANES)], after(keep, root_kept), came)
        parts, (m2r,) = gather_front(
            cut_mid, lambda x: load((after(mid_to_root_lower, x), "own"), pinned=True)
        )
        root_came = swap("leaf", root_sent, 1)
        (y_mid,) = kernel(
            mid_lower,
            [(n1 // 2, LANES)],
            ml,
            *parts,
            scratch=[pltpu.VMEM((s1, 2 * COLS), F32)],
        )
    with jax.named_scope("root_cut"):
        parts, (rl,) = gather_front(y_mid, lambda x: load((after(root_lower_inv, x), None)))
        keep, send, y_mid_full = kernel(
            mid_to_root,
            [(n2 // 4, LANES), (n2 // 4, LANES), (s1, 2 * COLS)],
            m2r,
            root_kept,
            root_came,
            root_own,
            *parts,
        )
        came = swap("leaf", send, 2)
        mu, l2r_up = load((after(mid_upper_inv, send), "own"), (leaf_to_root_upper, "leaf"))
        (cut_root,) = kernel(add, [(n2 // 4, LANES)], after(keep, mu), came)
    with jax.named_scope("root_solve"):
        parts, (ru,) = gather_front(cut_root, lambda x: load((after(root_upper_inv, x), None)))
        (y_root,) = kernel(
            root_rows,
            [(n2 // 4, LANES)],
            rl,
            *parts,
            scratch=[pltpu.VMEM((s2, COLS), F32)],
        )
        parts, (m2r_up, l2m_up, lu) = gather_front(
            y_root,
            lambda x: load(
                (after(mid_to_root_upper, x), "own"), (leaf_to_mid_upper, "leaf"), (leaf_upper_inv, "leaf")
            ),
        )
        (x_root,) = kernel(
            root_rows,
            [(n2 // 4, LANES)],
            ru,
            *parts,
            scratch=[pltpu.VMEM((s2, COLS), F32)],
        )
    with jax.named_scope("mid_upper"):
        keep, send, x_root = kernel(
            root_to_mid,
            [(s1 // 4, LANES)] * 2 + [(n2 // 2, LANES)],
            m2r_up,
            x_root,
            swap("leaf", x_root, 2),
        )
        pieces = sum_front(keep, send)
        (x_mid,) = kernel(mid_upper, [(n1 // 2, LANES)], mu, y_mid_full, *pieces)
        from_root, root_field, root_adjoint = kernel(
            root_to_leaf,
            [(s0, LANES), (2, COLS, n2), (2, COLS, n2)],
            l2r_up,
            x_root,
            swap("leaf", after(x_root, send), 1),
        )
    with jax.named_scope("leaf_upper"):
        keep, send, x_mid = kernel(
            mid_to_leaf,
            [(s0 // 2, LANES)] * 2 + [(n1, LANES)],
            l2m_up,
            from_root,
            x_mid,
            swap("leaf", x_mid, 1),
        )
        pieces = sum_front(keep, send)
        x_other = swap("leaf", after(x_mid, send), 2)
        mid_field, mid_adjoint = kernel(mid_outputs, [(2, 2, COLS, n1)] * 2, x_mid, x_other)
        leaf_field, leaf_adjoint = kernel(leaf_upper, [(2, COLS, n0)] * 2, lu, y_full, *pieces)
    return tuple(
        jnp.swapaxes(x, -1, -2)
        for x in (leaf_field, mid_field, root_field, leaf_adjoint, mid_adjoint, root_adjoint)
    )


def solution(mesh):
    in_specs = (
        P(None, "leaf", "front", None),
        P(None, "leaf", "front", None),
        P(None, "leaf", "front", None),
        P(None, "leaf", "front", None),
        P(None, "leaf", None, "front"),
        P(None, "leaf", None, "front"),
        P(None, None, "front", None),
        P(None, None, "front", None),
        P(None, None, "front", None),
        P(None, None, None, "front"),
        P(None, "front", None),
        P(None, "front", None),
        P(None, ("leaf", "front"), None),
        P(None, None, "front", None),
        P(None, "front", None),
        P(None, ("leaf", "front"), None),
        P(("leaf", "front"), None),
        P(("leaf", "front")),
    )
    out_specs = (
        P(None, ("leaf", "front"), None),
        P(None, None, "front", None),
        P(None, "front", None),
        P(None, ("leaf", "front"), None),
        P(None, None, "front", None),
        P(None, "front", None),
    )
    return jax.shard_map(body, mesh=mesh, in_specs=in_specs, out_specs=out_specs, check_vma=False)
```

```python
import functools

import jax
import jax.numpy as jnp
from jax import lax
from jax.experimental import pallas as pl
from jax.experimental.pallas import tpu as pltpu
from jax.sharding import PartitionSpec as P

CAP = 2
CHUNKS = 4
LANES = 128
COLS = 32
F32 = jnp.float32
BF16 = jnp.bfloat16
VM = pl.BlockSpec(memory_space=pltpu.VMEM)
HB = pl.BlockSpec(memory_space=pltpu.HBM)


def split(x):
    high = x.astype(BF16)
    return high, (x - high.astype(F32)).astype(BF16)


def dot(a, b):
    return jnp.dot(a, b, preferred_element_type=F32)


def complex_dot(matrix, x):
    half = x.shape[1] // 2
    turned = jnp.concatenate([-x[:, half:], x[:, :half]], axis=1)
    both = jnp.concatenate([x, turned], axis=0)
    columns = jnp.concatenate(split(both), axis=1)
    product = dot(matrix, columns)
    rows, n = product.shape[0] // 2, x.shape[1]
    return (product[:rows, n:] + product[rows:, :n]) + product[:rows, :n]


def pack(x):
    chunks = LANES // x.shape[1]
    rows = x.shape[0] // chunks
    return jnp.concatenate([x[rows * j : rows * j + rows] for j in range(chunks)], axis=1)


def unpack(x, width):
    return jnp.concatenate([x[:, at : at + width] for at in range(0, LANES, width)], axis=0)


def halves(x):
    c = COLS
    return (
        jnp.concatenate([x[:, :c], x[:, 2 * c : 3 * c]], axis=1),
        jnp.concatenate([x[:, c : 2 * c], x[:, 3 * c :]], axis=1),
    )


def joined(forward, adjoint):
    c = COLS
    return jnp.concatenate([forward[:, :c], adjoint[:, :c], forward[:, c:], adjoint[:, c:]], axis=1)


def own_first(group, forward, adjoint):
    even = (group & 1) == 0
    return jnp.where(even, forward, adjoint), jnp.where(even, adjoint, forward)


def by_solve(group, own, other):
    even = (group & 1) == 0
    return joined(jnp.where(even, own, other), jnp.where(even, other, own))


def assemble(where, parts, here, width=LANES):
    rows = parts[0].shape[0] * (LANES // width)
    for k, part in blocks_of(parts):
        start = pl.multiple_of((here ^ k) * rows, 8)
        where[pl.ds(start, rows), :] = part[...] if width == LANES else unpack(part[...], width)


def fields_of(x, forward, adjoint, where):
    y = x.T
    c = COLS
    forward[(0, *where)] = y[0:c]
    forward[(1, *where)] = y[2 * c : 3 * c]
    adjoint[(0, *where)] = y[c : 2 * c]
    adjoint[(1, *where)] = -y[3 * c :]


def swap(axis, x, k):
    size = lax.axis_size(axis)
    return lax.ppermute(x, axis, [(i, i ^ k) for i in range(size)])


def stack(*refs):
    at = 0
    for ref in refs[:-1]:
        refs[-1][at : at + ref.shape[0], :] = ref[...]
        at += ref.shape[0]


def gather_front(x, meanwhile=None):
    fronts = lax.axis_size("front")
    mine = [swap("front", x, k) for k in range(2, fronts, 2)]
    own = swap("front", x, 1)
    extra = tuple(meanwhile(own)) if meanwhile else ()
    near, last = mine[:-1], mine[-1]
    if extra:
        near = [after(near[0], *extra), *near[1:]]
    (both,) = kernel(stack, [(len(near) * x.shape[0], LANES)], *near)
    return [x, own, last, *near[::-1], swap("front", last, 1), swap("front", both, 1)], extra


def blocks_of(parts):
    rows, fronts = parts[0].shape[0], 2 * len(parts) - 6
    evens = list(range(2, fronts, 2))
    yield 0, parts[0]
    yield 1, parts[1]
    for k, part in zip(evens[::-1], parts[2:-2]):
        yield k, part
    yield evens[-1] + 1, parts[-2]
    for i, k in enumerate(evens[:-1]):
        yield k + 1, parts[-1].at[rows * i : rows * i + rows, :]


def kernel(fn, outs, *args, scratch=(), vmem=8, work=0, hbm=(), pinned=()):
    outs = [o if isinstance(o[0], tuple) else (o, F32) for o in outs]
    return pl.pallas_call(
        fn,
        out_shape=[jax.ShapeDtypeStruct(*o) for o in outs],
        in_specs=[HB if i in hbm else VM for i in range(len(args))],
        out_specs=[VM] * len(outs),
        scratch_shapes=list(scratch),
        compiler_params=pltpu.CompilerParams(vmem_limit_bytes=vmem * 2**20),
        cost_estimate=pl.CostEstimate(flops=work, bytes_accessed=work // 700, transcendentals=0),
    )(*(pltpu.with_memory_space_constraint(a, pltpu.HBM) if i in pinned else a for i, a in enumerate(args)))


def load_matrices(picks, *refs):
    count = len(picks)
    sources, outs, buffers, sems = (
        refs[:count],
        refs[count : 2 * count],
        refs[2 * count : 3 * count],
        refs[3 * count],
    )
    parent = lax.axis_index("leaf") // 2
    copies = []
    for i, (src, pick) in enumerate(zip(sources, picks)):
        rows = buffers[i].shape[1]
        step = max(rows // CHUNKS, 16)
        for n, at in enumerate(range(0, rows, step)):
            span = pl.ds(at, step)
            view = src.at[:, span, :] if pick is None else src.at[:, parent if pick == "own" else 0, span, :]
            copy = pltpu.make_async_copy(view, buffers[i].at[:, span, :], sems.at[CHUNKS * i + n])
            copy.start()
            copies.append((i, at, step, copy))
    for i, at, step, copy in copies:
        copy.wait()
        rows, depth = buffers[i].shape[1:]
        for part in range(2):
            high, low = split(buffers[i][part, at : at + step, :])
            outs[i][at : at + step, part * depth : part * depth + depth] = high
            outs[i][rows + at : rows + at + step, part * depth : part * depth + depth] = low


def load(*matrices, pinned=False):
    shapes = [m.shape[-2:] for m, _ in matrices]
    size = sum(r * d for r, d in shapes)
    return kernel(
        functools.partial(load_matrices, tuple(pick for _, pick in matrices)),
        [((2 * r, 2 * d), BF16) for r, d in shapes],
        *[m for m, _ in matrices],
        scratch=[pltpu.VMEM((2, r, d), F32) for r, d in shapes]
        + [pltpu.SemaphoreType.DMA((CHUNKS * len(shapes),))],
        hbm=range(len(shapes)),
        pinned=range(len(shapes)) if pinned else (),
        vmem=4 + -(-size * 8 // 2**20),
        work=size * 1000,
    )


def pack_receivers(fronts, rows, data_hbm, block_hbm, offset_hbm, *refs):
    own, far, near = refs[:3]
    data, block, offset, sems = refs[3:]
    copies = [
        pltpu.make_async_copy(src, dst, sems.at[i])
        for i, (src, dst) in enumerate(((data_hbm, data), (block_hbm, block), (offset_hbm, offset)))
    ]
    for copy in copies:
        copy.start()
    for copy in copies:
        copy.wait()
    group = lax.axis_index("leaf")
    count = data.shape[1]
    slots = fronts * CAP
    down = lax.broadcasted_iota(jnp.int32, (count, count), 0)
    across = lax.broadcasted_iota(jnp.int32, (count, count), 1)
    eye = down == across
    block_row = block[...]
    block_col = jnp.sum(jnp.where(eye, block_row, 0), axis=1, keepdims=True)
    offset_col = jnp.sum(jnp.where(eye, offset[...], 0), axis=1, keepdims=True)
    same = (block_col == block_row) & (down < across)
    slot_row = block_row * CAP + jnp.sum(same.astype(jnp.int32), axis=0, keepdims=True)
    row_col = (block_col & (fronts - 1)) * rows + offset_col + 1
    lane = lax.broadcasted_iota(jnp.int32, (count, COLS), 1)
    index = jnp.where(lane == 0, row_col, 0).astype(F32)
    lines = jnp.concatenate([index, data[0], jnp.zeros((count, COLS), F32), -data[1]], axis=1)
    targets = [group, group ^ 2, group ^ 1, group ^ 3]
    place = lax.broadcasted_iota(jnp.int32, (slots, count), 0)
    pick = jnp.concatenate([place + target * slots == slot_row for target in targets], axis=0)
    picked = jnp.dot(
        pick.astype(F32), lines, precision=lax.Precision.HIGHEST, preferred_element_type=F32
    )
    own[...] = picked[:slots]
    far[...] = picked[slots : 2 * slots]
    near[...] = picked[2 * slots :]


def pass_on(far, came, out):
    rows = far.shape[0]
    out[0:rows, :] = far[...]
    out[rows:, :] = came[rows:, :]


def load_sources(leaf_hbm, mid_hbm, root_hbm, leaf_out, mid_out, root_out, leaf, mid, root, sems):
    group = lax.axis_index("leaf")
    copies = [
        pltpu.make_async_copy(src, dst, sems.at[i])
        for i, (src, dst) in enumerate(
            ((leaf_hbm, leaf), (mid_hbm.at[:, group // 2], mid), (root_hbm, root))
        )
    ]
    for copy in copies:
        copy.start()
    for copy in copies:
        copy.wait()
    forward = ((group & 1) == 0).astype(F32)
    real, imag = leaf[0].T, leaf[1].T
    zero = jnp.zeros_like(real)
    leaf_out[...] = jnp.concatenate([real, zero, imag, zero], axis=1)
    mid_out[...] = pack(jnp.concatenate([mid[0], mid[1]], axis=0).T) * forward
    width = COLS // 2
    low = jnp.concatenate([root[0, :width], root[1, :width]], axis=0)
    high = jnp.concatenate([root[0, width:], root[1, width:]], axis=0)
    root_out[...] = pack(jnp.where(group < 2, low, high).T) * forward


def message_rows(rows, slots):
    return max(rows, slots), 8 * -(-slots // (8 * LANES))


def pack_leaf(own, mine, near, far, out):
    lines = jnp.concatenate([mine[...], near[0 : mine.shape[0], :], far[...]], axis=0)
    slots = lines.shape[0]
    body, tail = message_rows(own.shape[0], slots)
    lane = lax.broadcasted_iota(jnp.int32, (slots, LANES), 1)
    data = jnp.where((lane // COLS) % 2 == 1, lines, 0.0)
    index = lines[:, 0:1]

    def padded(x):
        if x.shape[0] == body:
            return x
        return jnp.concatenate([x, jnp.zeros((body - x.shape[0], LANES), F32)], axis=0)

    out[0:body, :] = padded(own[...]) + padded(data)
    out[body:, :] = jnp.zeros((tail, LANES), F32)
    for at in range(0, slots, LANES):
        size = min(LANES, slots - at)
        eye = lax.broadcasted_iota(jnp.int32, (size, size), 0) == lax.broadcasted_iota(
            jnp.int32, (size, size), 1
        )
        line = jnp.sum(jnp.where(eye, index[at : at + size], 0.0), axis=0, keepdims=True)
        out[body + at // LANES : body + at // LANES + 1, 0:size] = line


def leaf_lower(slots, matrix, *refs):
    parts, (out, rhs, messages) = refs[:-3], refs[-3:]
    rows = out.shape[0]
    here = lax.axis_index("front")
    for k, part in blocks_of(parts):
        messages[here ^ k] = part[...]
    fronts = messages.shape[0]
    total = rows * fronts
    body, _ = message_rows(rows, slots)
    lane = lax.broadcasted_iota(jnp.int32, (slots, LANES), 1)
    taken = (lane // COLS) % 2 == 1
    own = lax.broadcasted_iota(jnp.int32, (rows, LANES), 1)
    own = (own // COLS) % 2 == 0
    for k in range(fronts):
        rhs[rows * k : rows * k + rows, :] = jnp.where(own, messages[k, 0:rows, :], 0.0)
    group = max(1, 512 // slots)
    for k in range(0, fronts, group):
        chosen = range(k, min(k + group, fronts))
        lines = jnp.concatenate([jnp.where(taken, messages[i, 0:slots, :], 0.0) for i in chosen], axis=0)
        index = jnp.concatenate(
            [
                messages[i, body + at // LANES : body + at // LANES + 1, 0 : min(LANES, slots - at)]
                for i in chosen
                for at in range(0, slots, LANES)
            ],
            axis=1,
        )
        row = lax.broadcasted_iota(jnp.int32, (total, index.shape[1]), 0)
        pick = (row + 1 == index.astype(jnp.int32)).astype(BF16)
        both = dot(pick, jnp.concatenate(split(lines), axis=1))
        rhs[...] += both[:, :LANES] + both[:, LANES:]
    out[...] = complex_dot(matrix[...], rhs[...])


def leaf_to_mid(matrix, sources, *refs):
    parts, (keep, send, full) = refs[:-3], refs[-3:]
    assemble(full, parts, lax.axis_index("front"))
    mine, theirs = own_first(lax.axis_index("leaf"), *halves(complex_dot(matrix[...], full[...])))
    keep[...] = sources[...] - pack(mine)
    send[...] = -pack(theirs)


def leaf_to_root(matrix, full, keep, send):
    keep[...], send[...] = own_first(lax.axis_index("leaf"), *halves(complex_dot(matrix[...], full[...])))


def add(*refs):
    total = refs[0][...]
    for ref in refs[1:-1]:
        total = total + ref[...]
    refs[-1][...] = total


def mid_lower(matrix, *refs):
    parts, (out, whole) = refs[:-2], refs[-2:]
    assemble(whole, parts, lax.axis_index("front"), 2 * COLS)
    out[...] = pack(complex_dot(matrix[...], whole[...]))


def mid_to_root(matrix, kept, came, sources, *refs):
    parts, (keep, send, full) = refs[:-3], refs[-3:]
    assemble(full, parts, lax.axis_index("front"), 2 * COLS)
    cut = -(kept[...] + came[...] + complex_dot(matrix[...], full[...]))
    width = COLS // 2
    low = pack(jnp.concatenate([cut[:, :width], cut[:, COLS : COLS + width]], axis=1))
    high = pack(jnp.concatenate([cut[:, width:COLS], cut[:, COLS + width :]], axis=1))
    first = lax.axis_index("leaf") < 2
    keep[...] = jnp.where(first, low, high) + sources[...]
    send[...] = jnp.where(first, high, low)


def root_rows(matrix, *refs):
    parts, (out, whole) = refs[:-2], refs[-2:]
    assemble(whole, parts, lax.axis_index("front"), COLS)
    out[...] = pack(complex_dot(matrix[...], whole[...]))


def halved(value, keep, send):
    rows = keep.shape[0]
    odd = (lax.axis_index("front") & 1) == 1
    low, high = value[:rows], value[rows:]
    keep[...] = jnp.where(odd, high, low)
    send[...] = jnp.where(odd, low, high)


def root_to_mid(matrix, mine, other, keep, send, x_root):
    first = lax.axis_index("leaf") < 2
    mine, other = unpack(mine[...], COLS), unpack(other[...], COLS)
    low, high = jnp.where(first, mine, other), jnp.where(first, other, mine)
    width = COLS // 2
    x = jnp.concatenate([low[:, :width], high[:, :width], low[:, width:], high[:, width:]], axis=1)
    x_root[...] = pack(x)
    halved(pack(complex_dot(matrix[...], x)), keep, send)


def root_to_leaf(matrix, mine, other, out, forward, adjoint):
    x = by_solve(lax.axis_index("leaf"), unpack(mine[...], 2 * COLS), unpack(other[...], 2 * COLS))
    out[...] = complex_dot(matrix[...], x)
    fields_of(x, forward, adjoint, ())


def sum_front(kept, sent, *others):
    fronts = lax.axis_size("front")
    (total,) = kernel(add, [kept.shape], kept, swap("front", sent, 1))
    hops = [1 << i for i in range(1, fronts.bit_length() - 1)]
    for hop, back in zip(hops, hops[::-1]):
        pairs = [(i, i ^ (back if i & 1 else hop)) for i in range(fronts)]
        (total,) = kernel(add, [kept.shape], total, lax.ppermute(total, "front", pairs))
    return [total, swap("front", after(total, *others), 1)]


def summed(pieces):
    mine, theirs = (ref[...] for ref in pieces)
    odd = (lax.axis_index("front") & 1) == 1
    return jnp.concatenate([jnp.where(odd, theirs, mine), jnp.where(odd, mine, theirs)], axis=0)


def mid_upper(matrix, y, *refs):
    tail, out = unpack(summed(refs[:2]), 2 * COLS), refs[2]
    out[...] = pack(complex_dot(matrix[...], y[...] - tail))


def mid_to_leaf(matrix, from_root, mine, other, keep, send, x_mid):
    x = by_solve(lax.axis_index("leaf"), unpack(mine[...], 2 * COLS), unpack(other[...], 2 * COLS))
    x_mid[...] = x
    halved(complex_dot(matrix[...], x) + from_root[...], keep, send)


def leaf_upper(matrix, y, *refs):
    forward, adjoint = refs[2:]
    fields_of(complex_dot(matrix[...], y[...] - summed(refs[:2])), forward, adjoint, ())


def mid_outputs(mine, other, forward, adjoint):
    parent = lax.axis_index("leaf") // 2
    fields_of(mine[...], forward, adjoint, (parent,))
    fields_of(other[...], forward, adjoint, (1 - parent,))


def after(x, *others):
    return lax.optimization_barrier((x, *others))[0]


def body(
    leaf_lower_inv,
    leaf_upper_inv,
    leaf_to_mid_lower,
    leaf_to_root_lower,
    leaf_to_mid_upper,
    leaf_to_root_upper,
    mid_lower_inv,
    mid_upper_inv,
    mid_to_root_lower,
    mid_to_root_upper,
    root_lower_inv,
    root_upper_inv,
    leaf_sources,
    mid_sources,
    root_sources,
    receiver_data,
    receiver_block,
    receiver_offset,
):
    groups, fronts = lax.axis_size("leaf"), lax.axis_size("front")
    n0, n1, n2 = leaf_sources.shape[1], mid_sources.shape[2], root_sources.shape[1]
    s0, s1, s2 = n0 * fronts, n1 * fronts, n2 * fronts
    slots, count = fronts * CAP, receiver_data.shape[1]
    dma = pltpu.SemaphoreType.DMA

    with jax.named_scope("right_hand_sides"):
        payload = kernel(
            functools.partial(pack_receivers, fronts, n0),
            [(slots, LANES), (slots, LANES), (2 * slots, LANES)],
            receiver_data,
            receiver_block.reshape(1, -1),
            receiver_offset.reshape(1, -1),
            scratch=[
                pltpu.VMEM((2, count, COLS), F32),
                pltpu.VMEM((1, count), jnp.int32),
                pltpu.VMEM((1, count), jnp.int32),
                dma((3,)),
            ],
            hbm=range(3),
            pinned=range(3),
        )
        own, far, near = payload
        came = swap("leaf", near, 1)
        (both,) = kernel(pass_on, [(2 * slots, LANES)], far, came)
        arrived = [own, came, swap("leaf", both, 2)]
        leaf_own, mid_own, root_own = kernel(
            load_sources,
            [(n0, LANES), (n1 // 2, LANES), (n2 // 4, LANES)],
            after(leaf_sources.transpose(0, 2, 1), *payload),
            mid_sources.transpose(0, 1, 3, 2),
            root_sources.transpose(0, 2, 1),
            scratch=[
                pltpu.VMEM((2, COLS, n0), F32),
                pltpu.VMEM((2, COLS, n1), F32),
                pltpu.VMEM((2, COLS, n2), F32),
                dma((3,)),
            ],
            hbm=range(3),
            pinned=range(3),
        )
        (message,) = kernel(
            pack_leaf, [(sum(message_rows(n0, groups * slots)), LANES)], leaf_own, *arrived
        )
    with jax.named_scope("leaf_lower"):
        messages, (ll, l2m) = gather_front(
            message,
            lambda x: load((after(leaf_lower_inv, x), "leaf"), (leaf_to_mid_lower, "leaf"), pinned=True),
        )
        (y_leaf,) = kernel(
            functools.partial(leaf_lower, groups * slots),
            [(n0, LANES)],
            ll,
            *messages,
            scratch=[pltpu.VMEM((s0, LANES), F32), pltpu.VMEM((fronts, *message.shape), F32)],
        )
    with jax.named_scope("mid_lower"):
        parts, (l2r, ml) = gather_front(
            y_leaf,
            lambda x: load((after(leaf_to_root_lower, x), "leaf"), (mid_lower_inv, "own"), pinned=True),
        )
        keep, send, y_full = kernel(
            leaf_to_mid,
            [(n1 // 2, LANES), (n1 // 2, LANES), (s0, LANES)],
            l2m,
            mid_own,
            *parts,
        )
        came = swap("leaf", send, 1)
        root_kept, root_sent = kernel(leaf_to_root, [(n2, 2 * COLS)] * 2, l2r, after(y_full, send))
        (cut_mid,) = kernel(add, [(n1 // 2, LANES)], after(keep, root_kept), came)
        parts, (m2r,) = gather_front(
            cut_mid, lambda x: load((after(mid_to_root_lower, x), "own"), pinned=True)
        )
        root_came = swap("leaf", root_sent, 1)
        (y_mid,) = kernel(
            mid_lower,
            [(n1 // 2, LANES)],
            ml,
            *parts,
            scratch=[pltpu.VMEM((s1, 2 * COLS), F32)],
        )
    with jax.named_scope("root_cut"):
        parts, (rl,) = gather_front(y_mid, lambda x: load((after(root_lower_inv, x), None)))
        keep, send, y_mid_full = kernel(
            mid_to_root,
            [(n2 // 4, LANES), (n2 // 4, LANES), (s1, 2 * COLS)],
            m2r,
            root_kept,
            root_came,
            root_own,
            *parts,
        )
        came = swap("leaf", send, 2)
        mu, l2r_up = load((after(mid_upper_inv, send), "own"), (leaf_to_root_upper, "leaf"))
        (cut_root,) = kernel(add, [(n2 // 4, LANES)], after(keep, mu), came)
    with jax.named_scope("root_solve"):
        parts, (ru,) = gather_front(cut_root, lambda x: load((after(root_upper_inv, x), None)))
        (y_root,) = kernel(
            root_rows,
            [(n2 // 4, LANES)],
            rl,
            *parts,
            scratch=[pltpu.VMEM((s2, COLS), F32)],
        )
        parts, (m2r_up, l2m_up, lu) = gather_front(
            y_root,
            lambda x: load(
                (after(mid_to_root_upper, x), "own"), (leaf_to_mid_upper, "leaf"), (leaf_upper_inv, "leaf")
            ),
        )
        (x_root,) = kernel(
            root_rows,
            [(n2 // 4, LANES)],
            ru,
            *parts,
            scratch=[pltpu.VMEM((s2, COLS), F32)],
        )
    with jax.named_scope("mid_upper"):
        keep, send, x_root = kernel(
            root_to_mid,
            [(s1 // 4, LANES)] * 2 + [(n2 // 2, LANES)],
            m2r_up,
            x_root,
            swap("leaf", x_root, 2),
        )
        pieces = sum_front(keep, send)
        (x_mid,) = kernel(mid_upper, [(n1 // 2, LANES)], mu, y_mid_full, *pieces)
        from_root, root_field, root_adjoint = kernel(
            root_to_leaf,
            [(s0, LANES), (2, COLS, n2), (2, COLS, n2)],
            l2r_up,
            x_root,
            swap("leaf", after(x_root, send), 1),
        )
    with jax.named_scope("leaf_upper"):
        keep, send, x_mid = kernel(
            mid_to_leaf,
            [(s0 // 2, LANES)] * 2 + [(n1, LANES)],
            l2m_up,
            from_root,
            x_mid,
            swap("leaf", x_mid, 1),
        )
        x_other = swap("leaf", x_mid, 2)
        mid_field, mid_adjoint = kernel(mid_outputs, [(2, 2, COLS, n1)] * 2, x_mid, x_other)
        pieces = sum_front(keep, send, mid_field)
        leaf_field, leaf_adjoint = kernel(leaf_upper, [(2, COLS, n0)] * 2, lu, y_full, *pieces)
    return tuple(
        jnp.swapaxes(x, -1, -2)
        for x in (leaf_field, mid_field, root_field, leaf_adjoint, mid_adjoint, root_adjoint)
    )


def solution(mesh):
    in_specs = (
        P(None, "leaf", "front", None),
        P(None, "leaf", "front", None),
        P(None, "leaf", "front", None),
        P(None, "leaf", "front", None),
        P(None, "leaf", None, "front"),
        P(None, "leaf", None, "front"),
        P(None, None, "front", None),
        P(None, None, "front", None),
        P(None, None, "front", None),
        P(None, None, None, "front"),
        P(None, "front", None),
        P(None, "front", None),
        P(None, ("leaf", "front"), None),
        P(None, None, "front", None),
        P(None, "front", None),
        P(None, ("leaf", "front"), None),
        P(("leaf", "front"), None),
        P(("leaf", "front")),
    )
    out_specs = (
        P(None, ("leaf", "front"), None),
        P(None, None, "front", None),
        P(None, "front", None),
        P(None, ("leaf", "front"), None),
        P(None, None, "front", None),
        P(None, "front", None),
    )
    return jax.shard_map(body, mesh=mesh, in_specs=in_specs, out_specs=out_specs, check_vma=False)
```

```python
import functools

import jax
import jax.numpy as jnp
from jax import lax
from jax.experimental import pallas as pl
from jax.experimental.pallas import tpu as pltpu
from jax.sharding import PartitionSpec as P

CAP = 2
CHUNKS = 4
LANES = 128
COLS = 32
F32 = jnp.float32
BF16 = jnp.bfloat16
VM = pl.BlockSpec(memory_space=pltpu.VMEM)
HB = pl.BlockSpec(memory_space=pltpu.HBM)


def split(x):
    high = x.astype(BF16)
    return high, (x - high.astype(F32)).astype(BF16)


def dot(a, b):
    return jnp.dot(a, b, preferred_element_type=F32)


def complex_dot(matrix, x):
    half = x.shape[1] // 2
    turned = jnp.concatenate([-x[:, half:], x[:, :half]], axis=1)
    both = jnp.concatenate([x, turned], axis=0)
    columns = jnp.concatenate(split(both), axis=1)
    product = dot(matrix, columns)
    rows, n = product.shape[0] // 2, x.shape[1]
    return (product[:rows, n:] + product[rows:, :n]) + product[:rows, :n]


def pack(x):
    chunks = LANES // x.shape[1]
    rows = x.shape[0] // chunks
    return jnp.concatenate([x[rows * j : rows * j + rows] for j in range(chunks)], axis=1)


def unpack(x, width):
    return jnp.concatenate([x[:, at : at + width] for at in range(0, LANES, width)], axis=0)


def halves(x):
    c = COLS
    return (
        jnp.concatenate([x[:, :c], x[:, 2 * c : 3 * c]], axis=1),
        jnp.concatenate([x[:, c : 2 * c], x[:, 3 * c :]], axis=1),
    )


def joined(forward, adjoint):
    c = COLS
    return jnp.concatenate([forward[:, :c], adjoint[:, :c], forward[:, c:], adjoint[:, c:]], axis=1)


def own_first(group, forward, adjoint):
    even = (group & 1) == 0
    return jnp.where(even, forward, adjoint), jnp.where(even, adjoint, forward)


def by_solve(group, own, other):
    even = (group & 1) == 0
    return joined(jnp.where(even, own, other), jnp.where(even, other, own))


def assemble(where, parts, here, width=LANES):
    rows = parts[0].shape[0] * (LANES // width)
    for k, part in blocks_of(parts):
        start = pl.multiple_of((here ^ k) * rows, 8)
        where[pl.ds(start, rows), :] = part[...] if width == LANES else unpack(part[...], width)


def fields_of(x, forward, adjoint, where):
    y = x.T
    c = COLS
    forward[(0, *where)] = y[0:c]
    forward[(1, *where)] = y[2 * c : 3 * c]
    adjoint[(0, *where)] = y[c : 2 * c]
    adjoint[(1, *where)] = -y[3 * c :]


def swap(axis, x, k):
    size = lax.axis_size(axis)
    return lax.ppermute(x, axis, [(i, i ^ k) for i in range(size)])


def stack(*refs):
    at = 0
    for ref in refs[:-1]:
        refs[-1][at : at + ref.shape[0], :] = ref[...]
        at += ref.shape[0]


def gather_front(x, meanwhile=None, others=()):
    fronts = lax.axis_size("front")
    mine = [swap("front", x, k) for k in range(2, fronts, 2)]
    near, last = mine[:-1], mine[-1]
    own = swap("front", x, 1)
    (both,) = kernel(stack, [(len(near) * x.shape[0], LANES)], *near)
    extra = tuple(meanwhile((both, own))) if meanwhile else ()
    last = after(last, *extra, *others)
    return [x, own, last, *near[::-1], swap("front", last, 1), swap("front", both, 1)], extra


def blocks_of(parts):
    rows, fronts = parts[0].shape[0], 2 * len(parts) - 6
    evens = list(range(2, fronts, 2))
    yield 0, parts[0]
    yield 1, parts[1]
    for k, part in zip(evens[::-1], parts[2:-2]):
        yield k, part
    yield evens[-1] + 1, parts[-2]
    for i, k in enumerate(evens[:-1]):
        yield k + 1, parts[-1].at[rows * i : rows * i + rows, :]


def kernel(fn, outs, *args, scratch=(), vmem=8, work=0, hbm=(), pinned=()):
    outs = [o if isinstance(o[0], tuple) else (o, F32) for o in outs]
    return pl.pallas_call(
        fn,
        out_shape=[jax.ShapeDtypeStruct(*o) for o in outs],
        in_specs=[HB if i in hbm else VM for i in range(len(args))],
        out_specs=[VM] * len(outs),
        scratch_shapes=list(scratch),
        compiler_params=pltpu.CompilerParams(vmem_limit_bytes=vmem * 2**20),
        cost_estimate=pl.CostEstimate(flops=work, bytes_accessed=work // 700, transcendentals=0),
    )(*(pltpu.with_memory_space_constraint(a, pltpu.HBM) if i in pinned else a for i, a in enumerate(args)))


def load_matrices(picks, *refs):
    count = len(picks)
    sources, outs, buffers, sems = (
        refs[:count],
        refs[count : 2 * count],
        refs[2 * count : 3 * count],
        refs[3 * count],
    )
    parent = lax.axis_index("leaf") // 2
    copies = []
    for i, (src, pick) in enumerate(zip(sources, picks)):
        rows = buffers[i].shape[1]
        step = max(rows // CHUNKS, 16)
        for n, at in enumerate(range(0, rows, step)):
            span = pl.ds(at, step)
            view = src.at[:, span, :] if pick is None else src.at[:, parent if pick == "own" else 0, span, :]
            copy = pltpu.make_async_copy(view, buffers[i].at[:, span, :], sems.at[CHUNKS * i + n])
            copy.start()
            copies.append((i, at, step, copy))
    for i, at, step, copy in copies:
        copy.wait()
        rows, depth = buffers[i].shape[1:]
        for part in range(2):
            high, low = split(buffers[i][part, at : at + step, :])
            outs[i][at : at + step, part * depth : part * depth + depth] = high
            outs[i][rows + at : rows + at + step, part * depth : part * depth + depth] = low


def load(*matrices, pinned=False):
    shapes = [m.shape[-2:] for m, _ in matrices]
    size = sum(r * d for r, d in shapes)
    return kernel(
        functools.partial(load_matrices, tuple(pick for _, pick in matrices)),
        [((2 * r, 2 * d), BF16) for r, d in shapes],
        *[m for m, _ in matrices],
        scratch=[pltpu.VMEM((2, r, d), F32) for r, d in shapes]
        + [pltpu.SemaphoreType.DMA((CHUNKS * len(shapes),))],
        hbm=range(len(shapes)),
        pinned=range(len(shapes)) if pinned else (),
        vmem=4 + -(-size * 8 // 2**20),
        work=size * 1000,
    )


def pack_receivers(fronts, rows, data_hbm, block_hbm, offset_hbm, *refs):
    own, far, near = refs[:3]
    data, block, offset, sems = refs[3:]
    copies = [
        pltpu.make_async_copy(src, dst, sems.at[i])
        for i, (src, dst) in enumerate(((data_hbm, data), (block_hbm, block), (offset_hbm, offset)))
    ]
    for copy in copies:
        copy.start()
    for copy in copies:
        copy.wait()
    group = lax.axis_index("leaf")
    count = data.shape[1]
    slots = fronts * CAP
    down = lax.broadcasted_iota(jnp.int32, (count, count), 0)
    across = lax.broadcasted_iota(jnp.int32, (count, count), 1)
    eye = down == across
    block_row = block[...]
    block_col = jnp.sum(jnp.where(eye, block_row, 0), axis=1, keepdims=True)
    offset_col = jnp.sum(jnp.where(eye, offset[...], 0), axis=1, keepdims=True)
    same = (block_col == block_row) & (down < across)
    slot_row = block_row * CAP + jnp.sum(same.astype(jnp.int32), axis=0, keepdims=True)
    row_col = (block_col & (fronts - 1)) * rows + offset_col + 1
    lane = lax.broadcasted_iota(jnp.int32, (count, COLS), 1)
    index = jnp.where(lane == 0, row_col, 0).astype(F32)
    lines = jnp.concatenate([index, data[0], jnp.zeros((count, COLS), F32), -data[1]], axis=1)
    targets = [group, group ^ 2, group ^ 1, group ^ 3]
    place = lax.broadcasted_iota(jnp.int32, (slots, count), 0)
    pick = jnp.concatenate([place + target * slots == slot_row for target in targets], axis=0)
    picked = jnp.dot(
        pick.astype(F32), lines, precision=lax.Precision.HIGHEST, preferred_element_type=F32
    )
    own[...] = picked[:slots]
    far[...] = picked[slots : 2 * slots]
    near[...] = picked[2 * slots :]


def pass_on(far, came, out):
    rows = far.shape[0]
    out[0:rows, :] = far[...]
    out[rows:, :] = came[rows:, :]


def load_sources(leaf_hbm, mid_hbm, root_hbm, leaf_out, mid_out, root_out, leaf, mid, root, sems):
    group = lax.axis_index("leaf")
    copies = [
        pltpu.make_async_copy(src, dst, sems.at[i])
        for i, (src, dst) in enumerate(
            ((leaf_hbm, leaf), (mid_hbm.at[:, group // 2], mid), (root_hbm, root))
        )
    ]
    for copy in copies:
        copy.start()
    for copy in copies:
        copy.wait()
    forward = ((group & 1) == 0).astype(F32)
    real, imag = leaf[0].T, leaf[1].T
    zero = jnp.zeros_like(real)
    leaf_out[...] = jnp.concatenate([real, zero, imag, zero], axis=1)
    mid_out[...] = pack(jnp.concatenate([mid[0], mid[1]], axis=0).T) * forward
    width = COLS // 2
    low = jnp.concatenate([root[0, :width], root[1, :width]], axis=0)
    high = jnp.concatenate([root[0, width:], root[1, width:]], axis=0)
    root_out[...] = pack(jnp.where(group < 2, low, high).T) * forward


def message_rows(rows, slots):
    return max(rows, slots), 8 * -(-slots // (8 * LANES))


def pack_leaf(own, mine, near, far, out):
    lines = jnp.concatenate([mine[...], near[0 : mine.shape[0], :], far[...]], axis=0)
    slots = lines.shape[0]
    body, tail = message_rows(own.shape[0], slots)
    lane = lax.broadcasted_iota(jnp.int32, (slots, LANES), 1)
    data = jnp.where((lane // COLS) % 2 == 1, lines, 0.0)
    index = lines[:, 0:1]

    def padded(x):
        if x.shape[0] == body:
            return x
        return jnp.concatenate([x, jnp.zeros((body - x.shape[0], LANES), F32)], axis=0)

    out[0:body, :] = padded(own[...]) + padded(data)
    out[body:, :] = jnp.zeros((tail, LANES), F32)
    for at in range(0, slots, LANES):
        size = min(LANES, slots - at)
        eye = lax.broadcasted_iota(jnp.int32, (size, size), 0) == lax.broadcasted_iota(
            jnp.int32, (size, size), 1
        )
        line = jnp.sum(jnp.where(eye, index[at : at + size], 0.0), axis=0, keepdims=True)
        out[body + at // LANES : body + at // LANES + 1, 0:size] = line


def leaf_lower(slots, matrix, *refs):
    parts, (out, rhs, messages) = refs[:-3], refs[-3:]
    rows = out.shape[0]
    here = lax.axis_index("front")
    for k, part in blocks_of(parts):
        messages[here ^ k] = part[...]
    fronts = messages.shape[0]
    total = rows * fronts
    body, _ = message_rows(rows, slots)
    lane = lax.broadcasted_iota(jnp.int32, (slots, LANES), 1)
    taken = (lane // COLS) % 2 == 1
    own = lax.broadcasted_iota(jnp.int32, (rows, LANES), 1)
    own = (own // COLS) % 2 == 0
    for k in range(fronts):
        rhs[rows * k : rows * k + rows, :] = jnp.where(own, messages[k, 0:rows, :], 0.0)
    group = max(1, 512 // slots)
    for k in range(0, fronts, group):
        chosen = range(k, min(k + group, fronts))
        lines = jnp.concatenate([jnp.where(taken, messages[i, 0:slots, :], 0.0) for i in chosen], axis=0)
        index = jnp.concatenate(
            [
                messages[i, body + at // LANES : body + at // LANES + 1, 0 : min(LANES, slots - at)]
                for i in chosen
                for at in range(0, slots, LANES)
            ],
            axis=1,
        )
        row = lax.broadcasted_iota(jnp.int32, (total, index.shape[1]), 0)
        pick = (row + 1 == index.astype(jnp.int32)).astype(BF16)
        both = dot(pick, jnp.concatenate(split(lines), axis=1))
        rhs[...] += both[:, :LANES] + both[:, LANES:]
    out[...] = complex_dot(matrix[...], rhs[...])


def leaf_to_mid(matrix, sources, *refs):
    parts, (keep, send, full) = refs[:-3], refs[-3:]
    assemble(full, parts, lax.axis_index("front"))
    mine, theirs = own_first(lax.axis_index("leaf"), *halves(complex_dot(matrix[...], full[...])))
    keep[...] = sources[...] - pack(mine)
    send[...] = -pack(theirs)


def leaf_to_root(matrix, full, keep, send):
    mine, theirs = own_first(lax.axis_index("leaf"), *halves(complex_dot(matrix[...], full[...])))
    keep[...], send[...] = pack(mine), pack(theirs)


def add(*refs):
    total = refs[0][...]
    for ref in refs[1:-1]:
        total = total + ref[...]
    refs[-1][...] = total


def mid_lower(matrix, *refs):
    parts, (out, whole) = refs[:-2], refs[-2:]
    assemble(whole, parts, lax.axis_index("front"), 2 * COLS)
    out[...] = pack(complex_dot(matrix[...], whole[...]))


def mid_to_root(matrix, kept, came, sources, *refs):
    parts, (keep, send, full) = refs[:-3], refs[-3:]
    assemble(full, parts, lax.axis_index("front"), 2 * COLS)
    cut = -(unpack(kept[...] + came[...], 2 * COLS) + complex_dot(matrix[...], full[...]))
    width = COLS // 2
    low = pack(jnp.concatenate([cut[:, :width], cut[:, COLS : COLS + width]], axis=1))
    high = pack(jnp.concatenate([cut[:, width:COLS], cut[:, COLS + width :]], axis=1))
    first = lax.axis_index("leaf") < 2
    keep[...] = jnp.where(first, low, high) + sources[...]
    send[...] = jnp.where(first, high, low)


def root_rows(matrix, *refs):
    parts, (out, whole) = refs[:-2], refs[-2:]
    assemble(whole, parts, lax.axis_index("front"), COLS)
    out[...] = pack(complex_dot(matrix[...], whole[...]))


def halved(value, keep, send):
    rows = keep.shape[0]
    odd = (lax.axis_index("front") & 1) == 1
    low, high = value[:rows], value[rows:]
    keep[...] = jnp.where(odd, high, low)
    send[...] = jnp.where(odd, low, high)


def root_to_mid(matrix, mine, other, keep, send, x_root):
    first = lax.axis_index("leaf") < 2
    mine, other = unpack(mine[...], COLS), unpack(other[...], COLS)
    low, high = jnp.where(first, mine, other), jnp.where(first, other, mine)
    width = COLS // 2
    x = jnp.concatenate([low[:, :width], high[:, :width], low[:, width:], high[:, width:]], axis=1)
    x_root[...] = pack(x)
    halved(pack(complex_dot(matrix[...], x)), keep, send)


def root_to_leaf(matrix, mine, other, out, forward, adjoint):
    x = by_solve(lax.axis_index("leaf"), unpack(mine[...], 2 * COLS), unpack(other[...], 2 * COLS))
    out[...] = complex_dot(matrix[...], x)
    fields_of(x, forward, adjoint, ())


def sum_front(kept, sent, *others):
    fronts = lax.axis_size("front")
    (total,) = kernel(add, [kept.shape], kept, swap("front", sent, 1))
    hops = [1 << i for i in range(1, fronts.bit_length() - 1)]
    for hop, back in zip(hops, hops[::-1]):
        pairs = [(i, i ^ (back if i & 1 else hop)) for i in range(fronts)]
        (total,) = kernel(add, [kept.shape], total, lax.ppermute(total, "front", pairs))
    return [total, swap("front", after(total, *others), 1)]


def summed(pieces):
    mine, theirs = (ref[...] for ref in pieces)
    odd = (lax.axis_index("front") & 1) == 1
    return jnp.concatenate([jnp.where(odd, theirs, mine), jnp.where(odd, mine, theirs)], axis=0)


def mid_upper(matrix, y, *refs):
    tail, out = unpack(summed(refs[:2]), 2 * COLS), refs[2]
    out[...] = pack(complex_dot(matrix[...], y[...] - tail))


def mid_to_leaf(matrix, from_root, mine, other, keep, send, x_mid):
    x = by_solve(lax.axis_index("leaf"), unpack(mine[...], 2 * COLS), unpack(other[...], 2 * COLS))
    x_mid[...] = x
    halved(complex_dot(matrix[...], x) + from_root[...], keep, send)


def leaf_upper(matrix, y, *refs):
    forward, adjoint = refs[2:]
    fields_of(complex_dot(matrix[...], y[...] - summed(refs[:2])), forward, adjoint, ())


def mid_outputs(mine, other, forward, adjoint):
    parent = lax.axis_index("leaf") // 2
    fields_of(mine[...], forward, adjoint, (parent,))
    fields_of(other[...], forward, adjoint, (1 - parent,))


def after(x, *others):
    return lax.optimization_barrier((x, *others))[0]


def body(
    leaf_lower_inv,
    leaf_upper_inv,
    leaf_to_mid_lower,
    leaf_to_root_lower,
    leaf_to_mid_upper,
    leaf_to_root_upper,
    mid_lower_inv,
    mid_upper_inv,
    mid_to_root_lower,
    mid_to_root_upper,
    root_lower_inv,
    root_upper_inv,
    leaf_sources,
    mid_sources,
    root_sources,
    receiver_data,
    receiver_block,
    receiver_offset,
):
    groups, fronts = lax.axis_size("leaf"), lax.axis_size("front")
    n0, n1, n2 = leaf_sources.shape[1], mid_sources.shape[2], root_sources.shape[1]
    s0, s1, s2 = n0 * fronts, n1 * fronts, n2 * fronts
    slots, count = fronts * CAP, receiver_data.shape[1]
    dma = pltpu.SemaphoreType.DMA

    with jax.named_scope("right_hand_sides"):
        payload = kernel(
            functools.partial(pack_receivers, fronts, n0),
            [(slots, LANES), (slots, LANES), (2 * slots, LANES)],
            receiver_data,
            receiver_block.reshape(1, -1),
            receiver_offset.reshape(1, -1),
            scratch=[
                pltpu.VMEM((2, count, COLS), F32),
                pltpu.VMEM((1, count), jnp.int32),
                pltpu.VMEM((1, count), jnp.int32),
                dma((3,)),
            ],
            hbm=range(3),
            pinned=range(3),
        )
        own, far, near = payload
        came = swap("leaf", near, 1)
        (both,) = kernel(pass_on, [(2 * slots, LANES)], far, came)
        arrived = [own, came, swap("leaf", both, 2)]
        leaf_own, mid_own, root_own = kernel(
            load_sources,
            [(n0, LANES), (n1 // 2, LANES), (n2 // 4, LANES)],
            after(leaf_sources.transpose(0, 2, 1), *payload),
            mid_sources.transpose(0, 1, 3, 2),
            root_sources.transpose(0, 2, 1),
            scratch=[
                pltpu.VMEM((2, COLS, n0), F32),
                pltpu.VMEM((2, COLS, n1), F32),
                pltpu.VMEM((2, COLS, n2), F32),
                dma((3,)),
            ],
            hbm=range(3),
            pinned=range(3),
        )
        (message,) = kernel(
            pack_leaf, [(sum(message_rows(n0, groups * slots)), LANES)], leaf_own, *arrived
        )
    with jax.named_scope("leaf_lower"):
        messages, (ll, l2m) = gather_front(
            message,
            lambda x: load((after(leaf_lower_inv, *x), "leaf"), (leaf_to_mid_lower, "leaf"), pinned=True),
        )
        (y_leaf,) = kernel(
            functools.partial(leaf_lower, groups * slots),
            [(n0, LANES)],
            ll,
            *messages,
            scratch=[pltpu.VMEM((s0, LANES), F32), pltpu.VMEM((fronts, *message.shape), F32)],
        )
    with jax.named_scope("mid_lower"):
        parts, (l2r, ml) = gather_front(
            y_leaf,
            lambda x: load((after(leaf_to_root_lower, *x), "leaf"), (mid_lower_inv, "own"), pinned=True),
        )
        keep, send, y_full = kernel(
            leaf_to_mid,
            [(n1 // 2, LANES), (n1 // 2, LANES), (s0, LANES)],
            l2m,
            mid_own,
            *parts,
        )
        came = swap("leaf", send, 1)
        root_kept, root_sent = kernel(leaf_to_root, [(n2 // 2, LANES)] * 2, l2r, after(y_full, send))
        (cut_mid,) = kernel(add, [(n1 // 2, LANES)], after(keep, root_kept), came)
        root_came = swap("leaf", root_sent, 1)
        parts, (m2r,) = gather_front(
            cut_mid, lambda x: load((after(mid_to_root_lower, *x), "own"), pinned=True), (root_came,)
        )
        (y_mid,) = kernel(
            mid_lower,
            [(n1 // 2, LANES)],
            ml,
            *parts,
            scratch=[pltpu.VMEM((s1, 2 * COLS), F32)],
        )
    with jax.named_scope("root_cut"):
        parts, (rl,) = gather_front(y_mid, lambda x: load((after(root_lower_inv, *x), None)))
        keep, send, y_mid_full = kernel(
            mid_to_root,
            [(n2 // 4, LANES), (n2 // 4, LANES), (s1, 2 * COLS)],
            m2r,
            root_kept,
            root_came,
            root_own,
            *parts,
        )
        came = swap("leaf", send, 2)
        mu, l2r_up = load((after(mid_upper_inv, send), "own"), (leaf_to_root_upper, "leaf"))
        (cut_root,) = kernel(add, [(n2 // 4, LANES)], after(keep, mu), came)
    with jax.named_scope("root_solve"):
        parts, (ru,) = gather_front(cut_root, lambda x: load((after(root_upper_inv, *x), None)))
        (y_root,) = kernel(
            root_rows,
            [(n2 // 4, LANES)],
            rl,
            *parts,
            scratch=[pltpu.VMEM((s2, COLS), F32)],
        )
        parts, (m2r_up, l2m_up, lu) = gather_front(
            y_root,
            lambda x: load(
                (after(mid_to_root_upper, *x), "own"), (leaf_to_mid_upper, "leaf"), (leaf_upper_inv, "leaf")
            ),
        )
        (x_root,) = kernel(
            root_rows,
            [(n2 // 4, LANES)],
            ru,
            *parts,
            scratch=[pltpu.VMEM((s2, COLS), F32)],
        )
    with jax.named_scope("mid_upper"):
        keep, send, x_root = kernel(
            root_to_mid,
            [(s1 // 4, LANES)] * 2 + [(n2 // 2, LANES)],
            m2r_up,
            x_root,
            swap("leaf", x_root, 2),
        )
        pieces = sum_front(keep, send)
        (x_mid,) = kernel(mid_upper, [(n1 // 2, LANES)], mu, y_mid_full, *pieces)
        from_root, root_field, root_adjoint = kernel(
            root_to_leaf,
            [(s0, LANES), (2, COLS, n2), (2, COLS, n2)],
            l2r_up,
            x_root,
            swap("leaf", after(x_root, send), 1),
        )
    with jax.named_scope("leaf_upper"):
        keep, send, x_mid = kernel(
            mid_to_leaf,
            [(s0 // 2, LANES)] * 2 + [(n1, LANES)],
            l2m_up,
            from_root,
            x_mid,
            swap("leaf", x_mid, 1),
        )
        x_other = swap("leaf", x_mid, 2)
        mid_field, mid_adjoint = kernel(mid_outputs, [(2, 2, COLS, n1)] * 2, x_mid, x_other)
        pieces = sum_front(keep, send, mid_field)
        leaf_field, leaf_adjoint = kernel(leaf_upper, [(2, COLS, n0)] * 2, lu, y_full, *pieces)
    return tuple(
        jnp.swapaxes(x, -1, -2)
        for x in (leaf_field, mid_field, root_field, leaf_adjoint, mid_adjoint, root_adjoint)
    )


def solution(mesh):
    in_specs = (
        P(None, "leaf", "front", None),
        P(None, "leaf", "front", None),
        P(None, "leaf", "front", None),
        P(None, "leaf", "front", None),
        P(None, "leaf", None, "front"),
        P(None, "leaf", None, "front"),
        P(None, None, "front", None),
        P(None, None, "front", None),
        P(None, None, "front", None),
        P(None, None, None, "front"),
        P(None, "front", None),
        P(None, "front", None),
        P(None, ("leaf", "front"), None),
        P(None, None, "front", None),
        P(None, "front", None),
        P(None, ("leaf", "front"), None),
        P(("leaf", "front"), None),
        P(("leaf", "front")),
    )
    out_specs = (
        P(None, ("leaf", "front"), None),
        P(None, None, "front", None),
        P(None, "front", None),
        P(None, ("leaf", "front"), None),
        P(None, None, "front", None),
        P(None, "front", None),
    )
    return jax.shard_map(body, mesh=mesh, in_specs=in_specs, out_specs=out_specs, check_vma=False)
```

```python
import functools

import jax
import jax.numpy as jnp
from jax import lax
from jax.experimental import pallas as pl
from jax.experimental.pallas import tpu as pltpu
from jax.sharding import PartitionSpec as P

CAP = 2
CHUNKS = 4
LANES = 128
COLS = 32
F32 = jnp.float32
BF16 = jnp.bfloat16
VM = pl.BlockSpec(memory_space=pltpu.VMEM)
HB = pl.BlockSpec(memory_space=pltpu.HBM)


def split(x):
    high = x.astype(BF16)
    return high, (x - high.astype(F32)).astype(BF16)


def dot(a, b):
    return jnp.dot(a, b, preferred_element_type=F32)


def complex_dot(matrix, x):
    half = x.shape[1] // 2
    turned = jnp.concatenate([-x[:, half:], x[:, :half]], axis=1)
    both = jnp.concatenate([x, turned], axis=0)
    columns = jnp.concatenate(split(both), axis=1)
    product = dot(matrix, columns)
    rows, n = product.shape[0] // 2, x.shape[1]
    return (product[:rows, n:] + product[rows:, :n]) + product[:rows, :n]


def part_dot(matrix, at, x):
    depth, count, half = matrix.shape[1] // 2, x.shape[0], x.shape[1] // 2
    at = pl.multiple_of(at, LANES)
    turned = jnp.concatenate([-x[:, half:], x[:, :half]], axis=1)
    product = dot(matrix[:, pl.ds(at, count)], jnp.concatenate(split(x), axis=1))
    product += dot(matrix[:, pl.ds(depth + at, count)], jnp.concatenate(split(turned), axis=1))
    rows, n = product.shape[0] // 2, x.shape[1]
    return (product[:rows, n:] + product[rows:, :n]) + product[:rows, :n]


def pack(x):
    chunks = LANES // x.shape[1]
    rows = x.shape[0] // chunks
    return jnp.concatenate([x[rows * j : rows * j + rows] for j in range(chunks)], axis=1)


def unpack(x, width):
    return jnp.concatenate([x[:, at : at + width] for at in range(0, LANES, width)], axis=0)


def halves(x):
    c = COLS
    return (
        jnp.concatenate([x[:, :c], x[:, 2 * c : 3 * c]], axis=1),
        jnp.concatenate([x[:, c : 2 * c], x[:, 3 * c :]], axis=1),
    )


def joined(forward, adjoint):
    c = COLS
    return jnp.concatenate([forward[:, :c], adjoint[:, :c], forward[:, c:], adjoint[:, c:]], axis=1)


def own_first(group, forward, adjoint):
    even = (group & 1) == 0
    return jnp.where(even, forward, adjoint), jnp.where(even, adjoint, forward)


def by_solve(group, own, other):
    even = (group & 1) == 0
    return joined(jnp.where(even, own, other), jnp.where(even, other, own))


def assemble(where, parts, here, width=LANES):
    rows = parts[0].shape[0] * (LANES // width)
    for k, part in blocks_of(parts):
        start = pl.multiple_of((here ^ k) * rows, 8)
        where[pl.ds(start, rows), :] = part[...] if width == LANES else unpack(part[...], width)


def fields_of(x, forward, adjoint, where):
    y = x.T
    c = COLS
    forward[(0, *where)] = y[0:c]
    forward[(1, *where)] = y[2 * c : 3 * c]
    adjoint[(0, *where)] = y[c : 2 * c]
    adjoint[(1, *where)] = -y[3 * c :]


def swap(axis, x, k):
    size = lax.axis_size(axis)
    return lax.ppermute(x, axis, [(i, i ^ k) for i in range(size)])


def stack(*refs):
    at = 0
    for ref in refs[:-1]:
        refs[-1][at : at + ref.shape[0], :] = ref[...]
        at += ref.shape[0]


def gather_front(x, meanwhile=None, others=()):
    fronts = lax.axis_size("front")
    mine = [swap("front", x, k) for k in range(2, fronts, 2)]
    near, last = mine[:-1], mine[-1]
    own = swap("front", x, 1)
    (both,) = kernel(stack, [(len(near) * x.shape[0], LANES)], *near)
    extra = tuple(meanwhile((both, own))) if meanwhile else ()
    last = after(last, *extra, *others)
    return [x, own, last, *near[::-1], swap("front", last, 1), swap("front", both, 1)], extra


def blocks_of(parts):
    rows, fronts = parts[0].shape[0], 2 * len(parts) - 6
    evens = list(range(2, fronts, 2))
    yield 0, parts[0]
    yield 1, parts[1]
    for k, part in zip(evens[::-1], parts[2:-2]):
        yield k, part
    yield evens[-1] + 1, parts[-2]
    for i, k in enumerate(evens[:-1]):
        yield k + 1, parts[-1].at[rows * i : rows * i + rows, :]


def kernel(fn, outs, *args, scratch=(), vmem=8, work=0, hbm=(), pinned=()):
    outs = [o if isinstance(o[0], tuple) else (o, F32) for o in outs]
    return pl.pallas_call(
        fn,
        out_shape=[jax.ShapeDtypeStruct(*o) for o in outs],
        in_specs=[HB if i in hbm else VM for i in range(len(args))],
        out_specs=[VM] * len(outs),
        scratch_shapes=list(scratch),
        compiler_params=pltpu.CompilerParams(vmem_limit_bytes=vmem * 2**20),
        cost_estimate=pl.CostEstimate(flops=work, bytes_accessed=work // 700, transcendentals=0),
    )(*(pltpu.with_memory_space_constraint(a, pltpu.HBM) if i in pinned else a for i, a in enumerate(args)))


def chip_product(matrix, k, mine, other, width):
    here = lax.axis_index("front")
    odd = (here & 1) == 1
    if width < LANES:
        mine, other = unpack(mine, width), unpack(other, width)
    x = jnp.concatenate([jnp.where(odd, other, mine), jnp.where(odd, mine, other)], axis=0)
    return part_dot(matrix, ((here ^ k) // 2) * x.shape[0], x)


def first_products(width, matrix, mine, other, *refs):
    near, both, out = refs[:-2], refs[-2], refs[-1]
    rows = mine.shape[0]
    total = chip_product(matrix, 0, mine[...], other[...], width)
    for i, block in enumerate(near):
        second = both[rows * i : rows * i + rows, :]
        total += chip_product(matrix, 2 * i + 2, block[...], second, width)
    out[...] = total


def last_product(finish, width, count, matrix, *refs):
    parts, rest = refs[:count], refs[count:]
    if count == 3:
        known, mine, other = parts
        k = lax.axis_size("front") - 2
        finish(known[...] + chip_product(matrix, k, mine[...], other[...], width), *rest)
    else:
        assemble(rest[-1], parts, lax.axis_index("front"), width)
        finish(complex_dot(matrix[...], rest[-1][...]), *rest[:-1])


def gathered(finish, width, outs, matrix, parts, *args):
    rows = parts[0].shape[0] * (LANES // width)
    scratch = []
    if 2 * rows % LANES == 0:
        mine, other, last, *near, last_other, both = parts
        shape = (matrix.shape[0] // 2, width)
        (known,) = kernel(
            functools.partial(first_products, width), [shape], matrix, mine, other, *near[::-1], both
        )
        parts = [known, last, last_other]
    else:
        scratch = [pltpu.VMEM((rows * lax.axis_size("front"), width), F32)]
    return kernel(
        functools.partial(last_product, finish, width, len(parts)),
        outs,
        matrix,
        *parts,
        *args,
        scratch=scratch,
    )


def whole_of(width, *refs):
    assemble(refs[-1], refs[:-1], lax.axis_index("front"), width)


def half_product(theirs, width, matrix, y, piece):
    odd = (lax.axis_index("front") & 1) ^ theirs
    rows, total = piece.shape[0], None
    for chunk in range(LANES // width):
        at = chunk * 2 * rows + odd * rows
        x = y[pl.ds(pl.multiple_of(at, 8), rows), :] - piece[:, chunk * width : chunk * width + width]
        part = part_dot(matrix, at, x)
        total = part if total is None else total + part
    return total


def own_half(width, matrix, y, piece, out):
    out[...] = half_product(0, width, matrix, y, piece)


def load_matrices(picks, *refs):
    count = len(picks)
    sources, outs, buffers, sems = (
        refs[:count],
        refs[count : 2 * count],
        refs[2 * count : 3 * count],
        refs[3 * count],
    )
    parent = lax.axis_index("leaf") // 2
    copies = []
    for i, (src, pick) in enumerate(zip(sources, picks)):
        rows = buffers[i].shape[1]
        step = max(rows // CHUNKS, 16)
        for n, at in enumerate(range(0, rows, step)):
            span = pl.ds(at, step)
            view = src.at[:, span, :] if pick is None else src.at[:, parent if pick == "own" else 0, span, :]
            copy = pltpu.make_async_copy(view, buffers[i].at[:, span, :], sems.at[CHUNKS * i + n])
            copy.start()
            copies.append((i, at, step, copy))
    for i, at, step, copy in copies:
        copy.wait()
        rows, depth = buffers[i].shape[1:]
        for part in range(2):
            high, low = split(buffers[i][part, at : at + step, :])
            outs[i][at : at + step, part * depth : part * depth + depth] = high
            outs[i][rows + at : rows + at + step, part * depth : part * depth + depth] = low


def load(*matrices, pinned=False):
    shapes = [m.shape[-2:] for m, _ in matrices]
    size = sum(r * d for r, d in shapes)
    return kernel(
        functools.partial(load_matrices, tuple(pick for _, pick in matrices)),
        [((2 * r, 2 * d), BF16) for r, d in shapes],
        *[m for m, _ in matrices],
        scratch=[pltpu.VMEM((2, r, d), F32) for r, d in shapes]
        + [pltpu.SemaphoreType.DMA((CHUNKS * len(shapes),))],
        hbm=range(len(shapes)),
        pinned=range(len(shapes)) if pinned else (),
        vmem=4 + -(-size * 8 // 2**20),
        work=size * 1000,
    )


def pack_receivers(fronts, rows, data_hbm, block_hbm, offset_hbm, *refs):
    own, far, near = refs[:3]
    data, block, offset, sems = refs[3:]
    copies = [
        pltpu.make_async_copy(src, dst, sems.at[i])
        for i, (src, dst) in enumerate(((data_hbm, data), (block_hbm, block), (offset_hbm, offset)))
    ]
    for copy in copies:
        copy.start()
    for copy in copies:
        copy.wait()
    group = lax.axis_index("leaf")
    count = data.shape[1]
    slots = fronts * CAP
    down = lax.broadcasted_iota(jnp.int32, (count, count), 0)
    across = lax.broadcasted_iota(jnp.int32, (count, count), 1)
    eye = down == across
    block_row = block[...]
    block_col = jnp.sum(jnp.where(eye, block_row, 0), axis=1, keepdims=True)
    offset_col = jnp.sum(jnp.where(eye, offset[...], 0), axis=1, keepdims=True)
    same = (block_col == block_row) & (down < across)
    slot_row = block_row * CAP + jnp.sum(same.astype(jnp.int32), axis=0, keepdims=True)
    row_col = (block_col & (fronts - 1)) * rows + offset_col + 1
    lane = lax.broadcasted_iota(jnp.int32, (count, COLS), 1)
    index = jnp.where(lane == 0, row_col, 0).astype(F32)
    lines = jnp.concatenate([index, data[0], jnp.zeros((count, COLS), F32), -data[1]], axis=1)
    targets = [group, group ^ 2, group ^ 1, group ^ 3]
    place = lax.broadcasted_iota(jnp.int32, (slots, count), 0)
    pick = jnp.concatenate([place + target * slots == slot_row for target in targets], axis=0)
    picked = jnp.dot(
        pick.astype(F32), lines, precision=lax.Precision.HIGHEST, preferred_element_type=F32
    )
    own[...] = picked[:slots]
    far[...] = picked[slots : 2 * slots]
    near[...] = picked[2 * slots :]


def pass_on(far, came, out):
    rows = far.shape[0]
    out[0:rows, :] = far[...]
    out[rows:, :] = came[rows:, :]


def load_sources(leaf_hbm, mid_hbm, root_hbm, leaf_out, mid_out, root_out, leaf, mid, root, sems):
    group = lax.axis_index("leaf")
    copies = [
        pltpu.make_async_copy(src, dst, sems.at[i])
        for i, (src, dst) in enumerate(
            ((leaf_hbm, leaf), (mid_hbm.at[:, group // 2], mid), (root_hbm, root))
        )
    ]
    for copy in copies:
        copy.start()
    for copy in copies:
        copy.wait()
    forward = ((group & 1) == 0).astype(F32)
    real, imag = leaf[0].T, leaf[1].T
    zero = jnp.zeros_like(real)
    leaf_out[...] = jnp.concatenate([real, zero, imag, zero], axis=1)
    mid_out[...] = pack(jnp.concatenate([mid[0], mid[1]], axis=0).T) * forward
    width = COLS // 2
    low = jnp.concatenate([root[0, :width], root[1, :width]], axis=0)
    high = jnp.concatenate([root[0, width:], root[1, width:]], axis=0)
    root_out[...] = pack(jnp.where(group < 2, low, high).T) * forward


def message_rows(rows, slots):
    return max(rows, slots), 8 * -(-slots // (8 * LANES))


def pack_leaf(own, mine, near, far, out):
    lines = jnp.concatenate([mine[...], near[0 : mine.shape[0], :], far[...]], axis=0)
    slots = lines.shape[0]
    body, tail = message_rows(own.shape[0], slots)
    lane = lax.broadcasted_iota(jnp.int32, (slots, LANES), 1)
    data = jnp.where((lane // COLS) % 2 == 1, lines, 0.0)
    index = lines[:, 0:1]

    def padded(x):
        if x.shape[0] == body:
            return x
        return jnp.concatenate([x, jnp.zeros((body - x.shape[0], LANES), F32)], axis=0)

    out[0:body, :] = padded(own[...]) + padded(data)
    out[body:, :] = jnp.zeros((tail, LANES), F32)
    for at in range(0, slots, LANES):
        size = min(LANES, slots - at)
        eye = lax.broadcasted_iota(jnp.int32, (size, size), 0) == lax.broadcasted_iota(
            jnp.int32, (size, size), 1
        )
        line = jnp.sum(jnp.where(eye, index[at : at + size], 0.0), axis=0, keepdims=True)
        out[body + at // LANES : body + at // LANES + 1, 0:size] = line


def leaf_lower(slots, matrix, *refs):
    parts, (out, rhs, messages) = refs[:-3], refs[-3:]
    rows = out.shape[0]
    here = lax.axis_index("front")
    for k, part in blocks_of(parts):
        messages[here ^ k] = part[...]
    fronts = messages.shape[0]
    total = rows * fronts
    body, _ = message_rows(rows, slots)
    lane = lax.broadcasted_iota(jnp.int32, (slots, LANES), 1)
    taken = (lane // COLS) % 2 == 1
    own = lax.broadcasted_iota(jnp.int32, (rows, LANES), 1)
    own = (own // COLS) % 2 == 0
    for k in range(fronts):
        rhs[rows * k : rows * k + rows, :] = jnp.where(own, messages[k, 0:rows, :], 0.0)
    group = max(1, 512 // slots)
    for k in range(0, fronts, group):
        chosen = range(k, min(k + group, fronts))
        lines = jnp.concatenate([jnp.where(taken, messages[i, 0:slots, :], 0.0) for i in chosen], axis=0)
        index = jnp.concatenate(
            [
                messages[i, body + at // LANES : body + at // LANES + 1, 0 : min(LANES, slots - at)]
                for i in chosen
                for at in range(0, slots, LANES)
            ],
            axis=1,
        )
        row = lax.broadcasted_iota(jnp.int32, (total, index.shape[1]), 0)
        pick = (row + 1 == index.astype(jnp.int32)).astype(BF16)
        both = dot(pick, jnp.concatenate(split(lines), axis=1))
        rhs[...] += both[:, :LANES] + both[:, LANES:]
    out[...] = complex_dot(matrix[...], rhs[...])


def leaf_to_mid(value, sources, keep, send):
    mine, theirs = own_first(lax.axis_index("leaf"), *halves(value))
    keep[...] = sources[...] - pack(mine)
    send[...] = -pack(theirs)


def leaf_to_root(matrix, *refs):
    parts, (keep, send, full) = refs[:-3], refs[-3:]
    assemble(full, parts, lax.axis_index("front"))
    mine, theirs = own_first(lax.axis_index("leaf"), *halves(complex_dot(matrix[...], full[...])))
    keep[...], send[...] = pack(mine), pack(theirs)


def add(*refs):
    total = refs[0][...]
    for ref in refs[1:-1]:
        total = total + ref[...]
    refs[-1][...] = total


def packed_to(value, out):
    out[...] = pack(value)


def mid_to_root(value, kept, came, sources, keep, send):
    cut = -(unpack(kept[...] + came[...], 2 * COLS) + value)
    width = COLS // 2
    low = pack(jnp.concatenate([cut[:, :width], cut[:, COLS : COLS + width]], axis=1))
    high = pack(jnp.concatenate([cut[:, width:COLS], cut[:, COLS + width :]], axis=1))
    first = lax.axis_index("leaf") < 2
    keep[...] = jnp.where(first, low, high) + sources[...]
    send[...] = jnp.where(first, high, low)


def halved(value, keep, send):
    rows = keep.shape[0]
    odd = (lax.axis_index("front") & 1) == 1
    low, high = value[:rows], value[rows:]
    keep[...] = jnp.where(odd, high, low)
    send[...] = jnp.where(odd, low, high)


def root_to_mid(matrix, mine, other, keep, send, x_root):
    first = lax.axis_index("leaf") < 2
    mine, other = unpack(mine[...], COLS), unpack(other[...], COLS)
    low, high = jnp.where(first, mine, other), jnp.where(first, other, mine)
    width = COLS // 2
    x = jnp.concatenate([low[:, :width], high[:, :width], low[:, width:], high[:, width:]], axis=1)
    x_root[...] = pack(x)
    halved(pack(complex_dot(matrix[...], x)), keep, send)


def root_to_leaf(matrix, mine, other, out, forward, adjoint):
    x = by_solve(lax.axis_index("leaf"), unpack(mine[...], 2 * COLS), unpack(other[...], 2 * COLS))
    out[...] = complex_dot(matrix[...], x)
    fields_of(x, forward, adjoint, ())


def sum_front(kept, sent, *others):
    fronts = lax.axis_size("front")
    (total,) = kernel(add, [kept.shape], kept, swap("front", sent, 1))
    hops = [1 << i for i in range(1, fronts.bit_length() - 1)]
    for hop, back in zip(hops, hops[::-1]):
        pairs = [(i, i ^ (back if i & 1 else hop)) for i in range(fronts)]
        (total,) = kernel(add, [kept.shape], total, lax.ppermute(total, "front", pairs))
    return [total, swap("front", after(total, *others), 1)]


def mid_upper(matrix, y, piece, known, out):
    out[...] = pack(known[...] + half_product(1, 2 * COLS, matrix, y, piece))


def mid_to_leaf(matrix, from_root, mine, other, keep, send, x_mid):
    x = by_solve(lax.axis_index("leaf"), unpack(mine[...], 2 * COLS), unpack(other[...], 2 * COLS))
    x_mid[...] = x
    halved(complex_dot(matrix[...], x) + from_root[...], keep, send)


def leaf_upper(matrix, y, piece, known, forward, adjoint):
    fields_of(known[...] + half_product(1, LANES, matrix, y, piece), forward, adjoint, ())


def mid_outputs(mine, other, forward, adjoint):
    parent = lax.axis_index("leaf") // 2
    fields_of(mine[...], forward, adjoint, (parent,))
    fields_of(other[...], forward, adjoint, (1 - parent,))


def after(x, *others):
    return lax.optimization_barrier((x, *others))[0]


def body(
    leaf_lower_inv,
    leaf_upper_inv,
    leaf_to_mid_lower,
    leaf_to_root_lower,
    leaf_to_mid_upper,
    leaf_to_root_upper,
    mid_lower_inv,
    mid_upper_inv,
    mid_to_root_lower,
    mid_to_root_upper,
    root_lower_inv,
    root_upper_inv,
    leaf_sources,
    mid_sources,
    root_sources,
    receiver_data,
    receiver_block,
    receiver_offset,
):
    groups, fronts = lax.axis_size("leaf"), lax.axis_size("front")
    n0, n1, n2 = leaf_sources.shape[1], mid_sources.shape[2], root_sources.shape[1]
    s0, s1, s2 = n0 * fronts, n1 * fronts, n2 * fronts
    slots, count = fronts * CAP, receiver_data.shape[1]
    dma = pltpu.SemaphoreType.DMA

    with jax.named_scope("right_hand_sides"):
        payload = kernel(
            functools.partial(pack_receivers, fronts, n0),
            [(slots, LANES), (slots, LANES), (2 * slots, LANES)],
            receiver_data,
            receiver_block.reshape(1, -1),
            receiver_offset.reshape(1, -1),
            scratch=[
                pltpu.VMEM((2, count, COLS), F32),
                pltpu.VMEM((1, count), jnp.int32),
                pltpu.VMEM((1, count), jnp.int32),
                dma((3,)),
            ],
            hbm=range(3),
            pinned=range(3),
        )
        own, far, near = payload
        came = swap("leaf", near, 1)
        (both,) = kernel(pass_on, [(2 * slots, LANES)], far, came)
        arrived = [own, came, swap("leaf", both, 2)]
        leaf_own, mid_own, root_own = kernel(
            load_sources,
            [(n0, LANES), (n1 // 2, LANES), (n2 // 4, LANES)],
            after(leaf_sources.transpose(0, 2, 1), *payload),
            mid_sources.transpose(0, 1, 3, 2),
            root_sources.transpose(0, 2, 1),
            scratch=[
                pltpu.VMEM((2, COLS, n0), F32),
                pltpu.VMEM((2, COLS, n1), F32),
                pltpu.VMEM((2, COLS, n2), F32),
                dma((3,)),
            ],
            hbm=range(3),
            pinned=range(3),
        )
        (message,) = kernel(
            pack_leaf, [(sum(message_rows(n0, groups * slots)), LANES)], leaf_own, *arrived
        )
    with jax.named_scope("leaf_lower"):
        messages, (ll, l2m) = gather_front(
            message,
            lambda x: load((after(leaf_lower_inv, *x), "leaf"), (leaf_to_mid_lower, "leaf"), pinned=True),
        )
        (y_leaf,) = kernel(
            functools.partial(leaf_lower, groups * slots),
            [(n0, LANES)],
            ll,
            *messages,
            scratch=[pltpu.VMEM((s0, LANES), F32), pltpu.VMEM((fronts, *message.shape), F32)],
        )
    with jax.named_scope("mid_lower"):
        parts, (l2r, ml) = gather_front(
            y_leaf,
            lambda x: load((after(leaf_to_root_lower, *x), "leaf"), (mid_lower_inv, "own"), pinned=True),
        )
        keep, send = gathered(leaf_to_mid, LANES, [(n1 // 2, LANES)] * 2, l2m, parts, mid_own)
        came = swap("leaf", send, 1)
        root_kept, root_sent, y_full = kernel(
            leaf_to_root, [(n2 // 2, LANES)] * 2 + [(s0, LANES)], l2r, after(parts[0], send), *parts[1:]
        )
        (cut_mid,) = kernel(add, [(n1 // 2, LANES)], after(keep, root_kept), came)
        root_came = swap("leaf", root_sent, 1)
        parts, (m2r,) = gather_front(
            cut_mid, lambda x: load((after(mid_to_root_lower, *x), "own"), pinned=True), (root_came,)
        )
        (y_mid,) = gathered(packed_to, 2 * COLS, [(n1 // 2, LANES)], ml, parts)
    with jax.named_scope("root_cut"):
        parts, (rl,) = gather_front(y_mid, lambda x: load((after(root_lower_inv, *x), None)))
        keep, send = gathered(
            mid_to_root, 2 * COLS, [(n2 // 4, LANES)] * 2, m2r, parts, root_kept, root_came, root_own
        )
        came = swap("leaf", send, 2)
        mu, l2r_up = load((after(mid_upper_inv, send), "own"), (leaf_to_root_upper, "leaf"))
        (y_mid_full,) = kernel(
            functools.partial(whole_of, 2 * COLS), [(s1, 2 * COLS)], after(parts[0], send), *parts[1:]
        )
        (cut_root,) = kernel(add, [(n2 // 4, LANES)], after(keep, mu, y_mid_full), came)
    with jax.named_scope("root_solve"):
        parts, (ru,) = gather_front(cut_root, lambda x: load((after(root_upper_inv, *x), None)))
        (y_root,) = gathered(packed_to, COLS, [(n2 // 4, LANES)], rl, parts)
        parts, (m2r_up, l2m_up, lu) = gather_front(
            y_root,
            lambda x: load(
                (after(mid_to_root_upper, *x), "own"), (leaf_to_mid_upper, "leaf"), (leaf_upper_inv, "leaf")
            ),
        )
        (x_root,) = gathered(packed_to, COLS, [(n2 // 4, LANES)], ru, parts)
    with jax.named_scope("mid_upper"):
        keep, send, x_root = kernel(
            root_to_mid,
            [(s1 // 4, LANES)] * 2 + [(n2 // 2, LANES)],
            m2r_up,
            x_root,
            swap("leaf", x_root, 2),
        )
        mine, theirs = sum_front(keep, send)
        (known,) = kernel(functools.partial(own_half, 2 * COLS), [(n1, 2 * COLS)], mu, y_mid_full, mine)
        (x_mid,) = kernel(mid_upper, [(n1 // 2, LANES)], mu, y_mid_full, theirs, known)
        from_root, root_field, root_adjoint = kernel(
            root_to_leaf,
            [(s0, LANES), (2, COLS, n2), (2, COLS, n2)],
            l2r_up,
            x_root,
            swap("leaf", after(x_root, send), 1),
        )
    with jax.named_scope("leaf_upper"):
        keep, send, x_mid = kernel(
            mid_to_leaf,
            [(s0 // 2, LANES)] * 2 + [(n1, LANES)],
            l2m_up,
            from_root,
            x_mid,
            swap("leaf", x_mid, 1),
        )
        x_other = swap("leaf", x_mid, 2)
        mid_field, mid_adjoint = kernel(mid_outputs, [(2, 2, COLS, n1)] * 2, x_mid, x_other)
        mine, theirs = sum_front(keep, send, x_other)
        (known,) = kernel(functools.partial(own_half, LANES), [(n0, LANES)], lu, y_full, mine)
        leaf_field, leaf_adjoint = kernel(
            leaf_upper, [(2, COLS, n0)] * 2, lu, y_full, theirs, after(known, mid_field)
        )
    return tuple(
        jnp.swapaxes(x, -1, -2)
        for x in (leaf_field, mid_field, root_field, leaf_adjoint, mid_adjoint, root_adjoint)
    )


def solution(mesh):
    in_specs = (
        P(None, "leaf", "front", None),
        P(None, "leaf", "front", None),
        P(None, "leaf", "front", None),
        P(None, "leaf", "front", None),
        P(None, "leaf", None, "front"),
        P(None, "leaf", None, "front"),
        P(None, None, "front", None),
        P(None, None, "front", None),
        P(None, None, "front", None),
        P(None, None, None, "front"),
        P(None, "front", None),
        P(None, "front", None),
        P(None, ("leaf", "front"), None),
        P(None, None, "front", None),
        P(None, "front", None),
        P(None, ("leaf", "front"), None),
        P(("leaf", "front"), None),
        P(("leaf", "front")),
    )
    out_specs = (
        P(None, ("leaf", "front"), None),
        P(None, None, "front", None),
        P(None, "front", None),
        P(None, ("leaf", "front"), None),
        P(None, None, "front", None),
        P(None, "front", None),
    )
    return jax.shard_map(body, mesh=mesh, in_specs=in_specs, out_specs=out_specs, check_vma=False)
```

```python
import functools

import jax
import jax.numpy as jnp
from jax import lax
from jax.experimental import pallas as pl
from jax.experimental.pallas import tpu as pltpu
from jax.sharding import PartitionSpec as P

CAP = 2
CHUNKS = 4
LANES = 128
COLS = 32
F32 = jnp.float32
BF16 = jnp.bfloat16
VM = pl.BlockSpec(memory_space=pltpu.VMEM)
HB = pl.BlockSpec(memory_space=pltpu.HBM)


def split(x):
    high = x.astype(BF16)
    return high, (x - high.astype(F32)).astype(BF16)


def dot(a, b):
    return jnp.dot(a, b, preferred_element_type=F32)


def complex_dot(matrix, x):
    half = x.shape[1] // 2
    turned = jnp.concatenate([-x[:, half:], x[:, :half]], axis=1)
    both = jnp.concatenate([x, turned], axis=0)
    columns = jnp.concatenate(split(both), axis=1)
    product = dot(matrix, columns)
    rows, n = product.shape[0] // 2, x.shape[1]
    return (product[:rows, n:] + product[rows:, :n]) + product[:rows, :n]


def combined(product):
    rows, n = product.shape[0] // 2, product.shape[1] // 2
    return (product[:rows, n:] + product[rows:, :n]) + product[:rows, :n]


def turn(x, width):
    half = width // 2
    lane = lax.broadcasted_iota(jnp.int32, x.shape, 1) % width
    return jnp.where(lane < half, -pltpu.roll(x, LANES - half, 1), pltpu.roll(x, half, 1))


def spread(x, width):
    high, low = split(x)
    return jnp.concatenate(
        [
            jnp.concatenate([high[:, at : at + width], low[:, at : at + width]], axis=1)
            for at in range(0, LANES, width)
        ],
        axis=0,
    )


def part_dot(matrix, at, blocks, width):
    depth = matrix.shape[1] // 2
    columns = jnp.concatenate([spread(x, width) for x in blocks], axis=0)
    turned = jnp.concatenate([spread(turn(x, width), width) for x in blocks], axis=0)
    count, at = columns.shape[0], pl.multiple_of(at, LANES)
    return dot(matrix[:, pl.ds(at, count)], columns) + dot(matrix[:, pl.ds(depth + at, count)], turned)


def pack(x):
    chunks = LANES // x.shape[1]
    rows = x.shape[0] // chunks
    return jnp.concatenate([x[rows * j : rows * j + rows] for j in range(chunks)], axis=1)


def unpack(x, width):
    return jnp.concatenate([x[:, at : at + width] for at in range(0, LANES, width)], axis=0)


def halves(x):
    c = COLS
    return (
        jnp.concatenate([x[:, :c], x[:, 2 * c : 3 * c]], axis=1),
        jnp.concatenate([x[:, c : 2 * c], x[:, 3 * c :]], axis=1),
    )


def joined(forward, adjoint):
    c = COLS
    return jnp.concatenate([forward[:, :c], adjoint[:, :c], forward[:, c:], adjoint[:, c:]], axis=1)


def own_first(group, forward, adjoint):
    even = (group & 1) == 0
    return jnp.where(even, forward, adjoint), jnp.where(even, adjoint, forward)


def by_solve(group, own, other):
    even = (group & 1) == 0
    return joined(jnp.where(even, own, other), jnp.where(even, other, own))


def assemble(where, parts, here, width=LANES):
    rows = parts[0].shape[0] * (LANES // width)
    for k, part in blocks_of(parts):
        start = pl.multiple_of((here ^ k) * rows, 8)
        where[pl.ds(start, rows), :] = part[...] if width == LANES else unpack(part[...], width)


def fields_of(x, forward, adjoint, where):
    y = x.T
    c = COLS
    forward[(0, *where)] = y[0:c]
    forward[(1, *where)] = y[2 * c : 3 * c]
    adjoint[(0, *where)] = y[c : 2 * c]
    adjoint[(1, *where)] = -y[3 * c :]


def swap(axis, x, k):
    size = lax.axis_size(axis)
    return lax.ppermute(x, axis, [(i, i ^ k) for i in range(size)])


def stack(*refs):
    at = 0
    for ref in refs[:-1]:
        refs[-1][at : at + ref.shape[0], :] = ref[...]
        at += ref.shape[0]


def gather_front(x, meanwhile=None, others=()):
    fronts = lax.axis_size("front")
    mine = [swap("front", x, k) for k in range(2, fronts, 2)]
    near, last = mine[:-1], mine[-1]
    own = swap("front", x, 1)
    (both,) = kernel(stack, [(len(near) * x.shape[0], LANES)], *near)
    extra = tuple(meanwhile((both, own))) if meanwhile else ()
    last = after(last, *extra, *others)
    return [x, own, last, *near[::-1], swap("front", last, 1), swap("front", both, 1)], extra


def blocks_of(parts):
    rows, fronts = parts[0].shape[0], 2 * len(parts) - 6
    evens = list(range(2, fronts, 2))
    yield 0, parts[0]
    yield 1, parts[1]
    for k, part in zip(evens[::-1], parts[2:-2]):
        yield k, part
    yield evens[-1] + 1, parts[-2]
    for i, k in enumerate(evens[:-1]):
        yield k + 1, parts[-1].at[rows * i : rows * i + rows, :]


def kernel(fn, outs, *args, scratch=(), vmem=8, work=0, hbm=(), pinned=()):
    outs = [o if isinstance(o[0], tuple) else (o, F32) for o in outs]
    return pl.pallas_call(
        fn,
        out_shape=[jax.ShapeDtypeStruct(*o) for o in outs],
        in_specs=[HB if i in hbm else VM for i in range(len(args))],
        out_specs=[VM] * len(outs),
        scratch_shapes=list(scratch),
        compiler_params=pltpu.CompilerParams(vmem_limit_bytes=vmem * 2**20),
        cost_estimate=pl.CostEstimate(flops=work, bytes_accessed=work // 700, transcendentals=0),
    )(*(pltpu.with_memory_space_constraint(a, pltpu.HBM) if i in pinned else a for i, a in enumerate(args)))


def chip_product(matrix, k, mine, other, width):
    here = lax.axis_index("front")
    odd = (here & 1) == 1
    blocks = [jnp.where(odd, other, mine), jnp.where(odd, mine, other)]
    return part_dot(matrix, ((here ^ k) // 2) * (2 * mine.shape[0] * (LANES // width)), blocks, width)


def first_products(width, matrix, mine, other, *refs):
    near, both, out = refs[:-2], refs[-2], refs[-1]
    rows = mine.shape[0]
    total = chip_product(matrix, 0, mine[...], other[...], width)
    for i, block in enumerate(near):
        second = both[rows * i : rows * i + rows, :]
        total += chip_product(matrix, 2 * i + 2, block[...], second, width)
    out[...] = total


def last_product(finish, width, count, matrix, *refs):
    parts, rest = refs[:count], refs[count:]
    if count == 3:
        known, mine, other = parts
        k = lax.axis_size("front") - 2
        finish(combined(known[...] + chip_product(matrix, k, mine[...], other[...], width)), *rest)
    else:
        assemble(rest[-1], parts, lax.axis_index("front"), width)
        finish(complex_dot(matrix[...], rest[-1][...]), *rest[:-1])


def gathered(finish, width, outs, matrix, parts, *args):
    rows = parts[0].shape[0] * (LANES // width)
    scratch = []
    if 2 * rows % LANES == 0:
        mine, other, last, *near, last_other, both = parts
        shape = (matrix.shape[0], 2 * width)
        (known,) = kernel(
            functools.partial(first_products, width), [shape], matrix, mine, other, *near[::-1], both
        )
        parts = [known, last, last_other]
    else:
        scratch = [pltpu.VMEM((rows * lax.axis_size("front"), width), F32)]
    return kernel(
        functools.partial(last_product, finish, width, len(parts)),
        outs,
        matrix,
        *parts,
        *args,
        scratch=scratch,
    )


def whole_of(width, *refs):
    assemble(refs[-1], refs[:-1], lax.axis_index("front"), width)


def half_product(theirs, width, matrix, y, piece):
    odd = (lax.axis_index("front") & 1) ^ theirs
    rows, chunks = piece.shape[0], LANES // width
    starts = [chunk * 2 * rows + odd * rows for chunk in range(chunks)]
    own = [y[pl.ds(pl.multiple_of(at, 8), rows), :] for at in starts]
    x = jnp.concatenate(own, axis=1) - piece[...]
    if chunks == 1:
        return part_dot(matrix, starts[0], [x], width)
    total, depth = None, matrix.shape[1] // 2
    columns, turned = spread(x, width), spread(turn(x, width), width)
    for chunk, at in enumerate(starts):
        at, span = pl.multiple_of(at, LANES), slice(rows * chunk, rows * chunk + rows)
        part = dot(matrix[:, pl.ds(at, rows)], columns[span])
        part += dot(matrix[:, pl.ds(depth + at, rows)], turned[span])
        total = part if total is None else total + part
    return total


def own_half(width, matrix, y, piece, out):
    out[...] = half_product(0, width, matrix, y, piece)


def load_matrices(picks, *refs):
    count = len(picks)
    sources, outs, buffers, sems = (
        refs[:count],
        refs[count : 2 * count],
        refs[2 * count : 3 * count],
        refs[3 * count],
    )
    parent = lax.axis_index("leaf") // 2
    copies = []
    for i, (src, pick) in enumerate(zip(sources, picks)):
        rows = buffers[i].shape[1]
        step = max(rows // CHUNKS, 16)
        for n, at in enumerate(range(0, rows, step)):
            span = pl.ds(at, step)
            view = src.at[:, span, :] if pick is None else src.at[:, parent if pick == "own" else 0, span, :]
            copy = pltpu.make_async_copy(view, buffers[i].at[:, span, :], sems.at[CHUNKS * i + n])
            copy.start()
            copies.append((i, at, step, copy))
    for i, at, step, copy in copies:
        copy.wait()
        rows, depth = buffers[i].shape[1:]
        for part in range(2):
            high, low = split(buffers[i][part, at : at + step, :])
            outs[i][at : at + step, part * depth : part * depth + depth] = high
            outs[i][rows + at : rows + at + step, part * depth : part * depth + depth] = low


def load(*matrices, pinned=False):
    shapes = [m.shape[-2:] for m, _ in matrices]
    size = sum(r * d for r, d in shapes)
    return kernel(
        functools.partial(load_matrices, tuple(pick for _, pick in matrices)),
        [((2 * r, 2 * d), BF16) for r, d in shapes],
        *[m for m, _ in matrices],
        scratch=[pltpu.VMEM((2, r, d), F32) for r, d in shapes]
        + [pltpu.SemaphoreType.DMA((CHUNKS * len(shapes),))],
        hbm=range(len(shapes)),
        pinned=range(len(shapes)) if pinned else (),
        vmem=4 + -(-size * 8 // 2**20),
        work=size * 1000,
    )


def pack_receivers(fronts, rows, data_hbm, block_hbm, offset_hbm, *refs):
    own, far, near = refs[:3]
    data, block, offset, sems = refs[3:]
    copies = [
        pltpu.make_async_copy(src, dst, sems.at[i])
        for i, (src, dst) in enumerate(((data_hbm, data), (block_hbm, block), (offset_hbm, offset)))
    ]
    for copy in copies:
        copy.start()
    for copy in copies:
        copy.wait()
    group = lax.axis_index("leaf")
    count = data.shape[1]
    slots = fronts * CAP
    down = lax.broadcasted_iota(jnp.int32, (count, count), 0)
    across = lax.broadcasted_iota(jnp.int32, (count, count), 1)
    eye = down == across
    block_row = block[...]
    block_col = jnp.sum(jnp.where(eye, block_row, 0), axis=1, keepdims=True)
    offset_col = jnp.sum(jnp.where(eye, offset[...], 0), axis=1, keepdims=True)
    same = (block_col == block_row) & (down < across)
    slot_row = block_row * CAP + jnp.sum(same.astype(jnp.int32), axis=0, keepdims=True)
    row_col = (block_col & (fronts - 1)) * rows + offset_col + 1
    lane = lax.broadcasted_iota(jnp.int32, (count, COLS), 1)
    index = jnp.where(lane == 0, row_col, 0).astype(F32)
    lines = jnp.concatenate([index, data[0], jnp.zeros((count, COLS), F32), -data[1]], axis=1)
    targets = [group, group ^ 2, group ^ 1, group ^ 3]
    place = lax.broadcasted_iota(jnp.int32, (slots, count), 0)
    pick = jnp.concatenate([place + target * slots == slot_row for target in targets], axis=0)
    picked = jnp.dot(
        pick.astype(F32), lines, precision=lax.Precision.HIGHEST, preferred_element_type=F32
    )
    own[...] = picked[:slots]
    far[...] = picked[slots : 2 * slots]
    near[...] = picked[2 * slots :]


def pass_on(far, came, out):
    rows = far.shape[0]
    out[0:rows, :] = far[...]
    out[rows:, :] = came[rows:, :]


def load_sources(leaf_hbm, mid_hbm, root_hbm, leaf_out, mid_out, root_out, leaf, mid, root, sems):
    group = lax.axis_index("leaf")
    copies = [
        pltpu.make_async_copy(src, dst, sems.at[i])
        for i, (src, dst) in enumerate(
            ((leaf_hbm, leaf), (mid_hbm.at[:, group // 2], mid), (root_hbm, root))
        )
    ]
    for copy in copies:
        copy.start()
    for copy in copies:
        copy.wait()
    forward = ((group & 1) == 0).astype(F32)
    real, imag = leaf[0].T, leaf[1].T
    zero = jnp.zeros_like(real)
    leaf_out[...] = jnp.concatenate([real, zero, imag, zero], axis=1)
    mid_out[...] = pack(jnp.concatenate([mid[0], mid[1]], axis=0).T) * forward
    width = COLS // 2
    low = jnp.concatenate([root[0, :width], root[1, :width]], axis=0)
    high = jnp.concatenate([root[0, width:], root[1, width:]], axis=0)
    root_out[...] = pack(jnp.where(group < 2, low, high).T) * forward


def message_rows(rows, slots):
    return max(rows, slots), 8 * -(-slots // (8 * LANES))


def pack_leaf(own, mine, near, far, out):
    lines = jnp.concatenate([mine[...], near[0 : mine.shape[0], :], far[...]], axis=0)
    slots = lines.shape[0]
    body, tail = message_rows(own.shape[0], slots)
    lane = lax.broadcasted_iota(jnp.int32, (slots, LANES), 1)
    data = jnp.where((lane // COLS) % 2 == 1, lines, 0.0)
    index = lines[:, 0:1]

    def padded(x):
        if x.shape[0] == body:
            return x
        return jnp.concatenate([x, jnp.zeros((body - x.shape[0], LANES), F32)], axis=0)

    out[0:body, :] = padded(own[...]) + padded(data)
    out[body:, :] = jnp.zeros((tail, LANES), F32)
    for at in range(0, slots, LANES):
        size = min(LANES, slots - at)
        eye = lax.broadcasted_iota(jnp.int32, (size, size), 0) == lax.broadcasted_iota(
            jnp.int32, (size, size), 1
        )
        line = jnp.sum(jnp.where(eye, index[at : at + size], 0.0), axis=0, keepdims=True)
        out[body + at // LANES : body + at // LANES + 1, 0:size] = line


def leaf_lower(slots, matrix, *refs):
    parts, (out, rhs, messages) = refs[:-3], refs[-3:]
    rows = out.shape[0]
    here = lax.axis_index("front")
    for k, part in blocks_of(parts):
        messages[here ^ k] = part[...]
    fronts = messages.shape[0]
    total = rows * fronts
    body, _ = message_rows(rows, slots)
    lane = lax.broadcasted_iota(jnp.int32, (slots, LANES), 1)
    taken = (lane // COLS) % 2 == 1
    own = lax.broadcasted_iota(jnp.int32, (rows, LANES), 1)
    own = (own // COLS) % 2 == 0
    for k in range(fronts):
        rhs[rows * k : rows * k + rows, :] = jnp.where(own, messages[k, 0:rows, :], 0.0)
    group = max(1, 512 // slots)
    for k in range(0, fronts, group):
        chosen = range(k, min(k + group, fronts))
        lines = jnp.concatenate([jnp.where(taken, messages[i, 0:slots, :], 0.0) for i in chosen], axis=0)
        index = jnp.concatenate(
            [
                messages[i, body + at // LANES : body + at // LANES + 1, 0 : min(LANES, slots - at)]
                for i in chosen
                for at in range(0, slots, LANES)
            ],
            axis=1,
        )
        row = lax.broadcasted_iota(jnp.int32, (total, index.shape[1]), 0)
        pick = (row + 1 == index.astype(jnp.int32)).astype(BF16)
        both = dot(pick, jnp.concatenate(split(lines), axis=1))
        rhs[...] += both[:, :LANES] + both[:, LANES:]
    out[...] = complex_dot(matrix[...], rhs[...])


def leaf_to_mid(value, sources, keep, send):
    mine, theirs = own_first(lax.axis_index("leaf"), *halves(value))
    keep[...] = sources[...] - pack(mine)
    send[...] = -pack(theirs)


def leaf_to_root(matrix, *refs):
    parts, (keep, send, full) = refs[:-3], refs[-3:]
    assemble(full, parts, lax.axis_index("front"))
    mine, theirs = own_first(lax.axis_index("leaf"), *halves(complex_dot(matrix[...], full[...])))
    keep[...], send[...] = pack(mine), pack(theirs)


def add(*refs):
    total = refs[0][...]
    for ref in refs[1:-1]:
        total = total + ref[...]
    refs[-1][...] = total


def packed_to(value, out):
    out[...] = pack(value)


def mid_to_root(value, kept, came, sources, keep, send):
    cut = -(unpack(kept[...] + came[...], 2 * COLS) + value)
    width = COLS // 2
    low = pack(jnp.concatenate([cut[:, :width], cut[:, COLS : COLS + width]], axis=1))
    high = pack(jnp.concatenate([cut[:, width:COLS], cut[:, COLS + width :]], axis=1))
    first = lax.axis_index("leaf") < 2
    keep[...] = jnp.where(first, low, high) + sources[...]
    send[...] = jnp.where(first, high, low)


def halved(value, keep, send):
    rows = keep.shape[0]
    odd = (lax.axis_index("front") & 1) == 1
    low, high = value[:rows], value[rows:]
    keep[...] = jnp.where(odd, high, low)
    send[...] = jnp.where(odd, low, high)


def root_to_mid(matrix, mine, other, keep, send, x_root):
    first = lax.axis_index("leaf") < 2
    mine, other = unpack(mine[...], COLS), unpack(other[...], COLS)
    low, high = jnp.where(first, mine, other), jnp.where(first, other, mine)
    width = COLS // 2
    x = jnp.concatenate([low[:, :width], high[:, :width], low[:, width:], high[:, width:]], axis=1)
    x_root[...] = pack(x)
    halved(pack(complex_dot(matrix[...], x)), keep, send)


def root_to_leaf(matrix, mine, other, out, forward, adjoint):
    x = by_solve(lax.axis_index("leaf"), unpack(mine[...], 2 * COLS), unpack(other[...], 2 * COLS))
    out[...] = complex_dot(matrix[...], x)
    fields_of(x, forward, adjoint, ())


def sum_front(kept, sent, *others):
    fronts = lax.axis_size("front")
    (total,) = kernel(add, [kept.shape], kept, swap("front", sent, 1))
    hops = [1 << i for i in range(1, fronts.bit_length() - 1)]
    for hop, back in zip(hops, hops[::-1]):
        pairs = [(i, i ^ (back if i & 1 else hop)) for i in range(fronts)]
        (total,) = kernel(add, [kept.shape], total, lax.ppermute(total, "front", pairs))
    return [total, swap("front", after(total, *others), 1)]


def mid_upper(matrix, y, piece, known, out):
    out[...] = pack(combined(known[...] + half_product(1, 2 * COLS, matrix, y, piece)))


def mid_to_leaf(matrix, from_root, mine, other, keep, send, x_mid):
    x = by_solve(lax.axis_index("leaf"), unpack(mine[...], 2 * COLS), unpack(other[...], 2 * COLS))
    x_mid[...] = x
    halved(complex_dot(matrix[...], x) + from_root[...], keep, send)


def leaf_upper(matrix, y, piece, known, forward, adjoint):
    fields_of(combined(known[...] + half_product(1, LANES, matrix, y, piece)), forward, adjoint, ())


def mid_outputs(mine, other, forward, adjoint):
    parent = lax.axis_index("leaf") // 2
    fields_of(mine[...], forward, adjoint, (parent,))
    fields_of(other[...], forward, adjoint, (1 - parent,))


def after(x, *others):
    return lax.optimization_barrier((x, *others))[0]


def body(
    leaf_lower_inv,
    leaf_upper_inv,
    leaf_to_mid_lower,
    leaf_to_root_lower,
    leaf_to_mid_upper,
    leaf_to_root_upper,
    mid_lower_inv,
    mid_upper_inv,
    mid_to_root_lower,
    mid_to_root_upper,
    root_lower_inv,
    root_upper_inv,
    leaf_sources,
    mid_sources,
    root_sources,
    receiver_data,
    receiver_block,
    receiver_offset,
):
    groups, fronts = lax.axis_size("leaf"), lax.axis_size("front")
    n0, n1, n2 = leaf_sources.shape[1], mid_sources.shape[2], root_sources.shape[1]
    s0, s1, s2 = n0 * fronts, n1 * fronts, n2 * fronts
    slots, count = fronts * CAP, receiver_data.shape[1]
    dma = pltpu.SemaphoreType.DMA

    with jax.named_scope("right_hand_sides"):
        payload = kernel(
            functools.partial(pack_receivers, fronts, n0),
            [(slots, LANES), (slots, LANES), (2 * slots, LANES)],
            receiver_data,
            receiver_block.reshape(1, -1),
            receiver_offset.reshape(1, -1),
            scratch=[
                pltpu.VMEM((2, count, COLS), F32),
                pltpu.VMEM((1, count), jnp.int32),
                pltpu.VMEM((1, count), jnp.int32),
                dma((3,)),
            ],
            hbm=range(3),
            pinned=range(3),
        )
        own, far, near = payload
        came = swap("leaf", near, 1)
        (both,) = kernel(pass_on, [(2 * slots, LANES)], far, came)
        arrived = [own, came, swap("leaf", both, 2)]
        leaf_own, mid_own, root_own = kernel(
            load_sources,
            [(n0, LANES), (n1 // 2, LANES), (n2 // 4, LANES)],
            after(leaf_sources.transpose(0, 2, 1), *payload),
            mid_sources.transpose(0, 1, 3, 2),
            root_sources.transpose(0, 2, 1),
            scratch=[
                pltpu.VMEM((2, COLS, n0), F32),
                pltpu.VMEM((2, COLS, n1), F32),
                pltpu.VMEM((2, COLS, n2), F32),
                dma((3,)),
            ],
            hbm=range(3),
            pinned=range(3),
        )
        (message,) = kernel(
            pack_leaf, [(sum(message_rows(n0, groups * slots)), LANES)], leaf_own, *arrived
        )
    with jax.named_scope("leaf_lower"):
        messages, (ll, l2m) = gather_front(
            message,
            lambda x: load((after(leaf_lower_inv, *x), "leaf"), (leaf_to_mid_lower, "leaf"), pinned=True),
        )
        (y_leaf,) = kernel(
            functools.partial(leaf_lower, groups * slots),
            [(n0, LANES)],
            ll,
            *messages,
            scratch=[pltpu.VMEM((s0, LANES), F32), pltpu.VMEM((fronts, *message.shape), F32)],
        )
    with jax.named_scope("mid_lower"):
        parts, (l2r, ml) = gather_front(
            y_leaf,
            lambda x: load((after(leaf_to_root_lower, *x), "leaf"), (mid_lower_inv, "own"), pinned=True),
        )
        keep, send = gathered(leaf_to_mid, LANES, [(n1 // 2, LANES)] * 2, l2m, parts, mid_own)
        came = swap("leaf", send, 1)
        root_kept, root_sent, y_full = kernel(
            leaf_to_root, [(n2 // 2, LANES)] * 2 + [(s0, LANES)], l2r, after(parts[0], send), *parts[1:]
        )
        (cut_mid,) = kernel(add, [(n1 // 2, LANES)], after(keep, root_kept), came)
        root_came = swap("leaf", root_sent, 1)
        parts, (m2r,) = gather_front(
            cut_mid, lambda x: load((after(mid_to_root_lower, *x), "own"), pinned=True), (root_came,)
        )
        (y_mid,) = gathered(packed_to, 2 * COLS, [(n1 // 2, LANES)], ml, parts)
    with jax.named_scope("root_cut"):
        parts, (rl,) = gather_front(y_mid, lambda x: load((after(root_lower_inv, *x), None)))
        keep, send = gathered(
            mid_to_root, 2 * COLS, [(n2 // 4, LANES)] * 2, m2r, parts, root_kept, root_came, root_own
        )
        came = swap("leaf", send, 2)
        mu, l2r_up = load((after(mid_upper_inv, send), "own"), (leaf_to_root_upper, "leaf"))
        (y_mid_full,) = kernel(
            functools.partial(whole_of, 2 * COLS), [(s1, 2 * COLS)], after(parts[0], send), *parts[1:]
        )
        (cut_root,) = kernel(add, [(n2 // 4, LANES)], after(keep, mu, y_mid_full), came)
    with jax.named_scope("root_solve"):
        parts, (ru,) = gather_front(cut_root, lambda x: load((after(root_upper_inv, *x), None)))
        (y_root,) = gathered(packed_to, COLS, [(n2 // 4, LANES)], rl, parts)
        parts, (m2r_up, l2m_up, lu) = gather_front(
            y_root,
            lambda x: load(
                (after(mid_to_root_upper, *x), "own"), (leaf_to_mid_upper, "leaf"), (leaf_upper_inv, "leaf")
            ),
        )
        (x_root,) = gathered(packed_to, COLS, [(n2 // 4, LANES)], ru, parts)
    with jax.named_scope("mid_upper"):
        keep, send, x_root = kernel(
            root_to_mid,
            [(s1 // 4, LANES)] * 2 + [(n2 // 2, LANES)],
            m2r_up,
            x_root,
            swap("leaf", x_root, 2),
        )
        mine, theirs = sum_front(keep, send)
        (known,) = kernel(functools.partial(own_half, 2 * COLS), [(2 * n1, 4 * COLS)], mu, y_mid_full, mine)
        (x_mid,) = kernel(mid_upper, [(n1 // 2, LANES)], mu, y_mid_full, theirs, known)
        from_root, root_field, root_adjoint = kernel(
            root_to_leaf,
            [(s0, LANES), (2, COLS, n2), (2, COLS, n2)],
            l2r_up,
            x_root,
            swap("leaf", after(x_root, send), 1),
        )
    with jax.named_scope("leaf_upper"):
        keep, send, x_mid = kernel(
            mid_to_leaf,
            [(s0 // 2, LANES)] * 2 + [(n1, LANES)],
            l2m_up,
            from_root,
            x_mid,
            swap("leaf", x_mid, 1),
        )
        x_other = swap("leaf", x_mid, 2)
        mid_field, mid_adjoint = kernel(mid_outputs, [(2, 2, COLS, n1)] * 2, x_mid, x_other)
        mine, theirs = sum_front(keep, send, x_other)
        (known,) = kernel(functools.partial(own_half, LANES), [(2 * n0, 2 * LANES)], lu, y_full, mine)
        leaf_field, leaf_adjoint = kernel(
            leaf_upper, [(2, COLS, n0)] * 2, lu, y_full, theirs, after(known, mid_field)
        )
    return tuple(
        jnp.swapaxes(x, -1, -2)
        for x in (leaf_field, mid_field, root_field, leaf_adjoint, mid_adjoint, root_adjoint)
    )


def solution(mesh):
    in_specs = (
        P(None, "leaf", "front", None),
        P(None, "leaf", "front", None),
        P(None, "leaf", "front", None),
        P(None, "leaf", "front", None),
        P(None, "leaf", None, "front"),
        P(None, "leaf", None, "front"),
        P(None, None, "front", None),
        P(None, None, "front", None),
        P(None, None, "front", None),
        P(None, None, None, "front"),
        P(None, "front", None),
        P(None, "front", None),
        P(None, ("leaf", "front"), None),
        P(None, None, "front", None),
        P(None, "front", None),
        P(None, ("leaf", "front"), None),
        P(("leaf", "front"), None),
        P(("leaf", "front")),
    )
    out_specs = (
        P(None, ("leaf", "front"), None),
        P(None, None, "front", None),
        P(None, "front", None),
        P(None, ("leaf", "front"), None),
        P(None, None, "front", None),
        P(None, "front", None),
    )
    return jax.shard_map(body, mesh=mesh, in_specs=in_specs, out_specs=out_specs, check_vma=False)
```

```python
import functools

import jax
import jax.numpy as jnp
from jax import lax
from jax.experimental import pallas as pl
from jax.experimental.pallas import tpu as pltpu
from jax.sharding import PartitionSpec as P

CAP = 2
CHUNKS = 4
LANES = 128
COLS = 32
F32 = jnp.float32
BF16 = jnp.bfloat16
VM = pl.BlockSpec(memory_space=pltpu.VMEM)
HB = pl.BlockSpec(memory_space=pltpu.HBM)


def split(x):
    high = x.astype(BF16)
    return high, (x - high.astype(F32)).astype(BF16)


def dot(a, b):
    return jnp.dot(a, b, preferred_element_type=F32)


def complex_dot(matrix, x):
    half = x.shape[1] // 2
    turned = jnp.concatenate([-x[:, half:], x[:, :half]], axis=1)
    both = jnp.concatenate([x, turned], axis=0)
    columns = jnp.concatenate(split(both), axis=1)
    product = dot(matrix, columns)
    rows, n = product.shape[0] // 2, x.shape[1]
    return (product[:rows, n:] + product[rows:, :n]) + product[:rows, :n]


def combined(product):
    rows, n = product.shape[0] // 2, product.shape[1] // 2
    return (product[:rows, n:] + product[rows:, :n]) + product[:rows, :n]


def turn(x, width):
    half = width // 2
    lane = lax.broadcasted_iota(jnp.int32, x.shape, 1) % width
    return jnp.where(lane < half, -pltpu.roll(x, LANES - half, 1), pltpu.roll(x, half, 1))


def spread(x, width):
    high, low = split(x)
    return jnp.concatenate(
        [
            jnp.concatenate([high[:, at : at + width], low[:, at : at + width]], axis=1)
            for at in range(0, LANES, width)
        ],
        axis=0,
    )


def part_dot(matrix, at, blocks, width):
    depth = matrix.shape[1] // 2
    columns = jnp.concatenate([spread(x, width) for x in blocks], axis=0)
    turned = jnp.concatenate([spread(turn(x, width), width) for x in blocks], axis=0)
    count, at = columns.shape[0], pl.multiple_of(at, LANES)
    return dot(matrix[:, pl.ds(at, count)], columns) + dot(matrix[:, pl.ds(depth + at, count)], turned)


def pack(x):
    chunks = LANES // x.shape[1]
    rows = x.shape[0] // chunks
    return jnp.concatenate([x[rows * j : rows * j + rows] for j in range(chunks)], axis=1)


def unpack(x, width):
    return jnp.concatenate([x[:, at : at + width] for at in range(0, LANES, width)], axis=0)


def halves(x):
    c = COLS
    return (
        jnp.concatenate([x[:, :c], x[:, 2 * c : 3 * c]], axis=1),
        jnp.concatenate([x[:, c : 2 * c], x[:, 3 * c :]], axis=1),
    )


def joined(forward, adjoint):
    c = COLS
    return jnp.concatenate([forward[:, :c], adjoint[:, :c], forward[:, c:], adjoint[:, c:]], axis=1)


def own_first(group, forward, adjoint):
    even = (group & 1) == 0
    return jnp.where(even, forward, adjoint), jnp.where(even, adjoint, forward)


def by_solve(group, own, other):
    even = (group & 1) == 0
    return joined(jnp.where(even, own, other), jnp.where(even, other, own))


def assemble(where, parts, here, width=LANES):
    rows = parts[0].shape[0] * (LANES // width)
    for k, part in blocks_of(parts):
        start = pl.multiple_of((here ^ k) * rows, 8)
        where[pl.ds(start, rows), :] = part[...] if width == LANES else unpack(part[...], width)


def fields_of(x, forward, adjoint, where):
    y = x.T
    c = COLS
    forward[(0, *where)] = y[0:c]
    forward[(1, *where)] = y[2 * c : 3 * c]
    adjoint[(0, *where)] = y[c : 2 * c]
    adjoint[(1, *where)] = -y[3 * c :]


def swap(axis, x, k):
    size = lax.axis_size(axis)
    return lax.ppermute(x, axis, [(i, i ^ k) for i in range(size)])


def stack(*refs):
    at = 0
    for ref in refs[:-1]:
        refs[-1][at : at + ref.shape[0], :] = ref[...]
        at += ref.shape[0]


def hop(fronts, step, odd):
    return 2 << (step ^ odd) if fronts == 8 else 2 * step + 2


def gather_front(x, meanwhile=None, others=()):
    fronts = lax.axis_size("front")
    last = swap("front", x, fronts - 2)
    near = [
        lax.ppermute(x, "front", [(i, i ^ hop(fronts, step, i & 1)) for i in range(fronts)])
        for step in range(fronts // 2 - 2)
    ]
    own = swap("front", x, 1)
    (both,) = kernel(stack, [(len(near) * x.shape[0], LANES)], *near)
    extra = tuple(meanwhile((both, own))) if meanwhile else ()
    last = after(last, *extra, *others)
    return [x, own, last, *near[::-1], swap("front", last, 1), swap("front", both, 1)], extra


def blocks_of(parts):
    rows, fronts = parts[0].shape[0], 2 * len(parts) - 6
    odd = lax.axis_index("front") & 1
    yield 0, parts[0]
    yield 1, parts[1]
    yield fronts - 2, parts[2]
    yield fronts - 1, parts[-2]
    for step, part in enumerate(parts[-3:2:-1]):
        yield hop(fronts, step, odd), part
        yield hop(fronts, step, odd ^ 1) + 1, parts[-1].at[rows * step : rows * step + rows, :]


def kernel(fn, outs, *args, scratch=(), vmem=8, work=0, hbm=(), pinned=()):
    outs = [o if isinstance(o[0], tuple) else (o, F32) for o in outs]
    return pl.pallas_call(
        fn,
        out_shape=[jax.ShapeDtypeStruct(*o) for o in outs],
        in_specs=[HB if i in hbm else VM for i in range(len(args))],
        out_specs=[VM] * len(outs),
        scratch_shapes=list(scratch),
        compiler_params=pltpu.CompilerParams(vmem_limit_bytes=vmem * 2**20),
        cost_estimate=pl.CostEstimate(flops=work, bytes_accessed=work // 700, transcendentals=0),
    )(*(pltpu.with_memory_space_constraint(a, pltpu.HBM) if i in pinned else a for i, a in enumerate(args)))


def chip_product(matrix, k, mine, other, width):
    here = lax.axis_index("front")
    odd = (here & 1) == 1
    blocks = [jnp.where(odd, other, mine), jnp.where(odd, mine, other)]
    return part_dot(matrix, ((here ^ k) // 2) * (2 * mine.shape[0] * (LANES // width)), blocks, width)


def first_products(width, matrix, mine, other, *refs):
    near, both, out = refs[:-2], refs[-2], refs[-1]
    rows, fronts = mine.shape[0], lax.axis_size("front")
    odd = lax.axis_index("front") & 1
    total = chip_product(matrix, 0, mine[...], other[...], width)
    for step, block in enumerate(near):
        at = rows * (len(near) - 1 - step if fronts == 8 else step)
        total += chip_product(
            matrix, hop(fronts, step, odd), block[...], both[at : at + rows, :], width
        )
    out[...] = total


def last_product(finish, width, count, matrix, *refs):
    parts, rest = refs[:count], refs[count:]
    if count == 3:
        known, mine, other = parts
        k = lax.axis_size("front") - 2
        finish(combined(known[...] + chip_product(matrix, k, mine[...], other[...], width)), *rest)
    else:
        assemble(rest[-1], parts, lax.axis_index("front"), width)
        finish(complex_dot(matrix[...], rest[-1][...]), *rest[:-1])


def gathered(finish, width, outs, matrix, parts, *args):
    rows = parts[0].shape[0] * (LANES // width)
    scratch = []
    if 2 * rows % LANES == 0:
        mine, other, last, *near, last_other, both = parts
        shape = (matrix.shape[0], 2 * width)
        (known,) = kernel(
            functools.partial(first_products, width), [shape], matrix, mine, other, *near[::-1], both
        )
        parts = [known, last, last_other]
    else:
        scratch = [pltpu.VMEM((rows * lax.axis_size("front"), width), F32)]
    return kernel(
        functools.partial(last_product, finish, width, len(parts)),
        outs,
        matrix,
        *parts,
        *args,
        scratch=scratch,
    )


def whole_of(width, *refs):
    assemble(refs[-1], refs[:-1], lax.axis_index("front"), width)


def half_product(theirs, width, matrix, y, piece):
    odd = (lax.axis_index("front") & 1) ^ theirs
    rows, chunks = piece.shape[0], LANES // width
    starts = [chunk * 2 * rows + odd * rows for chunk in range(chunks)]
    own = [y[pl.ds(pl.multiple_of(at, 8), rows), :] for at in starts]
    x = jnp.concatenate(own, axis=1) - piece[...]
    if chunks == 1:
        return part_dot(matrix, starts[0], [x], width)
    total, depth = None, matrix.shape[1] // 2
    columns, turned = spread(x, width), spread(turn(x, width), width)
    for chunk, at in enumerate(starts):
        at, span = pl.multiple_of(at, LANES), slice(rows * chunk, rows * chunk + rows)
        part = dot(matrix[:, pl.ds(at, rows)], columns[span])
        part += dot(matrix[:, pl.ds(depth + at, rows)], turned[span])
        total = part if total is None else total + part
    return total


def own_half(width, matrix, y, piece, out):
    out[...] = half_product(0, width, matrix, y, piece)


def load_matrices(picks, *refs):
    count = len(picks)
    sources, outs, buffers, sems = (
        refs[:count],
        refs[count : 2 * count],
        refs[2 * count : 3 * count],
        refs[3 * count],
    )
    parent = lax.axis_index("leaf") // 2
    copies = []
    for i, (src, pick) in enumerate(zip(sources, picks)):
        rows = buffers[i].shape[1]
        step = max(rows // CHUNKS, 16)
        for n, at in enumerate(range(0, rows, step)):
            span = pl.ds(at, step)
            view = src.at[:, span, :] if pick is None else src.at[:, parent if pick == "own" else 0, span, :]
            copy = pltpu.make_async_copy(view, buffers[i].at[:, span, :], sems.at[CHUNKS * i + n])
            copy.start()
            copies.append((i, at, step, copy))
    for i, at, step, copy in copies:
        copy.wait()
        rows, depth = buffers[i].shape[1:]
        for part in range(2):
            high, low = split(buffers[i][part, at : at + step, :])
            outs[i][at : at + step, part * depth : part * depth + depth] = high
            outs[i][rows + at : rows + at + step, part * depth : part * depth + depth] = low


def load(*matrices, pinned=False):
    shapes = [m.shape[-2:] for m, _ in matrices]
    size = sum(r * d for r, d in shapes)
    return kernel(
        functools.partial(load_matrices, tuple(pick for _, pick in matrices)),
        [((2 * r, 2 * d), BF16) for r, d in shapes],
        *[m for m, _ in matrices],
        scratch=[pltpu.VMEM((2, r, d), F32) for r, d in shapes]
        + [pltpu.SemaphoreType.DMA((CHUNKS * len(shapes),))],
        hbm=range(len(shapes)),
        pinned=range(len(shapes)) if pinned else (),
        vmem=4 + -(-size * 8 // 2**20),
        work=size * 1000,
    )


def pack_receivers(fronts, rows, data_hbm, block_hbm, offset_hbm, *refs):
    own, far, near = refs[:3]
    data, block, offset, sems = refs[3:]
    copies = [
        pltpu.make_async_copy(src, dst, sems.at[i])
        for i, (src, dst) in enumerate(((data_hbm, data), (block_hbm, block), (offset_hbm, offset)))
    ]
    for copy in copies:
        copy.start()
    for copy in copies:
        copy.wait()
    group = lax.axis_index("leaf")
    count = data.shape[1]
    slots = fronts * CAP
    down = lax.broadcasted_iota(jnp.int32, (count, count), 0)
    across = lax.broadcasted_iota(jnp.int32, (count, count), 1)
    eye = down == across
    block_row = block[...]
    block_col = jnp.sum(jnp.where(eye, block_row, 0), axis=1, keepdims=True)
    offset_col = jnp.sum(jnp.where(eye, offset[...], 0), axis=1, keepdims=True)
    same = (block_col == block_row) & (down < across)
    slot_row = block_row * CAP + jnp.sum(same.astype(jnp.int32), axis=0, keepdims=True)
    row_col = (block_col & (fronts - 1)) * rows + offset_col + 1
    lane = lax.broadcasted_iota(jnp.int32, (count, COLS), 1)
    index = jnp.where(lane == 0, row_col, 0).astype(F32)
    lines = jnp.concatenate([index, data[0], jnp.zeros((count, COLS), F32), -data[1]], axis=1)
    targets = [group, group ^ 2, group ^ 1, group ^ 3]
    place = lax.broadcasted_iota(jnp.int32, (slots, count), 0)
    pick = jnp.concatenate([place + target * slots == slot_row for target in targets], axis=0)
    picked = jnp.dot(
        pick.astype(F32), lines, precision=lax.Precision.HIGHEST, preferred_element_type=F32
    )
    own[...] = picked[:slots]
    far[...] = picked[slots : 2 * slots]
    near[...] = picked[2 * slots :]


def pass_on(far, came, out):
    rows = far.shape[0]
    out[0:rows, :] = far[...]
    out[rows:, :] = came[rows:, :]


def load_sources(leaf_hbm, mid_hbm, root_hbm, leaf_out, mid_out, root_out, leaf, mid, root, sems):
    group = lax.axis_index("leaf")
    copies = [
        pltpu.make_async_copy(src, dst, sems.at[i])
        for i, (src, dst) in enumerate(
            ((leaf_hbm, leaf), (mid_hbm.at[:, group // 2], mid), (root_hbm, root))
        )
    ]
    for copy in copies:
        copy.start()
    for copy in copies:
        copy.wait()
    forward = ((group & 1) == 0).astype(F32)
    real, imag = leaf[0].T, leaf[1].T
    zero = jnp.zeros_like(real)
    leaf_out[...] = jnp.concatenate([real, zero, imag, zero], axis=1)
    mid_out[...] = pack(jnp.concatenate([mid[0], mid[1]], axis=0).T) * forward
    width = COLS // 2
    low = jnp.concatenate([root[0, :width], root[1, :width]], axis=0)
    high = jnp.concatenate([root[0, width:], root[1, width:]], axis=0)
    root_out[...] = pack(jnp.where(group < 2, low, high).T) * forward


def message_rows(rows, slots):
    return max(rows, slots), 8 * -(-slots // (8 * LANES))


def pack_leaf(own, mine, near, far, out):
    lines = jnp.concatenate([mine[...], near[0 : mine.shape[0], :], far[...]], axis=0)
    slots = lines.shape[0]
    body, tail = message_rows(own.shape[0], slots)
    lane = lax.broadcasted_iota(jnp.int32, (slots, LANES), 1)
    data = jnp.where((lane // COLS) % 2 == 1, lines, 0.0)
    index = lines[:, 0:1]

    def padded(x):
        if x.shape[0] == body:
            return x
        return jnp.concatenate([x, jnp.zeros((body - x.shape[0], LANES), F32)], axis=0)

    out[0:body, :] = padded(own[...]) + padded(data)
    out[body:, :] = jnp.zeros((tail, LANES), F32)
    for at in range(0, slots, LANES):
        size = min(LANES, slots - at)
        eye = lax.broadcasted_iota(jnp.int32, (size, size), 0) == lax.broadcasted_iota(
            jnp.int32, (size, size), 1
        )
        line = jnp.sum(jnp.where(eye, index[at : at + size], 0.0), axis=0, keepdims=True)
        out[body + at // LANES : body + at // LANES + 1, 0:size] = line


def leaf_lower(slots, matrix, *refs):
    parts, (out, rhs, messages) = refs[:-3], refs[-3:]
    rows = out.shape[0]
    here = lax.axis_index("front")
    for k, part in blocks_of(parts):
        messages[here ^ k] = part[...]
    fronts = messages.shape[0]
    total = rows * fronts
    body, _ = message_rows(rows, slots)
    lane = lax.broadcasted_iota(jnp.int32, (slots, LANES), 1)
    taken = (lane // COLS) % 2 == 1
    own = lax.broadcasted_iota(jnp.int32, (rows, LANES), 1)
    own = (own // COLS) % 2 == 0
    for k in range(fronts):
        rhs[rows * k : rows * k + rows, :] = jnp.where(own, messages[k, 0:rows, :], 0.0)
    group = max(1, 512 // slots)
    for k in range(0, fronts, group):
        chosen = range(k, min(k + group, fronts))
        lines = jnp.concatenate([jnp.where(taken, messages[i, 0:slots, :], 0.0) for i in chosen], axis=0)
        index = jnp.concatenate(
            [
                messages[i, body + at // LANES : body + at // LANES + 1, 0 : min(LANES, slots - at)]
                for i in chosen
                for at in range(0, slots, LANES)
            ],
            axis=1,
        )
        row = lax.broadcasted_iota(jnp.int32, (total, index.shape[1]), 0)
        pick = (row + 1 == index.astype(jnp.int32)).astype(BF16)
        both = dot(pick, jnp.concatenate(split(lines), axis=1))
        rhs[...] += both[:, :LANES] + both[:, LANES:]
    out[...] = complex_dot(matrix[...], rhs[...])


def leaf_to_mid(value, sources, keep, send):
    mine, theirs = own_first(lax.axis_index("leaf"), *halves(value))
    keep[...] = sources[...] - pack(mine)
    send[...] = -pack(theirs)


def leaf_to_root(matrix, *refs):
    parts, (keep, send, full) = refs[:-3], refs[-3:]
    assemble(full, parts, lax.axis_index("front"))
    mine, theirs = own_first(lax.axis_index("leaf"), *halves(complex_dot(matrix[...], full[...])))
    keep[...], send[...] = pack(mine), pack(theirs)


def add(*refs):
    total = refs[0][...]
    for ref in refs[1:-1]:
        total = total + ref[...]
    refs[-1][...] = total


def packed_to(value, out):
    out[...] = pack(value)


def mid_to_root(value, kept, came, sources, keep, send):
    cut = -(unpack(kept[...] + came[...], 2 * COLS) + value)
    width = COLS // 2
    low = pack(jnp.concatenate([cut[:, :width], cut[:, COLS : COLS + width]], axis=1))
    high = pack(jnp.concatenate([cut[:, width:COLS], cut[:, COLS + width :]], axis=1))
    first = lax.axis_index("leaf") < 2
    keep[...] = jnp.where(first, low, high) + sources[...]
    send[...] = jnp.where(first, high, low)


def column_half(matrix, x, theirs):
    core = (lax.axis_index("front") & 1) ^ theirs
    half, n = x.shape[1] // 2, x.shape[1]
    turned = jnp.concatenate([-x[:, half:], x[:, :half]], axis=1)
    columns = jnp.concatenate(split(jnp.concatenate([x, turned], axis=0)), axis=1)
    height, chunks = matrix.shape[0] // 2, LANES // n
    rows, pieces = height // chunks // 2, []
    for chunk in range(chunks):
        at = pl.multiple_of((2 * chunk + core) * rows, 16)
        high = dot(matrix[pl.ds(at, rows), :], columns)
        low = dot(matrix[pl.ds(height + at, rows), :], columns[:, :n])
        pieces.append((high[:, n:] + low) + high[:, :n])
    return jnp.concatenate(pieces, axis=1)


def root_to_mid(matrix, mine, other, send, x_root):
    first = lax.axis_index("leaf") < 2
    mine, other = unpack(mine[...], COLS), unpack(other[...], COLS)
    low, high = jnp.where(first, mine, other), jnp.where(first, other, mine)
    width = COLS // 2
    x = jnp.concatenate([low[:, :width], high[:, :width], low[:, width:], high[:, width:]], axis=1)
    x_root[...] = pack(x)
    send[...] = column_half(matrix, x, 1)


def root_to_mid_kept(matrix, x_root, keep):
    keep[...] = column_half(matrix, unpack(x_root[...], 2 * COLS), 0)


def root_to_leaf(matrix, mine, other, out, forward, adjoint):
    x = by_solve(lax.axis_index("leaf"), unpack(mine[...], 2 * COLS), unpack(other[...], 2 * COLS))
    out[...] = complex_dot(matrix[...], x)
    fields_of(x, forward, adjoint, ())


def sum_front(kept, sent, *others):
    fronts = lax.axis_size("front")
    (total,) = kernel(add, [kept.shape], kept, swap("front", sent, 1))
    hops = [1 << i for i in range(1, fronts.bit_length() - 1)]
    for hop, back in zip(hops, hops[::-1]):
        pairs = [(i, i ^ (back if i & 1 else hop)) for i in range(fronts)]
        (total,) = kernel(add, [kept.shape], total, lax.ppermute(total, "front", pairs))
    return [total, swap("front", after(total, *others), 1)]


def mid_upper(matrix, y, piece, known, out):
    out[...] = pack(combined(known[...] + half_product(1, 2 * COLS, matrix, y, piece)))


def core_rows(ref, theirs):
    rows = ref.shape[0] // 2
    core = (lax.axis_index("front") & 1) ^ theirs
    return ref[pl.ds(pl.multiple_of(core * rows, 8), rows), :]


def mid_to_leaf(matrix, from_root, mine, other, send, x_mid):
    x = by_solve(lax.axis_index("leaf"), unpack(mine[...], 2 * COLS), unpack(other[...], 2 * COLS))
    x_mid[...] = x
    send[...] = column_half(matrix, x, 1) + core_rows(from_root, 1)


def mid_to_leaf_kept(matrix, from_root, x_mid, keep):
    keep[...] = column_half(matrix, x_mid[...], 0) + core_rows(from_root, 0)


def leaf_upper(matrix, y, piece, known, forward, adjoint):
    fields_of(combined(known[...] + half_product(1, LANES, matrix, y, piece)), forward, adjoint, ())


def mid_outputs(mine, other, forward, adjoint):
    parent = lax.axis_index("leaf") // 2
    fields_of(mine[...], forward, adjoint, (parent,))
    fields_of(other[...], forward, adjoint, (1 - parent,))


def after(x, *others):
    return lax.optimization_barrier((x, *others))[0]


def body(
    leaf_lower_inv,
    leaf_upper_inv,
    leaf_to_mid_lower,
    leaf_to_root_lower,
    leaf_to_mid_upper,
    leaf_to_root_upper,
    mid_lower_inv,
    mid_upper_inv,
    mid_to_root_lower,
    mid_to_root_upper,
    root_lower_inv,
    root_upper_inv,
    leaf_sources,
    mid_sources,
    root_sources,
    receiver_data,
    receiver_block,
    receiver_offset,
):
    groups, fronts = lax.axis_size("leaf"), lax.axis_size("front")
    n0, n1, n2 = leaf_sources.shape[1], mid_sources.shape[2], root_sources.shape[1]
    s0, s1, s2 = n0 * fronts, n1 * fronts, n2 * fronts
    slots, count = fronts * CAP, receiver_data.shape[1]
    dma = pltpu.SemaphoreType.DMA

    with jax.named_scope("right_hand_sides"):
        payload = kernel(
            functools.partial(pack_receivers, fronts, n0),
            [(slots, LANES), (slots, LANES), (2 * slots, LANES)],
            receiver_data,
            receiver_block.reshape(1, -1),
            receiver_offset.reshape(1, -1),
            scratch=[
                pltpu.VMEM((2, count, COLS), F32),
                pltpu.VMEM((1, count), jnp.int32),
                pltpu.VMEM((1, count), jnp.int32),
                dma((3,)),
            ],
            hbm=range(3),
            pinned=range(3),
        )
        own, far, near = payload
        came = swap("leaf", near, 1)
        (both,) = kernel(pass_on, [(2 * slots, LANES)], far, came)
        arrived = [own, came, swap("leaf", both, 2)]
        leaf_own, mid_own, root_own = kernel(
            load_sources,
            [(n0, LANES), (n1 // 2, LANES), (n2 // 4, LANES)],
            after(leaf_sources.transpose(0, 2, 1), *payload),
            mid_sources.transpose(0, 1, 3, 2),
            root_sources.transpose(0, 2, 1),
            scratch=[
                pltpu.VMEM((2, COLS, n0), F32),
                pltpu.VMEM((2, COLS, n1), F32),
                pltpu.VMEM((2, COLS, n2), F32),
                dma((3,)),
            ],
            hbm=range(3),
            pinned=range(3),
        )
        (message,) = kernel(
            pack_leaf, [(sum(message_rows(n0, groups * slots)), LANES)], leaf_own, *arrived
        )
    with jax.named_scope("leaf_lower"):
        messages, (ll, l2m) = gather_front(
            message,
            lambda x: load((after(leaf_lower_inv, *x), "leaf"), (leaf_to_mid_lower, "leaf"), pinned=True),
        )
        (y_leaf,) = kernel(
            functools.partial(leaf_lower, groups * slots),
            [(n0, LANES)],
            ll,
            *messages,
            scratch=[pltpu.VMEM((s0, LANES), F32), pltpu.VMEM((fronts, *message.shape), F32)],
        )
    with jax.named_scope("mid_lower"):
        parts, (l2r, ml) = gather_front(
            y_leaf,
            lambda x: load((after(leaf_to_root_lower, *x), "leaf"), (mid_lower_inv, "own"), pinned=True),
        )
        keep, send = gathered(leaf_to_mid, LANES, [(n1 // 2, LANES)] * 2, l2m, parts, mid_own)
        came = swap("leaf", send, 1)
        root_kept, root_sent, y_full = kernel(
            leaf_to_root, [(n2 // 2, LANES)] * 2 + [(s0, LANES)], l2r, after(parts[0], send), *parts[1:]
        )
        (cut_mid,) = kernel(add, [(n1 // 2, LANES)], after(keep, root_kept), came)
        root_came = swap("leaf", root_sent, 1)
        parts, (m2r,) = gather_front(
            cut_mid, lambda x: load((after(mid_to_root_lower, *x), "own"), pinned=True), (root_came,)
        )
        (y_mid,) = gathered(packed_to, 2 * COLS, [(n1 // 2, LANES)], ml, parts)
    with jax.named_scope("root_cut"):
        parts, (rl,) = gather_front(y_mid, lambda x: load((after(root_lower_inv, *x), None)))
        keep, send = gathered(
            mid_to_root, 2 * COLS, [(n2 // 4, LANES)] * 2, m2r, parts, root_kept, root_came, root_own
        )
        came = swap("leaf", send, 2)
        mu, l2r_up = load((after(mid_upper_inv, send), "own"), (leaf_to_root_upper, "leaf"))
        (y_mid_full,) = kernel(
            functools.partial(whole_of, 2 * COLS), [(s1, 2 * COLS)], after(parts[0], send), *parts[1:]
        )
        (cut_root,) = kernel(add, [(n2 // 4, LANES)], after(keep, mu, y_mid_full), came)
    with jax.named_scope("root_solve"):
        parts, (ru,) = gather_front(cut_root, lambda x: load((after(root_upper_inv, *x), None)))
        (y_root,) = gathered(packed_to, COLS, [(n2 // 4, LANES)], rl, parts)
        parts, (m2r_up, l2m_up, lu) = gather_front(
            y_root,
            lambda x: load(
                (after(mid_to_root_upper, *x), "own"), (leaf_to_mid_upper, "leaf"), (leaf_upper_inv, "leaf")
            ),
        )
        (x_root,) = gathered(packed_to, COLS, [(n2 // 4, LANES)], ru, parts)
    with jax.named_scope("mid_upper"):
        send, x_root = kernel(
            root_to_mid,
            [(s1 // 4, LANES), (n2 // 2, LANES)],
            m2r_up,
            x_root,
            swap("leaf", x_root, 2),
        )
        (keep,) = kernel(root_to_mid_kept, [(s1 // 4, LANES)], m2r_up, x_root)
        mine, theirs = sum_front(keep, send)
        (known,) = kernel(functools.partial(own_half, 2 * COLS), [(2 * n1, 4 * COLS)], mu, y_mid_full, mine)
        (x_mid,) = kernel(mid_upper, [(n1 // 2, LANES)], mu, y_mid_full, theirs, known)
        from_root, root_field, root_adjoint = kernel(
            root_to_leaf,
            [(s0, LANES), (2, COLS, n2), (2, COLS, n2)],
            l2r_up,
            x_root,
            swap("leaf", after(x_root, send), 1),
        )
    with jax.named_scope("leaf_upper"):
        send, x_mid = kernel(
            mid_to_leaf,
            [(s0 // 2, LANES), (n1, LANES)],
            l2m_up,
            from_root,
            x_mid,
            swap("leaf", x_mid, 1),
        )
        (keep,) = kernel(mid_to_leaf_kept, [(s0 // 2, LANES)], l2m_up, from_root, x_mid)
        x_other = swap("leaf", x_mid, 2)
        mid_field, mid_adjoint = kernel(mid_outputs, [(2, 2, COLS, n1)] * 2, x_mid, x_other)
        mine, theirs = sum_front(keep, send, x_other)
        (known,) = kernel(functools.partial(own_half, LANES), [(2 * n0, 2 * LANES)], lu, y_full, mine)
        leaf_field, leaf_adjoint = kernel(
            leaf_upper, [(2, COLS, n0)] * 2, lu, y_full, theirs, after(known, mid_field)
        )
    return tuple(
        jnp.swapaxes(x, -1, -2)
        for x in (leaf_field, mid_field, root_field, leaf_adjoint, mid_adjoint, root_adjoint)
    )


def solution(mesh):
    in_specs = (
        P(None, "leaf", "front", None),
        P(None, "leaf", "front", None),
        P(None, "leaf", "front", None),
        P(None, "leaf", "front", None),
        P(None, "leaf", None, "front"),
        P(None, "leaf", None, "front"),
        P(None, None, "front", None),
        P(None, None, "front", None),
        P(None, None, "front", None),
        P(None, None, None, "front"),
        P(None, "front", None),
        P(None, "front", None),
        P(None, ("leaf", "front"), None),
        P(None, None, "front", None),
        P(None, "front", None),
        P(None, ("leaf", "front"), None),
        P(("leaf", "front"), None),
        P(("leaf", "front")),
    )
    out_specs = (
        P(None, ("leaf", "front"), None),
        P(None, None, "front", None),
        P(None, "front", None),
        P(None, ("leaf", "front"), None),
        P(None, None, "front", None),
        P(None, "front", None),
    )
    return jax.shard_map(body, mesh=mesh, in_specs=in_specs, out_specs=out_specs, check_vma=False)
```

```python
import functools

import jax
import jax.numpy as jnp
from jax import lax
from jax.experimental import pallas as pl
from jax.experimental.pallas import tpu as pltpu
from jax.sharding import PartitionSpec as P

CAP = 2
CHUNKS = 4
LANES = 128
COLS = 32
F32 = jnp.float32
BF16 = jnp.bfloat16
VM = pl.BlockSpec(memory_space=pltpu.VMEM)
HB = pl.BlockSpec(memory_space=pltpu.HBM)


def split(x):
    high = x.astype(BF16)
    return high, (x - high.astype(F32)).astype(BF16)


def dot(a, b):
    return jnp.dot(a, b, preferred_element_type=F32)


def complex_dot(matrix, x):
    half = x.shape[1] // 2
    turned = jnp.concatenate([-x[:, half:], x[:, :half]], axis=1)
    both = jnp.concatenate([x, turned], axis=0)
    columns = jnp.concatenate(split(both), axis=1)
    product = dot(matrix, columns)
    rows, n = product.shape[0] // 2, x.shape[1]
    return (product[:rows, n:] + product[rows:, :n]) + product[:rows, :n]


def combined(product):
    rows, n = product.shape[0] // 2, product.shape[1] // 2
    return (product[:rows, n:] + product[rows:, :n]) + product[:rows, :n]


def turn(x, width):
    half = width // 2
    lane = lax.broadcasted_iota(jnp.int32, x.shape, 1) % width
    return jnp.where(lane < half, -pltpu.roll(x, LANES - half, 1), pltpu.roll(x, half, 1))


def spread(x, width):
    high, low = split(x)
    return jnp.concatenate(
        [
            jnp.concatenate([high[:, at : at + width], low[:, at : at + width]], axis=1)
            for at in range(0, LANES, width)
        ],
        axis=0,
    )


def part_dot(matrix, at, blocks, width):
    depth = matrix.shape[1] // 2
    columns = jnp.concatenate([spread(x, width) for x in blocks], axis=0)
    turned = jnp.concatenate([spread(turn(x, width), width) for x in blocks], axis=0)
    count, at = columns.shape[0], pl.multiple_of(at, LANES)
    return dot(matrix[:, pl.ds(at, count)], columns) + dot(matrix[:, pl.ds(depth + at, count)], turned)


def pack(x):
    chunks = LANES // x.shape[1]
    rows = x.shape[0] // chunks
    return jnp.concatenate([x[rows * j : rows * j + rows] for j in range(chunks)], axis=1)


def unpack(x, width):
    return jnp.concatenate([x[:, at : at + width] for at in range(0, LANES, width)], axis=0)


def halves(x):
    c = COLS
    return (
        jnp.concatenate([x[:, :c], x[:, 2 * c : 3 * c]], axis=1),
        jnp.concatenate([x[:, c : 2 * c], x[:, 3 * c :]], axis=1),
    )


def joined(forward, adjoint):
    c = COLS
    return jnp.concatenate([forward[:, :c], adjoint[:, :c], forward[:, c:], adjoint[:, c:]], axis=1)


def own_first(group, forward, adjoint):
    even = (group & 1) == 0
    return jnp.where(even, forward, adjoint), jnp.where(even, adjoint, forward)


def by_solve(group, own, other):
    even = (group & 1) == 0
    return joined(jnp.where(even, own, other), jnp.where(even, other, own))


def assemble(where, parts, here, width=LANES):
    rows = parts[0].shape[0] * (LANES // width)
    for k, part in blocks_of(parts):
        start = pl.multiple_of((here ^ k) * rows, 8)
        where[pl.ds(start, rows), :] = part[...] if width == LANES else unpack(part[...], width)


def fields_of(x, forward, adjoint, where):
    y = x.T
    c = COLS
    forward[(0, *where)] = y[0:c]
    forward[(1, *where)] = y[2 * c : 3 * c]
    adjoint[(0, *where)] = y[c : 2 * c]
    adjoint[(1, *where)] = -y[3 * c :]


def swap(axis, x, k):
    size = lax.axis_size(axis)
    return lax.ppermute(x, axis, [(i, i ^ k) for i in range(size)])


def stack(*refs):
    at = 0
    for ref in refs[:-1]:
        refs[-1][at : at + ref.shape[0], :] = ref[...]
        at += ref.shape[0]


def hop(fronts, step, odd):
    return 2 << (step ^ odd) if fronts == 8 else 2 * step + 2


def gather_front(x, meanwhile=None, others=()):
    fronts = lax.axis_size("front")
    last = swap("front", x, fronts - 2)
    near = [
        lax.ppermute(x, "front", [(i, i ^ hop(fronts, step, i & 1)) for i in range(fronts)])
        for step in range(fronts // 2 - 2)
    ]
    own = swap("front", x, 1)
    (both,) = kernel(stack, [(len(near) * x.shape[0], LANES)], *near)
    extra = tuple(meanwhile((both, own))) if meanwhile else ()
    last = after(last, *extra, *others)
    return [x, own, last, *near[::-1], swap("front", last, 1), swap("front", both, 1)], extra


def blocks_of(parts):
    rows, fronts = parts[0].shape[0], 2 * len(parts) - 6
    odd = lax.axis_index("front") & 1
    yield 0, parts[0]
    yield 1, parts[1]
    yield fronts - 2, parts[2]
    yield fronts - 1, parts[-2]
    for step, part in enumerate(parts[-3:2:-1]):
        yield hop(fronts, step, odd), part
        yield hop(fronts, step, odd ^ 1) + 1, parts[-1].at[rows * step : rows * step + rows, :]


def kernel(fn, outs, *args, scratch=(), vmem=8, work=0, hbm=(), pinned=()):
    outs = [o if isinstance(o[0], tuple) else (o, F32) for o in outs]
    return pl.pallas_call(
        fn,
        out_shape=[jax.ShapeDtypeStruct(*o) for o in outs],
        in_specs=[HB if i in hbm else VM for i in range(len(args))],
        out_specs=[VM] * len(outs),
        scratch_shapes=list(scratch),
        compiler_params=pltpu.CompilerParams(vmem_limit_bytes=vmem * 2**20),
        cost_estimate=pl.CostEstimate(flops=work, bytes_accessed=work // 700, transcendentals=0),
    )(*(pltpu.with_memory_space_constraint(a, pltpu.HBM) if i in pinned else a for i, a in enumerate(args)))


def chip_product(matrix, k, mine, other, width):
    here = lax.axis_index("front")
    odd = (here & 1) == 1
    blocks = [jnp.where(odd, other, mine), jnp.where(odd, mine, other)]
    return part_dot(matrix, ((here ^ k) // 2) * (2 * mine.shape[0] * (LANES // width)), blocks, width)


def first_products(width, matrix, mine, other, *refs):
    near, both, out = refs[:-2], refs[-2], refs[-1]
    rows, fronts = mine.shape[0], lax.axis_size("front")
    odd = lax.axis_index("front") & 1
    total = chip_product(matrix, 0, mine[...], other[...], width)
    for step, block in enumerate(near):
        at = rows * (len(near) - 1 - step if fronts == 8 else step)
        total += chip_product(
            matrix, hop(fronts, step, odd), block[...], both[at : at + rows, :], width
        )
    out[...] = total


def last_product(finish, width, count, matrix, *refs):
    parts, rest = refs[:count], refs[count:]
    if count == 3:
        known, mine, other = parts
        k = lax.axis_size("front") - 2
        finish(combined(known[...] + chip_product(matrix, k, mine[...], other[...], width)), *rest)
    else:
        assemble(rest[-1], parts, lax.axis_index("front"), width)
        finish(complex_dot(matrix[...], rest[-1][...]), *rest[:-1])


def gathered(finish, width, outs, matrix, parts, *args):
    rows = parts[0].shape[0] * (LANES // width)
    scratch = []
    if 2 * rows % LANES == 0:
        mine, other, last, *near, last_other, both = parts
        shape = (matrix.shape[0], 2 * width)
        (known,) = kernel(
            functools.partial(first_products, width), [shape], matrix, mine, other, *near[::-1], both
        )
        parts = [known, last, last_other]
    else:
        scratch = [pltpu.VMEM((rows * lax.axis_size("front"), width), F32)]
    return kernel(
        functools.partial(last_product, finish, width, len(parts)),
        outs,
        matrix,
        *parts,
        *args,
        scratch=scratch,
    )


def whole_of(width, *refs):
    assemble(refs[-1], refs[:-1], lax.axis_index("front"), width)


def half_product(theirs, width, matrix, y, piece):
    odd = (lax.axis_index("front") & 1) ^ theirs
    rows, chunks = piece.shape[0], LANES // width
    starts = [chunk * 2 * rows + odd * rows for chunk in range(chunks)]
    own = [y[pl.ds(pl.multiple_of(at, 8), rows), :] for at in starts]
    x = jnp.concatenate(own, axis=1) - piece[...]
    if chunks == 1:
        return part_dot(matrix, starts[0], [x], width)
    total, depth = None, matrix.shape[1] // 2
    columns, turned = spread(x, width), spread(turn(x, width), width)
    for chunk, at in enumerate(starts):
        at, span = pl.multiple_of(at, LANES), slice(rows * chunk, rows * chunk + rows)
        part = dot(matrix[:, pl.ds(at, rows)], columns[span])
        part += dot(matrix[:, pl.ds(depth + at, rows)], turned[span])
        total = part if total is None else total + part
    return total


def own_half(width, matrix, y, piece, out):
    out[...] = half_product(0, width, matrix, y, piece)


def load_matrices(picks, *refs):
    count = len(picks)
    sources, outs, buffers, sems = (
        refs[:count],
        refs[count : 2 * count],
        refs[2 * count : 3 * count],
        refs[3 * count],
    )
    parent = lax.axis_index("leaf") // 2
    copies = []
    for i, (src, pick) in enumerate(zip(sources, picks)):
        rows = buffers[i].shape[1]
        step = max(rows // CHUNKS, 16)
        for n, at in enumerate(range(0, rows, step)):
            span = pl.ds(at, step)
            view = src.at[:, span, :] if pick is None else src.at[:, parent if pick == "own" else 0, span, :]
            copy = pltpu.make_async_copy(view, buffers[i].at[:, span, :], sems.at[CHUNKS * i + n])
            copy.start()
            copies.append((i, at, step, copy))
    for i, at, step, copy in copies:
        copy.wait()
        rows, depth = buffers[i].shape[1:]
        for part in range(2):
            high, low = split(buffers[i][part, at : at + step, :])
            outs[i][at : at + step, part * depth : part * depth + depth] = high
            outs[i][rows + at : rows + at + step, part * depth : part * depth + depth] = low


def load(*matrices, pinned=False):
    shapes = [m.shape[-2:] for m, _ in matrices]
    size = sum(r * d for r, d in shapes)
    return kernel(
        functools.partial(load_matrices, tuple(pick for _, pick in matrices)),
        [((2 * r, 2 * d), BF16) for r, d in shapes],
        *[m for m, _ in matrices],
        scratch=[pltpu.VMEM((2, r, d), F32) for r, d in shapes]
        + [pltpu.SemaphoreType.DMA((CHUNKS * len(shapes),))],
        hbm=range(len(shapes)),
        pinned=range(len(shapes)) if pinned else (),
        vmem=4 + -(-size * 8 // 2**20),
        work=size * 1000,
    )


def pack_receivers(fronts, rows, data_hbm, block_hbm, offset_hbm, *refs):
    own, far, near = refs[:3]
    data, block, offset, sems = refs[3:]
    copies = [
        pltpu.make_async_copy(src, dst, sems.at[i])
        for i, (src, dst) in enumerate(((data_hbm, data), (block_hbm, block), (offset_hbm, offset)))
    ]
    for copy in copies:
        copy.start()
    for copy in copies:
        copy.wait()
    group = lax.axis_index("leaf")
    count = data.shape[1]
    slots = fronts * CAP
    down = lax.broadcasted_iota(jnp.int32, (count, count), 0)
    across = lax.broadcasted_iota(jnp.int32, (count, count), 1)
    eye = down == across
    block_row = block[...]
    block_col = jnp.sum(jnp.where(eye, block_row, 0), axis=1, keepdims=True)
    offset_col = jnp.sum(jnp.where(eye, offset[...], 0), axis=1, keepdims=True)
    same = (block_col == block_row) & (down < across)
    slot_row = block_row * CAP + jnp.sum(same.astype(jnp.int32), axis=0, keepdims=True)
    row_col = (block_col & (fronts - 1)) * rows + offset_col + 1
    lane = lax.broadcasted_iota(jnp.int32, (count, COLS), 1)
    index = jnp.where(lane == 0, row_col, 0).astype(F32)
    lines = jnp.concatenate([index, data[0], jnp.zeros((count, COLS), F32), -data[1]], axis=1)
    targets = [group, group ^ 2, group ^ 1, group ^ 3]
    place = lax.broadcasted_iota(jnp.int32, (slots, count), 0)
    pick = jnp.concatenate([place + target * slots == slot_row for target in targets], axis=0)
    picked = jnp.dot(
        pick.astype(F32), lines, precision=lax.Precision.HIGHEST, preferred_element_type=F32
    )
    own[...] = picked[:slots]
    far[...] = picked[slots : 2 * slots]
    near[...] = picked[2 * slots :]


def pass_on(far, came, out):
    rows = far.shape[0]
    out[0:rows, :] = far[...]
    out[rows:, :] = came[rows:, :]


def load_sources(leaf_hbm, mid_hbm, root_hbm, leaf_out, mid_out, root_out, leaf, mid, root, sems):
    group = lax.axis_index("leaf")
    copies = [
        pltpu.make_async_copy(src, dst, sems.at[i])
        for i, (src, dst) in enumerate(
            ((leaf_hbm, leaf), (mid_hbm.at[:, group // 2], mid), (root_hbm, root))
        )
    ]
    for copy in copies:
        copy.start()
    for copy in copies:
        copy.wait()
    forward = ((group & 1) == 0).astype(F32)
    real, imag = leaf[0].T, leaf[1].T
    zero = jnp.zeros_like(real)
    leaf_out[...] = jnp.concatenate([real, zero, imag, zero], axis=1)
    mid_out[...] = pack(jnp.concatenate([mid[0], mid[1]], axis=0).T) * forward
    width = COLS // 2
    low = jnp.concatenate([root[0, :width], root[1, :width]], axis=0)
    high = jnp.concatenate([root[0, width:], root[1, width:]], axis=0)
    root_out[...] = pack(jnp.where(group < 2, low, high).T) * forward


def message_rows(rows, slots):
    return max(rows, slots), 8 * -(-slots // (8 * LANES))


def pack_leaf(own, mine, near, far, out):
    lines = jnp.concatenate([mine[...], near[0 : mine.shape[0], :], far[...]], axis=0)
    slots = lines.shape[0]
    body, tail = message_rows(own.shape[0], slots)
    lane = lax.broadcasted_iota(jnp.int32, (slots, LANES), 1)
    data = jnp.where((lane // COLS) % 2 == 1, lines, 0.0)
    index = lines[:, 0:1]

    def padded(x):
        if x.shape[0] == body:
            return x
        return jnp.concatenate([x, jnp.zeros((body - x.shape[0], LANES), F32)], axis=0)

    out[0:body, :] = padded(own[...]) + padded(data)
    out[body:, :] = jnp.zeros((tail, LANES), F32)
    for at in range(0, slots, LANES):
        size = min(LANES, slots - at)
        eye = lax.broadcasted_iota(jnp.int32, (size, size), 0) == lax.broadcasted_iota(
            jnp.int32, (size, size), 1
        )
        line = jnp.sum(jnp.where(eye, index[at : at + size], 0.0), axis=0, keepdims=True)
        out[body + at // LANES : body + at // LANES + 1, 0:size] = line


def leaf_lower(slots, matrix, *refs):
    parts, (out, rhs, messages) = refs[:-3], refs[-3:]
    rows = out.shape[0]
    here = lax.axis_index("front")
    for k, part in blocks_of(parts):
        messages[here ^ k] = part[...]
    fronts = messages.shape[0]
    total = rows * fronts
    body, _ = message_rows(rows, slots)
    lane = lax.broadcasted_iota(jnp.int32, (slots, LANES), 1)
    taken = (lane // COLS) % 2 == 1
    own = lax.broadcasted_iota(jnp.int32, (rows, LANES), 1)
    own = (own // COLS) % 2 == 0
    for k in range(fronts):
        rhs[rows * k : rows * k + rows, :] = jnp.where(own, messages[k, 0:rows, :], 0.0)
    group = max(1, 512 // slots)
    for k in range(0, fronts, group):
        chosen = range(k, min(k + group, fronts))
        lines = jnp.concatenate([jnp.where(taken, messages[i, 0:slots, :], 0.0) for i in chosen], axis=0)
        index = jnp.concatenate(
            [
                messages[i, body + at // LANES : body + at // LANES + 1, 0 : min(LANES, slots - at)]
                for i in chosen
                for at in range(0, slots, LANES)
            ],
            axis=1,
        )
        row = lax.broadcasted_iota(jnp.int32, (total, index.shape[1]), 0)
        pick = (row + 1 == index.astype(jnp.int32)).astype(BF16)
        both = dot(pick, jnp.concatenate(split(lines), axis=1))
        rhs[...] += both[:, :LANES] + both[:, LANES:]
    out[...] = complex_dot(matrix[...], rhs[...])


def leaf_to_mid(value, sources, keep, send):
    mine, theirs = own_first(lax.axis_index("leaf"), *halves(value))
    keep[...] = sources[...] - pack(mine)
    send[...] = -pack(theirs)


def leaf_to_root(matrix, *refs):
    parts, (keep, send, full) = refs[:-3], refs[-3:]
    assemble(full, parts, lax.axis_index("front"))
    mine, theirs = own_first(lax.axis_index("leaf"), *halves(complex_dot(matrix[...], full[...])))
    keep[...], send[...] = pack(mine), pack(theirs)


def add(*refs):
    total = refs[0][...]
    for ref in refs[1:-1]:
        total = total + ref[...]
    refs[-1][...] = total


def packed_to(value, out):
    out[...] = pack(value)


def mid_to_root(value, kept, came, sources, keep, send):
    cut = -(unpack(kept[...] + came[...], 2 * COLS) + value)
    width = COLS // 2
    low = pack(jnp.concatenate([cut[:, :width], cut[:, COLS : COLS + width]], axis=1))
    high = pack(jnp.concatenate([cut[:, width:COLS], cut[:, COLS + width :]], axis=1))
    first = lax.axis_index("leaf") < 2
    keep[...] = jnp.where(first, low, high) + sources[...]
    send[...] = jnp.where(first, high, low)


def column_half(matrix, x, theirs):
    core = (lax.axis_index("front") & 1) ^ theirs
    half, n = x.shape[1] // 2, x.shape[1]
    turned = jnp.concatenate([-x[:, half:], x[:, :half]], axis=1)
    columns = jnp.concatenate(split(jnp.concatenate([x, turned], axis=0)), axis=1)
    height, chunks = matrix.shape[0] // 2, LANES // n
    rows, pieces = height // chunks // 2, []
    for chunk in range(chunks):
        at = pl.multiple_of((2 * chunk + core) * rows, 16)
        high = dot(matrix[pl.ds(at, rows), :], columns)
        low = dot(matrix[pl.ds(height + at, rows), :], columns[:, :n])
        pieces.append((high[:, n:] + low) + high[:, :n])
    return jnp.concatenate(pieces, axis=1)


def root_to_mid(matrix, mine, other, send, top, low_rows):
    first = lax.axis_index("leaf") < 2
    mine, other = unpack(mine[...], COLS), unpack(other[...], COLS)
    low, high = jnp.where(first, mine, other), jnp.where(first, other, mine)
    width = COLS // 2
    x = jnp.concatenate([low[:, :width], high[:, :width], low[:, width:], high[:, width:]], axis=1)
    packed, rows = pack(x), top.shape[0]
    top[...] = packed[:rows]
    low_rows[...] = packed[rows:]
    send[...] = column_half(matrix, x, 1)


def stacked(top, low):
    return unpack(jnp.concatenate([top[...], low[...]], axis=0), 2 * COLS)


def root_to_mid_kept(matrix, top, low, keep):
    keep[...] = column_half(matrix, stacked(top, low), 0)


def root_to_leaf(matrix, top, low, other_top, other_low, out, forward, adjoint):
    x = by_solve(lax.axis_index("leaf"), stacked(top, low), stacked(other_top, other_low))
    out[...] = complex_dot(matrix[...], x)
    fields_of(x, forward, adjoint, ())


def sum_front(kept, sent, before_last=(), at_end=()):
    fronts = lax.axis_size("front")
    (total,) = kernel(add, [kept.shape], kept, swap("front", sent, 1))
    hops = [1 << i for i in range(1, fronts.bit_length() - 1)]
    for hop, back in zip(hops, hops[::-1]):
        pairs = [(i, i ^ (back if i & 1 else hop)) for i in range(fronts)]
        if hop == hops[-1]:
            total = after(total, *before_last)
        (total,) = kernel(add, [kept.shape], total, lax.ppermute(total, "front", pairs))
    return [total, swap("front", after(total, *at_end), 1)]


def mid_upper(matrix, y, piece, known, out):
    out[...] = pack(combined(known[...] + half_product(1, 2 * COLS, matrix, y, piece)))


def core_rows(ref, theirs):
    rows = ref.shape[0] // 2
    core = (lax.axis_index("front") & 1) ^ theirs
    return ref[pl.ds(pl.multiple_of(core * rows, 8), rows), :]


def mid_to_leaf(matrix, from_root, mine, other, send, x_mid):
    x = by_solve(lax.axis_index("leaf"), unpack(mine[...], 2 * COLS), unpack(other[...], 2 * COLS))
    x_mid[...] = x
    send[...] = column_half(matrix, x, 1) + core_rows(from_root, 1)


def mid_to_leaf_kept(matrix, from_root, x_mid, keep):
    keep[...] = column_half(matrix, x_mid[...], 0) + core_rows(from_root, 0)


def leaf_upper(matrix, y, piece, known, forward, adjoint):
    fields_of(combined(known[...] + half_product(1, LANES, matrix, y, piece)), forward, adjoint, ())


def mid_outputs(mine, far, other, forward, adjoint):
    parent = lax.axis_index("leaf") // 2
    x = by_solve(lax.axis_index("leaf"), unpack(far[...], 2 * COLS), unpack(other[...], 2 * COLS))
    fields_of(mine[...], forward, adjoint, (parent,))
    fields_of(x, forward, adjoint, (1 - parent,))


def after(x, *others):
    return lax.optimization_barrier((x, *others))[0]


def body(
    leaf_lower_inv,
    leaf_upper_inv,
    leaf_to_mid_lower,
    leaf_to_root_lower,
    leaf_to_mid_upper,
    leaf_to_root_upper,
    mid_lower_inv,
    mid_upper_inv,
    mid_to_root_lower,
    mid_to_root_upper,
    root_lower_inv,
    root_upper_inv,
    leaf_sources,
    mid_sources,
    root_sources,
    receiver_data,
    receiver_block,
    receiver_offset,
):
    groups, fronts = lax.axis_size("leaf"), lax.axis_size("front")
    n0, n1, n2 = leaf_sources.shape[1], mid_sources.shape[2], root_sources.shape[1]
    s0, s1, s2 = n0 * fronts, n1 * fronts, n2 * fronts
    slots, count = fronts * CAP, receiver_data.shape[1]
    dma = pltpu.SemaphoreType.DMA

    with jax.named_scope("right_hand_sides"):
        payload = kernel(
            functools.partial(pack_receivers, fronts, n0),
            [(slots, LANES), (slots, LANES), (2 * slots, LANES)],
            receiver_data,
            receiver_block.reshape(1, -1),
            receiver_offset.reshape(1, -1),
            scratch=[
                pltpu.VMEM((2, count, COLS), F32),
                pltpu.VMEM((1, count), jnp.int32),
                pltpu.VMEM((1, count), jnp.int32),
                dma((3,)),
            ],
            hbm=range(3),
            pinned=range(3),
        )
        own, far, near = payload
        came = swap("leaf", near, 1)
        (both,) = kernel(pass_on, [(2 * slots, LANES)], far, came)
        arrived = [own, came, swap("leaf", both, 2)]
        leaf_own, mid_own, root_own = kernel(
            load_sources,
            [(n0, LANES), (n1 // 2, LANES), (n2 // 4, LANES)],
            after(leaf_sources.transpose(0, 2, 1), *payload),
            mid_sources.transpose(0, 1, 3, 2),
            root_sources.transpose(0, 2, 1),
            scratch=[
                pltpu.VMEM((2, COLS, n0), F32),
                pltpu.VMEM((2, COLS, n1), F32),
                pltpu.VMEM((2, COLS, n2), F32),
                dma((3,)),
            ],
            hbm=range(3),
            pinned=range(3),
        )
        (message,) = kernel(
            pack_leaf, [(sum(message_rows(n0, groups * slots)), LANES)], leaf_own, *arrived
        )
    with jax.named_scope("leaf_lower"):
        messages, (ll, l2m) = gather_front(
            message,
            lambda x: load((after(leaf_lower_inv, *x), "leaf"), (leaf_to_mid_lower, "leaf"), pinned=True),
        )
        (y_leaf,) = kernel(
            functools.partial(leaf_lower, groups * slots),
            [(n0, LANES)],
            ll,
            *messages,
            scratch=[pltpu.VMEM((s0, LANES), F32), pltpu.VMEM((fronts, *message.shape), F32)],
        )
    with jax.named_scope("mid_lower"):
        parts, (l2r, ml) = gather_front(
            y_leaf,
            lambda x: load((after(leaf_to_root_lower, *x), "leaf"), (mid_lower_inv, "own"), pinned=True),
        )
        keep, send = gathered(leaf_to_mid, LANES, [(n1 // 2, LANES)] * 2, l2m, parts, mid_own)
        came = swap("leaf", send, 1)
        root_kept, root_sent, y_full = kernel(
            leaf_to_root, [(n2 // 2, LANES)] * 2 + [(s0, LANES)], l2r, after(parts[0], send), *parts[1:]
        )
        (cut_mid,) = kernel(add, [(n1 // 2, LANES)], after(keep, root_kept), came)
        root_came = swap("leaf", root_sent, 1)
        parts, (m2r,) = gather_front(
            cut_mid, lambda x: load((after(mid_to_root_lower, *x), "own"), pinned=True), (root_came,)
        )
        (y_mid,) = gathered(packed_to, 2 * COLS, [(n1 // 2, LANES)], ml, parts)
    with jax.named_scope("root_cut"):
        parts, (rl,) = gather_front(y_mid, lambda x: load((after(root_lower_inv, *x), None)))
        keep, send = gathered(
            mid_to_root, 2 * COLS, [(n2 // 4, LANES)] * 2, m2r, parts, root_kept, root_came, root_own
        )
        came = swap("leaf", send, 2)
        mu, l2r_up = load((after(mid_upper_inv, send), "own"), (leaf_to_root_upper, "leaf"))
        (y_mid_full,) = kernel(
            functools.partial(whole_of, 2 * COLS), [(s1, 2 * COLS)], after(parts[0], send), *parts[1:]
        )
        (cut_root,) = kernel(add, [(n2 // 4, LANES)], after(keep, mu, y_mid_full), came)
    with jax.named_scope("root_solve"):
        parts, (ru,) = gather_front(cut_root, lambda x: load((after(root_upper_inv, *x), None)))
        (y_root,) = gathered(packed_to, COLS, [(n2 // 4, LANES)], rl, parts)
        parts, (m2r_up, l2m_up, lu) = gather_front(
            y_root,
            lambda x: load(
                (after(mid_to_root_upper, *x), "own"), (leaf_to_mid_upper, "leaf"), (leaf_upper_inv, "leaf")
            ),
        )
        (x_root,) = gathered(packed_to, COLS, [(n2 // 4, LANES)], ru, parts)
    with jax.named_scope("mid_upper"):
        send, *x_halves = kernel(
            root_to_mid,
            [(s1 // 4, LANES), (n2 // 4, LANES), (n2 // 4, LANES)],
            m2r_up,
            x_root,
            swap("leaf", x_root, 2),
        )
        (keep,) = kernel(root_to_mid_kept, [(s1 // 4, LANES)], m2r_up, *x_halves)
        came = [swap("leaf", after(half, send), 1) for half in x_halves]
        mine, theirs = sum_front(keep, send, (came[0],), (came[1],))
        (known,) = kernel(functools.partial(own_half, 2 * COLS), [(2 * n1, 4 * COLS)], mu, y_mid_full, mine)
        (x_mid,) = kernel(mid_upper, [(n1 // 2, LANES)], mu, y_mid_full, theirs, known)
        from_root, root_field, root_adjoint = kernel(
            root_to_leaf,
            [(s0, LANES), (2, COLS, n2), (2, COLS, n2)],
            l2r_up,
            *x_halves,
            *came,
        )
    with jax.named_scope("leaf_upper"):
        x_far = swap("leaf", x_mid, 2)
        send, x_mid = kernel(
            mid_to_leaf,
            [(s0 // 2, LANES), (n1, LANES)],
            l2m_up,
            from_root,
            x_mid,
            swap("leaf", x_mid, 1),
        )
        (keep,) = kernel(mid_to_leaf_kept, [(s0 // 2, LANES)], l2m_up, from_root, x_mid)
        x_other = swap("leaf", x_far, 1)
        mid_field, mid_adjoint = kernel(
            mid_outputs, [(2, 2, COLS, n1)] * 2, x_mid, x_far, x_other
        )
        mine, theirs = sum_front(keep, send, (x_far,), (x_other,))
        (known,) = kernel(functools.partial(own_half, LANES), [(2 * n0, 2 * LANES)], lu, y_full, mine)
        leaf_field, leaf_adjoint = kernel(
            leaf_upper, [(2, COLS, n0)] * 2, lu, y_full, theirs, after(known, mid_field)
        )
    return tuple(
        jnp.swapaxes(x, -1, -2)
        for x in (leaf_field, mid_field, root_field, leaf_adjoint, mid_adjoint, root_adjoint)
    )


def solution(mesh):
    in_specs = (
        P(None, "leaf", "front", None),
        P(None, "leaf", "front", None),
        P(None, "leaf", "front", None),
        P(None, "leaf", "front", None),
        P(None, "leaf", None, "front"),
        P(None, "leaf", None, "front"),
        P(None, None, "front", None),
        P(None, None, "front", None),
        P(None, None, "front", None),
        P(None, None, None, "front"),
        P(None, "front", None),
        P(None, "front", None),
        P(None, ("leaf", "front"), None),
        P(None, None, "front", None),
        P(None, "front", None),
        P(None, ("leaf", "front"), None),
        P(("leaf", "front"), None),
        P(("leaf", "front")),
    )
    out_specs = (
        P(None, ("leaf", "front"), None),
        P(None, None, "front", None),
        P(None, "front", None),
        P(None, ("leaf", "front"), None),
        P(None, None, "front", None),
        P(None, "front", None),
    )
    return jax.shard_map(body, mesh=mesh, in_specs=in_specs, out_specs=out_specs, check_vma=False)
```

```python
import functools

import jax
import jax.numpy as jnp
from jax import lax
from jax.experimental import pallas as pl
from jax.experimental.pallas import tpu as pltpu
from jax.sharding import PartitionSpec as P

CAP = 2
CHUNKS = 4
LANES = 128
COLS = 32
F32 = jnp.float32
BF16 = jnp.bfloat16
VM = pl.BlockSpec(memory_space=pltpu.VMEM)
HB = pl.BlockSpec(memory_space=pltpu.HBM)


def split(x):
    high = x.astype(BF16)
    return high, (x - high.astype(F32)).astype(BF16)


def dot(a, b):
    return jnp.dot(a, b, preferred_element_type=F32)


def complex_dot(matrix, x):
    half = x.shape[1] // 2
    turned = jnp.concatenate([-x[:, half:], x[:, :half]], axis=1)
    both = jnp.concatenate([x, turned], axis=0)
    columns = jnp.concatenate(split(both), axis=1)
    product = dot(matrix, columns)
    rows, n = product.shape[0] // 2, x.shape[1]
    return (product[:rows, n:] + product[rows:, :n]) + product[:rows, :n]


def combined(product):
    rows, n = product.shape[0] // 2, product.shape[1] // 2
    return (product[:rows, n:] + product[rows:, :n]) + product[:rows, :n]


def turn(x, width):
    half = width // 2
    lane = lax.broadcasted_iota(jnp.int32, x.shape, 1) % width
    return jnp.where(lane < half, -pltpu.roll(x, LANES - half, 1), pltpu.roll(x, half, 1))


def spread(x, width):
    high, low = split(x)
    return jnp.concatenate(
        [
            jnp.concatenate([high[:, at : at + width], low[:, at : at + width]], axis=1)
            for at in range(0, LANES, width)
        ],
        axis=0,
    )


def part_dot(matrix, at, blocks, width):
    depth = matrix.shape[1] // 2
    columns = jnp.concatenate([spread(x, width) for x in blocks], axis=0)
    turned = jnp.concatenate([spread(turn(x, width), width) for x in blocks], axis=0)
    count, at = columns.shape[0], pl.multiple_of(at, LANES)
    return dot(matrix[:, pl.ds(at, count)], columns) + dot(matrix[:, pl.ds(depth + at, count)], turned)


def pack(x):
    chunks = LANES // x.shape[1]
    rows = x.shape[0] // chunks
    return jnp.concatenate([x[rows * j : rows * j + rows] for j in range(chunks)], axis=1)


def unpack(x, width):
    return jnp.concatenate([x[:, at : at + width] for at in range(0, LANES, width)], axis=0)


def halves(x):
    c = COLS
    return (
        jnp.concatenate([x[:, :c], x[:, 2 * c : 3 * c]], axis=1),
        jnp.concatenate([x[:, c : 2 * c], x[:, 3 * c :]], axis=1),
    )


def joined(forward, adjoint):
    c = COLS
    return jnp.concatenate([forward[:, :c], adjoint[:, :c], forward[:, c:], adjoint[:, c:]], axis=1)


def own_first(group, forward, adjoint):
    even = (group & 1) == 0
    return jnp.where(even, forward, adjoint), jnp.where(even, adjoint, forward)


def by_solve(group, own, other):
    even = (group & 1) == 0
    return joined(jnp.where(even, own, other), jnp.where(even, other, own))


def assemble(where, parts, here, width=LANES):
    rows = parts[0].shape[0] * (LANES // width)
    for k, part in blocks_of(parts):
        start = pl.multiple_of((here ^ k) * rows, 8)
        where[pl.ds(start, rows), :] = part[...] if width == LANES else unpack(part[...], width)


def fields_of(x, forward, adjoint, where):
    y = x.T
    c = COLS
    forward[(0, *where)] = y[0:c]
    forward[(1, *where)] = y[2 * c : 3 * c]
    adjoint[(0, *where)] = y[c : 2 * c]
    adjoint[(1, *where)] = -y[3 * c :]


def swap(axis, x, k):
    size = lax.axis_size(axis)
    return lax.ppermute(x, axis, [(i, i ^ k) for i in range(size)])


def stack(*refs):
    at = 0
    for ref in refs[:-1]:
        refs[-1][at : at + ref.shape[0], :] = ref[...]
        at += ref.shape[0]


def hops(fronts):
    return [2, 6, 4] if fronts == 8 else list(range(2, fronts, 2))


def gather_front(x, meanwhile=None, others=()):
    fronts = lax.axis_size("front")
    *near, last = [swap("front", x, k) for k in hops(fronts)]
    own = swap("front", x, 1)
    (both,) = kernel(stack, [(len(near) * x.shape[0], LANES)], *near)
    extra = tuple(meanwhile((both, own))) if meanwhile else ()
    last = after(last, *extra, *others)
    return [x, own, last, *near[::-1], swap("front", last, 1), swap("front", both, 1)], extra


def blocks_of(parts):
    rows = parts[0].shape[0]
    *near, last = hops(2 * len(parts) - 6)
    yield 0, parts[0]
    yield 1, parts[1]
    yield last, parts[2]
    yield last + 1, parts[-2]
    for step, (k, part) in enumerate(zip(near, parts[-3:2:-1])):
        yield k, part
        yield k + 1, parts[-1].at[rows * step : rows * step + rows, :]


def kernel(fn, outs, *args, scratch=(), vmem=8, work=0, hbm=(), pinned=()):
    outs = [o if isinstance(o[0], tuple) else (o, F32) for o in outs]
    return pl.pallas_call(
        fn,
        out_shape=[jax.ShapeDtypeStruct(*o) for o in outs],
        in_specs=[HB if i in hbm else VM for i in range(len(args))],
        out_specs=[VM] * len(outs),
        scratch_shapes=list(scratch),
        compiler_params=pltpu.CompilerParams(vmem_limit_bytes=vmem * 2**20),
        cost_estimate=pl.CostEstimate(flops=work, bytes_accessed=work // 700, transcendentals=0),
    )(*(pltpu.with_memory_space_constraint(a, pltpu.HBM) if i in pinned else a for i, a in enumerate(args)))


def chip_product(matrix, k, mine, other, width):
    here = lax.axis_index("front")
    odd = (here & 1) == 1
    blocks = [jnp.where(odd, other, mine), jnp.where(odd, mine, other)]
    return part_dot(matrix, ((here ^ k) // 2) * (2 * mine.shape[0] * (LANES // width)), blocks, width)


def first_products(width, matrix, mine, other, *refs):
    near, both, out = refs[:-2], refs[-2], refs[-1]
    rows = mine.shape[0]
    total = chip_product(matrix, 0, mine[...], other[...], width)
    for step, (k, block) in enumerate(zip(hops(lax.axis_size("front")), near)):
        second = both[rows * step : rows * step + rows, :]
        total += chip_product(matrix, k, block[...], second, width)
    out[...] = total


def last_product(finish, width, count, matrix, *refs):
    parts, rest = refs[:count], refs[count:]
    if count == 3:
        known, mine, other = parts
        k = hops(lax.axis_size("front"))[-1]
        finish(combined(known[...] + chip_product(matrix, k, mine[...], other[...], width)), *rest)
    else:
        assemble(rest[-1], parts, lax.axis_index("front"), width)
        finish(complex_dot(matrix[...], rest[-1][...]), *rest[:-1])


def gathered(finish, width, outs, matrix, parts, *args):
    rows = parts[0].shape[0] * (LANES // width)
    scratch = []
    if 2 * rows % LANES == 0:
        mine, other, last, *near, last_other, both = parts
        shape = (matrix.shape[0], 2 * width)
        (known,) = kernel(
            functools.partial(first_products, width), [shape], matrix, mine, other, *near[::-1], both
        )
        parts = [known, last, last_other]
    else:
        scratch = [pltpu.VMEM((rows * lax.axis_size("front"), width), F32)]
    return kernel(
        functools.partial(last_product, finish, width, len(parts)),
        outs,
        matrix,
        *parts,
        *args,
        scratch=scratch,
    )


def whole_of(width, *refs):
    assemble(refs[-1], refs[:-1], lax.axis_index("front"), width)


def half_product(theirs, width, matrix, y, piece):
    odd = (lax.axis_index("front") & 1) ^ theirs
    rows, chunks = piece.shape[0], LANES // width
    starts = [chunk * 2 * rows + odd * rows for chunk in range(chunks)]
    own = [y[pl.ds(pl.multiple_of(at, 8), rows), :] for at in starts]
    x = jnp.concatenate(own, axis=1) - piece[...]
    if chunks == 1:
        return part_dot(matrix, starts[0], [x], width)
    total, depth = None, matrix.shape[1] // 2
    columns, turned = spread(x, width), spread(turn(x, width), width)
    for chunk, at in enumerate(starts):
        at, span = pl.multiple_of(at, LANES), slice(rows * chunk, rows * chunk + rows)
        part = dot(matrix[:, pl.ds(at, rows)], columns[span])
        part += dot(matrix[:, pl.ds(depth + at, rows)], turned[span])
        total = part if total is None else total + part
    return total


def own_half(width, matrix, y, piece, out):
    out[...] = half_product(0, width, matrix, y, piece)


def load_matrices(picks, *refs):
    count = len(picks)
    sources, outs, buffers, sems = (
        refs[:count],
        refs[count : 2 * count],
        refs[2 * count : 3 * count],
        refs[3 * count],
    )
    parent = lax.axis_index("leaf") // 2
    copies = []
    for i, (src, pick) in enumerate(zip(sources, picks)):
        rows = buffers[i].shape[1]
        step = max(rows // CHUNKS, 16)
        for n, at in enumerate(range(0, rows, step)):
            span = pl.ds(at, step)
            view = src.at[:, span, :] if pick is None else src.at[:, parent if pick == "own" else 0, span, :]
            copy = pltpu.make_async_copy(view, buffers[i].at[:, span, :], sems.at[CHUNKS * i + n])
            copy.start()
            copies.append((i, at, step, copy))
    for i, at, step, copy in copies:
        copy.wait()
        rows, depth = buffers[i].shape[1:]
        for part in range(2):
            high, low = split(buffers[i][part, at : at + step, :])
            outs[i][at : at + step, part * depth : part * depth + depth] = high
            outs[i][rows + at : rows + at + step, part * depth : part * depth + depth] = low


def load(*matrices, pinned=False):
    shapes = [m.shape[-2:] for m, _ in matrices]
    size = sum(r * d for r, d in shapes)
    return kernel(
        functools.partial(load_matrices, tuple(pick for _, pick in matrices)),
        [((2 * r, 2 * d), BF16) for r, d in shapes],
        *[m for m, _ in matrices],
        scratch=[pltpu.VMEM((2, r, d), F32) for r, d in shapes]
        + [pltpu.SemaphoreType.DMA((CHUNKS * len(shapes),))],
        hbm=range(len(shapes)),
        pinned=range(len(shapes)) if pinned else (),
        vmem=4 + -(-size * 8 // 2**20),
        work=size * 1000,
    )


def pack_receivers(fronts, rows, data_hbm, block_hbm, offset_hbm, *refs):
    own, far, near = refs[:3]
    data, block, offset, sems = refs[3:]
    copies = [
        pltpu.make_async_copy(src, dst, sems.at[i])
        for i, (src, dst) in enumerate(((data_hbm, data), (block_hbm, block), (offset_hbm, offset)))
    ]
    for copy in copies:
        copy.start()
    for copy in copies:
        copy.wait()
    group = lax.axis_index("leaf")
    count = data.shape[1]
    slots = fronts * CAP
    down = lax.broadcasted_iota(jnp.int32, (count, count), 0)
    across = lax.broadcasted_iota(jnp.int32, (count, count), 1)
    eye = down == across
    block_row = block[...]
    block_col = jnp.sum(jnp.where(eye, block_row, 0), axis=1, keepdims=True)
    offset_col = jnp.sum(jnp.where(eye, offset[...], 0), axis=1, keepdims=True)
    same = (block_col == block_row) & (down < across)
    slot_row = block_row * CAP + jnp.sum(same.astype(jnp.int32), axis=0, keepdims=True)
    row_col = (block_col & (fronts - 1)) * rows + offset_col + 1
    lane = lax.broadcasted_iota(jnp.int32, (count, COLS), 1)
    index = jnp.where(lane == 0, row_col, 0).astype(F32)
    lines = jnp.concatenate([index, data[0], jnp.zeros((count, COLS), F32), -data[1]], axis=1)
    targets = [group, group ^ 2, group ^ 1, group ^ 3]
    place = lax.broadcasted_iota(jnp.int32, (slots, count), 0)
    pick = jnp.concatenate([place + target * slots == slot_row for target in targets], axis=0)
    picked = jnp.dot(
        pick.astype(F32), lines, precision=lax.Precision.HIGHEST, preferred_element_type=F32
    )
    own[...] = picked[:slots]
    far[...] = picked[slots : 2 * slots]
    near[...] = picked[2 * slots :]


def pass_on(far, came, out):
    rows = far.shape[0]
    out[0:rows, :] = far[...]
    out[rows:, :] = came[rows:, :]


def load_sources(leaf_hbm, mid_hbm, root_hbm, leaf_out, mid_out, root_out, leaf, mid, root, sems):
    group = lax.axis_index("leaf")
    copies = [
        pltpu.make_async_copy(src, dst, sems.at[i])
        for i, (src, dst) in enumerate(
            ((leaf_hbm, leaf), (mid_hbm.at[:, group // 2], mid), (root_hbm, root))
        )
    ]
    for copy in copies:
        copy.start()
    for copy in copies:
        copy.wait()
    forward = ((group & 1) == 0).astype(F32)
    real, imag = leaf[0].T, leaf[1].T
    zero = jnp.zeros_like(real)
    leaf_out[...] = jnp.concatenate([real, zero, imag, zero], axis=1)
    mid_out[...] = pack(jnp.concatenate([mid[0], mid[1]], axis=0).T) * forward
    width = COLS // 2
    low = jnp.concatenate([root[0, :width], root[1, :width]], axis=0)
    high = jnp.concatenate([root[0, width:], root[1, width:]], axis=0)
    root_out[...] = pack(jnp.where(group < 2, low, high).T) * forward


def message_rows(rows, slots):
    return max(rows, slots), 8 * -(-slots // (8 * LANES))


def pack_leaf(own, mine, near, far, out):
    lines = jnp.concatenate([mine[...], near[0 : mine.shape[0], :], far[...]], axis=0)
    slots = lines.shape[0]
    body, tail = message_rows(own.shape[0], slots)
    lane = lax.broadcasted_iota(jnp.int32, (slots, LANES), 1)
    data = jnp.where((lane // COLS) % 2 == 1, lines, 0.0)
    index = lines[:, 0:1]

    def padded(x):
        if x.shape[0] == body:
            return x
        return jnp.concatenate([x, jnp.zeros((body - x.shape[0], LANES), F32)], axis=0)

    out[0:body, :] = padded(own[...]) + padded(data)
    out[body:, :] = jnp.zeros((tail, LANES), F32)
    for at in range(0, slots, LANES):
        size = min(LANES, slots - at)
        eye = lax.broadcasted_iota(jnp.int32, (size, size), 0) == lax.broadcasted_iota(
            jnp.int32, (size, size), 1
        )
        line = jnp.sum(jnp.where(eye, index[at : at + size], 0.0), axis=0, keepdims=True)
        out[body + at // LANES : body + at // LANES + 1, 0:size] = line


def leaf_lower(slots, matrix, *refs):
    parts, (out, rhs, messages) = refs[:-3], refs[-3:]
    rows = out.shape[0]
    here = lax.axis_index("front")
    for k, part in blocks_of(parts):
        messages[here ^ k] = part[...]
    fronts = messages.shape[0]
    total = rows * fronts
    body, _ = message_rows(rows, slots)
    lane = lax.broadcasted_iota(jnp.int32, (slots, LANES), 1)
    taken = (lane // COLS) % 2 == 1
    own = lax.broadcasted_iota(jnp.int32, (rows, LANES), 1)
    own = (own // COLS) % 2 == 0
    for k in range(fronts):
        rhs[rows * k : rows * k + rows, :] = jnp.where(own, messages[k, 0:rows, :], 0.0)
    group = max(1, 512 // slots)
    for k in range(0, fronts, group):
        chosen = range(k, min(k + group, fronts))
        lines = jnp.concatenate([jnp.where(taken, messages[i, 0:slots, :], 0.0) for i in chosen], axis=0)
        index = jnp.concatenate(
            [
                messages[i, body + at // LANES : body + at // LANES + 1, 0 : min(LANES, slots - at)]
                for i in chosen
                for at in range(0, slots, LANES)
            ],
            axis=1,
        )
        row = lax.broadcasted_iota(jnp.int32, (total, index.shape[1]), 0)
        pick = (row + 1 == index.astype(jnp.int32)).astype(BF16)
        both = dot(pick, jnp.concatenate(split(lines), axis=1))
        rhs[...] += both[:, :LANES] + both[:, LANES:]
    out[...] = complex_dot(matrix[...], rhs[...])


def leaf_to_mid(value, sources, keep, send):
    mine, theirs = own_first(lax.axis_index("leaf"), *halves(value))
    keep[...] = sources[...] - pack(mine)
    send[...] = -pack(theirs)


def leaf_to_root(matrix, *refs):
    parts, (keep, send, full) = refs[:-3], refs[-3:]
    assemble(full, parts, lax.axis_index("front"))
    mine, theirs = own_first(lax.axis_index("leaf"), *halves(complex_dot(matrix[...], full[...])))
    keep[...], send[...] = pack(mine), pack(theirs)


def add(*refs):
    total = refs[0][...]
    for ref in refs[1:-1]:
        total = total + ref[...]
    refs[-1][...] = total


def packed_to(value, out):
    out[...] = pack(value)


def mid_to_root(value, kept, came, sources, keep, send):
    cut = -(unpack(kept[...] + came[...], 2 * COLS) + value)
    width = COLS // 2
    low = pack(jnp.concatenate([cut[:, :width], cut[:, COLS : COLS + width]], axis=1))
    high = pack(jnp.concatenate([cut[:, width:COLS], cut[:, COLS + width :]], axis=1))
    first = lax.axis_index("leaf") < 2
    keep[...] = jnp.where(first, low, high) + sources[...]
    send[...] = jnp.where(first, high, low)


def column_half(matrix, x, theirs):
    core = (lax.axis_index("front") & 1) ^ theirs
    half, n = x.shape[1] // 2, x.shape[1]
    turned = jnp.concatenate([-x[:, half:], x[:, :half]], axis=1)
    columns = jnp.concatenate(split(jnp.concatenate([x, turned], axis=0)), axis=1)
    height, chunks = matrix.shape[0] // 2, LANES // n
    rows, pieces = height // chunks // 2, []
    for chunk in range(chunks):
        at = pl.multiple_of((2 * chunk + core) * rows, 16)
        high = dot(matrix[pl.ds(at, rows), :], columns)
        low = dot(matrix[pl.ds(height + at, rows), :], columns[:, :n])
        pieces.append((high[:, n:] + low) + high[:, :n])
    return jnp.concatenate(pieces, axis=1)


def root_to_mid(matrix, mine, other, send, x_root):
    first = lax.axis_index("leaf") < 2
    mine, other = unpack(mine[...], COLS), unpack(other[...], COLS)
    low, high = jnp.where(first, mine, other), jnp.where(first, other, mine)
    width = COLS // 2
    x = jnp.concatenate([low[:, :width], high[:, :width], low[:, width:], high[:, width:]], axis=1)
    x_root[...] = pack(x)
    send[...] = column_half(matrix, x, 1)


def root_to_mid_kept(matrix, x_root, keep):
    keep[...] = column_half(matrix, unpack(x_root[...], 2 * COLS), 0)


def root_to_leaf(matrix, mine, other, out, forward, adjoint):
    x = by_solve(lax.axis_index("leaf"), unpack(mine[...], 2 * COLS), unpack(other[...], 2 * COLS))
    out[...] = complex_dot(matrix[...], x)
    fields_of(x, forward, adjoint, ())


def sum_front(kept, sent, before_last=(), at_end=()):
    fronts = lax.axis_size("front")
    (total,) = kernel(add, [kept.shape], kept, swap("front", sent, 1))
    hops = [1 << i for i in range(1, fronts.bit_length() - 1)]
    for hop, back in zip(hops, hops[::-1]):
        pairs = [(i, i ^ (back if i & 1 else hop)) for i in range(fronts)]
        if hop == hops[-1]:
            total = after(total, *before_last)
        (total,) = kernel(add, [kept.shape], total, lax.ppermute(total, "front", pairs))
    return [total, swap("front", after(total, *at_end), 1)]


def mid_upper(matrix, y, piece, known, out):
    out[...] = pack(combined(known[...] + half_product(1, 2 * COLS, matrix, y, piece)))


def core_rows(ref, theirs):
    rows = ref.shape[0] // 2
    core = (lax.axis_index("front") & 1) ^ theirs
    return ref[pl.ds(pl.multiple_of(core * rows, 8), rows), :]


def mid_to_leaf(matrix, from_root, mine, other, send, x_mid):
    x = by_solve(lax.axis_index("leaf"), unpack(mine[...], 2 * COLS), unpack(other[...], 2 * COLS))
    x_mid[...] = x
    send[...] = column_half(matrix, x, 1) + core_rows(from_root, 1)


def mid_to_leaf_kept(matrix, from_root, x_mid, keep):
    keep[...] = column_half(matrix, x_mid[...], 0) + core_rows(from_root, 0)


def leaf_upper(matrix, y, piece, known, forward, adjoint):
    fields_of(combined(known[...] + half_product(1, LANES, matrix, y, piece)), forward, adjoint, ())


def mid_outputs(mine, far, other, forward, adjoint):
    parent = lax.axis_index("leaf") // 2
    x = by_solve(lax.axis_index("leaf"), unpack(far[...], 2 * COLS), unpack(other[...], 2 * COLS))
    fields_of(mine[...], forward, adjoint, (parent,))
    fields_of(x, forward, adjoint, (1 - parent,))


def after(x, *others):
    return lax.optimization_barrier((x, *others))[0]


def body(
    leaf_lower_inv,
    leaf_upper_inv,
    leaf_to_mid_lower,
    leaf_to_root_lower,
    leaf_to_mid_upper,
    leaf_to_root_upper,
    mid_lower_inv,
    mid_upper_inv,
    mid_to_root_lower,
    mid_to_root_upper,
    root_lower_inv,
    root_upper_inv,
    leaf_sources,
    mid_sources,
    root_sources,
    receiver_data,
    receiver_block,
    receiver_offset,
):
    groups, fronts = lax.axis_size("leaf"), lax.axis_size("front")
    n0, n1, n2 = leaf_sources.shape[1], mid_sources.shape[2], root_sources.shape[1]
    s0, s1, s2 = n0 * fronts, n1 * fronts, n2 * fronts
    slots, count = fronts * CAP, receiver_data.shape[1]
    dma = pltpu.SemaphoreType.DMA

    with jax.named_scope("right_hand_sides"):
        payload = kernel(
            functools.partial(pack_receivers, fronts, n0),
            [(slots, LANES), (slots, LANES), (2 * slots, LANES)],
            receiver_data,
            receiver_block.reshape(1, -1),
            receiver_offset.reshape(1, -1),
            scratch=[
                pltpu.VMEM((2, count, COLS), F32),
                pltpu.VMEM((1, count), jnp.int32),
                pltpu.VMEM((1, count), jnp.int32),
                dma((3,)),
            ],
            hbm=range(3),
            pinned=range(3),
        )
        own, far, near = payload
        came = swap("leaf", near, 1)
        (both,) = kernel(pass_on, [(2 * slots, LANES)], far, came)
        arrived = [own, came, swap("leaf", both, 2)]
        leaf_own, mid_own, root_own = kernel(
            load_sources,
            [(n0, LANES), (n1 // 2, LANES), (n2 // 4, LANES)],
            after(leaf_sources.transpose(0, 2, 1), *payload),
            mid_sources.transpose(0, 1, 3, 2),
            root_sources.transpose(0, 2, 1),
            scratch=[
                pltpu.VMEM((2, COLS, n0), F32),
                pltpu.VMEM((2, COLS, n1), F32),
                pltpu.VMEM((2, COLS, n2), F32),
                dma((3,)),
            ],
            hbm=range(3),
            pinned=range(3),
        )
        (message,) = kernel(
            pack_leaf, [(sum(message_rows(n0, groups * slots)), LANES)], leaf_own, *arrived
        )
    with jax.named_scope("leaf_lower"):
        messages, (ll, l2m) = gather_front(
            message,
            lambda x: load((after(leaf_lower_inv, *x), "leaf"), (leaf_to_mid_lower, "leaf"), pinned=True),
        )
        (y_leaf,) = kernel(
            functools.partial(leaf_lower, groups * slots),
            [(n0, LANES)],
            ll,
            *messages,
            scratch=[pltpu.VMEM((s0, LANES), F32), pltpu.VMEM((fronts, *message.shape), F32)],
        )
    with jax.named_scope("mid_lower"):
        parts, (l2r, ml) = gather_front(
            y_leaf,
            lambda x: load((after(leaf_to_root_lower, *x), "leaf"), (mid_lower_inv, "own"), pinned=True),
        )
        keep, send = gathered(leaf_to_mid, LANES, [(n1 // 2, LANES)] * 2, l2m, parts, mid_own)
        came = swap("leaf", send, 1)
        root_kept, root_sent, y_full = kernel(
            leaf_to_root, [(n2 // 2, LANES)] * 2 + [(s0, LANES)], l2r, after(parts[0], send), *parts[1:]
        )
        (cut_mid,) = kernel(add, [(n1 // 2, LANES)], after(keep, root_kept), came)
        root_came = swap("leaf", root_sent, 1)
        parts, (m2r,) = gather_front(
            cut_mid, lambda x: load((after(mid_to_root_lower, *x), "own"), pinned=True), (root_came,)
        )
        (y_mid,) = gathered(packed_to, 2 * COLS, [(n1 // 2, LANES)], ml, parts)
    with jax.named_scope("root_cut"):
        parts, (rl,) = gather_front(y_mid, lambda x: load((after(root_lower_inv, *x), None)))
        keep, send = gathered(
            mid_to_root, 2 * COLS, [(n2 // 4, LANES)] * 2, m2r, parts, root_kept, root_came, root_own
        )
        came = swap("leaf", send, 2)
        mu, l2r_up = load((after(mid_upper_inv, send), "own"), (leaf_to_root_upper, "leaf"))
        (y_mid_full,) = kernel(
            functools.partial(whole_of, 2 * COLS), [(s1, 2 * COLS)], after(parts[0], send), *parts[1:]
        )
        (cut_root,) = kernel(add, [(n2 // 4, LANES)], after(keep, mu, y_mid_full), came)
    with jax.named_scope("root_solve"):
        parts, (ru,) = gather_front(cut_root, lambda x: load((after(root_upper_inv, *x), None)))
        (y_root,) = gathered(packed_to, COLS, [(n2 // 4, LANES)], rl, parts)
        parts, (m2r_up, l2m_up, lu) = gather_front(
            y_root,
            lambda x: load(
                (after(mid_to_root_upper, *x), "own"), (leaf_to_mid_upper, "leaf"), (leaf_upper_inv, "leaf")
            ),
        )
        (x_root,) = gathered(packed_to, COLS, [(n2 // 4, LANES)], ru, parts)
    with jax.named_scope("mid_upper"):
        send, x_root = kernel(
            root_to_mid,
            [(s1 // 4, LANES), (n2 // 2, LANES)],
            m2r_up,
            x_root,
            swap("leaf", x_root, 2),
        )
        (keep,) = kernel(root_to_mid_kept, [(s1 // 4, LANES)], m2r_up, x_root)
        mine, theirs = sum_front(keep, send)
        (known,) = kernel(functools.partial(own_half, 2 * COLS), [(2 * n1, 4 * COLS)], mu, y_mid_full, mine)
        (x_mid,) = kernel(mid_upper, [(n1 // 2, LANES)], mu, y_mid_full, theirs, known)
        from_root, root_field, root_adjoint = kernel(
            root_to_leaf,
            [(s0, LANES), (2, COLS, n2), (2, COLS, n2)],
            l2r_up,
            x_root,
            swap("leaf", after(x_root, send), 1),
        )
    with jax.named_scope("leaf_upper"):
        x_far = swap("leaf", x_mid, 2)
        send, x_mid = kernel(
            mid_to_leaf,
            [(s0 // 2, LANES), (n1, LANES)],
            l2m_up,
            from_root,
            x_mid,
            swap("leaf", x_mid, 1),
        )
        (keep,) = kernel(mid_to_leaf_kept, [(s0 // 2, LANES)], l2m_up, from_root, x_mid)
        x_other = swap("leaf", x_far, 1)
        mid_field, mid_adjoint = kernel(
            mid_outputs, [(2, 2, COLS, n1)] * 2, x_mid, x_far, x_other
        )
        mine, theirs = sum_front(keep, send, (x_far,), (x_other,))
        (known,) = kernel(functools.partial(own_half, LANES), [(2 * n0, 2 * LANES)], lu, y_full, mine)
        leaf_field, leaf_adjoint = kernel(
            leaf_upper, [(2, COLS, n0)] * 2, lu, y_full, theirs, after(known, mid_field)
        )
    return tuple(
        jnp.swapaxes(x, -1, -2)
        for x in (leaf_field, mid_field, root_field, leaf_adjoint, mid_adjoint, root_adjoint)
    )


def solution(mesh):
    in_specs = (
        P(None, "leaf", "front", None),
        P(None, "leaf", "front", None),
        P(None, "leaf", "front", None),
        P(None, "leaf", "front", None),
        P(None, "leaf", None, "front"),
        P(None, "leaf", None, "front"),
        P(None, None, "front", None),
        P(None, None, "front", None),
        P(None, None, "front", None),
        P(None, None, None, "front"),
        P(None, "front", None),
        P(None, "front", None),
        P(None, ("leaf", "front"), None),
        P(None, None, "front", None),
        P(None, "front", None),
        P(None, ("leaf", "front"), None),
        P(("leaf", "front"), None),
        P(("leaf", "front")),
    )
    out_specs = (
        P(None, ("leaf", "front"), None),
        P(None, None, "front", None),
        P(None, "front", None),
        P(None, ("leaf", "front"), None),
        P(None, None, "front", None),
        P(None, "front", None),
    )
    return jax.shard_map(body, mesh=mesh, in_specs=in_specs, out_specs=out_specs, check_vma=False)
```

```python
import functools

import jax
import jax.numpy as jnp
from jax import lax
from jax.experimental import pallas as pl
from jax.experimental.pallas import tpu as pltpu
from jax.sharding import PartitionSpec as P

CAP = 2
CHUNKS = 4
LANES = 128
COLS = 32
F32 = jnp.float32
BF16 = jnp.bfloat16
VM = pl.BlockSpec(memory_space=pltpu.VMEM)
HB = pl.BlockSpec(memory_space=pltpu.HBM)


def split(x):
    high = x.astype(BF16)
    return high, (x - high.astype(F32)).astype(BF16)


def dot(a, b):
    return jnp.dot(a, b, preferred_element_type=F32)


def complex_dot(matrix, x):
    half = x.shape[1] // 2
    turned = jnp.concatenate([-x[:, half:], x[:, :half]], axis=1)
    both = jnp.concatenate([x, turned], axis=0)
    columns = jnp.concatenate(split(both), axis=1)
    product = dot(matrix, columns)
    rows, n = product.shape[0] // 2, x.shape[1]
    return (product[:rows, n:] + product[rows:, :n]) + product[:rows, :n]


def combined(product):
    rows, n = product.shape[0] // 2, product.shape[1] // 2
    return (product[:rows, n:] + product[rows:, :n]) + product[:rows, :n]


def turn(x, width):
    half = width // 2
    lane = lax.broadcasted_iota(jnp.int32, x.shape, 1) % width
    return jnp.where(lane < half, -pltpu.roll(x, LANES - half, 1), pltpu.roll(x, half, 1))


def spread(x, width):
    high, low = split(x)
    return jnp.concatenate(
        [
            jnp.concatenate([high[:, at : at + width], low[:, at : at + width]], axis=1)
            for at in range(0, LANES, width)
        ],
        axis=0,
    )


def part_dot(matrix, at, blocks, width):
    depth = matrix.shape[1] // 2
    columns = jnp.concatenate([spread(x, width) for x in blocks], axis=0)
    turned = jnp.concatenate([spread(turn(x, width), width) for x in blocks], axis=0)
    count, at = columns.shape[0], pl.multiple_of(at, LANES)
    return dot(matrix[:, pl.ds(at, count)], columns) + dot(matrix[:, pl.ds(depth + at, count)], turned)


def pack(x):
    chunks = LANES // x.shape[1]
    rows = x.shape[0] // chunks
    return jnp.concatenate([x[rows * j : rows * j + rows] for j in range(chunks)], axis=1)


def unpack(x, width):
    return jnp.concatenate([x[:, at : at + width] for at in range(0, LANES, width)], axis=0)


def halves(x):
    c = COLS
    return (
        jnp.concatenate([x[:, :c], x[:, 2 * c : 3 * c]], axis=1),
        jnp.concatenate([x[:, c : 2 * c], x[:, 3 * c :]], axis=1),
    )


def joined(forward, adjoint):
    c = COLS
    return jnp.concatenate([forward[:, :c], adjoint[:, :c], forward[:, c:], adjoint[:, c:]], axis=1)


def own_first(group, forward, adjoint):
    even = (group & 1) == 0
    return jnp.where(even, forward, adjoint), jnp.where(even, adjoint, forward)


def by_solve(group, own, other):
    even = (group & 1) == 0
    return joined(jnp.where(even, own, other), jnp.where(even, other, own))


def assemble(where, parts, here, width=LANES):
    rows = parts[0].shape[0] * (LANES // width)
    for k, part in blocks_of(parts):
        start = pl.multiple_of((here ^ k) * rows, 8)
        where[pl.ds(start, rows), :] = part[...] if width == LANES else unpack(part[...], width)


def fields_of(x, forward, adjoint, where):
    y = x.T
    c = COLS
    forward[(0, *where)] = y[0:c]
    forward[(1, *where)] = y[2 * c : 3 * c]
    adjoint[(0, *where)] = y[c : 2 * c]
    adjoint[(1, *where)] = -y[3 * c :]


def swap(axis, x, k):
    size = lax.axis_size(axis)
    return lax.ppermute(x, axis, [(i, i ^ k) for i in range(size)])


def stack(*refs):
    at = 0
    for ref in refs[:-1]:
        refs[-1][at : at + ref.shape[0], :] = ref[...]
        at += ref.shape[0]


def hops(fronts):
    return [2, 6, 4] if fronts == 8 else list(range(2, fronts, 2))


def gather_front(x, meanwhile=None, others=()):
    fronts = lax.axis_size("front")
    *near, last = [swap("front", x, k) for k in hops(fronts)]
    own = swap("front", x, 1)
    extra = tuple(meanwhile((own,))) if meanwhile else ()
    (both,) = kernel(stack, [(len(near) * x.shape[0], LANES)], *near[:-1], after(near[-1], *extra))
    last = after(last, *extra, *others)
    return [x, own, last, *near[::-1], swap("front", last, 1), swap("front", both, 1)], extra


def blocks_of(parts):
    rows = parts[0].shape[0]
    *near, last = hops(2 * len(parts) - 6)
    yield 0, parts[0]
    yield 1, parts[1]
    yield last, parts[2]
    yield last + 1, parts[-2]
    for step, (k, part) in enumerate(zip(near, parts[-3:2:-1])):
        yield k, part
        yield k + 1, parts[-1].at[rows * step : rows * step + rows, :]


def kernel(fn, outs, *args, scratch=(), vmem=8, work=0, hbm=(), pinned=()):
    outs = [o if isinstance(o[0], tuple) else (o, F32) for o in outs]
    return pl.pallas_call(
        fn,
        out_shape=[jax.ShapeDtypeStruct(*o) for o in outs],
        in_specs=[HB if i in hbm else VM for i in range(len(args))],
        out_specs=[VM] * len(outs),
        scratch_shapes=list(scratch),
        compiler_params=pltpu.CompilerParams(vmem_limit_bytes=vmem * 2**20),
        cost_estimate=pl.CostEstimate(flops=work, bytes_accessed=work // 700, transcendentals=0),
    )(*(pltpu.with_memory_space_constraint(a, pltpu.HBM) if i in pinned else a for i, a in enumerate(args)))


def chip_product(matrix, k, mine, other, width):
    here = lax.axis_index("front")
    odd = (here & 1) == 1
    blocks = [jnp.where(odd, other, mine), jnp.where(odd, mine, other)]
    return part_dot(matrix, ((here ^ k) // 2) * (2 * mine.shape[0] * (LANES // width)), blocks, width)


def first_products(width, matrix, mine, other, *refs):
    near, both, out = refs[:-2], refs[-2], refs[-1]
    rows = mine.shape[0]
    total = chip_product(matrix, 0, mine[...], other[...], width)
    for step, (k, block) in enumerate(zip(hops(lax.axis_size("front")), near)):
        second = both[rows * step : rows * step + rows, :]
        total += chip_product(matrix, k, block[...], second, width)
    out[...] = total


def last_product(finish, width, count, matrix, *refs):
    parts, rest = refs[:count], refs[count:]
    if count == 3:
        known, mine, other = parts
        k = hops(lax.axis_size("front"))[-1]
        finish(combined(known[...] + chip_product(matrix, k, mine[...], other[...], width)), *rest)
    else:
        assemble(rest[-1], parts, lax.axis_index("front"), width)
        finish(complex_dot(matrix[...], rest[-1][...]), *rest[:-1])


def gathered(finish, width, outs, matrix, parts, *args):
    rows = parts[0].shape[0] * (LANES // width)
    scratch = []
    if 2 * rows % LANES == 0:
        mine, other, last, *near, last_other, both = parts
        shape = (matrix.shape[0], 2 * width)
        (known,) = kernel(
            functools.partial(first_products, width), [shape], matrix, mine, other, *near[::-1], both
        )
        parts = [known, last, last_other]
    else:
        scratch = [pltpu.VMEM((rows * lax.axis_size("front"), width), F32)]
    return kernel(
        functools.partial(last_product, finish, width, len(parts)),
        outs,
        matrix,
        *parts,
        *args,
        scratch=scratch,
    )


def whole_of(width, *refs):
    assemble(refs[-1], refs[:-1], lax.axis_index("front"), width)


def half_product(theirs, width, matrix, y, piece):
    odd = (lax.axis_index("front") & 1) ^ theirs
    rows, chunks = piece.shape[0], LANES // width
    starts = [chunk * 2 * rows + odd * rows for chunk in range(chunks)]
    own = [y[pl.ds(pl.multiple_of(at, 8), rows), :] for at in starts]
    x = jnp.concatenate(own, axis=1) - piece[...]
    if chunks == 1:
        return part_dot(matrix, starts[0], [x], width)
    total, depth = None, matrix.shape[1] // 2
    columns, turned = spread(x, width), spread(turn(x, width), width)
    for chunk, at in enumerate(starts):
        at, span = pl.multiple_of(at, LANES), slice(rows * chunk, rows * chunk + rows)
        part = dot(matrix[:, pl.ds(at, rows)], columns[span])
        part += dot(matrix[:, pl.ds(depth + at, rows)], turned[span])
        total = part if total is None else total + part
    return total


def own_half(width, matrix, y, piece, out):
    out[...] = half_product(0, width, matrix, y, piece)


def load_matrices(picks, *refs):
    count = len(picks)
    sources, outs, buffers, sems = (
        refs[:count],
        refs[count : 2 * count],
        refs[2 * count : 3 * count],
        refs[3 * count],
    )
    parent = lax.axis_index("leaf") // 2
    copies = []
    for i, (src, pick) in enumerate(zip(sources, picks)):
        rows = buffers[i].shape[1]
        step = max(rows // CHUNKS, 16)
        for n, at in enumerate(range(0, rows, step)):
            span = pl.ds(at, step)
            view = src.at[:, span, :] if pick is None else src.at[:, parent if pick == "own" else 0, span, :]
            copy = pltpu.make_async_copy(view, buffers[i].at[:, span, :], sems.at[CHUNKS * i + n])
            copy.start()
            copies.append((i, at, step, copy))
    for i, at, step, copy in copies:
        copy.wait()
        rows, depth = buffers[i].shape[1:]
        for part in range(2):
            high, low = split(buffers[i][part, at : at + step, :])
            outs[i][at : at + step, part * depth : part * depth + depth] = high
            outs[i][rows + at : rows + at + step, part * depth : part * depth + depth] = low


def load(*matrices, pinned=False):
    shapes = [m.shape[-2:] for m, _ in matrices]
    size = sum(r * d for r, d in shapes)
    return kernel(
        functools.partial(load_matrices, tuple(pick for _, pick in matrices)),
        [((2 * r, 2 * d), BF16) for r, d in shapes],
        *[m for m, _ in matrices],
        scratch=[pltpu.VMEM((2, r, d), F32) for r, d in shapes]
        + [pltpu.SemaphoreType.DMA((CHUNKS * len(shapes),))],
        hbm=range(len(shapes)),
        pinned=range(len(shapes)) if pinned else (),
        vmem=4 + -(-size * 8 // 2**20),
        work=size * 1000,
    )


def pack_receivers(fronts, rows, data_hbm, block_hbm, offset_hbm, *refs):
    own, far, near = refs[:3]
    data, block, offset, sems = refs[3:]
    copies = [
        pltpu.make_async_copy(src, dst, sems.at[i])
        for i, (src, dst) in enumerate(((data_hbm, data), (block_hbm, block), (offset_hbm, offset)))
    ]
    for copy in copies:
        copy.start()
    for copy in copies:
        copy.wait()
    group = lax.axis_index("leaf")
    count = data.shape[1]
    slots = fronts * CAP
    down = lax.broadcasted_iota(jnp.int32, (count, count), 0)
    across = lax.broadcasted_iota(jnp.int32, (count, count), 1)
    eye = down == across
    block_row = block[...]
    block_col = jnp.sum(jnp.where(eye, block_row, 0), axis=1, keepdims=True)
    offset_col = jnp.sum(jnp.where(eye, offset[...], 0), axis=1, keepdims=True)
    same = (block_col == block_row) & (down < across)
    slot_row = block_row * CAP + jnp.sum(same.astype(jnp.int32), axis=0, keepdims=True)
    row_col = (block_col & (fronts - 1)) * rows + offset_col + 1
    lane = lax.broadcasted_iota(jnp.int32, (count, COLS), 1)
    index = jnp.where(lane == 0, row_col, 0).astype(F32)
    lines = jnp.concatenate([index, data[0], jnp.zeros((count, COLS), F32), -data[1]], axis=1)
    targets = [group, group ^ 2, group ^ 1, group ^ 3]
    place = lax.broadcasted_iota(jnp.int32, (slots, count), 0)
    pick = jnp.concatenate([place + target * slots == slot_row for target in targets], axis=0)
    picked = jnp.dot(
        pick.astype(F32), lines, precision=lax.Precision.HIGHEST, preferred_element_type=F32
    )
    own[...] = picked[:slots]
    far[...] = picked[slots : 2 * slots]
    near[...] = picked[2 * slots :]


def pass_on(far, came, out):
    rows = far.shape[0]
    out[0:rows, :] = far[...]
    out[rows:, :] = came[rows:, :]


def load_sources(leaf_hbm, mid_hbm, root_hbm, leaf_out, mid_out, root_out, leaf, mid, root, sems):
    group = lax.axis_index("leaf")
    copies = [
        pltpu.make_async_copy(src, dst, sems.at[i])
        for i, (src, dst) in enumerate(
            ((leaf_hbm, leaf), (mid_hbm.at[:, group // 2], mid), (root_hbm, root))
        )
    ]
    for copy in copies:
        copy.start()
    for copy in copies:
        copy.wait()
    forward = ((group & 1) == 0).astype(F32)
    real, imag = leaf[0].T, leaf[1].T
    zero = jnp.zeros_like(real)
    leaf_out[...] = jnp.concatenate([real, zero, imag, zero], axis=1)
    mid_out[...] = pack(jnp.concatenate([mid[0], mid[1]], axis=0).T) * forward
    width = COLS // 2
    low = jnp.concatenate([root[0, :width], root[1, :width]], axis=0)
    high = jnp.concatenate([root[0, width:], root[1, width:]], axis=0)
    root_out[...] = pack(jnp.where(group < 2, low, high).T) * forward


def message_rows(rows, slots):
    return max(rows, slots), 8 * -(-slots // (8 * LANES))


def pack_leaf(own, mine, near, far, out):
    lines = jnp.concatenate([mine[...], near[0 : mine.shape[0], :], far[...]], axis=0)
    slots = lines.shape[0]
    body, tail = message_rows(own.shape[0], slots)
    lane = lax.broadcasted_iota(jnp.int32, (slots, LANES), 1)
    data = jnp.where((lane // COLS) % 2 == 1, lines, 0.0)
    index = lines[:, 0:1]

    def padded(x):
        if x.shape[0] == body:
            return x
        return jnp.concatenate([x, jnp.zeros((body - x.shape[0], LANES), F32)], axis=0)

    out[0:body, :] = padded(own[...]) + padded(data)
    out[body:, :] = jnp.zeros((tail, LANES), F32)
    for at in range(0, slots, LANES):
        size = min(LANES, slots - at)
        eye = lax.broadcasted_iota(jnp.int32, (size, size), 0) == lax.broadcasted_iota(
            jnp.int32, (size, size), 1
        )
        line = jnp.sum(jnp.where(eye, index[at : at + size], 0.0), axis=0, keepdims=True)
        out[body + at // LANES : body + at // LANES + 1, 0:size] = line


def leaf_lower(slots, matrix, *refs):
    parts, (out, rhs, messages) = refs[:-3], refs[-3:]
    rows = out.shape[0]
    here = lax.axis_index("front")
    for k, part in blocks_of(parts):
        messages[here ^ k] = part[...]
    fronts = messages.shape[0]
    total = rows * fronts
    body, _ = message_rows(rows, slots)
    lane = lax.broadcasted_iota(jnp.int32, (slots, LANES), 1)
    taken = (lane // COLS) % 2 == 1
    own = lax.broadcasted_iota(jnp.int32, (rows, LANES), 1)
    own = (own // COLS) % 2 == 0
    for k in range(fronts):
        rhs[rows * k : rows * k + rows, :] = jnp.where(own, messages[k, 0:rows, :], 0.0)
    group = max(1, 512 // slots)
    for k in range(0, fronts, group):
        chosen = range(k, min(k + group, fronts))
        lines = jnp.concatenate([jnp.where(taken, messages[i, 0:slots, :], 0.0) for i in chosen], axis=0)
        index = jnp.concatenate(
            [
                messages[i, body + at // LANES : body + at // LANES + 1, 0 : min(LANES, slots - at)]
                for i in chosen
                for at in range(0, slots, LANES)
            ],
            axis=1,
        )
        row = lax.broadcasted_iota(jnp.int32, (total, index.shape[1]), 0)
        pick = (row + 1 == index.astype(jnp.int32)).astype(BF16)
        both = dot(pick, jnp.concatenate(split(lines), axis=1))
        rhs[...] += both[:, :LANES] + both[:, LANES:]
    out[...] = complex_dot(matrix[...], rhs[...])


def leaf_to_mid(value, sources, keep, send):
    mine, theirs = own_first(lax.axis_index("leaf"), *halves(value))
    keep[...] = sources[...] - pack(mine)
    send[...] = -pack(theirs)


def leaf_to_root(matrix, *refs):
    parts, (keep, send, full) = refs[:-3], refs[-3:]
    assemble(full, parts, lax.axis_index("front"))
    mine, theirs = own_first(lax.axis_index("leaf"), *halves(complex_dot(matrix[...], full[...])))
    keep[...], send[...] = pack(mine), pack(theirs)


def add(*refs):
    total = refs[0][...]
    for ref in refs[1:-1]:
        total = total + ref[...]
    refs[-1][...] = total


def packed_to(value, out):
    out[...] = pack(value)


def mid_to_root(value, kept, came, sources, keep, send):
    cut = -(unpack(kept[...] + came[...], 2 * COLS) + value)
    width = COLS // 2
    low = pack(jnp.concatenate([cut[:, :width], cut[:, COLS : COLS + width]], axis=1))
    high = pack(jnp.concatenate([cut[:, width:COLS], cut[:, COLS + width :]], axis=1))
    first = lax.axis_index("leaf") < 2
    keep[...] = jnp.where(first, low, high) + sources[...]
    send[...] = jnp.where(first, high, low)


def column_half(matrix, x, theirs):
    core = (lax.axis_index("front") & 1) ^ theirs
    half, n = x.shape[1] // 2, x.shape[1]
    turned = jnp.concatenate([-x[:, half:], x[:, :half]], axis=1)
    columns = jnp.concatenate(split(jnp.concatenate([x, turned], axis=0)), axis=1)
    height, chunks = matrix.shape[0] // 2, LANES // n
    rows, pieces = height // chunks // 2, []
    for chunk in range(chunks):
        at = pl.multiple_of((2 * chunk + core) * rows, 16)
        high = dot(matrix[pl.ds(at, rows), :], columns)
        low = dot(matrix[pl.ds(height + at, rows), :], columns[:, :n])
        pieces.append((high[:, n:] + low) + high[:, :n])
    return jnp.concatenate(pieces, axis=1)


def root_to_mid(matrix, mine, other, send, x_root):
    first = lax.axis_index("leaf") < 2
    mine, other = unpack(mine[...], COLS), unpack(other[...], COLS)
    low, high = jnp.where(first, mine, other), jnp.where(first, other, mine)
    width = COLS // 2
    x = jnp.concatenate([low[:, :width], high[:, :width], low[:, width:], high[:, width:]], axis=1)
    x_root[...] = pack(x)
    send[...] = column_half(matrix, x, 1)


def root_to_mid_kept(matrix, x_root, keep):
    keep[...] = column_half(matrix, unpack(x_root[...], 2 * COLS), 0)


def root_to_leaf(matrix, mine, other, out, forward, adjoint):
    x = by_solve(lax.axis_index("leaf"), unpack(mine[...], 2 * COLS), unpack(other[...], 2 * COLS))
    out[...] = complex_dot(matrix[...], x)
    fields_of(x, forward, adjoint, ())


def sum_front(kept, sent, before_last=(), at_end=()):
    fronts = lax.axis_size("front")
    (total,) = kernel(add, [kept.shape], kept, swap("front", sent, 1))
    hops = [1 << i for i in range(1, fronts.bit_length() - 1)]
    for hop, back in zip(hops, hops[::-1]):
        pairs = [(i, i ^ (back if i & 1 else hop)) for i in range(fronts)]
        if hop == hops[-1]:
            total = after(total, *before_last)
        (total,) = kernel(add, [kept.shape], total, lax.ppermute(total, "front", pairs))
    return [total, swap("front", after(total, *at_end), 1)]


def mid_upper(matrix, y, piece, known, out):
    out[...] = pack(combined(known[...] + half_product(1, 2 * COLS, matrix, y, piece)))


def core_rows(ref, theirs):
    rows = ref.shape[0] // 2
    core = (lax.axis_index("front") & 1) ^ theirs
    return ref[pl.ds(pl.multiple_of(core * rows, 8), rows), :]


def mid_to_leaf(matrix, from_root, mine, other, send, x_mid):
    x = by_solve(lax.axis_index("leaf"), unpack(mine[...], 2 * COLS), unpack(other[...], 2 * COLS))
    x_mid[...] = x
    send[...] = column_half(matrix, x, 1) + core_rows(from_root, 1)


def mid_to_leaf_kept(matrix, from_root, x_mid, keep):
    keep[...] = column_half(matrix, x_mid[...], 0) + core_rows(from_root, 0)


def leaf_upper(matrix, y, piece, known, forward, adjoint):
    fields_of(combined(known[...] + half_product(1, LANES, matrix, y, piece)), forward, adjoint, ())


def mid_outputs(mine, far, other, forward, adjoint):
    parent = lax.axis_index("leaf") // 2
    x = by_solve(lax.axis_index("leaf"), unpack(far[...], 2 * COLS), unpack(other[...], 2 * COLS))
    fields_of(mine[...], forward, adjoint, (parent,))
    fields_of(x, forward, adjoint, (1 - parent,))


def after(x, *others):
    return lax.optimization_barrier((x, *others))[0]


def body(
    leaf_lower_inv,
    leaf_upper_inv,
    leaf_to_mid_lower,
    leaf_to_root_lower,
    leaf_to_mid_upper,
    leaf_to_root_upper,
    mid_lower_inv,
    mid_upper_inv,
    mid_to_root_lower,
    mid_to_root_upper,
    root_lower_inv,
    root_upper_inv,
    leaf_sources,
    mid_sources,
    root_sources,
    receiver_data,
    receiver_block,
    receiver_offset,
):
    groups, fronts = lax.axis_size("leaf"), lax.axis_size("front")
    n0, n1, n2 = leaf_sources.shape[1], mid_sources.shape[2], root_sources.shape[1]
    s0, s1, s2 = n0 * fronts, n1 * fronts, n2 * fronts
    slots, count = fronts * CAP, receiver_data.shape[1]
    dma = pltpu.SemaphoreType.DMA

    with jax.named_scope("right_hand_sides"):
        payload = kernel(
            functools.partial(pack_receivers, fronts, n0),
            [(slots, LANES), (slots, LANES), (2 * slots, LANES)],
            receiver_data,
            receiver_block.reshape(1, -1),
            receiver_offset.reshape(1, -1),
            scratch=[
                pltpu.VMEM((2, count, COLS), F32),
                pltpu.VMEM((1, count), jnp.int32),
                pltpu.VMEM((1, count), jnp.int32),
                dma((3,)),
            ],
            hbm=range(3),
            pinned=range(3),
        )
        own, far, near = payload
        came = swap("leaf", near, 1)
        (both,) = kernel(pass_on, [(2 * slots, LANES)], far, came)
        arrived = [own, came, swap("leaf", both, 2)]
        leaf_own, mid_own, root_own = kernel(
            load_sources,
            [(n0, LANES), (n1 // 2, LANES), (n2 // 4, LANES)],
            after(leaf_sources.transpose(0, 2, 1), *payload),
            mid_sources.transpose(0, 1, 3, 2),
            root_sources.transpose(0, 2, 1),
            scratch=[
                pltpu.VMEM((2, COLS, n0), F32),
                pltpu.VMEM((2, COLS, n1), F32),
                pltpu.VMEM((2, COLS, n2), F32),
                dma((3,)),
            ],
            hbm=range(3),
            pinned=range(3),
        )
        (message,) = kernel(
            pack_leaf, [(sum(message_rows(n0, groups * slots)), LANES)], leaf_own, *arrived
        )
    with jax.named_scope("leaf_lower"):
        messages, (ll, l2m) = gather_front(
            message,
            lambda x: load((after(leaf_lower_inv, *x), "leaf"), (leaf_to_mid_lower, "leaf"), pinned=True),
        )
        (y_leaf,) = kernel(
            functools.partial(leaf_lower, groups * slots),
            [(n0, LANES)],
            ll,
            *messages,
            scratch=[pltpu.VMEM((s0, LANES), F32), pltpu.VMEM((fronts, *message.shape), F32)],
        )
    with jax.named_scope("mid_lower"):
        parts, (l2r, ml) = gather_front(
            y_leaf,
            lambda x: load((after(leaf_to_root_lower, *x), "leaf"), (mid_lower_inv, "own"), pinned=True),
        )
        keep, send = gathered(leaf_to_mid, LANES, [(n1 // 2, LANES)] * 2, l2m, parts, mid_own)
        came = swap("leaf", send, 1)
        root_kept, root_sent, y_full = kernel(
            leaf_to_root, [(n2 // 2, LANES)] * 2 + [(s0, LANES)], l2r, after(parts[0], send), *parts[1:]
        )
        (cut_mid,) = kernel(add, [(n1 // 2, LANES)], after(keep, root_kept), came)
        root_came = swap("leaf", root_sent, 1)
        parts, (m2r,) = gather_front(
            cut_mid, lambda x: load((after(mid_to_root_lower, *x), "own"), pinned=True), (root_came,)
        )
        (y_mid,) = gathered(packed_to, 2 * COLS, [(n1 // 2, LANES)], ml, parts)
    with jax.named_scope("root_cut"):
        parts, (rl,) = gather_front(y_mid, lambda x: load((after(root_lower_inv, *x), None)))
        keep, send = gathered(
            mid_to_root, 2 * COLS, [(n2 // 4, LANES)] * 2, m2r, parts, root_kept, root_came, root_own
        )
        came = swap("leaf", send, 2)
        mu, l2r_up = load((after(mid_upper_inv, send), "own"), (leaf_to_root_upper, "leaf"))
        (y_mid_full,) = kernel(
            functools.partial(whole_of, 2 * COLS), [(s1, 2 * COLS)], after(parts[0], send), *parts[1:]
        )
        (cut_root,) = kernel(add, [(n2 // 4, LANES)], after(keep, mu, y_mid_full), came)
    with jax.named_scope("root_solve"):
        parts, (ru,) = gather_front(cut_root, lambda x: load((after(root_upper_inv, *x), None)))
        (y_root,) = gathered(packed_to, COLS, [(n2 // 4, LANES)], rl, parts)
        parts, (m2r_up, l2m_up, lu) = gather_front(
            y_root,
            lambda x: load(
                (after(mid_to_root_upper, *x), "own"), (leaf_to_mid_upper, "leaf"), (leaf_upper_inv, "leaf")
            ),
        )
        (x_root,) = gathered(packed_to, COLS, [(n2 // 4, LANES)], ru, parts)
    with jax.named_scope("mid_upper"):
        send, x_root = kernel(
            root_to_mid,
            [(s1 // 4, LANES), (n2 // 2, LANES)],
            m2r_up,
            x_root,
            swap("leaf", x_root, 2),
        )
        (keep,) = kernel(root_to_mid_kept, [(s1 // 4, LANES)], m2r_up, x_root)
        mine, theirs = sum_front(keep, send)
        (known,) = kernel(functools.partial(own_half, 2 * COLS), [(2 * n1, 4 * COLS)], mu, y_mid_full, mine)
        (x_mid,) = kernel(mid_upper, [(n1 // 2, LANES)], mu, y_mid_full, theirs, known)
        from_root, root_field, root_adjoint = kernel(
            root_to_leaf,
            [(s0, LANES), (2, COLS, n2), (2, COLS, n2)],
            l2r_up,
            x_root,
            swap("leaf", after(x_root, send), 1),
        )
    with jax.named_scope("leaf_upper"):
        x_far = swap("leaf", x_mid, 2)
        send, x_mid = kernel(
            mid_to_leaf,
            [(s0 // 2, LANES), (n1, LANES)],
            l2m_up,
            from_root,
            x_mid,
            swap("leaf", x_mid, 1),
        )
        (keep,) = kernel(mid_to_leaf_kept, [(s0 // 2, LANES)], l2m_up, from_root, x_mid)
        x_other = swap("leaf", x_far, 1)
        mid_field, mid_adjoint = kernel(
            mid_outputs, [(2, 2, COLS, n1)] * 2, x_mid, x_far, x_other
        )
        mine, theirs = sum_front(keep, send, (x_far,), (x_other,))
        (known,) = kernel(functools.partial(own_half, LANES), [(2 * n0, 2 * LANES)], lu, y_full, mine)
        leaf_field, leaf_adjoint = kernel(
            leaf_upper, [(2, COLS, n0)] * 2, lu, y_full, theirs, after(known, mid_field)
        )
    return tuple(
        jnp.swapaxes(x, -1, -2)
        for x in (leaf_field, mid_field, root_field, leaf_adjoint, mid_adjoint, root_adjoint)
    )


def solution(mesh):
    in_specs = (
        P(None, "leaf", "front", None),
        P(None, "leaf", "front", None),
        P(None, "leaf", "front", None),
        P(None, "leaf", "front", None),
        P(None, "leaf", None, "front"),
        P(None, "leaf", None, "front"),
        P(None, None, "front", None),
        P(None, None, "front", None),
        P(None, None, "front", None),
        P(None, None, None, "front"),
        P(None, "front", None),
        P(None, "front", None),
        P(None, ("leaf", "front"), None),
        P(None, None, "front", None),
        P(None, "front", None),
        P(None, ("leaf", "front"), None),
        P(("leaf", "front"), None),
        P(("leaf", "front")),
    )
    out_specs = (
        P(None, ("leaf", "front"), None),
        P(None, None, "front", None),
        P(None, "front", None),
        P(None, ("leaf", "front"), None),
        P(None, None, "front", None),
        P(None, "front", None),
    )
    return jax.shard_map(body, mesh=mesh, in_specs=in_specs, out_specs=out_specs, check_vma=False)
```

```python
import functools

import jax
import jax.numpy as jnp
from jax import lax
from jax.experimental import pallas as pl
from jax.experimental.pallas import tpu as pltpu
from jax.sharding import PartitionSpec as P

CAP = 2
CHUNKS = 4
LANES = 128
COLS = 32
F32 = jnp.float32
BF16 = jnp.bfloat16
VM = pl.BlockSpec(memory_space=pltpu.VMEM)
HB = pl.BlockSpec(memory_space=pltpu.HBM)


def split(x):
    high = x.astype(BF16)
    return high, (x - high.astype(F32)).astype(BF16)


def dot(a, b):
    return jnp.dot(a, b, preferred_element_type=F32)


def complex_dot(matrix, x):
    half = x.shape[1] // 2
    turned = jnp.concatenate([-x[:, half:], x[:, :half]], axis=1)
    both = jnp.concatenate([x, turned], axis=0)
    columns = jnp.concatenate(split(both), axis=1)
    product = dot(matrix, columns)
    rows, n = product.shape[0] // 2, x.shape[1]
    return (product[:rows, n:] + product[rows:, :n]) + product[:rows, :n]


def combined(product):
    rows, n = product.shape[0] // 2, product.shape[1] // 2
    return (product[:rows, n:] + product[rows:, :n]) + product[:rows, :n]


def turn(x, width):
    half = width // 2
    lane = lax.broadcasted_iota(jnp.int32, x.shape, 1) % width
    return jnp.where(lane < half, -pltpu.roll(x, LANES - half, 1), pltpu.roll(x, half, 1))


def spread(x, width):
    high, low = split(x)
    return jnp.concatenate(
        [
            jnp.concatenate([high[:, at : at + width], low[:, at : at + width]], axis=1)
            for at in range(0, LANES, width)
        ],
        axis=0,
    )


def part_dot(matrix, at, blocks, width):
    depth = matrix.shape[1] // 2
    columns = jnp.concatenate([spread(x, width) for x in blocks], axis=0)
    turned = jnp.concatenate([spread(turn(x, width), width) for x in blocks], axis=0)
    count, at = columns.shape[0], pl.multiple_of(at, LANES)
    return dot(matrix[:, pl.ds(at, count)], columns) + dot(matrix[:, pl.ds(depth + at, count)], turned)


def pack(x):
    chunks = LANES // x.shape[1]
    rows = x.shape[0] // chunks
    return jnp.concatenate([x[rows * j : rows * j + rows] for j in range(chunks)], axis=1)


def unpack(x, width):
    return jnp.concatenate([x[:, at : at + width] for at in range(0, LANES, width)], axis=0)


def halves(x):
    c = COLS
    return (
        jnp.concatenate([x[:, :c], x[:, 2 * c : 3 * c]], axis=1),
        jnp.concatenate([x[:, c : 2 * c], x[:, 3 * c :]], axis=1),
    )


def joined(forward, adjoint):
    c = COLS
    return jnp.concatenate([forward[:, :c], adjoint[:, :c], forward[:, c:], adjoint[:, c:]], axis=1)


def own_first(group, forward, adjoint):
    even = (group & 1) == 0
    return jnp.where(even, forward, adjoint), jnp.where(even, adjoint, forward)


def by_solve(group, own, other):
    even = (group & 1) == 0
    return joined(jnp.where(even, own, other), jnp.where(even, other, own))


def assemble(where, parts, here, width=LANES):
    rows = parts[0].shape[0] * (LANES // width)
    for k, part in blocks_of(parts):
        start = pl.multiple_of((here ^ k) * rows, 8)
        where[pl.ds(start, rows), :] = part[...] if width == LANES else unpack(part[...], width)


def fields_of(x, forward, adjoint, where):
    y = x.T
    c = COLS
    forward[(0, *where)] = y[0:c]
    forward[(1, *where)] = y[2 * c : 3 * c]
    adjoint[(0, *where)] = y[c : 2 * c]
    adjoint[(1, *where)] = -y[3 * c :]


def swap(axis, x, k):
    size = lax.axis_size(axis)
    return lax.ppermute(x, axis, [(i, i ^ k) for i in range(size)])


def stack(*refs):
    at = 0
    for ref in refs[:-1]:
        refs[-1][at : at + ref.shape[0], :] = ref[...]
        at += ref.shape[0]


def hops(fronts):
    return [6, 2, 4] if fronts == 8 else list(range(2, fronts, 2))


def gather_front(x, meanwhile=None, others=()):
    fronts = lax.axis_size("front")
    *near, last = [swap("front", x, k) for k in hops(fronts)]
    own = swap("front", x, 1)
    extra = tuple(meanwhile((own,))) if meanwhile else ()
    (both,) = kernel(stack, [(len(near) * x.shape[0], LANES)], after(near[0], *extra, *others), *near[1:])
    last = after(last, *extra, *others)
    return [x, own, last, *near[::-1], swap("front", last, 1), swap("front", both, 1)], extra


def blocks_of(parts):
    rows = parts[0].shape[0]
    *near, last = hops(2 * len(parts) - 6)
    yield 0, parts[0]
    yield 1, parts[1]
    yield last, parts[2]
    yield last + 1, parts[-2]
    for step, (k, part) in enumerate(zip(near, parts[-3:2:-1])):
        yield k, part
        yield k + 1, parts[-1].at[rows * step : rows * step + rows, :]


def kernel(fn, outs, *args, scratch=(), vmem=8, work=0, hbm=(), pinned=()):
    outs = [o if isinstance(o[0], tuple) else (o, F32) for o in outs]
    return pl.pallas_call(
        fn,
        out_shape=[jax.ShapeDtypeStruct(*o) for o in outs],
        in_specs=[HB if i in hbm else VM for i in range(len(args))],
        out_specs=[VM] * len(outs),
        scratch_shapes=list(scratch),
        compiler_params=pltpu.CompilerParams(vmem_limit_bytes=vmem * 2**20),
        cost_estimate=pl.CostEstimate(flops=work, bytes_accessed=work // 700, transcendentals=0),
    )(*(pltpu.with_memory_space_constraint(a, pltpu.HBM) if i in pinned else a for i, a in enumerate(args)))


def chip_product(matrix, k, mine, other, width):
    here = lax.axis_index("front")
    odd = (here & 1) == 1
    blocks = [jnp.where(odd, other, mine), jnp.where(odd, mine, other)]
    return part_dot(matrix, ((here ^ k) // 2) * (2 * mine.shape[0] * (LANES // width)), blocks, width)


def first_products(width, matrix, mine, other, *refs):
    near, both, out = refs[:-2], refs[-2], refs[-1]
    rows = mine.shape[0]
    total = chip_product(matrix, 0, mine[...], other[...], width)
    for step, (k, block) in enumerate(zip(hops(lax.axis_size("front")), near)):
        second = both[rows * step : rows * step + rows, :]
        total += chip_product(matrix, k, block[...], second, width)
    out[...] = total


def last_product(finish, width, count, matrix, *refs):
    parts, rest = refs[:count], refs[count:]
    if count == 3:
        known, mine, other = parts
        k = hops(lax.axis_size("front"))[-1]
        finish(combined(known[...] + chip_product(matrix, k, mine[...], other[...], width)), *rest)
    else:
        assemble(rest[-1], parts, lax.axis_index("front"), width)
        finish(complex_dot(matrix[...], rest[-1][...]), *rest[:-1])


def gathered(finish, width, outs, matrix, parts, *args):
    rows = parts[0].shape[0] * (LANES // width)
    scratch = []
    if 2 * rows % LANES == 0:
        mine, other, last, *near, last_other, both = parts
        shape = (matrix.shape[0], 2 * width)
        (known,) = kernel(
            functools.partial(first_products, width), [shape], matrix, mine, other, *near[::-1], both
        )
        parts = [known, last, last_other]
    else:
        scratch = [pltpu.VMEM((rows * lax.axis_size("front"), width), F32)]
    return kernel(
        functools.partial(last_product, finish, width, len(parts)),
        outs,
        matrix,
        *parts,
        *args,
        scratch=scratch,
    )


def whole_of(width, *refs):
    assemble(refs[-1], refs[:-1], lax.axis_index("front"), width)


def half_product(theirs, width, matrix, y, piece):
    odd = (lax.axis_index("front") & 1) ^ theirs
    rows, chunks = piece.shape[0], LANES // width
    starts = [chunk * 2 * rows + odd * rows for chunk in range(chunks)]
    own = [y[pl.ds(pl.multiple_of(at, 8), rows), :] for at in starts]
    x = jnp.concatenate(own, axis=1) - piece[...]
    if chunks == 1:
        return part_dot(matrix, starts[0], [x], width)
    total, depth = None, matrix.shape[1] // 2
    columns, turned = spread(x, width), spread(turn(x, width), width)
    for chunk, at in enumerate(starts):
        at, span = pl.multiple_of(at, LANES), slice(rows * chunk, rows * chunk + rows)
        part = dot(matrix[:, pl.ds(at, rows)], columns[span])
        part += dot(matrix[:, pl.ds(depth + at, rows)], turned[span])
        total = part if total is None else total + part
    return total


def own_half(width, matrix, y, piece, out):
    out[...] = half_product(0, width, matrix, y, piece)


def load_matrices(picks, *refs):
    count = len(picks)
    sources, outs, buffers, sems = (
        refs[:count],
        refs[count : 2 * count],
        refs[2 * count : 3 * count],
        refs[3 * count],
    )
    parent = lax.axis_index("leaf") // 2
    copies = []
    for i, (src, pick) in enumerate(zip(sources, picks)):
        rows = buffers[i].shape[1]
        step = max(rows // CHUNKS, 16)
        for n, at in enumerate(range(0, rows, step)):
            span = pl.ds(at, step)
            view = src.at[:, span, :] if pick is None else src.at[:, parent if pick == "own" else 0, span, :]
            copy = pltpu.make_async_copy(view, buffers[i].at[:, span, :], sems.at[CHUNKS * i + n])
            copy.start()
            copies.append((i, at, step, copy))
    for i, at, step, copy in copies:
        copy.wait()
        rows, depth = buffers[i].shape[1:]
        for part in range(2):
            high, low = split(buffers[i][part, at : at + step, :])
            outs[i][at : at + step, part * depth : part * depth + depth] = high
            outs[i][rows + at : rows + at + step, part * depth : part * depth + depth] = low


def load(*matrices, pinned=False):
    shapes = [m.shape[-2:] for m, _ in matrices]
    size = sum(r * d for r, d in shapes)
    return kernel(
        functools.partial(load_matrices, tuple(pick for _, pick in matrices)),
        [((2 * r, 2 * d), BF16) for r, d in shapes],
        *[m for m, _ in matrices],
        scratch=[pltpu.VMEM((2, r, d), F32) for r, d in shapes]
        + [pltpu.SemaphoreType.DMA((CHUNKS * len(shapes),))],
        hbm=range(len(shapes)),
        pinned=range(len(shapes)) if pinned else (),
        vmem=4 + -(-size * 8 // 2**20),
        work=size * 1000,
    )


def pack_receivers(fronts, rows, data_hbm, block_hbm, offset_hbm, *refs):
    own, far, near = refs[:3]
    data, block, offset, sems = refs[3:]
    copies = [
        pltpu.make_async_copy(src, dst, sems.at[i])
        for i, (src, dst) in enumerate(((data_hbm, data), (block_hbm, block), (offset_hbm, offset)))
    ]
    for copy in copies:
        copy.start()
    for copy in copies:
        copy.wait()
    group = lax.axis_index("leaf")
    count = data.shape[1]
    slots = fronts * CAP
    down = lax.broadcasted_iota(jnp.int32, (count, count), 0)
    across = lax.broadcasted_iota(jnp.int32, (count, count), 1)
    eye = down == across
    block_row = block[...]
    block_col = jnp.sum(jnp.where(eye, block_row, 0), axis=1, keepdims=True)
    offset_col = jnp.sum(jnp.where(eye, offset[...], 0), axis=1, keepdims=True)
    same = (block_col == block_row) & (down < across)
    slot_row = block_row * CAP + jnp.sum(same.astype(jnp.int32), axis=0, keepdims=True)
    row_col = (block_col & (fronts - 1)) * rows + offset_col + 1
    lane = lax.broadcasted_iota(jnp.int32, (count, COLS), 1)
    index = jnp.where(lane == 0, row_col, 0).astype(F32)
    lines = jnp.concatenate([index, data[0], jnp.zeros((count, COLS), F32), -data[1]], axis=1)
    targets = [group, group ^ 2, group ^ 1, group ^ 3]
    place = lax.broadcasted_iota(jnp.int32, (slots, count), 0)
    pick = jnp.concatenate([place + target * slots == slot_row for target in targets], axis=0)
    picked = jnp.dot(
        pick.astype(F32), lines, precision=lax.Precision.HIGHEST, preferred_element_type=F32
    )
    own[...] = picked[:slots]
    far[...] = picked[slots : 2 * slots]
    near[...] = picked[2 * slots :]


def pass_on(far, came, out):
    rows = far.shape[0]
    out[0:rows, :] = far[...]
    out[rows:, :] = came[rows:, :]


def load_sources(leaf_hbm, mid_hbm, root_hbm, leaf_out, mid_out, root_out, leaf, mid, root, sems):
    group = lax.axis_index("leaf")
    copies = [
        pltpu.make_async_copy(src, dst, sems.at[i])
        for i, (src, dst) in enumerate(
            ((leaf_hbm, leaf), (mid_hbm.at[:, group // 2], mid), (root_hbm, root))
        )
    ]
    for copy in copies:
        copy.start()
    for copy in copies:
        copy.wait()
    forward = ((group & 1) == 0).astype(F32)
    real, imag = leaf[0].T, leaf[1].T
    zero = jnp.zeros_like(real)
    leaf_out[...] = jnp.concatenate([real, zero, imag, zero], axis=1)
    mid_out[...] = pack(jnp.concatenate([mid[0], mid[1]], axis=0).T) * forward
    width = COLS // 2
    low = jnp.concatenate([root[0, :width], root[1, :width]], axis=0)
    high = jnp.concatenate([root[0, width:], root[1, width:]], axis=0)
    root_out[...] = pack(jnp.where(group < 2, low, high).T) * forward


def message_rows(rows, slots):
    return max(rows, slots), 8 * -(-slots // (8 * LANES))


def pack_leaf(own, mine, near, far, out):
    lines = jnp.concatenate([mine[...], near[0 : mine.shape[0], :], far[...]], axis=0)
    slots = lines.shape[0]
    body, tail = message_rows(own.shape[0], slots)
    lane = lax.broadcasted_iota(jnp.int32, (slots, LANES), 1)
    data = jnp.where((lane // COLS) % 2 == 1, lines, 0.0)
    index = lines[:, 0:1]

    def padded(x):
        if x.shape[0] == body:
            return x
        return jnp.concatenate([x, jnp.zeros((body - x.shape[0], LANES), F32)], axis=0)

    out[0:body, :] = padded(own[...]) + padded(data)
    out[body:, :] = jnp.zeros((tail, LANES), F32)
    for at in range(0, slots, LANES):
        size = min(LANES, slots - at)
        eye = lax.broadcasted_iota(jnp.int32, (size, size), 0) == lax.broadcasted_iota(
            jnp.int32, (size, size), 1
        )
        line = jnp.sum(jnp.where(eye, index[at : at + size], 0.0), axis=0, keepdims=True)
        out[body + at // LANES : body + at // LANES + 1, 0:size] = line


def leaf_lower(slots, matrix, *refs):
    parts, (out, rhs, messages) = refs[:-3], refs[-3:]
    rows = out.shape[0]
    here = lax.axis_index("front")
    for k, part in blocks_of(parts):
        messages[here ^ k] = part[...]
    fronts = messages.shape[0]
    total = rows * fronts
    body, _ = message_rows(rows, slots)
    lane = lax.broadcasted_iota(jnp.int32, (slots, LANES), 1)
    taken = (lane // COLS) % 2 == 1
    own = lax.broadcasted_iota(jnp.int32, (rows, LANES), 1)
    own = (own // COLS) % 2 == 0
    for k in range(fronts):
        rhs[rows * k : rows * k + rows, :] = jnp.where(own, messages[k, 0:rows, :], 0.0)
    group = max(1, 512 // slots)
    for k in range(0, fronts, group):
        chosen = range(k, min(k + group, fronts))
        lines = jnp.concatenate([jnp.where(taken, messages[i, 0:slots, :], 0.0) for i in chosen], axis=0)
        index = jnp.concatenate(
            [
                messages[i, body + at // LANES : body + at // LANES + 1, 0 : min(LANES, slots - at)]
                for i in chosen
                for at in range(0, slots, LANES)
            ],
            axis=1,
        )
        row = lax.broadcasted_iota(jnp.int32, (total, index.shape[1]), 0)
        pick = (row + 1 == index.astype(jnp.int32)).astype(BF16)
        both = dot(pick, jnp.concatenate(split(lines), axis=1))
        rhs[...] += both[:, :LANES] + both[:, LANES:]
    out[...] = complex_dot(matrix[...], rhs[...])


def leaf_to_mid(value, sources, keep, send):
    mine, theirs = own_first(lax.axis_index("leaf"), *halves(value))
    keep[...] = sources[...] - pack(mine)
    send[...] = -pack(theirs)


def leaf_to_root(matrix, *refs):
    parts, (keep, send, full) = refs[:-3], refs[-3:]
    assemble(full, parts, lax.axis_index("front"))
    mine, theirs = own_first(lax.axis_index("leaf"), *halves(complex_dot(matrix[...], full[...])))
    keep[...], send[...] = pack(mine), pack(theirs)


def add(*refs):
    total = refs[0][...]
    for ref in refs[1:-1]:
        total = total + ref[...]
    refs[-1][...] = total


def packed_to(value, out):
    out[...] = pack(value)


def mid_to_root(value, kept, came, sources, keep, send):
    cut = -(unpack(kept[...] + came[...], 2 * COLS) + value)
    width = COLS // 2
    low = pack(jnp.concatenate([cut[:, :width], cut[:, COLS : COLS + width]], axis=1))
    high = pack(jnp.concatenate([cut[:, width:COLS], cut[:, COLS + width :]], axis=1))
    first = lax.axis_index("leaf") < 2
    keep[...] = jnp.where(first, low, high) + sources[...]
    send[...] = jnp.where(first, high, low)


def column_half(matrix, x, theirs):
    core = (lax.axis_index("front") & 1) ^ theirs
    half, n = x.shape[1] // 2, x.shape[1]
    turned = jnp.concatenate([-x[:, half:], x[:, :half]], axis=1)
    columns = jnp.concatenate(split(jnp.concatenate([x, turned], axis=0)), axis=1)
    height, chunks = matrix.shape[0] // 2, LANES // n
    rows, pieces = height // chunks // 2, []
    for chunk in range(chunks):
        at = pl.multiple_of((2 * chunk + core) * rows, 16)
        high = dot(matrix[pl.ds(at, rows), :], columns)
        low = dot(matrix[pl.ds(height + at, rows), :], columns[:, :n])
        pieces.append((high[:, n:] + low) + high[:, :n])
    return jnp.concatenate(pieces, axis=1)


def root_to_mid(matrix, mine, other, send, x_root):
    first = lax.axis_index("leaf") < 2
    mine, other = unpack(mine[...], COLS), unpack(other[...], COLS)
    low, high = jnp.where(first, mine, other), jnp.where(first, other, mine)
    width = COLS // 2
    x = jnp.concatenate([low[:, :width], high[:, :width], low[:, width:], high[:, width:]], axis=1)
    x_root[...] = pack(x)
    send[...] = column_half(matrix, x, 1)


def root_to_mid_kept(matrix, x_root, keep):
    keep[...] = column_half(matrix, unpack(x_root[...], 2 * COLS), 0)


def root_to_leaf(matrix, mine, other, out, forward, adjoint):
    x = by_solve(lax.axis_index("leaf"), unpack(mine[...], 2 * COLS), unpack(other[...], 2 * COLS))
    out[...] = complex_dot(matrix[...], x)
    fields_of(x, forward, adjoint, ())


def sum_front(kept, sent, before_last=(), at_end=()):
    fronts = lax.axis_size("front")
    (total,) = kernel(add, [kept.shape], kept, swap("front", sent, 1))
    hops = [1 << i for i in range(1, fronts.bit_length() - 1)]
    for hop, back in zip(hops, hops[::-1]):
        pairs = [(i, i ^ (back if i & 1 else hop)) for i in range(fronts)]
        if hop == hops[-1]:
            total = after(total, *before_last)
        (total,) = kernel(add, [kept.shape], total, lax.ppermute(total, "front", pairs))
    return [total, swap("front", after(total, *at_end), 1)]


def mid_upper(matrix, y, piece, known, out):
    out[...] = pack(combined(known[...] + half_product(1, 2 * COLS, matrix, y, piece)))


def core_rows(ref, theirs):
    rows = ref.shape[0] // 2
    core = (lax.axis_index("front") & 1) ^ theirs
    return ref[pl.ds(pl.multiple_of(core * rows, 8), rows), :]


def mid_to_leaf(matrix, from_root, mine, other, send, x_mid):
    x = by_solve(lax.axis_index("leaf"), unpack(mine[...], 2 * COLS), unpack(other[...], 2 * COLS))
    x_mid[...] = x
    send[...] = column_half(matrix, x, 1) + core_rows(from_root, 1)


def mid_to_leaf_kept(matrix, from_root, x_mid, keep):
    keep[...] = column_half(matrix, x_mid[...], 0) + core_rows(from_root, 0)


def leaf_upper(matrix, y, piece, known, forward, adjoint):
    fields_of(combined(known[...] + half_product(1, LANES, matrix, y, piece)), forward, adjoint, ())


def mid_outputs(mine, far, other, forward, adjoint):
    parent = lax.axis_index("leaf") // 2
    x = by_solve(lax.axis_index("leaf"), unpack(far[...], 2 * COLS), unpack(other[...], 2 * COLS))
    fields_of(mine[...], forward, adjoint, (parent,))
    fields_of(x, forward, adjoint, (1 - parent,))


def after(x, *others):
    return lax.optimization_barrier((x, *others))[0]


def body(
    leaf_lower_inv,
    leaf_upper_inv,
    leaf_to_mid_lower,
    leaf_to_root_lower,
    leaf_to_mid_upper,
    leaf_to_root_upper,
    mid_lower_inv,
    mid_upper_inv,
    mid_to_root_lower,
    mid_to_root_upper,
    root_lower_inv,
    root_upper_inv,
    leaf_sources,
    mid_sources,
    root_sources,
    receiver_data,
    receiver_block,
    receiver_offset,
):
    groups, fronts = lax.axis_size("leaf"), lax.axis_size("front")
    n0, n1, n2 = leaf_sources.shape[1], mid_sources.shape[2], root_sources.shape[1]
    s0, s1, s2 = n0 * fronts, n1 * fronts, n2 * fronts
    slots, count = fronts * CAP, receiver_data.shape[1]
    dma = pltpu.SemaphoreType.DMA

    with jax.named_scope("right_hand_sides"):
        payload = kernel(
            functools.partial(pack_receivers, fronts, n0),
            [(slots, LANES), (slots, LANES), (2 * slots, LANES)],
            receiver_data,
            receiver_block.reshape(1, -1),
            receiver_offset.reshape(1, -1),
            scratch=[
                pltpu.VMEM((2, count, COLS), F32),
                pltpu.VMEM((1, count), jnp.int32),
                pltpu.VMEM((1, count), jnp.int32),
                dma((3,)),
            ],
            hbm=range(3),
            pinned=range(3),
        )
        own, far, near = payload
        came = swap("leaf", near, 1)
        (both,) = kernel(pass_on, [(2 * slots, LANES)], far, came)
        arrived = [own, came, swap("leaf", both, 2)]
        leaf_own, mid_own, root_own = kernel(
            load_sources,
            [(n0, LANES), (n1 // 2, LANES), (n2 // 4, LANES)],
            after(leaf_sources.transpose(0, 2, 1), *payload),
            mid_sources.transpose(0, 1, 3, 2),
            root_sources.transpose(0, 2, 1),
            scratch=[
                pltpu.VMEM((2, COLS, n0), F32),
                pltpu.VMEM((2, COLS, n1), F32),
                pltpu.VMEM((2, COLS, n2), F32),
                dma((3,)),
            ],
            hbm=range(3),
            pinned=range(3),
        )
        (message,) = kernel(
            pack_leaf, [(sum(message_rows(n0, groups * slots)), LANES)], leaf_own, *arrived
        )
    with jax.named_scope("leaf_lower"):
        messages, (ll, l2m) = gather_front(
            message,
            lambda x: load((after(leaf_lower_inv, *x), "leaf"), (leaf_to_mid_lower, "leaf"), pinned=True),
        )
        (y_leaf,) = kernel(
            functools.partial(leaf_lower, groups * slots),
            [(n0, LANES)],
            ll,
            *messages,
            scratch=[pltpu.VMEM((s0, LANES), F32), pltpu.VMEM((fronts, *message.shape), F32)],
        )
    with jax.named_scope("mid_lower"):
        parts, (l2r, ml) = gather_front(
            y_leaf,
            lambda x: load((after(leaf_to_root_lower, *x), "leaf"), (mid_lower_inv, "own"), pinned=True),
        )
        keep, send = gathered(leaf_to_mid, LANES, [(n1 // 2, LANES)] * 2, l2m, parts, mid_own)
        came = swap("leaf", send, 1)
        root_kept, root_sent, y_full = kernel(
            leaf_to_root, [(n2 // 2, LANES)] * 2 + [(s0, LANES)], l2r, after(parts[0], send), *parts[1:]
        )
        (cut_mid,) = kernel(add, [(n1 // 2, LANES)], after(keep, root_kept), came)
        root_came = swap("leaf", root_sent, 1)
        parts, (m2r,) = gather_front(
            cut_mid, lambda x: load((after(mid_to_root_lower, *x), "own"), pinned=True), (root_came,)
        )
        (y_mid,) = gathered(packed_to, 2 * COLS, [(n1 // 2, LANES)], ml, parts)
    with jax.named_scope("root_cut"):
        parts, (rl,) = gather_front(y_mid, lambda x: load((after(root_lower_inv, *x), None)))
        keep, send = gathered(
            mid_to_root, 2 * COLS, [(n2 // 4, LANES)] * 2, m2r, parts, root_kept, root_came, root_own
        )
        came = swap("leaf", send, 2)
        mu, l2r_up = load((after(mid_upper_inv, send), "own"), (leaf_to_root_upper, "leaf"))
        (y_mid_full,) = kernel(
            functools.partial(whole_of, 2 * COLS), [(s1, 2 * COLS)], after(parts[0], send), *parts[1:]
        )
        (cut_root,) = kernel(add, [(n2 // 4, LANES)], after(keep, mu, y_mid_full), came)
    with jax.named_scope("root_solve"):
        parts, (ru,) = gather_front(cut_root, lambda x: load((after(root_upper_inv, *x), None)))
        (y_root,) = gathered(packed_to, COLS, [(n2 // 4, LANES)], rl, parts)
        parts, (m2r_up, l2m_up, lu) = gather_front(
            y_root,
            lambda x: load(
                (after(mid_to_root_upper, *x), "own"), (leaf_to_mid_upper, "leaf"), (leaf_upper_inv, "leaf")
            ),
        )
        (x_root,) = gathered(packed_to, COLS, [(n2 // 4, LANES)], ru, parts)
    with jax.named_scope("mid_upper"):
        send, x_root = kernel(
            root_to_mid,
            [(s1 // 4, LANES), (n2 // 2, LANES)],
            m2r_up,
            x_root,
            swap("leaf", x_root, 2),
        )
        (keep,) = kernel(root_to_mid_kept, [(s1 // 4, LANES)], m2r_up, x_root)
        mine, theirs = sum_front(keep, send)
        (known,) = kernel(functools.partial(own_half, 2 * COLS), [(2 * n1, 4 * COLS)], mu, y_mid_full, mine)
        (x_mid,) = kernel(mid_upper, [(n1 // 2, LANES)], mu, y_mid_full, theirs, known)
        from_root, root_field, root_adjoint = kernel(
            root_to_leaf,
            [(s0, LANES), (2, COLS, n2), (2, COLS, n2)],
            l2r_up,
            x_root,
            swap("leaf", after(x_root, send), 1),
        )
    with jax.named_scope("leaf_upper"):
        x_far = swap("leaf", x_mid, 2)
        send, x_mid = kernel(
            mid_to_leaf,
            [(s0 // 2, LANES), (n1, LANES)],
            l2m_up,
            from_root,
            x_mid,
            swap("leaf", x_mid, 1),
        )
        (keep,) = kernel(mid_to_leaf_kept, [(s0 // 2, LANES)], l2m_up, from_root, x_mid)
        x_other = swap("leaf", x_far, 1)
        mid_field, mid_adjoint = kernel(
            mid_outputs, [(2, 2, COLS, n1)] * 2, x_mid, x_far, x_other
        )
        mine, theirs = sum_front(keep, send, (x_far,), (x_other,))
        (known,) = kernel(functools.partial(own_half, LANES), [(2 * n0, 2 * LANES)], lu, y_full, mine)
        leaf_field, leaf_adjoint = kernel(
            leaf_upper, [(2, COLS, n0)] * 2, lu, y_full, theirs, after(known, mid_field)
        )
    return tuple(
        jnp.swapaxes(x, -1, -2)
        for x in (leaf_field, mid_field, root_field, leaf_adjoint, mid_adjoint, root_adjoint)
    )


def solution(mesh):
    in_specs = (
        P(None, "leaf", "front", None),
        P(None, "leaf", "front", None),
        P(None, "leaf", "front", None),
        P(None, "leaf", "front", None),
        P(None, "leaf", None, "front"),
        P(None, "leaf", None, "front"),
        P(None, None, "front", None),
        P(None, None, "front", None),
        P(None, None, "front", None),
        P(None, None, None, "front"),
        P(None, "front", None),
        P(None, "front", None),
        P(None, ("leaf", "front"), None),
        P(None, None, "front", None),
        P(None, "front", None),
        P(None, ("leaf", "front"), None),
        P(("leaf", "front"), None),
        P(("leaf", "front")),
    )
    out_specs = (
        P(None, ("leaf", "front"), None),
        P(None, None, "front", None),
        P(None, "front", None),
        P(None, ("leaf", "front"), None),
        P(None, None, "front", None),
        P(None, "front", None),
    )
    return jax.shard_map(body, mesh=mesh, in_specs=in_specs, out_specs=out_specs, check_vma=False)
```

```python
import functools

import jax
import jax.numpy as jnp
from jax import lax
from jax.experimental import pallas as pl
from jax.experimental.pallas import tpu as pltpu
from jax.sharding import PartitionSpec as P

CAP = 2
CHUNKS = 4
LANES = 128
COLS = 32
F32 = jnp.float32
BF16 = jnp.bfloat16
VM = pl.BlockSpec(memory_space=pltpu.VMEM)
HB = pl.BlockSpec(memory_space=pltpu.HBM)


def split(x):
    high = x.astype(BF16)
    return high, (x - high.astype(F32)).astype(BF16)


def dot(a, b):
    return jnp.dot(a, b, preferred_element_type=F32)


def complex_dot(matrix, x):
    half = x.shape[1] // 2
    turned = jnp.concatenate([-x[:, half:], x[:, :half]], axis=1)
    both = jnp.concatenate([x, turned], axis=0)
    columns = jnp.concatenate(split(both), axis=1)
    product = dot(matrix, columns)
    rows, n = product.shape[0] // 2, x.shape[1]
    return (product[:rows, n:] + product[rows:, :n]) + product[:rows, :n]


def combined(product):
    rows, n = product.shape[0] // 2, product.shape[1] // 2
    return (product[:rows, n:] + product[rows:, :n]) + product[:rows, :n]


def turn(x, width):
    half = width // 2
    lane = lax.broadcasted_iota(jnp.int32, x.shape, 1) % width
    return jnp.where(lane < half, -pltpu.roll(x, LANES - half, 1), pltpu.roll(x, half, 1))


def spread(x, width):
    high, low = split(x)
    return jnp.concatenate(
        [
            jnp.concatenate([high[:, at : at + width], low[:, at : at + width]], axis=1)
            for at in range(0, LANES, width)
        ],
        axis=0,
    )


def part_dot(matrix, at, blocks, width):
    depth = matrix.shape[1] // 2
    columns = jnp.concatenate([spread(x, width) for x in blocks], axis=0)
    turned = jnp.concatenate([spread(turn(x, width), width) for x in blocks], axis=0)
    count, at = columns.shape[0], pl.multiple_of(at, LANES)
    return dot(matrix[:, pl.ds(at, count)], columns) + dot(matrix[:, pl.ds(depth + at, count)], turned)


def pack(x):
    chunks = LANES // x.shape[1]
    rows = x.shape[0] // chunks
    return jnp.concatenate([x[rows * j : rows * j + rows] for j in range(chunks)], axis=1)


def unpack(x, width):
    return jnp.concatenate([x[:, at : at + width] for at in range(0, LANES, width)], axis=0)


def halves(x):
    c = COLS
    return (
        jnp.concatenate([x[:, :c], x[:, 2 * c : 3 * c]], axis=1),
        jnp.concatenate([x[:, c : 2 * c], x[:, 3 * c :]], axis=1),
    )


def joined(forward, adjoint):
    c = COLS
    return jnp.concatenate([forward[:, :c], adjoint[:, :c], forward[:, c:], adjoint[:, c:]], axis=1)


def own_first(group, forward, adjoint):
    even = (group & 1) == 0
    return jnp.where(even, forward, adjoint), jnp.where(even, adjoint, forward)


def by_solve(group, own, other):
    even = (group & 1) == 0
    return joined(jnp.where(even, own, other), jnp.where(even, other, own))


def assemble(where, parts, here, width=LANES):
    rows = parts[0].shape[0] * (LANES // width)
    for k, part in blocks_of(parts):
        start = pl.multiple_of((here ^ k) * rows, 8)
        where[pl.ds(start, rows), :] = part[...] if width == LANES else unpack(part[...], width)


def fields_of(x, forward, adjoint, where):
    y = x.T
    c = COLS
    forward[(0, *where)] = y[0:c]
    forward[(1, *where)] = y[2 * c : 3 * c]
    adjoint[(0, *where)] = y[c : 2 * c]
    adjoint[(1, *where)] = -y[3 * c :]


def swap(axis, x, k):
    size = lax.axis_size(axis)
    return lax.ppermute(x, axis, [(i, i ^ k) for i in range(size)])


def stack(*refs):
    at = 0
    for ref in refs[:-1]:
        refs[-1][at : at + ref.shape[0], :] = ref[...]
        at += ref.shape[0]


def hops(fronts):
    return [6, 2, 4] if fronts == 8 else list(range(2, fronts, 2))


def gather_front(x, meanwhile=None, others=()):
    fronts = lax.axis_size("front")
    *near, last = [swap("front", x, k) for k in hops(fronts)]
    own = swap("front", x, 1)
    extra = tuple(meanwhile((own,))) if meanwhile else ()
    (both,) = kernel(stack, [(len(near) * x.shape[0], LANES)], after(near[0], *extra, *others), *near[1:])
    last = after(last, *extra, *others)
    return [x, own, last, *near[::-1], swap("front", last, 1), swap("front", both, 1)], extra


def blocks_of(parts):
    rows = parts[0].shape[0]
    *near, last = hops(2 * len(parts) - 6)
    yield 0, parts[0]
    yield 1, parts[1]
    yield last, parts[2]
    yield last + 1, parts[-2]
    for step, (k, part) in enumerate(zip(near, parts[-3:2:-1])):
        yield k, part
        yield k + 1, parts[-1].at[rows * step : rows * step + rows, :]


def kernel(fn, outs, *args, scratch=(), vmem=8, work=0, hbm=(), pinned=()):
    outs = [o if isinstance(o[0], tuple) else (o, F32) for o in outs]
    return pl.pallas_call(
        fn,
        out_shape=[jax.ShapeDtypeStruct(*o) for o in outs],
        in_specs=[HB if i in hbm else VM for i in range(len(args))],
        out_specs=[VM] * len(outs),
        scratch_shapes=list(scratch),
        compiler_params=pltpu.CompilerParams(vmem_limit_bytes=vmem * 2**20),
        cost_estimate=pl.CostEstimate(flops=work, bytes_accessed=work // 700, transcendentals=0),
    )(*(pltpu.with_memory_space_constraint(a, pltpu.HBM) if i in pinned else a for i, a in enumerate(args)))


def chip_product(matrix, k, mine, other, width):
    here = lax.axis_index("front")
    odd = (here & 1) == 1
    blocks = [jnp.where(odd, other, mine), jnp.where(odd, mine, other)]
    return part_dot(matrix, ((here ^ k) // 2) * (2 * mine.shape[0] * (LANES // width)), blocks, width)


def first_products(width, matrix, mine, other, *refs):
    near, both, out = refs[:-2], refs[-2], refs[-1]
    rows = mine.shape[0]
    total = chip_product(matrix, 0, mine[...], other[...], width)
    for step, (k, block) in enumerate(zip(hops(lax.axis_size("front")), near)):
        second = both[rows * step : rows * step + rows, :]
        total += chip_product(matrix, k, block[...], second, width)
    out[...] = total


def last_product(finish, width, count, matrix, *refs):
    parts, rest = refs[:count], refs[count:]
    if count == 3:
        known, mine, other = parts
        k = hops(lax.axis_size("front"))[-1]
        finish(combined(known[...] + chip_product(matrix, k, mine[...], other[...], width)), *rest)
    else:
        assemble(rest[-1], parts, lax.axis_index("front"), width)
        finish(complex_dot(matrix[...], rest[-1][...]), *rest[:-1])


def gathered(finish, width, outs, matrix, parts, *args):
    rows = parts[0].shape[0] * (LANES // width)
    scratch = []
    if 2 * rows % LANES == 0:
        mine, other, last, *near, last_other, both = parts
        shape = (matrix.shape[0], 2 * width)
        (known,) = kernel(
            functools.partial(first_products, width), [shape], matrix, mine, other, *near[::-1], both
        )
        parts = [known, last, last_other]
    else:
        scratch = [pltpu.VMEM((rows * lax.axis_size("front"), width), F32)]
    return kernel(
        functools.partial(last_product, finish, width, len(parts)),
        outs,
        matrix,
        *parts,
        *args,
        scratch=scratch,
    )


def whole_of(width, *refs):
    assemble(refs[-1], refs[:-1], lax.axis_index("front"), width)


def half_product(theirs, width, matrix, y, piece):
    odd = (lax.axis_index("front") & 1) ^ theirs
    rows, chunks = piece.shape[0], LANES // width
    starts = [chunk * 2 * rows + odd * rows for chunk in range(chunks)]
    own = [y[pl.ds(pl.multiple_of(at, 8), rows), :] for at in starts]
    x = jnp.concatenate(own, axis=1) - piece[...]
    if chunks == 1:
        return part_dot(matrix, starts[0], [x], width)
    total, depth = None, matrix.shape[1] // 2
    columns, turned = spread(x, width), spread(turn(x, width), width)
    for chunk, at in enumerate(starts):
        at, span = pl.multiple_of(at, LANES), slice(rows * chunk, rows * chunk + rows)
        part = dot(matrix[:, pl.ds(at, rows)], columns[span])
        part += dot(matrix[:, pl.ds(depth + at, rows)], turned[span])
        total = part if total is None else total + part
    return total


def own_half(width, matrix, y, piece, out):
    out[...] = half_product(0, width, matrix, y, piece)


def load_matrices(picks, *refs):
    count = len(picks)
    sources, outs, buffers, sems = (
        refs[:count],
        refs[count : 2 * count],
        refs[2 * count : 3 * count],
        refs[3 * count],
    )
    parent = lax.axis_index("leaf") // 2
    copies = []
    for i, (src, pick) in enumerate(zip(sources, picks)):
        rows = buffers[i].shape[1]
        step = max(rows // CHUNKS, 16)
        for n, at in enumerate(range(0, rows, step)):
            span = pl.ds(at, step)
            view = src.at[:, span, :] if pick is None else src.at[:, parent if pick == "own" else 0, span, :]
            copy = pltpu.make_async_copy(view, buffers[i].at[:, span, :], sems.at[CHUNKS * i + n])
            copy.start()
            copies.append((i, at, step, copy))
    for i, at, step, copy in copies:
        copy.wait()
        rows, depth = buffers[i].shape[1:]
        for part in range(2):
            high, low = split(buffers[i][part, at : at + step, :])
            outs[i][at : at + step, part * depth : part * depth + depth] = high
            outs[i][rows + at : rows + at + step, part * depth : part * depth + depth] = low


def load(*matrices, pinned=False):
    shapes = [m.shape[-2:] for m, _ in matrices]
    size = sum(r * d for r, d in shapes)
    return kernel(
        functools.partial(load_matrices, tuple(pick for _, pick in matrices)),
        [((2 * r, 2 * d), BF16) for r, d in shapes],
        *[m for m, _ in matrices],
        scratch=[pltpu.VMEM((2, r, d), F32) for r, d in shapes]
        + [pltpu.SemaphoreType.DMA((CHUNKS * len(shapes),))],
        hbm=range(len(shapes)),
        pinned=range(len(shapes)) if pinned else (),
        vmem=4 + -(-size * 8 // 2**20),
        work=size * 1000,
    )


def pack_receivers(fronts, rows, data_hbm, block_hbm, offset_hbm, *refs):
    own, far, near = refs[:3]
    data, block, offset, sems = refs[3:]
    copies = [
        pltpu.make_async_copy(src, dst, sems.at[i])
        for i, (src, dst) in enumerate(((data_hbm, data), (block_hbm, block), (offset_hbm, offset)))
    ]
    for copy in copies:
        copy.start()
    for copy in copies:
        copy.wait()
    group = lax.axis_index("leaf")
    count = data.shape[1]
    slots = fronts * CAP
    down = lax.broadcasted_iota(jnp.int32, (count, count), 0)
    across = lax.broadcasted_iota(jnp.int32, (count, count), 1)
    eye = down == across
    block_row = block[...]
    block_col = jnp.sum(jnp.where(eye, block_row, 0), axis=1, keepdims=True)
    offset_col = jnp.sum(jnp.where(eye, offset[...], 0), axis=1, keepdims=True)
    same = (block_col == block_row) & (down < across)
    slot_row = block_row * CAP + jnp.sum(same.astype(jnp.int32), axis=0, keepdims=True)
    row_col = (block_col & (fronts - 1)) * rows + offset_col + 1
    lane = lax.broadcasted_iota(jnp.int32, (count, COLS), 1)
    index = jnp.where(lane == 0, row_col, 0).astype(F32)
    lines = jnp.concatenate([index, data[0], jnp.zeros((count, COLS), F32), -data[1]], axis=1)
    targets = [group, group ^ 2, group ^ 1, group ^ 3]
    place = lax.broadcasted_iota(jnp.int32, (slots, count), 0)
    pick = jnp.concatenate([place + target * slots == slot_row for target in targets], axis=0)
    picked = jnp.dot(
        pick.astype(F32), lines, precision=lax.Precision.HIGHEST, preferred_element_type=F32
    )
    own[...] = picked[:slots]
    far[...] = picked[slots : 2 * slots]
    near[...] = picked[2 * slots :]


def pass_on(far, came, out):
    rows = far.shape[0]
    out[0:rows, :] = far[...]
    out[rows:, :] = came[rows:, :]


def load_sources(leaf_hbm, mid_hbm, root_hbm, leaf_out, mid_out, root_out, leaf, mid, root, sems):
    group = lax.axis_index("leaf")
    copies = [
        pltpu.make_async_copy(src, dst, sems.at[i])
        for i, (src, dst) in enumerate(
            ((leaf_hbm, leaf), (mid_hbm.at[:, group // 2], mid), (root_hbm, root))
        )
    ]
    for copy in copies:
        copy.start()
    for copy in copies:
        copy.wait()
    forward = ((group & 1) == 0).astype(F32)
    real, imag = leaf[0].T, leaf[1].T
    zero = jnp.zeros_like(real)
    leaf_out[...] = jnp.concatenate([real, zero, imag, zero], axis=1)
    mid_out[...] = pack(jnp.concatenate([mid[0], mid[1]], axis=0).T) * forward
    width = COLS // 2
    low = jnp.concatenate([root[0, :width], root[1, :width]], axis=0)
    high = jnp.concatenate([root[0, width:], root[1, width:]], axis=0)
    root_out[...] = pack(jnp.where(group < 2, low, high).T) * forward


def message_rows(rows, slots):
    return max(rows, slots), 8 * -(-slots // (8 * LANES))


def pack_leaf(own, mine, near, far, out):
    lines = jnp.concatenate([mine[...], near[0 : mine.shape[0], :], far[...]], axis=0)
    slots = lines.shape[0]
    body, tail = message_rows(own.shape[0], slots)
    lane = lax.broadcasted_iota(jnp.int32, (slots, LANES), 1)
    data = jnp.where((lane // COLS) % 2 == 1, lines, 0.0)
    index = lines[:, 0:1]

    def padded(x):
        if x.shape[0] == body:
            return x
        return jnp.concatenate([x, jnp.zeros((body - x.shape[0], LANES), F32)], axis=0)

    out[0:body, :] = padded(own[...]) + padded(data)
    out[body:, :] = jnp.zeros((tail, LANES), F32)
    for at in range(0, slots, LANES):
        size = min(LANES, slots - at)
        eye = lax.broadcasted_iota(jnp.int32, (size, size), 0) == lax.broadcasted_iota(
            jnp.int32, (size, size), 1
        )
        line = jnp.sum(jnp.where(eye, index[at : at + size], 0.0), axis=0, keepdims=True)
        out[body + at // LANES : body + at // LANES + 1, 0:size] = line


def leaf_lower(slots, matrix, *refs):
    parts, (out, rhs, messages) = refs[:-3], refs[-3:]
    rows = out.shape[0]
    here = lax.axis_index("front")
    for k, part in blocks_of(parts):
        messages[here ^ k] = part[...]
    fronts = messages.shape[0]
    total = rows * fronts
    body, _ = message_rows(rows, slots)
    lane = lax.broadcasted_iota(jnp.int32, (slots, LANES), 1)
    taken = (lane // COLS) % 2 == 1
    own = lax.broadcasted_iota(jnp.int32, (rows, LANES), 1)
    own = (own // COLS) % 2 == 0
    for k in range(fronts):
        rhs[rows * k : rows * k + rows, :] = jnp.where(own, messages[k, 0:rows, :], 0.0)
    group = max(1, 512 // slots)
    for k in range(0, fronts, group):
        chosen = range(k, min(k + group, fronts))
        lines = jnp.concatenate([jnp.where(taken, messages[i, 0:slots, :], 0.0) for i in chosen], axis=0)
        index = jnp.concatenate(
            [
                messages[i, body + at // LANES : body + at // LANES + 1, 0 : min(LANES, slots - at)]
                for i in chosen
                for at in range(0, slots, LANES)
            ],
            axis=1,
        )
        row = lax.broadcasted_iota(jnp.int32, (total, index.shape[1]), 0)
        pick = (row + 1 == index.astype(jnp.int32)).astype(BF16)
        both = dot(pick, jnp.concatenate(split(lines), axis=1))
        rhs[...] += both[:, :LANES] + both[:, LANES:]
    out[...] = complex_dot(matrix[...], rhs[...])


def leaf_to_mid(value, sources, keep, send):
    mine, theirs = own_first(lax.axis_index("leaf"), *halves(value))
    keep[...] = sources[...] - pack(mine)
    send[...] = -pack(theirs)


def leaf_to_root(matrix, *refs):
    parts, (keep, send, full) = refs[:-3], refs[-3:]
    assemble(full, parts, lax.axis_index("front"))
    mine, theirs = own_first(lax.axis_index("leaf"), *halves(complex_dot(matrix[...], full[...])))
    keep[...], send[...] = pack(mine), pack(theirs)


def add(*refs):
    total = refs[0][...]
    for ref in refs[1:-1]:
        total = total + ref[...]
    refs[-1][...] = total


def packed_to(value, out):
    out[...] = pack(value)


def mid_to_root(value, kept, came, sources, keep, send):
    cut = -(unpack(kept[...] + came[...], 2 * COLS) + value)
    width = COLS // 2
    low = pack(jnp.concatenate([cut[:, :width], cut[:, COLS : COLS + width]], axis=1))
    high = pack(jnp.concatenate([cut[:, width:COLS], cut[:, COLS + width :]], axis=1))
    first = lax.axis_index("leaf") < 2
    keep[...] = jnp.where(first, low, high) + sources[...]
    send[...] = jnp.where(first, high, low)


def column_half(matrix, x, theirs):
    core = (lax.axis_index("front") & 1) ^ theirs
    half, n = x.shape[1] // 2, x.shape[1]
    turned = jnp.concatenate([-x[:, half:], x[:, :half]], axis=1)
    columns = jnp.concatenate(split(jnp.concatenate([x, turned], axis=0)), axis=1)
    height, chunks = matrix.shape[0] // 2, LANES // n
    rows, pieces = height // chunks // 2, []
    for chunk in range(chunks):
        at = pl.multiple_of((2 * chunk + core) * rows, 16)
        high = dot(matrix[pl.ds(at, rows), :], columns)
        low = dot(matrix[pl.ds(height + at, rows), :], columns[:, :n])
        pieces.append((high[:, n:] + low) + high[:, :n])
    return jnp.concatenate(pieces, axis=1)


def root_to_mid(matrix, mine, other, send, x_root):
    first = lax.axis_index("leaf") < 2
    mine, other = unpack(mine[...], COLS), unpack(other[...], COLS)
    low, high = jnp.where(first, mine, other), jnp.where(first, other, mine)
    width = COLS // 2
    x = jnp.concatenate([low[:, :width], high[:, :width], low[:, width:], high[:, width:]], axis=1)
    x_root[...] = pack(x)
    send[...] = column_half(matrix, x, 1)


def root_to_mid_kept(matrix, x_root, keep):
    keep[...] = column_half(matrix, unpack(x_root[...], 2 * COLS), 0)


def root_to_leaf(matrix, mine, other, out, forward, adjoint):
    x = by_solve(lax.axis_index("leaf"), unpack(mine[...], 2 * COLS), unpack(other[...], 2 * COLS))
    out[...] = complex_dot(matrix[...], x)
    fields_of(x, forward, adjoint, ())


def sum_front(kept, sent, before_last=(), at_end=()):
    fronts = lax.axis_size("front")
    (total,) = kernel(add, [kept.shape], kept, swap("front", sent, 1))
    hops = [1 << i for i in range(1, fronts.bit_length() - 1)]
    for hop, back in zip(hops, hops[::-1]):
        pairs = [(i, i ^ (back if i & 1 else hop)) for i in range(fronts)]
        if hop == hops[-1]:
            total = after(total, *before_last)
        (total,) = kernel(add, [kept.shape], total, lax.ppermute(total, "front", pairs))
    return [total, swap("front", after(total, *at_end), 1)]


def mid_upper(matrix, y, piece, known, out):
    out[...] = pack(combined(known[...] + half_product(1, 2 * COLS, matrix, y, piece)))


def core_rows(ref, theirs):
    rows = ref.shape[0] // 2
    core = (lax.axis_index("front") & 1) ^ theirs
    return ref[pl.ds(pl.multiple_of(core * rows, 8), rows), :]


def mid_to_leaf(matrix, from_root, mine, other, send, x_mid):
    x = by_solve(lax.axis_index("leaf"), unpack(mine[...], 2 * COLS), unpack(other[...], 2 * COLS))
    x_mid[...] = x
    send[...] = column_half(matrix, x, 1) + core_rows(from_root, 1)


def mid_to_leaf_kept(matrix, from_root, x_mid, keep):
    keep[...] = column_half(matrix, x_mid[...], 0) + core_rows(from_root, 0)


def leaf_upper(matrix, y, piece, known, forward, adjoint):
    fields_of(combined(known[...] + half_product(1, LANES, matrix, y, piece)), forward, adjoint, ())


def mid_outputs(mine, far, other, forward, adjoint):
    parent = lax.axis_index("leaf") // 2
    x = by_solve(lax.axis_index("leaf"), unpack(far[...], 2 * COLS), unpack(other[...], 2 * COLS))
    fields_of(mine[...], forward, adjoint, (parent,))
    fields_of(x, forward, adjoint, (1 - parent,))


def after(x, *others):
    return lax.optimization_barrier((x, *others))[0]


def body(
    leaf_lower_inv,
    leaf_upper_inv,
    leaf_to_mid_lower,
    leaf_to_root_lower,
    leaf_to_mid_upper,
    leaf_to_root_upper,
    mid_lower_inv,
    mid_upper_inv,
    mid_to_root_lower,
    mid_to_root_upper,
    root_lower_inv,
    root_upper_inv,
    leaf_sources,
    mid_sources,
    root_sources,
    receiver_data,
    receiver_block,
    receiver_offset,
):
    groups, fronts = lax.axis_size("leaf"), lax.axis_size("front")
    n0, n1, n2 = leaf_sources.shape[1], mid_sources.shape[2], root_sources.shape[1]
    s0, s1, s2 = n0 * fronts, n1 * fronts, n2 * fronts
    slots, count = fronts * CAP, receiver_data.shape[1]
    dma = pltpu.SemaphoreType.DMA

    with jax.named_scope("right_hand_sides"):
        payload = kernel(
            functools.partial(pack_receivers, fronts, n0),
            [(slots, LANES), (slots, LANES), (2 * slots, LANES)],
            receiver_data,
            receiver_block.reshape(1, -1),
            receiver_offset.reshape(1, -1),
            scratch=[
                pltpu.VMEM((2, count, COLS), F32),
                pltpu.VMEM((1, count), jnp.int32),
                pltpu.VMEM((1, count), jnp.int32),
                dma((3,)),
            ],
            hbm=range(3),
            pinned=range(3),
        )
        own, far, near = payload
        came = swap("leaf", near, 1)
        (both,) = kernel(pass_on, [(2 * slots, LANES)], far, came)
        arrived = [own, came, swap("leaf", both, 2)]
        leaf_own, mid_own, root_own = kernel(
            load_sources,
            [(n0, LANES), (n1 // 2, LANES), (n2 // 4, LANES)],
            after(leaf_sources.transpose(0, 2, 1), *payload),
            mid_sources.transpose(0, 1, 3, 2),
            root_sources.transpose(0, 2, 1),
            scratch=[
                pltpu.VMEM((2, COLS, n0), F32),
                pltpu.VMEM((2, COLS, n1), F32),
                pltpu.VMEM((2, COLS, n2), F32),
                dma((3,)),
            ],
            hbm=range(3),
            pinned=range(3),
        )
        (message,) = kernel(
            pack_leaf, [(sum(message_rows(n0, groups * slots)), LANES)], leaf_own, *arrived
        )
    with jax.named_scope("leaf_lower"):
        messages, (ll, l2m) = gather_front(
            message,
            lambda x: load((after(leaf_lower_inv, *x), "leaf"), (leaf_to_mid_lower, "leaf"), pinned=True),
        )
        (y_leaf,) = kernel(
            functools.partial(leaf_lower, groups * slots),
            [(n0, LANES)],
            ll,
            *messages,
            scratch=[pltpu.VMEM((s0, LANES), F32), pltpu.VMEM((fronts, *message.shape), F32)],
        )
    with jax.named_scope("mid_lower"):
        parts, (l2r,) = gather_front(
            y_leaf, lambda x: load((after(leaf_to_root_lower, *x), "leaf"), pinned=True)
        )
        keep, send = gathered(leaf_to_mid, LANES, [(n1 // 2, LANES)] * 2, l2m, parts, mid_own)
        came = swap("leaf", send, 1)
        root_kept, root_sent, y_full = kernel(
            leaf_to_root, [(n2 // 2, LANES)] * 2 + [(s0, LANES)], l2r, after(parts[0], send), *parts[1:]
        )
        (ml,) = load((after(mid_lower_inv, root_kept), "own"), pinned=True)
        (cut_mid,) = kernel(add, [(n1 // 2, LANES)], after(keep, root_kept, ml), came)
        root_came = swap("leaf", root_sent, 1)
        parts, (m2r,) = gather_front(
            cut_mid, lambda x: load((after(mid_to_root_lower, *x), "own"), pinned=True), (root_came,)
        )
        (y_mid,) = gathered(packed_to, 2 * COLS, [(n1 // 2, LANES)], ml, parts)
    with jax.named_scope("root_cut"):
        parts, (rl,) = gather_front(y_mid, lambda x: load((after(root_lower_inv, *x), None)))
        keep, send = gathered(
            mid_to_root, 2 * COLS, [(n2 // 4, LANES)] * 2, m2r, parts, root_kept, root_came, root_own
        )
        came = swap("leaf", send, 2)
        mu, l2r_up = load((after(mid_upper_inv, send), "own"), (leaf_to_root_upper, "leaf"))
        (y_mid_full,) = kernel(
            functools.partial(whole_of, 2 * COLS), [(s1, 2 * COLS)], after(parts[0], send), *parts[1:]
        )
        (cut_root,) = kernel(add, [(n2 // 4, LANES)], after(keep, mu, y_mid_full), came)
    with jax.named_scope("root_solve"):
        parts, (ru,) = gather_front(cut_root, lambda x: load((after(root_upper_inv, *x), None)))
        (y_root,) = gathered(packed_to, COLS, [(n2 // 4, LANES)], rl, parts)
        parts, (m2r_up, l2m_up, lu) = gather_front(
            y_root,
            lambda x: load(
                (after(mid_to_root_upper, *x), "own"), (leaf_to_mid_upper, "leaf"), (leaf_upper_inv, "leaf")
            ),
        )
        (x_root,) = gathered(packed_to, COLS, [(n2 // 4, LANES)], ru, parts)
    with jax.named_scope("mid_upper"):
        send, x_root = kernel(
            root_to_mid,
            [(s1 // 4, LANES), (n2 // 2, LANES)],
            m2r_up,
            x_root,
            swap("leaf", x_root, 2),
        )
        (keep,) = kernel(root_to_mid_kept, [(s1 // 4, LANES)], m2r_up, x_root)
        mine, theirs = sum_front(keep, send)
        (known,) = kernel(functools.partial(own_half, 2 * COLS), [(2 * n1, 4 * COLS)], mu, y_mid_full, mine)
        (x_mid,) = kernel(mid_upper, [(n1 // 2, LANES)], mu, y_mid_full, theirs, known)
        from_root, root_field, root_adjoint = kernel(
            root_to_leaf,
            [(s0, LANES), (2, COLS, n2), (2, COLS, n2)],
            l2r_up,
            x_root,
            swap("leaf", after(x_root, send), 1),
        )
    with jax.named_scope("leaf_upper"):
        x_far = swap("leaf", x_mid, 2)
        send, x_mid = kernel(
            mid_to_leaf,
            [(s0 // 2, LANES), (n1, LANES)],
            l2m_up,
            from_root,
            x_mid,
            swap("leaf", x_mid, 1),
        )
        (keep,) = kernel(mid_to_leaf_kept, [(s0 // 2, LANES)], l2m_up, from_root, x_mid)
        x_other = swap("leaf", x_far, 1)
        mid_field, mid_adjoint = kernel(
            mid_outputs, [(2, 2, COLS, n1)] * 2, x_mid, x_far, x_other
        )
        mine, theirs = sum_front(keep, send, (x_far,), (x_other,))
        (known,) = kernel(functools.partial(own_half, LANES), [(2 * n0, 2 * LANES)], lu, y_full, mine)
        leaf_field, leaf_adjoint = kernel(
            leaf_upper, [(2, COLS, n0)] * 2, lu, y_full, theirs, after(known, mid_field)
        )
    return tuple(
        jnp.swapaxes(x, -1, -2)
        for x in (leaf_field, mid_field, root_field, leaf_adjoint, mid_adjoint, root_adjoint)
    )


def solution(mesh):
    in_specs = (
        P(None, "leaf", "front", None),
        P(None, "leaf", "front", None),
        P(None, "leaf", "front", None),
        P(None, "leaf", "front", None),
        P(None, "leaf", None, "front"),
        P(None, "leaf", None, "front"),
        P(None, None, "front", None),
        P(None, None, "front", None),
        P(None, None, "front", None),
        P(None, None, None, "front"),
        P(None, "front", None),
        P(None, "front", None),
        P(None, ("leaf", "front"), None),
        P(None, None, "front", None),
        P(None, "front", None),
        P(None, ("leaf", "front"), None),
        P(("leaf", "front"), None),
        P(("leaf", "front")),
    )
    out_specs = (
        P(None, ("leaf", "front"), None),
        P(None, None, "front", None),
        P(None, "front", None),
        P(None, ("leaf", "front"), None),
        P(None, None, "front", None),
        P(None, "front", None),
    )
    return jax.shard_map(body, mesh=mesh, in_specs=in_specs, out_specs=out_specs, check_vma=False)
```
